32 devices in a mesh: groups: 2 (over y), ctx: 4 (over z), dp: 2 (over x), mp: 2 (over core).
Axes of the slice: x: 2, y: 2, z: 4, core: 2. Of those that a mesh axis runs over, the one named last changes fastest.
Arguments:
- positions: int32 [4, 512], P(('groups', 'dp')), parts along dimension 0, may hold values from 0 to 4095, as said below
- queries: bfloat16 [4, 1024, 4096], P(('groups', 'dp'), 'ctx', 'mp'), parts along dimension 0, may hold values from -4 to 4
- keys: bfloat16 [4, 1024, 512], P(('groups', 'dp'), 'ctx', 'mp'), parts along dimension 0, may hold values from -36 to 36
- values: bfloat16 [4, 1024, 512], P(('groups', 'dp'), 'ctx', 'mp'), parts along dimension 0, may hold values from -6 to 6
- out_grad: bfloat16 [4, 1024, 4096], P(('groups', 'dp'), 'ctx', 'mp'), parts along dimension 0, may hold values from -6 to 6
Outputs:
- query_grad: bfloat16 [4, 1024, 4096], P(('groups', 'dp'), 'ctx', 'mp'), parts along dimension 0
- key_grad: bfloat16 [4, 1024, 512], P(('groups', 'dp'), 'ctx', 'mp'), parts along dimension 0
- value_grad: bfloat16 [4, 1024, 512], P(('groups', 'dp'), 'ctx', 'mp'), parts along dimension 0
The draws below stay inside these ranges and needn't reach their ends.
There are 2 independent parts, one for each index of `groups`. The reference program is written for one: setup_inputs(seed, part) draws one part's arguments, and reference() takes and returns one part's arrays. A program takes and returns all parts, laid end to end along the dimension named above; each array names one. Nothing has to cross between parts.
Inputs may be any that keep to these rules, and one draw needn't show every extreme that they name: In each sequence the positions rise strictly with the rank; the shard k * 1024 to (k + 1) * 1024 - 1 holds at most 256 of them, and some shard holds exactly 256.
All inputs are finite; a program needn't handle non-finite values.
Results may differ from the reference program's by a relative error of at most 0.007.
The reference program's roundings to bfloat16 on the way count: a program that leaves them out, or rounds other values in their place, can miss the bound.
Values may be sent and summed in bfloat16 or wider, within the bound.
No kernel may reach another device: no remote copies, remote signals or barrier semaphores. Data moves between devices by JAX's collectives and lax.ppermute only.
A program may use at most 128 MiB of HBM per device.

```python
import math
import jax
import jax.numpy as jnp
from jax import lax

HEADS = 32
KV_HEADS = 4
HEAD_DIM = 128
ROWS = 128
TOK_SHARD = 1024
CAP = 256
SLOTS = 1024
ROUTED = 512
BATCH = 2
N_CTX = 4


def normal_block(key, shape, reach):
    return jnp.clip(jax.random.normal(key, shape, jnp.float32), -reach, reach)


def one_layout(key):
    pick_key, swing_key, order_key = jax.random.split(key, 3)
    shard_order = jax.random.permutation(pick_key, N_CTX)
    swing_size = jax.random.randint(swing_key, (N_CTX // 2,), 0, ROWS)
    swing_size = swing_size.at[0].set(ROWS)
    paired = jnp.stack([ROWS + swing_size, ROWS - swing_size], axis=1).reshape(N_CTX)
    counts = jnp.zeros((N_CTX,), jnp.int32).at[shard_order].set(paired.astype(jnp.int32))
    firsts = jnp.cumsum(counts) - counts
    offsets = jnp.arange(TOK_SHARD, dtype=jnp.int32)
    scores = jax.random.randint(order_key, (N_CTX, TOK_SHARD), 0, TOK_SHARD) * TOK_SHARD + offsets[None, :]
    sort_order = jnp.argsort(scores, axis=1)
    place_rank = jnp.argsort(sort_order, axis=1)
    chosen = place_rank < counts[:, None]
    inner_rank = jnp.cumsum(chosen.astype(jnp.int32), axis=1) - 1
    global_rank = jnp.where(chosen, firsts[:, None] + inner_rank, ROUTED)
    shard_ids = jnp.arange(N_CTX, dtype=jnp.int32)
    spots = shard_ids[:, None] * TOK_SHARD + offsets[None, :]
    result = jnp.zeros((ROUTED,), jnp.int32).at[global_rank.reshape(-1)].set(spots.reshape(-1), mode='drop')
    return result


def draw_positions(key, part):
    key = jax.random.fold_in(key, 5)
    layout_keys = jax.random.split(key, BATCH)
    return jax.vmap(one_layout)(layout_keys)


def draw_queries(key, part):
    shape = (BATCH, SLOTS, HEADS * HEAD_DIM)
    field = normal_block(key, shape, 4.0)
    return field.astype(jnp.bfloat16)


def draw_keys(key, part):
    own_key = jax.random.fold_in(key, 9)
    shape = (BATCH, SLOTS, KV_HEADS * HEAD_DIM)
    field = normal_block(own_key, shape, 4.0)
    return field.astype(jnp.bfloat16)


def levels(stream_key, dims, shards, smallest, largest):
    gain, own = 1.0, jax.random.fold_in(stream_key, 6)
    for dim, shards_of in shards:
        draws = jnp.exp(jax.random.uniform(jax.random.fold_in(own, dim), (shards_of,), jnp.float32, smallest / len(shards), largest / len(shards)))
        gain = gain * jnp.repeat(draws, dims[dim] // shards_of).reshape([-1 if axis == dim else 1 for axis in range(len(dims))])
    return gain


def bell_draw(key, extent, spread, most, shards=(), kind=jnp.bfloat16):
    values = jax.random.normal(key, extent, jnp.float32) * spread
    if len(shards) > 0:
        values = levels(key, extent, shards, -0.22, 0.18) * values
    return jnp.clip(values, min=-most, max=most).astype(kind)


def setup_inputs(seed: int = 0, part: int = 0) -> dict:
    splits = jax.random.split(jax.random.key(seed), 6)
    part_splits = jax.random.split(jax.random.fold_in(splits[5], part), 6)
    positions = draw_positions(jax.random.fold_in(jax.random.fold_in(splits[5], part), 71), part)
    queries = draw_queries(jax.random.fold_in(jax.random.fold_in(splits[5], part), 71), part)
    keys = draw_keys(jax.random.fold_in(jax.random.fold_in(splits[5], part), 71), part)
    values = bell_draw(part_splits[3], (BATCH, SLOTS, KV_HEADS * HEAD_DIM), 1.0, 6.0, ((0, 2), (1, 4), (2, 2)))
    out_grad = bell_draw(part_splits[4], (BATCH, SLOTS, HEADS * HEAD_DIM), 1.0, 6.0, ((0, 2), (1, 4), (2, 2)))
    return {"positions": positions, "queries": queries, "keys": keys, "values": values, "out_grad": out_grad}


rope_base = 500000.0

def rope_tables(seq_pos):
    half_dim = HEAD_DIM // 2
    ladder = jnp.arange(half_dim).astype(jnp.float32)
    inverse_freq = jnp.exp(ladder * (-2.0 * math.log(rope_base) / HEAD_DIM))
    angles = seq_pos.astype(jnp.float32)[:, None] * inverse_freq[None, :]
    return (jnp.cos(angles), jnp.sin(angles))

def rotate(field, cos_table, sin_table, rotation):
    half_dim = field.shape[-1] // 2
    front_part = field[..., :half_dim]
    back_part = field[..., half_dim:]
    cos_part = cos_table[:, None, :]
    sin_part = rotation * sin_table[:, None, :]
    return jnp.concatenate([front_part * cos_part - back_part * sin_part, back_part * cos_part + front_part * sin_part], axis=-1)

def one_sequence(seq_pos, queries, keys, values, out_grad):
    rank_ids = jnp.arange(ROUTED, dtype=jnp.int32)
    shard_of = seq_pos // TOK_SHARD
    member = (shard_of[:, None] == jnp.arange(N_CTX, dtype=jnp.int32)[None, :]).astype(jnp.int32)
    counts = lax.optimization_barrier(jnp.sum(member, axis=0))
    firsts = jnp.cumsum(counts) - counts
    slot_of = (shard_of * CAP + rank_ids - jnp.take(firsts, shard_of)).astype(jnp.int32)
    cos_table, sin_table = rope_tables(seq_pos)
    group_size = HEADS // KV_HEADS
    score_scale = 1.0 / math.sqrt(HEAD_DIM)
    query_rows = jnp.take(queries, slot_of, axis=0).reshape(ROUTED, HEADS, HEAD_DIM).astype(jnp.float32)
    query_rot = rotate(query_rows, cos_table, sin_table, 1.0).astype(jnp.bfloat16)
    key_rows = jnp.take(keys, slot_of, axis=0).reshape(ROUTED, KV_HEADS, HEAD_DIM).astype(jnp.float32)
    key_rot = rotate(key_rows, cos_table, sin_table, 1.0).astype(jnp.bfloat16)
    value_rows = jnp.take(values, slot_of, axis=0).reshape(ROUTED, KV_HEADS, HEAD_DIM)
    grad_rows = jnp.take(out_grad, slot_of, axis=0).reshape(ROUTED, KV_HEADS, group_size, HEAD_DIM)
    causal = rank_ids[None, :] <= rank_ids[:, None]

    def one_group(packed):
        query_part, grad_part, key_part, value_part = packed
        query_wide = query_part.astype(jnp.float32)
        grad_wide = grad_part.astype(jnp.float32)
        key_wide = key_part.astype(jnp.float32)
        value_wide = value_part.astype(jnp.float32)
        scores = jnp.einsum('rgd,sd->grs', query_wide, key_wide) * score_scale
        scores = jnp.where(causal[None], scores, -jnp.inf)
        row_peak = lax.optimization_barrier(jnp.max(scores, axis=-1, keepdims=True))
        weights = jnp.exp(scores - row_peak)
        prob_rows = weights / lax.optimization_barrier(jnp.sum(weights, axis=-1, keepdims=True))
        prob_half = prob_rows.astype(jnp.bfloat16)
        prob_grad = jnp.einsum('rgd,sd->grs', grad_wide, value_wide)
        row_delta = lax.optimization_barrier(jnp.sum(prob_rows * prob_grad, axis=-1, keepdims=True))
        score_grad = (prob_rows * (prob_grad - row_delta)).astype(jnp.bfloat16)
        value_term = jnp.einsum('grs,rgd->sd', prob_half.astype(jnp.float32), grad_wide)
        query_term = jnp.einsum('grs,sd->rgd', score_grad.astype(jnp.float32), key_wide) * score_scale
        key_term = jnp.einsum('grs,rgd->sd', score_grad.astype(jnp.float32), query_wide) * score_scale
        return (query_term, key_term, value_term)
    query_term, key_term, value_term = lax.map(one_group, (query_rot.reshape(ROUTED, KV_HEADS, group_size, HEAD_DIM).transpose(1, 0, 2, 3), grad_rows.transpose(1, 0, 2, 3), key_rot.transpose(1, 0, 2), value_rows.transpose(1, 0, 2)))
    query_term = query_term.transpose(1, 0, 2, 3).reshape(ROUTED, HEADS, HEAD_DIM)
    key_term = key_term.transpose(1, 0, 2)
    value_term = value_term.transpose(1, 0, 2)
    query_back = rotate(query_term, cos_table, sin_table, -1.0).astype(jnp.bfloat16).reshape(ROUTED, HEADS * HEAD_DIM)
    key_back = rotate(key_term, cos_table, sin_table, -1.0).astype(jnp.bfloat16).reshape(ROUTED, KV_HEADS * HEAD_DIM)
    value_back = value_term.astype(jnp.bfloat16).reshape(ROUTED, KV_HEADS * HEAD_DIM)
    query_out = jnp.zeros((SLOTS, HEADS * HEAD_DIM), jnp.bfloat16).at[slot_of].set(query_back)
    key_out = jnp.zeros((SLOTS, KV_HEADS * HEAD_DIM), jnp.bfloat16).at[slot_of].set(key_back)
    value_out = jnp.zeros((SLOTS, KV_HEADS * HEAD_DIM), jnp.bfloat16).at[slot_of].set(value_back)
    return (query_out, key_out, value_out)

def run_sequence(packed):
    seq_pos, queries, keys, values, out_grad = packed
    return one_sequence(seq_pos, queries, keys, values, out_grad)

def reference(positions, queries, keys, values, out_grad):
    query_grad, key_grad, value_grad = lax.map(run_sequence, (positions, queries, keys, values, out_grad))
    return (query_grad, key_grad, value_grad)
```

```python
import functools
import math

import jax
import jax.numpy as jnp
from jax import lax
from jax.experimental import pallas as pl
from jax.experimental.pallas import tpu as pltpu
from jax.sharding import PartitionSpec as P

HEAD_DIM = 128
TOK_SHARD = 1024
ROPE_BASE = 500000.0
SCORE_SCALE = 1.0 / math.sqrt(HEAD_DIM)
EXP2_SCALE = SCORE_SCALE * math.log2(math.e)
HIDDEN = -1e30


def rope_tables(seq_pos):
    half_dim = HEAD_DIM // 2
    ladder = jnp.arange(half_dim).astype(jnp.float32)
    inverse_freq = jnp.exp(ladder * (-2.0 * math.log(ROPE_BASE) / HEAD_DIM))
    angles = seq_pos.astype(jnp.float32)[:, None] * inverse_freq[None, :]
    cos_part, sin_part = jnp.cos(angles), jnp.sin(angles)
    return (
        jnp.concatenate([cos_part, cos_part], axis=-1),
        jnp.concatenate([-sin_part, sin_part], axis=-1),
    )


def rotate(field, cos_full, sin_full, rotation):
    rows, width = field.shape
    half_dim = HEAD_DIM // 2
    heads = field.reshape(rows, width // HEAD_DIM, HEAD_DIM).astype(jnp.float32)
    swapped = jnp.concatenate([heads[..., half_dim:], heads[..., :half_dim]], axis=-1)
    turned = heads * cos_full[:, None, :] + swapped * (rotation * sin_full[:, None, :])
    return turned.reshape(rows, width)


def dot(left, right, contract):
    return lax.dot_general(left, right, (contract, ((), ())), preferred_element_type=jnp.float32)


def attention_kernel(
    hops,
    key_heads,
    group_size,
    step_heads,
    meta_ref,
    cos_ref,
    sin_ref,
    query_ref,
    grad_ref,
    *refs,
):
    blocks = refs[:hops]
    dq_ref, dkv_ref, key_ref, value_ref, key_t_ref, bias_ref = refs[hops:]
    slots = query_ref.shape[0]
    routed = dkv_ref.shape[0]
    width = key_heads * HEAD_DIM
    my_first, my_count = meta_ref[hops], meta_ref[hops + 1]

    key_rank = lax.broadcasted_iota(jnp.int32, (routed, slots), 0)
    slot_id = lax.broadcasted_iota(jnp.int32, (routed, slots), 1)
    gap = key_rank - slot_id
    ranked = None
    for hop in range(hops):
        named = (gap == meta_ref[hop]) & (slot_id < meta_ref[hops + 2 + hop])
        term = dot(named.astype(jnp.float32).astype(jnp.bfloat16), blocks[hop][...], ((1,), (0,)))
        ranked = term if ranked is None else ranked + term
    key_ref[...] = ranked[:, :width].astype(jnp.bfloat16)
    value_ref[...] = ranked[:, width:].astype(jnp.bfloat16)
    for head in range(key_heads):
        key_t_ref[head] = ranked[:, head * HEAD_DIM : (head + 1) * HEAD_DIM].T.astype(jnp.bfloat16)
    bias_ref[...] = jnp.where(gap <= my_first, 0.0, HIDDEN)
    dkv_ref[...] = jnp.zeros_like(dkv_ref)
    live = lax.broadcasted_iota(jnp.int32, (slots, HEAD_DIM), 0) < my_count

    for key_head in range(key_heads):
        lanes = slice(key_head * HEAD_DIM, (key_head + 1) * HEAD_DIM)
        value_lanes = slice(width + key_head * HEAD_DIM, width + (key_head + 1) * HEAD_DIM)

        def step(index, carry):
            queries, grads, probs, score_grads = [], [], [], []
            for part in range(step_heads):
                head = key_head * group_size + index * step_heads + part
                columns = pl.ds(pl.multiple_of(head * HEAD_DIM, HEAD_DIM), HEAD_DIM)
                query = query_ref[:, columns].astype(jnp.float32)
                query = query * cos_ref[...] + pltpu.roll(query, HEAD_DIM // 2, 1) * sin_ref[...]
                query = jnp.where(live, query, 0.0).astype(jnp.bfloat16)
                grad = jnp.where(live, grad_ref[:, columns].astype(jnp.float32), 0.0)
                grad = grad.astype(jnp.bfloat16)
                scores = dot(key_ref[:, lanes], query, ((1,), (1,))) + bias_ref[...]
                prob_grad = dot(value_ref[:, lanes], grad, ((1,), (1,)))
                peak = jnp.max(scores, axis=0, keepdims=True)
                weights = jnp.exp2((scores - peak) * EXP2_SCALE)
                inverse = 1.0 / jnp.sum(weights, axis=0, keepdims=True)
                delta = jnp.sum(weights * prob_grad, axis=0, keepdims=True) * inverse
                prob = weights * inverse
                score_grad = (prob * (prob_grad - delta)).astype(jnp.bfloat16)
                turned = dot(key_t_ref[key_head], score_grad, ((1,), (0,))) * SCORE_SCALE
                turned = turned.T
                turned = turned * cos_ref[...] - pltpu.roll(turned, HEAD_DIM // 2, 1) * sin_ref[...]
                dq_ref[:, columns] = turned.astype(jnp.bfloat16)
                queries.append(query)
                grads.append(grad)
                probs.append(prob.astype(jnp.bfloat16))
                score_grads.append(score_grad)
            dkv_ref[:, lanes] += dot(
                jnp.concatenate(score_grads, axis=1),
                jnp.concatenate(queries, axis=0),
                ((1,), (0,)),
            )
            dkv_ref[:, value_lanes] += dot(
                jnp.concatenate(probs, axis=1), jnp.concatenate(grads, axis=0), ((1,), (0,))
            )
            return carry

        lax.fori_loop(0, group_size // step_heads, step, 0)
    dkv_ref[:, :width] = dkv_ref[:, :width] * SCORE_SCALE


def attention(meta, cos_full, sin_full, queries, out_grad, blocks, routed):
    slots, width = blocks[0].shape
    key_heads = width // HEAD_DIM // 2
    heads = queries.shape[1] // HEAD_DIM
    step_heads = 2 if routed <= 512 else 1
    whole = pl.BlockSpec(memory_space=pltpu.VMEM)
    flops = 10 * slots * routed * queries.shape[1]
    return pl.pallas_call(
        functools.partial(
            attention_kernel, len(blocks), key_heads, heads // key_heads, step_heads
        ),
        out_shape=(
            jax.ShapeDtypeStruct(queries.shape, jnp.bfloat16),
            jax.ShapeDtypeStruct((routed, width), jnp.float32),
        ),
        in_specs=[pl.BlockSpec(memory_space=pltpu.SMEM)] + [whole] * (4 + len(blocks)),
        out_specs=(whole, whole),
        scratch_shapes=[
            pltpu.VMEM((routed, width // 2), jnp.bfloat16),
            pltpu.VMEM((routed, width // 2), jnp.bfloat16),
            pltpu.VMEM((key_heads, HEAD_DIM, routed), jnp.bfloat16),
            pltpu.VMEM((routed, slots), jnp.float32),
        ],
        compiler_params=pltpu.CompilerParams(vmem_limit_bytes=48 * 1024 * 1024),
        cost_estimate=pl.CostEstimate(
            flops=flops, bytes_accessed=8 * 1024 * 1024, transcendentals=flops // 1280
        ),
        name="attention_backward",
    )(meta, cos_full, sin_full, queries, out_grad, *blocks)


def body(positions, queries, keys, values, out_grad):
    ctx_size = lax.axis_size("ctx")
    ctx_rank = lax.axis_index("ctx")
    seq_pos = positions[0]
    routed = seq_pos.shape[0]
    row_count = routed // ctx_size
    slots = queries.shape[1]
    width = keys.shape[2]
    shard_of = seq_pos // TOK_SHARD
    my_first = jnp.sum((shard_of < ctx_rank).astype(jnp.int32))
    my_count = jnp.sum((shard_of == ctx_rank).astype(jnp.int32))
    padded_pos = jnp.concatenate([seq_pos, jnp.zeros((slots,), jnp.int32)])
    cos_full, sin_full = rope_tables(lax.dynamic_slice(padded_pos, (my_first,), (slots,)))

    own = jnp.concatenate(
        [rotate(keys[0], cos_full, sin_full, 1.0).astype(jnp.bfloat16), values[0]], axis=1
    )
    blocks = [own]
    forward = [(shard, shard + 1) for shard in range(ctx_size - 1)]
    for hop in range(ctx_size - 1):
        blocks.append(lax.ppermute(blocks[-1], "ctx", forward[hop:]))
    blocks = blocks[::-1]
    sources = ctx_rank - jnp.arange(ctx_size - 1, -1, -1, dtype=jnp.int32)
    starts = jnp.sum((shard_of[None, :] < sources[:, None]).astype(jnp.int32), axis=1)
    counts = jnp.sum((shard_of[None, :] == sources[:, None]).astype(jnp.int32), axis=1)
    meta = jnp.concatenate([starts, my_first[None], my_count[None], counts])
    query_grad, terms = attention(
        meta, cos_full, sin_full, queries[0], out_grad[0], blocks, routed
    )

    total = lax.psum_scatter(terms, "ctx", scatter_dimension=0, tiled=True)
    owned_pos = lax.dynamic_slice(seq_pos, (ctx_rank * row_count,), (row_count,))
    cos_owned, sin_owned = rope_tables(owned_pos)
    owned = jnp.concatenate(
        [rotate(total[:, :width], cos_owned, sin_owned, -1.0), total[:, width:]], axis=1
    ).astype(jnp.bfloat16)
    ranked = lax.all_gather(owned, "ctx", axis=0, tiled=True)
    padded = jnp.concatenate([ranked, jnp.zeros((slots, 2 * width), jnp.bfloat16)], axis=0)
    placed = lax.dynamic_slice(padded, (my_first, 0), (slots, 2 * width))
    placed = jnp.where(
        jnp.arange(slots)[:, None] < my_count, placed, jnp.zeros((), jnp.bfloat16)
    )
    return (query_grad[None], placed[None, :, :width], placed[None, :, width:])


def solution(mesh):
    split = P(("groups", "dp"), "ctx", "mp")
    return jax.shard_map(
        body,
        mesh=mesh,
        in_specs=(P(("groups", "dp"), None), split, split, split, split),
        out_specs=(split, split, split),
        check_vma=False,
    )
```

```python
import functools
import math

import jax
import jax.numpy as jnp
import numpy as np
from jax import lax
from jax.experimental import pallas as pl
from jax.experimental.pallas import tpu as pltpu
from jax.sharding import PartitionSpec as P

HEAD_DIM = 128
HALF_DIM = HEAD_DIM // 2
TOK_SHARD = 1024
ROPE_BASE = 500000.0
SCORE_SCALE = 1.0 / math.sqrt(HEAD_DIM)
EXP2_SCALE = SCORE_SCALE * math.log2(math.e)
HIDDEN = -1e30
ALIGN = 16
VMEM_LIMIT = 48 * 1024 * 1024

VMEM = pl.BlockSpec(memory_space=pltpu.VMEM)
SMEM = pl.BlockSpec(memory_space=pltpu.SMEM)


def dot(left, right, contract):
    return lax.dot_general(left, right, (contract, ((), ())), preferred_element_type=jnp.float32)


def turn(field, cos_full, sin_full):
    return field * cos_full + pltpu.roll(field, HALF_DIM, 1) * sin_full


def turn_back(field, cos_full, sin_full):
    return field * cos_full - pltpu.roll(field, HALF_DIM, 1) * sin_full


def rope_rows():
    ladder = np.arange(HALF_DIM, dtype=np.float32)
    exponent = ladder * np.float32(-2.0 * math.log(ROPE_BASE) / HEAD_DIM)
    freq = np.exp(exponent.astype(np.float64)).astype(np.float32)
    sign = np.repeat(np.array([-1.0, 1.0], np.float32), HALF_DIM)
    return np.stack([np.concatenate([freq, freq]), sign])


def prepare_kernel(ctx_size, rows_ref, pos_ref, keys_ref, meta_ref, cos_ref, sin_ref, *key_refs):
    me = lax.axis_index("ctx")
    slots = keys_ref.shape[0]
    pos = pos_ref[...]
    shard_of = pos // TOK_SHARD
    start = jnp.int32(0)
    first = jnp.int32(0)
    my_first = jnp.int32(0)
    my_start = jnp.int32(0)
    my_count = jnp.int32(0)
    for shard in range(ctx_size):
        count = jnp.sum(jnp.where(shard_of == shard, 1.0, 0.0)).astype(jnp.int32)
        meta_ref[shard] = start
        meta_ref[ctx_size + shard] = count
        mine = me == shard
        my_first = jnp.where(mine, first, my_first)
        my_start = jnp.where(mine, start, my_start)
        my_count = jnp.where(mine, count, my_count)
        first = first + count
        start = start + (count + ALIGN - 1) // ALIGN * ALIGN
    meta_ref[2 * ctx_size] = my_start
    meta_ref[2 * ctx_size + 1] = my_count
    meta_ref[2 * ctx_size + 2] = me

    shape = (slots, pos.shape[1])
    gap = lax.broadcasted_iota(jnp.int32, shape, 1) - lax.broadcasted_iota(jnp.int32, shape, 0)
    named = jnp.where(gap == my_first, pos.astype(jnp.float32), 0.0)
    angles = jnp.sum(named, axis=1, keepdims=True) * rows_ref[0:1, :]
    cos_full = jnp.cos(angles)
    sin_full = jnp.sin(angles) * rows_ref[1:2, :]
    cos_ref[...] = cos_full
    sin_ref[...] = sin_full
    for head, key_ref in enumerate(key_refs):
        key = keys_ref[:, head * HEAD_DIM : (head + 1) * HEAD_DIM].astype(jnp.float32)
        key = turn(key, cos_full, sin_full).astype(jnp.bfloat16)
        for shard in range(ctx_size):
            key_ref[shard] = key


def prepare(positions, keys, ctx_size):
    slots, width = keys.shape
    key_heads = width // HEAD_DIM
    table = jax.ShapeDtypeStruct((slots, HEAD_DIM), jnp.float32)
    sent = jax.ShapeDtypeStruct((ctx_size, slots, HEAD_DIM), jnp.bfloat16)
    return pl.pallas_call(
        functools.partial(prepare_kernel, ctx_size),
        out_shape=(
            jax.ShapeDtypeStruct((2 * ctx_size + 3,), jnp.int32),
            table,
            table,
            *[sent] * key_heads,
        ),
        in_specs=[VMEM] * 3,
        out_specs=(SMEM,) + (VMEM,) * (2 + key_heads),
        compiler_params=pltpu.CompilerParams(vmem_limit_bytes=VMEM_LIMIT),
        name="prepare",
    )(jnp.asarray(rope_rows()), positions, keys)


def attention_kernel(
    ctx_size,
    step_heads,
    meta_ref,
    cos_ref,
    sin_ref,
    query_ref,
    grad_ref,
    key_all_ref,
    value_all_ref,
    *refs,
):
    dq_ref, terms_ref, own_ref, key_ref, value_ref, key_t_ref, bias_ref, acc_ref = refs[-8:]
    slots = query_ref.shape[0]
    span = bias_ref.shape[0]
    my_start, my_count, me = [meta_ref[2 * ctx_size + item] for item in range(3)]
    starts = [pl.multiple_of(meta_ref[shard], ALIGN) for shard in range(ctx_size)]

    key_ref[...] = jnp.zeros_like(key_ref)
    value_ref[...] = jnp.zeros_like(value_ref)
    for shard in range(ctx_size):
        key_ref[pl.ds(starts[shard], slots), :] = key_all_ref[shard]
        value_ref[pl.ds(starts[shard], slots), :] = value_all_ref[shard]
    key_t_ref[...] = key_ref[:span, :].astype(jnp.float32).T.astype(jnp.bfloat16)

    place = lax.broadcasted_iota(jnp.int32, (span, slots), 0)
    slot_id = lax.broadcasted_iota(jnp.int32, (span, slots), 1)
    seen = (place >= my_start) & (place - slot_id <= my_start)
    for shard in range(ctx_size):
        count = jnp.where(shard < me, meta_ref[ctx_size + shard], 0)
        seen = seen | ((place >= starts[shard]) & (place < starts[shard] + count))
    bias_ref[...] = jnp.where(seen, 0.0, HIDDEN)
    acc_ref[...] = jnp.zeros_like(acc_ref)
    live = lax.broadcasted_iota(jnp.int32, (slots, HEAD_DIM), 0) < my_count

    def step(index, carry):
        queries, grads, probs, score_grads = [], [], [], []
        for part in range(step_heads):
            head = index * step_heads + part
            columns = pl.ds(pl.multiple_of(head * HEAD_DIM, HEAD_DIM), HEAD_DIM)
            query = turn(query_ref[:, columns].astype(jnp.float32), cos_ref[...], sin_ref[...])
            query = jnp.where(live, query, 0.0).astype(jnp.bfloat16)
            grad = jnp.where(live, grad_ref[:, columns].astype(jnp.float32), 0.0)
            grad = grad.astype(jnp.bfloat16)
            scores = dot(key_ref[:span, :], query, ((1,), (1,))) + bias_ref[...]
            prob_grad = dot(value_ref[:span, :], grad, ((1,), (1,)))
            peak = jnp.max(scores, axis=0, keepdims=True)
            weights = jnp.exp2((scores - peak) * EXP2_SCALE)
            inverse = 1.0 / jnp.sum(weights, axis=0, keepdims=True)
            delta = jnp.sum(weights * prob_grad, axis=0, keepdims=True) * inverse
            prob = weights * inverse
            score_grad = (prob * (prob_grad - delta)).astype(jnp.bfloat16)
            turned = (dot(key_t_ref[...], score_grad, ((1,), (0,))) * SCORE_SCALE).T
            turned = turn_back(turned, cos_ref[...], sin_ref[...])
            dq_ref[:, columns] = turned.astype(jnp.bfloat16)
            queries.append(query)
            grads.append(grad)
            probs.append(prob.astype(jnp.bfloat16))
            score_grads.append(score_grad)
        acc_ref[:span, :HEAD_DIM] += dot(
            jnp.concatenate(score_grads, axis=1), jnp.concatenate(queries, axis=0), ((1,), (0,))
        )
        acc_ref[:span, HEAD_DIM:] += dot(
            jnp.concatenate(probs, axis=1), jnp.concatenate(grads, axis=0), ((1,), (0,))
        )
        return carry

    heads = query_ref.shape[1] // HEAD_DIM
    lax.fori_loop(0, heads // step_heads, step, 0)
    acc_ref[:span, :HEAD_DIM] = acc_ref[:span, :HEAD_DIM] * SCORE_SCALE
    own_ref[...] = acc_ref[pl.ds(pl.multiple_of(my_start, ALIGN), slots), :]
    for shard in range(ctx_size):
        terms_ref[shard] = acc_ref[pl.ds(starts[shard], slots), :].astype(jnp.bfloat16)


def attention(meta, cos_full, sin_full, queries, out_grad, key_all, value_all, routed, head, dq):
    ctx_size, slots, _ = key_all.shape
    width = queries.shape[1] // (value_all.shape[2] // HEAD_DIM)
    span = routed + ctx_size * ALIGN
    columns = pl.BlockSpec((slots, width), lambda step: (0, head))
    whole = lambda *shape: pl.BlockSpec(shape, lambda step: (0,) * len(shape))
    operands = [meta, cos_full, sin_full, queries, out_grad, key_all, value_all]
    in_specs = [
        SMEM,
        whole(slots, HEAD_DIM),
        whole(slots, HEAD_DIM),
        columns,
        columns,
        whole(*key_all.shape),
        pl.BlockSpec((ctx_size, slots, HEAD_DIM), lambda step: (0, 0, head)),
    ]
    aliases = {}
    if dq is not None:
        aliases = {len(operands): 0}
        operands.append(dq)
        in_specs.append(pl.BlockSpec(memory_space=pl.ANY))
    flops = 10 * slots * span * width
    return pl.pallas_call(
        functools.partial(attention_kernel, ctx_size, 4 if routed <= 512 else 1),
        grid=(1,),
        out_shape=(
            jax.ShapeDtypeStruct(queries.shape, jnp.bfloat16),
            jax.ShapeDtypeStruct((ctx_size, slots, 2 * HEAD_DIM), jnp.bfloat16),
            jax.ShapeDtypeStruct((slots, 2 * HEAD_DIM), jnp.float32),
        ),
        in_specs=in_specs,
        out_specs=(columns, whole(ctx_size, slots, 2 * HEAD_DIM), whole(slots, 2 * HEAD_DIM)),
        scratch_shapes=[
            pltpu.VMEM((span + slots, HEAD_DIM), jnp.bfloat16),
            pltpu.VMEM((span + slots, HEAD_DIM), jnp.bfloat16),
            pltpu.VMEM((HEAD_DIM, span), jnp.bfloat16),
            pltpu.VMEM((span, slots), jnp.float32),
            pltpu.VMEM((span + slots, 2 * HEAD_DIM), jnp.float32),
        ],
        input_output_aliases=aliases,
        compiler_params=pltpu.CompilerParams(vmem_limit_bytes=VMEM_LIMIT),
        cost_estimate=pl.CostEstimate(
            flops=flops, bytes_accessed=4 * 1024 * 1024, transcendentals=flops // 1280
        ),
        name="attention_backward",
    )(*operands)


def finish_kernel(ctx_size, key_heads, meta_ref, cos_ref, sin_ref, *refs):
    owns, terms = refs[:key_heads], refs[key_heads : 2 * key_heads]
    key_grad_ref, value_grad_ref = refs[2 * key_heads :]
    my_count, me = meta_ref[2 * ctx_size + 1], meta_ref[2 * ctx_size + 2]
    slots = cos_ref.shape[0]
    live = lax.broadcasted_iota(jnp.int32, (slots, HEAD_DIM), 0) < my_count
    for head in range(key_heads):
        total = owns[head][...]
        for shard in range(ctx_size):
            total += jnp.where(shard > me, terms[head][shard].astype(jnp.float32), 0.0)
        columns = slice(head * HEAD_DIM, (head + 1) * HEAD_DIM)
        turned = turn_back(total[:, :HEAD_DIM], cos_ref[...], sin_ref[...])
        key_grad_ref[:, columns] = jnp.where(live, turned, 0.0).astype(jnp.bfloat16)
        value_grad_ref[:, columns] = jnp.where(live, total[:, HEAD_DIM:], 0.0).astype(jnp.bfloat16)


def finish(meta, cos_full, sin_full, owns, terms):
    ctx_size, slots, _ = terms[0].shape
    key_heads = len(owns)
    grad = jax.ShapeDtypeStruct((slots, key_heads * HEAD_DIM), jnp.bfloat16)
    return pl.pallas_call(
        functools.partial(finish_kernel, ctx_size, key_heads),
        out_shape=(grad, grad),
        in_specs=[SMEM] + [VMEM] * (2 + 2 * key_heads),
        out_specs=(VMEM, VMEM),
        compiler_params=pltpu.CompilerParams(vmem_limit_bytes=VMEM_LIMIT),
        name="finish",
    )(meta, cos_full, sin_full, *owns, *terms)


def exchange(chunks):
    return lax.all_to_all(chunks, "ctx", split_axis=0, concat_axis=0, tiled=True)


def body(positions, queries, keys, values, out_grad):
    ctx_size = lax.axis_size("ctx")
    routed = positions.shape[1]
    value_all = exchange(jnp.broadcast_to(values, (ctx_size, *values.shape[1:])))
    meta, cos_full, sin_full, *own_keys = prepare(positions, keys[0], ctx_size)
    key_alls = [exchange(own_key) for own_key in own_keys]
    dq, owns, arrived = None, [], []
    for head, key_all in enumerate(key_alls):
        dq, terms, own = attention(
            meta, cos_full, sin_full, queries[0], out_grad[0], key_all, value_all, routed, head, dq
        )
        owns.append(own)
        arrived.append(exchange(terms))
    key_grad, value_grad = finish(meta, cos_full, sin_full, owns, arrived)
    return (dq[None], key_grad[None], value_grad[None])


def solution(mesh):
    split = P(("groups", "dp"), "ctx", "mp")
    return jax.shard_map(
        body,
        mesh=mesh,
        in_specs=(P(("groups", "dp"), None), split, split, split, split),
        out_specs=(split, split, split),
        check_vma=False,
    )
```

```python
import functools
import math

import jax
import jax.numpy as jnp
import numpy as np
from jax import lax
from jax.experimental import pallas as pl
from jax.experimental.pallas import tpu as pltpu
from jax.sharding import PartitionSpec as P

HEAD_DIM = 128
HALF_DIM = HEAD_DIM // 2
TOK_SHARD = 1024
ROPE_BASE = 500000.0
SCORE_SCALE = 1.0 / math.sqrt(HEAD_DIM)
EXP2_SCALE = SCORE_SCALE * math.log2(math.e)
HIDDEN = -1e30
ALIGN = 16
CHUNK = 288
MIB = 1024 * 1024

VMEM = pl.BlockSpec(memory_space=pltpu.VMEM)
SMEM = pl.BlockSpec(memory_space=pltpu.SMEM)


def vmem(routed, small, large):
    return pltpu.CompilerParams(vmem_limit_bytes=(small if routed <= 512 else large) * MIB)


def dot(left, right, contract):
    return lax.dot_general(left, right, (contract, ((), ())), preferred_element_type=jnp.float32)


def turn(field, cos_full, sin_full):
    return field * cos_full + pltpu.roll(field, HALF_DIM, 1) * sin_full


def turn_back(field, cos_full, sin_full):
    return field * cos_full - pltpu.roll(field, HALF_DIM, 1) * sin_full


def rope_rows():
    ladder = np.arange(HALF_DIM, dtype=np.float32)
    exponent = ladder * np.float32(-2.0 * math.log(ROPE_BASE) / HEAD_DIM)
    freq = np.exp(exponent.astype(np.float64)).astype(np.float32)
    sign = np.repeat(np.array([-1.0, 1.0], np.float32), HALF_DIM)
    return np.stack([np.concatenate([freq, freq]), sign])


def shard_layout(ctx_size, me, pos, meta_ref):
    shard_of = pos // TOK_SHARD
    for hop in range(2 * ctx_size):
        meta_ref[hop] = 0
    start = jnp.int32(0)
    first = jnp.int32(0)
    my_first = jnp.int32(0)
    for shard in range(ctx_size):
        count = jnp.sum(jnp.where(shard_of == shard, 1.0, 0.0)).astype(jnp.int32)
        my_first = jnp.where(me == shard, first, my_first)

        @pl.when(me >= shard)
        def _():
            meta_ref[me - shard] = start
            meta_ref[ctx_size + me - shard] = count

        first = first + count
        start = start + (count + ALIGN - 1) // ALIGN * ALIGN
    return my_first


def prepare_kernel(ctx_size, rows_ref, pos_ref, keys_ref, values_ref, meta_ref, cos_ref, sin_ref, sent_ref):
    slots, width = keys_ref.shape
    pos = pos_ref[...]
    my_first = shard_layout(ctx_size, lax.axis_index("ctx"), pos, meta_ref)
    shape = (slots, pos.shape[1])
    gap = lax.broadcasted_iota(jnp.int32, shape, 1) - lax.broadcasted_iota(jnp.int32, shape, 0)
    named = jnp.where(gap == my_first, pos.astype(jnp.float32), 0.0)
    angles = jnp.sum(named, axis=1, keepdims=True) * rows_ref[0:1, :]
    cos_full = jnp.cos(angles)
    sin_full = jnp.sin(angles) * rows_ref[1:2, :]
    cos_ref[...] = cos_full
    sin_ref[...] = sin_full
    for lane in range(0, width, HEAD_DIM):
        key = turn(keys_ref[:, lane : lane + HEAD_DIM].astype(jnp.float32), cos_full, sin_full)
        middle = 2 * lane + HEAD_DIM
        sent_ref[:, 2 * lane : middle] = key.astype(jnp.bfloat16)
        sent_ref[:, middle : middle + HEAD_DIM] = values_ref[:, lane : lane + HEAD_DIM]


def prepare(positions, keys, values, ctx_size):
    slots, width = keys.shape
    table = jax.ShapeDtypeStruct((slots, HEAD_DIM), jnp.float32)
    return pl.pallas_call(
        functools.partial(prepare_kernel, ctx_size),
        out_shape=(
            jax.ShapeDtypeStruct((2 * ctx_size,), jnp.int32),
            table,
            table,
            jax.ShapeDtypeStruct((slots, 2 * width), jnp.bfloat16),
        ),
        in_specs=[VMEM] * 4,
        out_specs=(SMEM, VMEM, VMEM, VMEM),
        compiler_params=vmem(positions.shape[1], 16, 32),
        name="prepare",
    )(jnp.asarray(rope_rows()), positions, keys, values)


def queries_kernel(cos_ref, sin_ref, query_ref, grad_ref, turned_ref, turned_t_ref, grad_t_ref):
    for lane in range(0, query_ref.shape[1], HEAD_DIM):
        lanes = slice(lane, lane + HEAD_DIM)
        query = turn(query_ref[:, lanes].astype(jnp.float32), cos_ref[...], sin_ref[...])
        turned_ref[:, lanes] = query.astype(jnp.bfloat16)
        turned_t_ref[lanes, :] = query.T.astype(jnp.bfloat16)
        grad_t_ref[lanes, :] = grad_ref[:, lanes].astype(jnp.float32).T.astype(jnp.bfloat16)


def rotate_queries(cos_full, sin_full, queries, out_grad):
    slots, width = queries.shape
    straight = jax.ShapeDtypeStruct((slots, width), jnp.bfloat16)
    across = jax.ShapeDtypeStruct((width, slots), jnp.bfloat16)
    return pl.pallas_call(
        queries_kernel,
        out_shape=(straight, across, across),
        in_specs=[VMEM] * 4,
        out_specs=(VMEM,) * 3,
        compiler_params=vmem(0, 16, 16),
        cost_estimate=pl.CostEstimate(
            flops=4 * 10**9, bytes_accessed=5 * 1024 * 1024, transcendentals=0
        ),
        name="rotate_queries",
    )(cos_full, sin_full, queries, out_grad)


def stacked(ref, lane, heads):
    parts = [ref[:, lane + h * HEAD_DIM : lane + (h + 1) * HEAD_DIM] for h in range(heads)]
    return jnp.concatenate(parts, axis=0)


def terms_of(probs, score_grads, queries, grads):
    key_term = dot(score_grads, queries, ((1,), (0,))) * SCORE_SCALE
    return jnp.concatenate([key_term, dot(probs, grads, ((1,), (0,)))], axis=1)


def own_rows(my_start, span, slots):
    return pl.multiple_of(jnp.minimum(my_start, span - slots), ALIGN)


def scores_kernel(ctx_size, key_heads, step_heads, meta_ref, turned_ref, grad_ref, turned_t_ref, grad_t_ref, *refs):
    blocks, refs = refs[:ctx_size], refs[ctx_size:]
    terms, refs = refs[: ctx_size - 1], refs[ctx_size - 1 :]
    score_grad_ref, own_prob_ref, key_t_ref, key_ref, bias_ref, prob_ref, acc_ref = refs
    slots = turned_ref.shape[0]
    span = bias_ref.shape[0]
    width = key_heads * HEAD_DIM
    heads = turned_ref.shape[1] // width
    starts = [pl.multiple_of(meta_ref[hop], ALIGN) for hop in range(ctx_size)]
    my_start = starts[0]

    key_ref[...] = jnp.zeros_like(key_ref)
    for hop in range(ctx_size - 1, -1, -1):
        key_ref[pl.ds(starts[hop], slots), :] = blocks[hop][...]
    place = lax.broadcasted_iota(jnp.int32, (span, slots), 0)
    slot_id = lax.broadcasted_iota(jnp.int32, (span, slots), 1)
    seen = (place >= my_start) & (place - slot_id <= my_start)
    for hop in range(1, ctx_size):
        end = starts[hop] + meta_ref[ctx_size + hop]
        seen = seen | ((place >= starts[hop]) & (place < end))
    bias_ref[...] = jnp.where(seen, 0.0, HIDDEN)
    live = lax.broadcasted_iota(jnp.int32, (1, slots), 1) < meta_ref[ctx_size]
    acc_ref[...] = jnp.zeros_like(acc_ref)

    for key_head in range(key_heads):
        lanes = slice(2 * key_head * HEAD_DIM, (2 * key_head + 1) * HEAD_DIM)
        value_lanes = slice((2 * key_head + 1) * HEAD_DIM, 2 * (key_head + 1) * HEAD_DIM)
        key_t = key_ref[:span, lanes].astype(jnp.float32).T.astype(jnp.bfloat16)
        key_t_ref[key_head * HEAD_DIM : (key_head + 1) * HEAD_DIM, :] = key_t

        def step(index, carry):
            for part in range(step_heads):
                head = index * step_heads + part
                row = pl.multiple_of((key_head * heads + head) * HEAD_DIM, HEAD_DIM)
                rows = pl.ds(row, HEAD_DIM)
                columns = pl.ds(pl.multiple_of(head * slots, slots), slots)
                scores = dot(key_ref[:span, lanes], turned_t_ref[rows, :], ((1,), (0,)))
                scores = scores + bias_ref[...]
                prob_grad = dot(key_ref[:span, value_lanes], grad_t_ref[rows, :], ((1,), (0,)))
                peak = jnp.max(scores, axis=0, keepdims=True)
                weights = jnp.exp2((scores - peak) * EXP2_SCALE)
                inverse = 1.0 / jnp.sum(weights, axis=0, keepdims=True)
                delta = jnp.sum(weights * prob_grad, axis=0, keepdims=True) * inverse
                prob = weights * jnp.where(live, inverse, 0.0)
                prob_ref[:, columns] = prob.astype(jnp.bfloat16)
                score_grad = (prob * (prob_grad - delta)).astype(jnp.bfloat16)
                score_grad_ref[key_head, :, columns] = score_grad
            return carry

        lax.fori_loop(0, heads // step_heads, step, 0)
        own_prob_ref[key_head] = prob_ref[pl.ds(own_rows(my_start, span, slots), slots), :]
        for chunk in range(0, span, CHUNK):

            @pl.when(chunk < my_start)
            def _():
                rows = slice(chunk, chunk + CHUNK)
                acc_ref[rows, :] = terms_of(
                    prob_ref[rows, :],
                    score_grad_ref[key_head, rows, :],
                    stacked(turned_ref, key_head * heads * HEAD_DIM, heads),
                    stacked(grad_ref, key_head * heads * HEAD_DIM, heads),
                )

        for hop in range(1, ctx_size):
            term = acc_ref[pl.ds(starts[hop], slots), :].astype(jnp.bfloat16)
            terms[hop - 1][:, 2 * key_head * HEAD_DIM : 2 * (key_head + 1) * HEAD_DIM] = term


def scores(meta, turned, out_grad, turned_t, grad_t, blocks, routed):
    ctx_size = len(blocks)
    slots, width = blocks[0].shape
    key_heads = width // HEAD_DIM // 2
    heads = turned.shape[1] // HEAD_DIM // key_heads
    span = -(-(routed + ctx_size * ALIGN) // CHUNK) * CHUNK
    term = jax.ShapeDtypeStruct((slots, width), jnp.bfloat16)
    outs = pl.pallas_call(
        functools.partial(scores_kernel, ctx_size, key_heads, 4 if routed <= 512 else 1),
        out_shape=(
            *[term] * (ctx_size - 1),
            jax.ShapeDtypeStruct((key_heads, span, heads * slots), jnp.bfloat16),
            jax.ShapeDtypeStruct((key_heads, slots, heads * slots), jnp.bfloat16),
            jax.ShapeDtypeStruct((key_heads * HEAD_DIM, span), jnp.bfloat16),
        ),
        in_specs=[SMEM] + [VMEM] * (4 + ctx_size),
        out_specs=(VMEM,) * (ctx_size + 2),
        scratch_shapes=[
            pltpu.VMEM((span + slots, width), jnp.bfloat16),
            pltpu.VMEM((span, slots), jnp.float32),
            pltpu.VMEM((span, heads * slots), jnp.bfloat16),
            pltpu.VMEM((span + slots, 2 * HEAD_DIM), jnp.float32),
        ],
        compiler_params=vmem(routed, 28, 60),
        cost_estimate=pl.CostEstimate(
            flops=12 * 10**9, bytes_accessed=12 * 1024 * 1024, transcendentals=0
        ),
        name="scores",
    )(meta, turned, out_grad, turned_t, grad_t, *blocks)
    return outs[: ctx_size - 1], outs[ctx_size - 1 :]


def local_kernel(
    key_heads,
    meta_ref,
    cos_ref,
    sin_ref,
    turned_ref,
    grad_ref,
    score_grad_ref,
    own_prob_ref,
    key_t_ref,
    dq_ref,
    own_ref,
    shift_ref,
):
    slots = turned_ref.shape[0]
    heads = turned_ref.shape[1] // HEAD_DIM // key_heads
    first_row = own_rows(meta_ref[0], score_grad_ref.shape[1], slots)
    shift = pl.multiple_of(meta_ref[0] - first_row, ALIGN)
    shift_ref[slots:, :] = jnp.zeros_like(own_ref)
    for key_head in range(key_heads):
        key_t = key_t_ref[key_head * HEAD_DIM : (key_head + 1) * HEAD_DIM, :]
        for head in range(heads):
            score_grad = score_grad_ref[key_head, :, head * slots : (head + 1) * slots]
            grad = (dot(key_t, score_grad, ((1,), (0,))) * SCORE_SCALE).T
            lane = (key_head * heads + head) * HEAD_DIM
            grad = turn_back(grad, cos_ref[...], sin_ref[...])
            dq_ref[:, lane : lane + HEAD_DIM] = grad.astype(jnp.bfloat16)
        lane = key_head * heads * HEAD_DIM
        shift_ref[:slots, 2 * key_head * HEAD_DIM : 2 * (key_head + 1) * HEAD_DIM] = terms_of(
            own_prob_ref[key_head],
            score_grad_ref[key_head, pl.ds(first_row, slots), :],
            stacked(turned_ref, lane, heads),
            stacked(grad_ref, lane, heads),
        )
    own_ref[...] = shift_ref[pl.ds(shift, slots), :]


def local_terms(meta, cos_full, sin_full, turned, out_grad, score_grad, own_prob, key_t):
    slots = turned.shape[0]
    key_heads = score_grad.shape[0]
    return pl.pallas_call(
        functools.partial(local_kernel, key_heads),
        out_shape=(
            jax.ShapeDtypeStruct(turned.shape, jnp.bfloat16),
            jax.ShapeDtypeStruct((slots, 2 * key_heads * HEAD_DIM), jnp.float32),
        ),
        in_specs=[SMEM] + [VMEM] * 7,
        out_specs=(VMEM, VMEM),
        scratch_shapes=[pltpu.VMEM((2 * slots, 2 * key_heads * HEAD_DIM), jnp.float32)],
        compiler_params=vmem(key_t.shape[1] // 2, 24, 48),
        cost_estimate=pl.CostEstimate(
            flops=5 * 10**9, bytes_accessed=10 * 1024 * 1024, transcendentals=0
        ),
        name="local_terms",
    )(meta, cos_full, sin_full, turned, out_grad, score_grad, own_prob, key_t)


def finish_kernel(ctx_size, meta_ref, cos_ref, sin_ref, own_ref, *refs):
    terms, (key_grad_ref, value_grad_ref) = refs[: ctx_size - 1], refs[ctx_size - 1 :]
    slots = own_ref.shape[0]
    live = lax.broadcasted_iota(jnp.int32, (slots, HEAD_DIM), 0) < meta_ref[ctx_size]
    total = own_ref[...]
    for term in terms:
        total += term[...].astype(jnp.float32)
    for lane in range(0, key_grad_ref.shape[1], HEAD_DIM):
        lanes = slice(lane, lane + HEAD_DIM)
        key_term = turn_back(total[:, 2 * lane : 2 * lane + HEAD_DIM], cos_ref[...], sin_ref[...])
        value_term = total[:, 2 * lane + HEAD_DIM : 2 * (lane + HEAD_DIM)]
        key_grad_ref[:, lanes] = jnp.where(live, key_term, 0.0).astype(jnp.bfloat16)
        value_grad_ref[:, lanes] = jnp.where(live, value_term, 0.0).astype(jnp.bfloat16)


def finish(meta, cos_full, sin_full, own, terms):
    slots, width = own.shape
    grad = jax.ShapeDtypeStruct((slots, width // 2), jnp.bfloat16)
    return pl.pallas_call(
        functools.partial(finish_kernel, len(terms) + 1),
        out_shape=(grad, grad),
        in_specs=[SMEM] + [VMEM] * (3 + len(terms)),
        out_specs=(VMEM, VMEM),
        compiler_params=vmem(0, 16, 16),
        name="finish",
    )(meta, cos_full, sin_full, own, *terms)


def part_of(part, size):
    return slice(part * size, (part + 1) * size)


def body(positions, queries, keys, values, out_grad):
    ctx_size = lax.axis_size("ctx")
    routed = positions.shape[1]
    meta, cos_full, sin_full, sent = prepare(positions, keys[0], values[0], ctx_size)
    hops = range(1, ctx_size)
    blocks = [sent]
    for hop in hops:
        pairs = [(shard, shard + hop) for shard in range(ctx_size - hop)]
        blocks.append(lax.ppermute(sent, "ctx", pairs))
    turned, turned_t, grad_t = rotate_queries(cos_full, sin_full, queries[0], out_grad[0])
    parts = 1 if routed <= 512 else keys.shape[2] // HEAD_DIM
    wide, narrow = queries.shape[2] // parts, sent.shape[1] // parts
    terms, local = [], []
    for part in range(parts):
        columns, lanes = part_of(part, wide), part_of(part, narrow)
        outs = scores(
            meta,
            turned[:, columns],
            out_grad[0][:, columns],
            turned_t[columns],
            grad_t[columns],
            [block[:, lanes] for block in blocks],
            routed,
        )
        terms.append(outs[0])
        local.append(outs[1])
    terms = [jnp.concatenate(term, axis=1) for term in zip(*terms)]
    arrived = []
    for hop in hops:
        pairs = [(shard + hop, shard) for shard in range(ctx_size - hop)]
        arrived.append(lax.ppermute(terms[hop - 1], "ctx", pairs))
    finals = []
    for part in range(parts):
        columns = part_of(part, wide)
        finals.append(
            local_terms(
                meta, cos_full, sin_full, turned[:, columns], out_grad[0][:, columns], *local[part]
            )
        )
    dq, own = [jnp.concatenate(final, axis=1) for final in zip(*finals)]
    key_grad, value_grad = finish(meta, cos_full, sin_full, own, arrived)
    return (dq[None], key_grad[None], value_grad[None])


def solution(mesh):
    split = P(("groups", "dp"), "ctx", "mp")
    return jax.shard_map(
        body,
        mesh=mesh,
        in_specs=(P(("groups", "dp"), None), split, split, split, split),
        out_specs=(split, split, split),
        check_vma=False,
    )
```

```python
import functools
import math

import jax
import jax.numpy as jnp
import numpy as np
from jax import lax
from jax.experimental import pallas as pl
from jax.experimental.pallas import tpu as pltpu
from jax.sharding import PartitionSpec as P

HEAD_DIM = 128
HALF_DIM = HEAD_DIM // 2
TOK_SHARD = 1024
ROPE_BASE = 500000.0
SCORE_SCALE = 1.0 / math.sqrt(HEAD_DIM)
EXP2_SCALE = SCORE_SCALE * math.log2(math.e)
HIDDEN = -1e30
ALIGN = 16
CHUNK = 288
MIB = 1024 * 1024

VMEM = pl.BlockSpec(memory_space=pltpu.VMEM)
SMEM = pl.BlockSpec(memory_space=pltpu.SMEM)


def vmem(routed, small, large):
    return pltpu.CompilerParams(vmem_limit_bytes=(small if routed <= 512 else large) * MIB)


def dot(left, right, contract):
    return lax.dot_general(left, right, (contract, ((), ())), preferred_element_type=jnp.float32)


def turn(field, cos_full, sin_full):
    return field * cos_full + pltpu.roll(field, HALF_DIM, 1) * sin_full


def turn_back(field, cos_full, sin_full):
    return field * cos_full - pltpu.roll(field, HALF_DIM, 1) * sin_full


def rope_rows():
    ladder = np.arange(HALF_DIM, dtype=np.float32)
    exponent = ladder * np.float32(-2.0 * math.log(ROPE_BASE) / HEAD_DIM)
    freq = np.exp(exponent.astype(np.float64)).astype(np.float32)
    sign = np.repeat(np.array([-1.0, 1.0], np.float32), HALF_DIM)
    return np.stack([np.concatenate([freq, freq]), sign])


def shard_layout(ctx_size, me, pos, meta_ref):
    shard_of = pos // TOK_SHARD
    for hop in range(2 * ctx_size):
        meta_ref[hop] = 0
    start = jnp.int32(0)
    first = jnp.int32(0)
    my_first = jnp.int32(0)
    for shard in range(ctx_size):
        count = jnp.sum(jnp.where(shard_of == shard, 1.0, 0.0)).astype(jnp.int32)
        my_first = jnp.where(me == shard, first, my_first)

        @pl.when(me >= shard)
        def _():
            meta_ref[me - shard] = start
            meta_ref[ctx_size + me - shard] = count

        first = first + count
        start = start + (count + ALIGN - 1) // ALIGN * ALIGN
    return my_first


def prepare_kernel(
    ctx_size, rows_hbm, pos_hbm, keys_hbm, values_hbm, meta_ref, cos_ref, sin_ref, *refs
):
    sent_refs, (rows_ref, pos_ref, keys_ref, values_ref, sems) = refs[:-5], refs[-5:]
    sources = (pos_hbm, rows_hbm, keys_hbm, values_hbm)
    targets = (pos_ref, rows_ref, keys_ref, values_ref)
    copies = [
        pltpu.make_async_copy(source, target, sems.at[index])
        for index, (source, target) in enumerate(zip(sources, targets))
    ]
    for copy in copies:
        copy.start()
    copies[0].wait()
    slots = keys_ref.shape[0]
    pos = pos_ref[...]
    my_first = shard_layout(ctx_size, lax.axis_index("ctx"), pos, meta_ref)
    shape = (slots, pos.shape[1])
    gap = lax.broadcasted_iota(jnp.int32, shape, 1) - lax.broadcasted_iota(jnp.int32, shape, 0)
    named = jnp.where(gap == my_first, pos.astype(jnp.float32), 0.0)
    copies[1].wait()
    angles = jnp.sum(named, axis=1, keepdims=True) * rows_ref[0:1, :]
    cos_full = jnp.cos(angles)
    sin_full = jnp.sin(angles) * rows_ref[1:2, :]
    cos_ref[...] = cos_full
    sin_ref[...] = sin_full
    copies[2].wait()
    copies[3].wait()
    for head, sent_ref in enumerate(sent_refs):
        lanes = slice(head * HEAD_DIM, (head + 1) * HEAD_DIM)
        key = turn(keys_ref[:, lanes].astype(jnp.float32), cos_full, sin_full)
        sent_ref[:, :HEAD_DIM] = key.astype(jnp.bfloat16)
        sent_ref[:, HEAD_DIM:] = values_ref[:, lanes]


def prepare(positions, keys, values, ctx_size):
    slots, width = keys.shape
    rows = jnp.asarray(rope_rows())
    table = jax.ShapeDtypeStruct((slots, HEAD_DIM), jnp.float32)
    sent = jax.ShapeDtypeStruct((slots, 2 * HEAD_DIM), jnp.bfloat16)
    operands = (rows, positions, keys, values)
    return pl.pallas_call(
        functools.partial(prepare_kernel, ctx_size),
        out_shape=(
            jax.ShapeDtypeStruct((2 * ctx_size,), jnp.int32),
            table,
            table,
            *[sent] * (width // HEAD_DIM),
        ),
        in_specs=[pl.BlockSpec(memory_space=pl.ANY)] * 4,
        out_specs=(SMEM,) + (VMEM,) * (2 + width // HEAD_DIM),
        scratch_shapes=[pltpu.VMEM(operand.shape, operand.dtype) for operand in operands]
        + [pltpu.SemaphoreType.DMA((4,))],
        compiler_params=vmem(positions.shape[1], 60, 60),
        name="prepare",
    )(*operands)


def queries_kernel(cos_ref, sin_ref, query_ref, grad_ref, turned_ref, turned_t_ref, grad_t_ref):
    for lane in range(0, query_ref.shape[1], HEAD_DIM):
        lanes = slice(lane, lane + HEAD_DIM)
        query = turn(query_ref[:, lanes].astype(jnp.float32), cos_ref[...], sin_ref[...])
        turned_ref[:, lanes] = query.astype(jnp.bfloat16)
        turned_t_ref[lanes, :] = query.T.astype(jnp.bfloat16)
        grad_t_ref[lanes, :] = grad_ref[:, lanes].astype(jnp.float32).T.astype(jnp.bfloat16)


def rotate_queries(cos_full, sin_full, queries, out_grad):
    slots, width = queries.shape
    straight = jax.ShapeDtypeStruct((slots, width), jnp.bfloat16)
    across = jax.ShapeDtypeStruct((width, slots), jnp.bfloat16)
    return pl.pallas_call(
        queries_kernel,
        out_shape=(straight, across, across),
        in_specs=[VMEM] * 4,
        out_specs=(VMEM,) * 3,
        compiler_params=vmem(0, 16, 16),
        cost_estimate=pl.CostEstimate(
            flops=4 * 10**9, bytes_accessed=5 * 1024 * 1024, transcendentals=0
        ),
        name="rotate_queries",
    )(cos_full, sin_full, queries, out_grad)


def stacked(ref, lane, heads):
    parts = [ref[:, lane + h * HEAD_DIM : lane + (h + 1) * HEAD_DIM] for h in range(heads)]
    return jnp.concatenate(parts, axis=0)


def terms_of(probs, score_grads, queries, grads):
    key_term = dot(score_grads, queries, ((1,), (0,))) * SCORE_SCALE
    return jnp.concatenate([key_term, dot(probs, grads, ((1,), (0,)))], axis=1)


def own_rows(my_start, span, slots):
    return pl.multiple_of(jnp.minimum(my_start, span - slots), ALIGN)


def scores_kernel(ctx_size, key_heads, step_heads, meta_ref, turned_ref, grad_ref, turned_t_ref, grad_t_ref, *refs):
    blocks, refs = refs[: ctx_size * key_heads], refs[ctx_size * key_heads :]
    terms, refs = refs[: ctx_size - 1], refs[ctx_size - 1 :]
    score_grad_ref, own_prob_ref, key_t_ref, key_ref, bias_ref, prob_ref, acc_ref = refs
    slots = turned_ref.shape[0]
    span = bias_ref.shape[0]
    width = key_heads * HEAD_DIM
    heads = turned_ref.shape[1] // width
    starts = [pl.multiple_of(meta_ref[hop], ALIGN) for hop in range(ctx_size)]
    my_start = starts[0]
    sent_hops = list(range(1, ctx_size))
    if relayed(ctx_size):
        last = lax.axis_index("ctx") == ctx_size - 1
        sent_hops = [jnp.where(last, 3, 1), 2, jnp.where(last, 1, 2)]

    key_ref[...] = jnp.zeros_like(key_ref)
    for hop in range(ctx_size - 1, -1, -1):
        for head in range(key_heads):
            lanes = slice(2 * head * HEAD_DIM, 2 * (head + 1) * HEAD_DIM)
            key_ref[pl.ds(starts[hop], slots), lanes] = blocks[head * ctx_size + hop][...]
    place = lax.broadcasted_iota(jnp.int32, (span, slots), 0)
    slot_id = lax.broadcasted_iota(jnp.int32, (span, slots), 1)
    seen = (place >= my_start) & (place - slot_id <= my_start)
    for hop in range(1, ctx_size):
        end = starts[hop] + meta_ref[ctx_size + hop]
        seen = seen | ((place >= starts[hop]) & (place < end))
    bias_ref[...] = jnp.where(seen, 0.0, HIDDEN)
    live = lax.broadcasted_iota(jnp.int32, (1, slots), 1) < meta_ref[ctx_size]
    acc_ref[...] = jnp.zeros_like(acc_ref)

    for key_head in range(key_heads):
        lanes = slice(2 * key_head * HEAD_DIM, (2 * key_head + 1) * HEAD_DIM)
        value_lanes = slice((2 * key_head + 1) * HEAD_DIM, 2 * (key_head + 1) * HEAD_DIM)
        key_t = key_ref[:span, lanes].astype(jnp.float32).T.astype(jnp.bfloat16)
        key_t_ref[key_head * HEAD_DIM : (key_head + 1) * HEAD_DIM, :] = key_t

        def step(index, carry):
            for part in range(step_heads):
                head = index * step_heads + part
                row = pl.multiple_of((key_head * heads + head) * HEAD_DIM, HEAD_DIM)
                rows = pl.ds(row, HEAD_DIM)
                columns = pl.ds(pl.multiple_of(head * slots, slots), slots)
                scores = dot(key_ref[:span, lanes], turned_t_ref[rows, :], ((1,), (0,)))
                scores = scores + bias_ref[...]
                prob_grad = dot(key_ref[:span, value_lanes], grad_t_ref[rows, :], ((1,), (0,)))
                peak = jnp.max(scores, axis=0, keepdims=True)
                weights = jnp.exp2((scores - peak) * EXP2_SCALE)
                inverse = 1.0 / jnp.sum(weights, axis=0, keepdims=True)
                delta = jnp.sum(weights * prob_grad, axis=0, keepdims=True) * inverse
                prob = weights * jnp.where(live, inverse, 0.0)
                prob_ref[:, columns] = prob.astype(jnp.bfloat16)
                score_grad = (prob * (prob_grad - delta)).astype(jnp.bfloat16)
                score_grad_ref[key_head, :, columns] = score_grad
            return carry

        lax.fori_loop(0, heads // step_heads, step, 0)
        own_prob_ref[key_head] = prob_ref[pl.ds(own_rows(my_start, span, slots), slots), :]
        for chunk in range(0, span, CHUNK):

            @pl.when(chunk < my_start)
            def _():
                rows = slice(chunk, chunk + CHUNK)
                acc_ref[rows, :] = terms_of(
                    prob_ref[rows, :],
                    score_grad_ref[key_head, rows, :],
                    stacked(turned_ref, key_head * heads * HEAD_DIM, heads),
                    stacked(grad_ref, key_head * heads * HEAD_DIM, heads),
                )

        for hop, term_ref in zip(sent_hops, terms):
            start = pl.multiple_of(meta_ref[hop], ALIGN)
            term = acc_ref[pl.ds(start, slots), :].astype(term_ref.dtype)
            term_ref[:, 2 * key_head * HEAD_DIM : 2 * (key_head + 1) * HEAD_DIM] = term


def relayed(ctx_size):
    return ctx_size == 4


def scores(meta, turned, out_grad, turned_t, grad_t, blocks, routed):
    key_heads, ctx_size = len(blocks), len(blocks[0])
    slots = turned.shape[0]
    width = 2 * key_heads * HEAD_DIM
    heads = turned.shape[1] // HEAD_DIM // key_heads
    span = -(-(routed + ctx_size * ALIGN) // CHUNK) * CHUNK
    terms = [jax.ShapeDtypeStruct((slots, width), jnp.bfloat16)] * (ctx_size - 1)
    if relayed(ctx_size):
        terms[2] = jax.ShapeDtypeStruct((slots, width), jnp.float32)
    outs = pl.pallas_call(
        functools.partial(scores_kernel, ctx_size, key_heads, 4 if routed <= 512 else 1),
        out_shape=(
            *terms,
            jax.ShapeDtypeStruct((key_heads, span, heads * slots), jnp.bfloat16),
            jax.ShapeDtypeStruct((key_heads, slots, heads * slots), jnp.bfloat16),
            jax.ShapeDtypeStruct((key_heads * HEAD_DIM, span), jnp.bfloat16),
        ),
        in_specs=[SMEM] + [VMEM] * (4 + ctx_size * key_heads),
        out_specs=(VMEM,) * (ctx_size + 2),
        scratch_shapes=[
            pltpu.VMEM((span + slots, width), jnp.bfloat16),
            pltpu.VMEM((span, slots), jnp.float32),
            pltpu.VMEM((span, heads * slots), jnp.bfloat16),
            pltpu.VMEM((span + slots, 2 * HEAD_DIM), jnp.float32),
        ],
        compiler_params=vmem(routed, 28, 60),
        cost_estimate=pl.CostEstimate(
            flops=12 * 10**9, bytes_accessed=12 * 1024 * 1024, transcendentals=0
        ),
        name="scores",
    )(meta, turned, out_grad, turned_t, grad_t, *[block for head in blocks for block in head])
    return outs[: ctx_size - 1], outs[ctx_size - 1 :]


def local_kernel(
    key_heads,
    meta_ref,
    cos_ref,
    sin_ref,
    turned_ref,
    grad_ref,
    score_grad_ref,
    own_prob_ref,
    key_t_ref,
    dq_ref,
    own_ref,
    shift_ref,
):
    slots = turned_ref.shape[0]
    heads = turned_ref.shape[1] // HEAD_DIM // key_heads
    first_row = own_rows(meta_ref[0], score_grad_ref.shape[1], slots)
    shift = pl.multiple_of(meta_ref[0] - first_row, ALIGN)
    shift_ref[slots:, :] = jnp.zeros_like(own_ref)
    for key_head in range(key_heads):
        key_t = key_t_ref[key_head * HEAD_DIM : (key_head + 1) * HEAD_DIM, :]
        for head in range(heads):
            score_grad = score_grad_ref[key_head, :, head * slots : (head + 1) * slots]
            grad = (dot(key_t, score_grad, ((1,), (0,))) * SCORE_SCALE).T
            lane = (key_head * heads + head) * HEAD_DIM
            grad = turn_back(grad, cos_ref[...], sin_ref[...])
            dq_ref[:, lane : lane + HEAD_DIM] = grad.astype(jnp.bfloat16)
        lane = key_head * heads * HEAD_DIM
        shift_ref[:slots, 2 * key_head * HEAD_DIM : 2 * (key_head + 1) * HEAD_DIM] = terms_of(
            own_prob_ref[key_head],
            score_grad_ref[key_head, pl.ds(first_row, slots), :],
            stacked(turned_ref, lane, heads),
            stacked(grad_ref, lane, heads),
        )
    own_ref[...] = shift_ref[pl.ds(shift, slots), :]


def local_terms(meta, cos_full, sin_full, turned, out_grad, score_grad, own_prob, key_t):
    slots = turned.shape[0]
    key_heads = score_grad.shape[0]
    return pl.pallas_call(
        functools.partial(local_kernel, key_heads),
        out_shape=(
            jax.ShapeDtypeStruct(turned.shape, jnp.bfloat16),
            jax.ShapeDtypeStruct((slots, 2 * key_heads * HEAD_DIM), jnp.float32),
        ),
        in_specs=[SMEM] + [VMEM] * 7,
        out_specs=(VMEM, VMEM),
        scratch_shapes=[pltpu.VMEM((2 * slots, 2 * key_heads * HEAD_DIM), jnp.float32)],
        compiler_params=vmem(key_t.shape[1] // 2, 24, 48),
        cost_estimate=pl.CostEstimate(
            flops=5 * 10**9, bytes_accessed=10 * 1024 * 1024, transcendentals=0
        ),
        name="local_terms",
    )(meta, cos_full, sin_full, turned, out_grad, score_grad, own_prob, key_t)


def finish_kernel(ctx_size, meta_ref, cos_ref, sin_ref, own_ref, *refs):
    terms, (key_grad_ref, value_grad_ref) = refs[: ctx_size - 1], refs[ctx_size - 1 :]
    slots = own_ref.shape[0]
    live = lax.broadcasted_iota(jnp.int32, (slots, HEAD_DIM), 0) < meta_ref[ctx_size]
    total = own_ref[...]
    for index, term in enumerate(terms):
        term = term[...].astype(jnp.float32)
        if index == 0 and relayed(ctx_size):
            term = jnp.where(lax.axis_index("ctx") == 2, 0.0, term)
        total += term
    for lane in range(0, key_grad_ref.shape[1], HEAD_DIM):
        lanes = slice(lane, lane + HEAD_DIM)
        key_term = turn_back(total[:, 2 * lane : 2 * lane + HEAD_DIM], cos_ref[...], sin_ref[...])
        value_term = total[:, 2 * lane + HEAD_DIM : 2 * (lane + HEAD_DIM)]
        key_grad_ref[:, lanes] = jnp.where(live, key_term, 0.0).astype(jnp.bfloat16)
        value_grad_ref[:, lanes] = jnp.where(live, value_term, 0.0).astype(jnp.bfloat16)


def finish(meta, cos_full, sin_full, own, terms):
    slots, width = own.shape
    grad = jax.ShapeDtypeStruct((slots, width // 2), jnp.bfloat16)
    return pl.pallas_call(
        functools.partial(finish_kernel, len(terms) + 1),
        out_shape=(grad, grad),
        in_specs=[SMEM] + [VMEM] * (3 + len(terms)),
        out_specs=(VMEM, VMEM),
        compiler_params=vmem(0, 16, 16),
        name="finish",
    )(meta, cos_full, sin_full, own, *terms)


def part_of(part, size):
    return slice(part * size, (part + 1) * size)


def climb(sent, ctx_size):
    blocks = [sent]
    for hop in range(1, ctx_size):
        pairs = [(shard, shard + 1) for shard in range(hop - 1, ctx_size - 1)]
        blocks.append(lax.ppermute(blocks[-1], "ctx", pairs))
    return blocks


def relay(first, second, third):
    first = lax.ppermute(first, "ctx", [(3, 2), (2, 1), (1, 0)])
    second = lax.ppermute(second, "ctx", [(3, 1)])
    third = (third + first.astype(jnp.float32)).astype(jnp.bfloat16)
    return [first, second, lax.ppermute(third, "ctx", [(3, 2), (2, 0)])]


def descend(terms, ctx_size):
    arrived = []
    for hop, term in enumerate(terms, 1):
        pairs = [(shard + hop, shard) for shard in range(ctx_size - hop)]
        arrived.append(lax.ppermute(term, "ctx", pairs))
    return arrived


def body(positions, queries, keys, values, out_grad):
    ctx_size = lax.axis_size("ctx")
    routed = positions.shape[1]
    meta, cos_full, sin_full, *sent = prepare(positions, keys[0], values[0], ctx_size)
    blocks = [climb(head, ctx_size) for head in sent]
    turned, turned_t, grad_t = rotate_queries(cos_full, sin_full, queries[0], out_grad[0])
    parts = 1 if routed <= 512 else len(sent)
    wide, key_heads = queries.shape[2] // parts, len(sent) // parts
    terms, local = [], []
    for part in range(parts):
        columns = part_of(part, wide)
        outs = scores(
            meta,
            turned[:, columns],
            out_grad[0][:, columns],
            turned_t[columns],
            grad_t[columns],
            blocks[part_of(part, key_heads)],
            routed,
        )
        terms.append(outs[0])
        local.append(outs[1])
    terms = [jnp.concatenate(term, axis=1) for term in zip(*terms)]
    arrived = relay(*terms) if relayed(ctx_size) else descend(terms, ctx_size)
    finals = []
    for part in range(parts):
        columns = part_of(part, wide)
        finals.append(
            local_terms(
                meta, cos_full, sin_full, turned[:, columns], out_grad[0][:, columns], *local[part]
            )
        )
    dq, own = [jnp.concatenate(final, axis=1) for final in zip(*finals)]
    key_grad, value_grad = finish(meta, cos_full, sin_full, own, arrived)
    return (dq[None], key_grad[None], value_grad[None])


def solution(mesh):
    split = P(("groups", "dp"), "ctx", "mp")
    return jax.shard_map(
        body,
        mesh=mesh,
        in_specs=(P(("groups", "dp"), None), split, split, split, split),
        out_specs=(split, split, split),
        check_vma=False,
    )
```

```python
import functools
import math

import jax
import jax.numpy as jnp
import numpy as np
from jax import lax
from jax.experimental import pallas as pl
from jax.experimental.pallas import tpu as pltpu
from jax.sharding import PartitionSpec as P

HEAD_DIM = 128
HALF_DIM = HEAD_DIM // 2
TOK_SHARD = 1024
ROPE_BASE = 500000.0
SCORE_SCALE = 1.0 / math.sqrt(HEAD_DIM)
EXP2_SCALE = SCORE_SCALE * math.log2(math.e)
HIDDEN = -1e30
ALIGN = 16
CHUNK = 288
MIB = 1024 * 1024

VMEM = pl.BlockSpec(memory_space=pltpu.VMEM)
SMEM = pl.BlockSpec(memory_space=pltpu.SMEM)


def vmem(routed, small, large):
    return pltpu.CompilerParams(vmem_limit_bytes=(small if routed <= 512 else large) * MIB)


def dot(left, right, contract):
    return lax.dot_general(left, right, (contract, ((), ())), preferred_element_type=jnp.float32)


def turn(field, cos_full, sin_full):
    return field * cos_full + pltpu.roll(field, HALF_DIM, 1) * sin_full


def turn_back(field, cos_full, sin_full):
    return field * cos_full - pltpu.roll(field, HALF_DIM, 1) * sin_full


def rope_rows():
    ladder = np.arange(HALF_DIM, dtype=np.float32)
    exponent = ladder * np.float32(-2.0 * math.log(ROPE_BASE) / HEAD_DIM)
    freq = np.exp(exponent.astype(np.float64)).astype(np.float32)
    sign = np.repeat(np.array([-1.0, 1.0], np.float32), HALF_DIM)
    return np.stack([np.concatenate([freq, freq]), sign])


def shard_layout(ctx_size, me, pos, meta_ref):
    shard_of = pos // TOK_SHARD
    for hop in range(2 * ctx_size):
        meta_ref[hop] = 0
    start = jnp.int32(0)
    first = jnp.int32(0)
    my_first = jnp.int32(0)
    for shard in range(ctx_size):
        count = jnp.sum(jnp.where(shard_of == shard, 1.0, 0.0)).astype(jnp.int32)
        my_first = jnp.where(me == shard, first, my_first)

        @pl.when(me >= shard)
        def _():
            meta_ref[me - shard] = start
            meta_ref[ctx_size + me - shard] = count

        first = first + count
        start = start + (count + ALIGN - 1) // ALIGN * ALIGN
    return my_first


def prepare_kernel(
    ctx_size, rows_hbm, pos_hbm, keys_hbm, values_hbm, meta_ref, cos_ref, sin_ref, sent_ref, *refs
):
    rows_ref, pos_ref, keys_ref, values_ref, sems = refs
    sources = (pos_hbm, rows_hbm, keys_hbm, values_hbm)
    targets = (pos_ref, rows_ref, keys_ref, values_ref)
    copies = [
        pltpu.make_async_copy(source, target, sems.at[index])
        for index, (source, target) in enumerate(zip(sources, targets))
    ]
    for copy in copies:
        copy.start()
    copies[0].wait()
    slots = keys_ref.shape[0]
    pos = pos_ref[...]
    my_first = shard_layout(ctx_size, lax.axis_index("ctx"), pos, meta_ref)
    shape = (slots, pos.shape[1])
    gap = lax.broadcasted_iota(jnp.int32, shape, 1) - lax.broadcasted_iota(jnp.int32, shape, 0)
    named = jnp.where(gap == my_first, pos.astype(jnp.float32), 0.0)
    copies[1].wait()
    angles = jnp.sum(named, axis=1, keepdims=True) * rows_ref[0:1, :]
    cos_full = jnp.cos(angles)
    sin_full = jnp.sin(angles) * rows_ref[1:2, :]
    cos_ref[...] = cos_full
    sin_ref[...] = sin_full
    copies[2].wait()
    copies[3].wait()
    for lane in range(0, keys_ref.shape[1], HEAD_DIM):
        lanes = slice(lane, lane + HEAD_DIM)
        key = turn(keys_ref[:, lanes].astype(jnp.float32), cos_full, sin_full)
        middle = 2 * lane + HEAD_DIM
        sent_ref[:, 2 * lane : middle] = key.astype(jnp.bfloat16)
        sent_ref[:, middle : middle + HEAD_DIM] = values_ref[:, lanes]


def prepare(positions, keys, values, ctx_size):
    slots, width = keys.shape
    rows = jnp.asarray(rope_rows())
    table = jax.ShapeDtypeStruct((slots, HEAD_DIM), jnp.float32)
    sent = jax.ShapeDtypeStruct((slots, 2 * width), jnp.bfloat16)
    operands = (rows, positions, keys, values)
    return pl.pallas_call(
        functools.partial(prepare_kernel, ctx_size),
        out_shape=(
            jax.ShapeDtypeStruct((2 * ctx_size,), jnp.int32),
            table,
            table,
            sent,
        ),
        in_specs=[pl.BlockSpec(memory_space=pl.ANY)] * 4,
        out_specs=(SMEM, VMEM, VMEM, VMEM),
        scratch_shapes=[pltpu.VMEM(operand.shape, operand.dtype) for operand in operands]
        + [pltpu.SemaphoreType.DMA((4,))],
        compiler_params=vmem(positions.shape[1], 60, 60),
        name="prepare",
    )(*operands)


def queries_kernel(cos_ref, sin_ref, query_ref, grad_ref, turned_ref, turned_t_ref, grad_t_ref):
    for lane in range(0, query_ref.shape[1], HEAD_DIM):
        lanes = slice(lane, lane + HEAD_DIM)
        query = turn(query_ref[:, lanes].astype(jnp.float32), cos_ref[...], sin_ref[...])
        turned_ref[:, lanes] = query.astype(jnp.bfloat16)
        turned_t_ref[lanes, :] = query.T.astype(jnp.bfloat16)
        grad_t_ref[lanes, :] = grad_ref[:, lanes].astype(jnp.float32).T.astype(jnp.bfloat16)


def rotate_queries(cos_full, sin_full, queries, out_grad):
    slots, width = queries.shape
    straight = jax.ShapeDtypeStruct((slots, width), jnp.bfloat16)
    across = jax.ShapeDtypeStruct((width, slots), jnp.bfloat16)
    return pl.pallas_call(
        queries_kernel,
        out_shape=(straight, across, across),
        in_specs=[VMEM] * 4,
        out_specs=(VMEM,) * 3,
        compiler_params=vmem(0, 16, 16),
        cost_estimate=pl.CostEstimate(
            flops=4 * 10**9, bytes_accessed=5 * 1024 * 1024, transcendentals=0
        ),
        name="rotate_queries",
    )(cos_full, sin_full, queries, out_grad)


def stacked(ref, lane, heads):
    parts = [ref[:, lane + h * HEAD_DIM : lane + (h + 1) * HEAD_DIM] for h in range(heads)]
    return jnp.concatenate(parts, axis=0)


def terms_of(probs, score_grads, queries, grads):
    key_term = dot(score_grads, queries, ((1,), (0,))) * SCORE_SCALE
    return jnp.concatenate([key_term, dot(probs, grads, ((1,), (0,)))], axis=1)


def own_rows(my_start, span, slots):
    return pl.multiple_of(jnp.minimum(my_start, span - slots), ALIGN)


def scores_kernel(ctx_size, key_heads, step_heads, meta_ref, turned_ref, grad_ref, turned_t_ref, grad_t_ref, *refs):
    inputs = refs[: -6 - ctx_size]
    refs = refs[len(inputs) :]
    terms, refs = refs[: ctx_size - 1], refs[ctx_size - 1 :]
    score_grad_ref, own_prob_ref, key_t_ref, key_ref, bias_ref, prob_ref, acc_ref = refs
    blocks = [block[...] for block in inputs]
    slots = turned_ref.shape[0]
    span = bias_ref.shape[0]
    width = key_heads * HEAD_DIM
    heads = turned_ref.shape[1] // width
    starts = [pl.multiple_of(meta_ref[hop], ALIGN) for hop in range(ctx_size)]
    my_start = starts[0]
    sent_hops = list(range(1, ctx_size))
    if relayed(ctx_size):
        last = lax.axis_index("ctx") == ctx_size - 1
        own, alpha, beta, gamma, delta = blocks
        blocks = [own, jnp.where(last, alpha, gamma), jnp.where(last, beta, alpha), delta]
        sent_hops = [jnp.where(last, 3, 1), 2, jnp.where(last, 1, 2)]

    key_ref[...] = jnp.zeros_like(key_ref)
    for hop in range(ctx_size - 1, -1, -1):
        key_ref[pl.ds(starts[hop], slots), :] = blocks[hop]
    place = lax.broadcasted_iota(jnp.int32, (span, slots), 0)
    slot_id = lax.broadcasted_iota(jnp.int32, (span, slots), 1)
    seen = (place >= my_start) & (place - slot_id <= my_start)
    for hop in range(1, ctx_size):
        end = starts[hop] + meta_ref[ctx_size + hop]
        seen = seen | ((place >= starts[hop]) & (place < end))
    bias_ref[...] = jnp.where(seen, 0.0, HIDDEN)
    live = lax.broadcasted_iota(jnp.int32, (1, slots), 1) < meta_ref[ctx_size]
    acc_ref[...] = jnp.zeros_like(acc_ref)

    for key_head in range(key_heads):
        lanes = slice(2 * key_head * HEAD_DIM, (2 * key_head + 1) * HEAD_DIM)
        value_lanes = slice((2 * key_head + 1) * HEAD_DIM, 2 * (key_head + 1) * HEAD_DIM)
        key_t = key_ref[:span, lanes].astype(jnp.float32).T.astype(jnp.bfloat16)
        key_t_ref[key_head * HEAD_DIM : (key_head + 1) * HEAD_DIM, :] = key_t

        def step(index, carry):
            for part in range(step_heads):
                head = index * step_heads + part
                row = pl.multiple_of((key_head * heads + head) * HEAD_DIM, HEAD_DIM)
                rows = pl.ds(row, HEAD_DIM)
                columns = pl.ds(pl.multiple_of(head * slots, slots), slots)
                scores = dot(key_ref[:span, lanes], turned_t_ref[rows, :], ((1,), (0,)))
                scores = scores + bias_ref[...]
                prob_grad = dot(key_ref[:span, value_lanes], grad_t_ref[rows, :], ((1,), (0,)))
                peak = jnp.max(scores, axis=0, keepdims=True)
                weights = jnp.exp2((scores - peak) * EXP2_SCALE)
                inverse = 1.0 / jnp.sum(weights, axis=0, keepdims=True)
                delta = jnp.sum(weights * prob_grad, axis=0, keepdims=True) * inverse
                prob = weights * jnp.where(live, inverse, 0.0)
                prob_ref[:, columns] = prob.astype(jnp.bfloat16)
                score_grad = (prob * (prob_grad - delta)).astype(jnp.bfloat16)
                score_grad_ref[key_head, :, columns] = score_grad
            return carry

        lax.fori_loop(0, heads // step_heads, step, 0)
        own_prob_ref[key_head] = prob_ref[pl.ds(own_rows(my_start, span, slots), slots), :]
        for chunk in range(0, span, CHUNK):

            @pl.when(chunk < my_start)
            def _():
                rows = slice(chunk, chunk + CHUNK)
                acc_ref[rows, :] = terms_of(
                    prob_ref[rows, :],
                    score_grad_ref[key_head, rows, :],
                    stacked(turned_ref, key_head * heads * HEAD_DIM, heads),
                    stacked(grad_ref, key_head * heads * HEAD_DIM, heads),
                )

        for hop, term_ref in zip(sent_hops, terms):
            start = pl.multiple_of(meta_ref[hop], ALIGN)
            term = acc_ref[pl.ds(start, slots), :].astype(term_ref.dtype)
            term_ref[:, 2 * key_head * HEAD_DIM : 2 * (key_head + 1) * HEAD_DIM] = term


def relayed(ctx_size):
    return ctx_size == 4


def scores(meta, turned, out_grad, turned_t, grad_t, blocks, routed, ctx_size):
    slots, width = blocks[0].shape
    key_heads = width // HEAD_DIM // 2
    heads = turned.shape[1] // HEAD_DIM // key_heads
    span = -(-(routed + ctx_size * ALIGN) // CHUNK) * CHUNK
    terms = [jax.ShapeDtypeStruct((slots, width), jnp.bfloat16)] * (ctx_size - 1)
    if relayed(ctx_size):
        terms[2] = jax.ShapeDtypeStruct((slots, width), jnp.float32)
    outs = pl.pallas_call(
        functools.partial(scores_kernel, ctx_size, key_heads, 4 if routed <= 512 else 1),
        out_shape=(
            *terms,
            jax.ShapeDtypeStruct((key_heads, span, heads * slots), jnp.bfloat16),
            jax.ShapeDtypeStruct((key_heads, slots, heads * slots), jnp.bfloat16),
            jax.ShapeDtypeStruct((key_heads * HEAD_DIM, span), jnp.bfloat16),
        ),
        in_specs=[SMEM] + [VMEM] * (4 + len(blocks)),
        out_specs=(VMEM,) * (ctx_size + 2),
        scratch_shapes=[
            pltpu.VMEM((span + slots, width), jnp.bfloat16),
            pltpu.VMEM((span, slots), jnp.float32),
            pltpu.VMEM((span, heads * slots), jnp.bfloat16),
            pltpu.VMEM((span + slots, 2 * HEAD_DIM), jnp.float32),
        ],
        compiler_params=vmem(routed, 28, 60),
        cost_estimate=pl.CostEstimate(
            flops=12 * 10**9, bytes_accessed=12 * 1024 * 1024, transcendentals=0
        ),
        name="scores",
    )(meta, turned, out_grad, turned_t, grad_t, *blocks)
    return outs[: ctx_size - 1], outs[ctx_size - 1 :]


def local_kernel(
    key_heads,
    meta_ref,
    cos_ref,
    sin_ref,
    turned_ref,
    grad_ref,
    score_grad_ref,
    own_prob_ref,
    key_t_ref,
    *refs,
):
    later = (len(refs) - 3) // 2
    dq_ref, own_ref = refs[later : later + 2]
    shift_ref = refs[-1]
    for index in range(later):
        refs[later + 2 + index][...] = refs[index][...]
    slots = turned_ref.shape[0]
    heads = turned_ref.shape[1] // HEAD_DIM // key_heads
    first_row = own_rows(meta_ref[0], score_grad_ref.shape[1], slots)
    shift = pl.multiple_of(meta_ref[0] - first_row, ALIGN)
    shift_ref[slots:, :] = jnp.zeros_like(own_ref)
    for key_head in range(key_heads):
        key_t = key_t_ref[key_head * HEAD_DIM : (key_head + 1) * HEAD_DIM, :]
        for head in range(heads):
            score_grad = score_grad_ref[key_head, :, head * slots : (head + 1) * slots]
            grad = (dot(key_t, score_grad, ((1,), (0,))) * SCORE_SCALE).T
            lane = (key_head * heads + head) * HEAD_DIM
            grad = turn_back(grad, cos_ref[...], sin_ref[...])
            dq_ref[:, lane : lane + HEAD_DIM] = grad.astype(jnp.bfloat16)
        lane = key_head * heads * HEAD_DIM
        shift_ref[:slots, 2 * key_head * HEAD_DIM : 2 * (key_head + 1) * HEAD_DIM] = terms_of(
            own_prob_ref[key_head],
            score_grad_ref[key_head, pl.ds(first_row, slots), :],
            stacked(turned_ref, lane, heads),
            stacked(grad_ref, lane, heads),
        )
    own_ref[...] = shift_ref[pl.ds(shift, slots), :]


def local_terms(meta, cos_full, sin_full, turned, out_grad, score_grad, own_prob, key_t, later):
    slots = turned.shape[0]
    key_heads = score_grad.shape[0]
    return pl.pallas_call(
        functools.partial(local_kernel, key_heads),
        out_shape=(
            jax.ShapeDtypeStruct(turned.shape, jnp.bfloat16),
            jax.ShapeDtypeStruct((slots, 2 * key_heads * HEAD_DIM), jnp.float32),
            *[jax.ShapeDtypeStruct(term.shape, term.dtype) for term in later],
        ),
        in_specs=[SMEM] + [VMEM] * (7 + len(later)),
        out_specs=(VMEM,) * (2 + len(later)),
        scratch_shapes=[pltpu.VMEM((2 * slots, 2 * key_heads * HEAD_DIM), jnp.float32)],
        compiler_params=vmem(key_t.shape[1] // 2, 24, 48),
        cost_estimate=pl.CostEstimate(
            flops=5 * 10**9, bytes_accessed=10 * 1024 * 1024, transcendentals=0
        ),
        name="local_terms",
    )(meta, cos_full, sin_full, turned, out_grad, score_grad, own_prob, key_t, *later)


def finish_kernel(ctx_size, meta_ref, cos_ref, sin_ref, own_ref, *refs):
    terms, (key_grad_ref, value_grad_ref) = refs[: ctx_size - 1], refs[ctx_size - 1 :]
    slots = own_ref.shape[0]
    live = lax.broadcasted_iota(jnp.int32, (slots, HEAD_DIM), 0) < meta_ref[ctx_size]
    total = own_ref[...]
    for index, term in enumerate(terms):
        term = term[...].astype(jnp.float32)
        if index == 0 and relayed(ctx_size):
            term = jnp.where(lax.axis_index("ctx") == 2, 0.0, term)
        total += term
    for lane in range(0, key_grad_ref.shape[1], HEAD_DIM):
        lanes = slice(lane, lane + HEAD_DIM)
        key_term = turn_back(total[:, 2 * lane : 2 * lane + HEAD_DIM], cos_ref[...], sin_ref[...])
        value_term = total[:, 2 * lane + HEAD_DIM : 2 * (lane + HEAD_DIM)]
        key_grad_ref[:, lanes] = jnp.where(live, key_term, 0.0).astype(jnp.bfloat16)
        value_grad_ref[:, lanes] = jnp.where(live, value_term, 0.0).astype(jnp.bfloat16)


def finish(meta, cos_full, sin_full, own, terms):
    slots, width = own.shape
    grad = jax.ShapeDtypeStruct((slots, width // 2), jnp.bfloat16)
    return pl.pallas_call(
        functools.partial(finish_kernel, len(terms) + 1),
        out_shape=(grad, grad),
        in_specs=[SMEM] + [VMEM] * (3 + len(terms)),
        out_specs=(VMEM, VMEM),
        compiler_params=vmem(0, 16, 16),
        name="finish",
    )(meta, cos_full, sin_full, own, *terms)


def part_of(part, size):
    return slice(part * size, (part + 1) * size)


def spread(sent, ctx_size):
    if relayed(ctx_size):
        alpha = lax.ppermute(sent, "ctx", [(0, 2), (2, 3)])
        beta = lax.ppermute(sent, "ctx", [(1, 3)])
        gamma = lax.ppermute(sent, "ctx", [(0, 1), (1, 2)])
        return [sent, alpha, beta, gamma, lax.ppermute(alpha, "ctx", [(2, 3)])]
    blocks = [sent]
    for hop in range(1, ctx_size):
        pairs = [(shard, shard + 1) for shard in range(hop - 1, ctx_size - 1)]
        blocks.append(lax.ppermute(blocks[-1], "ctx", pairs))
    return blocks


def relay_first(first, third):
    first = lax.ppermute(first, "ctx", [(3, 2), (2, 1), (1, 0)])
    third = (third + first.astype(jnp.float32)).astype(jnp.bfloat16)
    return [first, lax.ppermute(third, "ctx", [(3, 2), (2, 0)])]


def descend(terms, ctx_size):
    arrived = []
    for hop, term in enumerate(terms, 1):
        pairs = [(shard + hop, shard) for shard in range(ctx_size - hop)]
        arrived.append(lax.ppermute(term, "ctx", pairs))
    return arrived


def body(positions, queries, keys, values, out_grad):
    ctx_size = lax.axis_size("ctx")
    routed = positions.shape[1]
    meta, cos_full, sin_full, sent = prepare(positions, keys[0], values[0], ctx_size)
    blocks = spread(sent, ctx_size)
    turned, turned_t, grad_t = rotate_queries(cos_full, sin_full, queries[0], out_grad[0])
    parts = 1 if routed <= 512 else keys.shape[2] // HEAD_DIM
    wide, narrow = queries.shape[2] // parts, sent.shape[1] // parts
    terms, local = [], []
    for part in range(parts):
        columns = part_of(part, wide)
        outs = scores(
            meta,
            turned[:, columns],
            out_grad[0][:, columns],
            turned_t[columns],
            grad_t[columns],
            [block[:, part_of(part, narrow)] for block in blocks],
            routed,
            ctx_size,
        )
        terms.append(outs[0])
        local.append(outs[1])
    terms = [jnp.concatenate(term, axis=1) for term in zip(*terms)]
    if relayed(ctx_size):
        arrived, later = relay_first(terms[0], terms[2]), [terms[1]]
    else:
        arrived, later = descend(terms, ctx_size), []
    finals = []
    for part in range(parts):
        columns = part_of(part, wide)
        finals.append(
            local_terms(
                meta,
                cos_full,
                sin_full,
                turned[:, columns],
                out_grad[0][:, columns],
                *local[part],
                later,
            )
        )
    dq, own = [jnp.concatenate(final, axis=1) for final in zip(*[final[:2] for final in finals])]
    for term in finals[0][2:]:
        arrived.append(lax.ppermute(term, "ctx", [(3, 1)]))
    key_grad, value_grad = finish(meta, cos_full, sin_full, own, arrived)
    return (dq[None], key_grad[None], value_grad[None])


def solution(mesh):
    split = P(("groups", "dp"), "ctx", "mp")
    return jax.shard_map(
        body,
        mesh=mesh,
        in_specs=(P(("groups", "dp"), None), split, split, split, split),
        out_specs=(split, split, split),
        check_vma=False,
    )
```

```python
import functools
import math

import jax
import jax.numpy as jnp
import numpy as np
from jax import lax
from jax.experimental import pallas as pl
from jax.experimental.pallas import tpu as pltpu
from jax.sharding import PartitionSpec as P

HEAD_DIM = 128
HALF_DIM = HEAD_DIM // 2
TOK_SHARD = 1024
ROPE_BASE = 500000.0
SCORE_SCALE = 1.0 / math.sqrt(HEAD_DIM)
EXP2_SCALE = SCORE_SCALE * math.log2(math.e)
HIDDEN = -1e30
ALIGN = 16
CHUNK = 288
MIB = 1024 * 1024

VMEM = pl.BlockSpec(memory_space=pltpu.VMEM)
SMEM = pl.BlockSpec(memory_space=pltpu.SMEM)
HBM = pl.BlockSpec(memory_space=pltpu.HBM)


def vmem(routed, small, large):
    return pltpu.CompilerParams(vmem_limit_bytes=(small if routed <= 512 else large) * MIB)


def dot(left, right, contract):
    return lax.dot_general(left, right, (contract, ((), ())), preferred_element_type=jnp.float32)


def turn(field, cos_full, sin_full):
    return field * cos_full + pltpu.roll(field, HALF_DIM, 1) * sin_full


def turn_back(field, cos_full, sin_full):
    return field * cos_full - pltpu.roll(field, HALF_DIM, 1) * sin_full


def rope_rows():
    ladder = np.arange(HALF_DIM, dtype=np.float32)
    exponent = ladder * np.float32(-2.0 * math.log(ROPE_BASE) / HEAD_DIM)
    freq = np.exp(exponent.astype(np.float64)).astype(np.float32)
    sign = np.repeat(np.array([-1.0, 1.0], np.float32), HALF_DIM)
    return np.stack([np.concatenate([freq, freq]), sign])


def shard_layout(ctx_size, me, pos, meta_ref):
    shard_of = pos // TOK_SHARD
    for hop in range(2 * ctx_size):
        meta_ref[hop] = 0
    start = jnp.int32(0)
    first = jnp.int32(0)
    my_first = jnp.int32(0)
    for shard in range(ctx_size):
        count = jnp.sum(jnp.where(shard_of == shard, 1.0, 0.0)).astype(jnp.int32)
        my_first = jnp.where(me == shard, first, my_first)

        @pl.when(me >= shard)
        def _():
            meta_ref[me - shard] = start
            meta_ref[ctx_size + me - shard] = count

        first = first + count
        start = start + (count + ALIGN - 1) // ALIGN * ALIGN
    return my_first


def prepare_kernel(
    ctx_size, rows_hbm, pos_hbm, keys_hbm, values_hbm, meta_ref, cos_ref, sin_ref, sent_ref, *refs
):
    rows_ref, pos_ref, keys_ref, values_ref, sems = refs
    sources = (pos_hbm, rows_hbm, keys_hbm, values_hbm)
    targets = (pos_ref, rows_ref, keys_ref, values_ref)
    copies = [
        pltpu.make_async_copy(source, target, sems.at[index])
        for index, (source, target) in enumerate(zip(sources, targets))
    ]
    for copy in copies:
        copy.start()
    copies[0].wait()
    slots = keys_ref.shape[0]
    pos = pos_ref[...]
    my_first = shard_layout(ctx_size, lax.axis_index("ctx"), pos, meta_ref)
    shape = (slots, pos.shape[1])
    gap = lax.broadcasted_iota(jnp.int32, shape, 1) - lax.broadcasted_iota(jnp.int32, shape, 0)
    named = jnp.where(gap == my_first, pos.astype(jnp.float32), 0.0)
    copies[1].wait()
    angles = jnp.sum(named, axis=1, keepdims=True) * rows_ref[0:1, :]
    cos_full = jnp.cos(angles)
    sin_full = jnp.sin(angles) * rows_ref[1:2, :]
    cos_ref[...] = cos_full
    sin_ref[...] = sin_full
    copies[2].wait()
    copies[3].wait()
    for lane in range(0, keys_ref.shape[1], HEAD_DIM):
        lanes = slice(lane, lane + HEAD_DIM)
        key = turn(keys_ref[:, lanes].astype(jnp.float32), cos_full, sin_full)
        middle = 2 * lane + HEAD_DIM
        sent_ref[:, 2 * lane : middle] = key.astype(jnp.bfloat16)
        sent_ref[:, middle : middle + HEAD_DIM] = values_ref[:, lanes]


def prepare(positions, keys, values, ctx_size):
    slots, width = keys.shape
    rows = jnp.asarray(rope_rows())
    table = jax.ShapeDtypeStruct((slots, HEAD_DIM), jnp.float32)
    sent = jax.ShapeDtypeStruct((slots, 2 * width), jnp.bfloat16)
    operands = (rows, positions, keys, values)
    return pl.pallas_call(
        functools.partial(prepare_kernel, ctx_size),
        out_shape=(
            jax.ShapeDtypeStruct((2 * ctx_size,), jnp.int32),
            table,
            table,
            sent,
        ),
        in_specs=[HBM] * 4,
        out_specs=(SMEM, VMEM, VMEM, VMEM),
        scratch_shapes=[pltpu.VMEM(operand.shape, operand.dtype) for operand in operands]
        + [pltpu.SemaphoreType.DMA((4,))],
        compiler_params=vmem(positions.shape[1], 60, 60),
        name="prepare",
    )(*operands)


def queries_kernel(
    cos_ref,
    sin_ref,
    query_ref,
    grad_ref,
    sent_ref,
    turned_ref,
    turned_t_ref,
    grad_t_ref,
    sent_again_ref,
):
    sent_again_ref[...] = sent_ref[...]
    for lane in range(0, query_ref.shape[1], HEAD_DIM):
        lanes = slice(lane, lane + HEAD_DIM)
        query = turn(query_ref[:, lanes].astype(jnp.float32), cos_ref[...], sin_ref[...])
        turned_ref[:, lanes] = query.astype(jnp.bfloat16)
        turned_t_ref[lanes, :] = query.T.astype(jnp.bfloat16)
        grad_t_ref[lanes, :] = grad_ref[:, lanes].astype(jnp.float32).T.astype(jnp.bfloat16)


def rotate_queries(cos_full, sin_full, queries, out_grad, sent):
    slots, width = queries.shape
    straight = jax.ShapeDtypeStruct((slots, width), jnp.bfloat16)
    across = jax.ShapeDtypeStruct((width, slots), jnp.bfloat16)
    return pl.pallas_call(
        queries_kernel,
        out_shape=(straight, across, across, jax.ShapeDtypeStruct(sent.shape, sent.dtype)),
        in_specs=[VMEM] * 5,
        out_specs=(VMEM,) * 4,
        compiler_params=vmem(0, 16, 16),
        cost_estimate=pl.CostEstimate(
            flops=3 * 10**9, bytes_accessed=4 * 1024 * 1024, transcendentals=0
        ),
        name="rotate_queries",
    )(cos_full, sin_full, queries, out_grad, sent)


def stacked(ref, lane, heads):
    parts = [ref[:, lane + h * HEAD_DIM : lane + (h + 1) * HEAD_DIM] for h in range(heads)]
    return jnp.concatenate(parts, axis=0)


def terms_of(probs, score_grads, queries, grads):
    key_term = dot(score_grads, queries, ((1,), (0,))) * SCORE_SCALE
    return jnp.concatenate([key_term, dot(probs, grads, ((1,), (0,)))], axis=1)


def fold(field, join, reduce):
    while field.shape[0] % 16 == 0:
        half = field.shape[0] // 2
        field = join(field[:half], field[half:])
    return reduce(field, axis=0, keepdims=True)


def own_rows(my_start, span, slots):
    return pl.multiple_of(jnp.minimum(my_start, span - slots), ALIGN)


def scores_kernel(ctx_size, key_heads, step_heads, meta_ref, turned_ref, grad_ref, turned_t_ref, grad_t_ref, *refs):
    inputs = refs[: -6 - ctx_size]
    refs = refs[len(inputs) :]
    terms, refs = refs[: ctx_size - 1], refs[ctx_size - 1 :]
    score_grad_ref, own_prob_ref, key_t_ref, key_ref, bias_ref, prob_ref, acc_ref = refs
    blocks = [block[...] for block in inputs]
    slots = turned_ref.shape[0]
    span = bias_ref.shape[0]
    width = key_heads * HEAD_DIM
    heads = turned_ref.shape[1] // width
    starts = [pl.multiple_of(meta_ref[hop], ALIGN) for hop in range(ctx_size)]
    my_start = starts[0]
    sent_hops = list(range(1, ctx_size))
    if relayed(ctx_size):
        last = lax.axis_index("ctx") == ctx_size - 1
        own, alpha, beta, gamma, delta = blocks
        blocks = [own, jnp.where(last, alpha, gamma), jnp.where(last, beta, alpha), delta]
        sent_hops = [jnp.where(last, 3, 1), 2, jnp.where(last, 1, 2)]

    key_ref[...] = jnp.zeros_like(key_ref)
    for hop in range(ctx_size - 1, -1, -1):
        key_ref[pl.ds(starts[hop], slots), :] = blocks[hop]
    place = lax.broadcasted_iota(jnp.int32, (span, slots), 0)
    slot_id = lax.broadcasted_iota(jnp.int32, (span, slots), 1)
    seen = (place >= my_start) & (place - slot_id <= my_start)
    for hop in range(1, ctx_size):
        end = starts[hop] + meta_ref[ctx_size + hop]
        seen = seen | ((place >= starts[hop]) & (place < end))
    bias_ref[...] = jnp.where(seen, 0.0, HIDDEN)
    live = lax.broadcasted_iota(jnp.int32, (1, slots), 1) < meta_ref[ctx_size]
    acc_ref[...] = jnp.zeros_like(acc_ref)

    for key_head in range(key_heads):
        lanes = slice(2 * key_head * HEAD_DIM, (2 * key_head + 1) * HEAD_DIM)
        value_lanes = slice((2 * key_head + 1) * HEAD_DIM, 2 * (key_head + 1) * HEAD_DIM)
        key_t = key_ref[:span, lanes].astype(jnp.float32).T.astype(jnp.bfloat16)
        key_t_ref[key_head * HEAD_DIM : (key_head + 1) * HEAD_DIM, :] = key_t

        def step(index, carry):
            for part in range(step_heads):
                head = index * step_heads + part
                row = pl.multiple_of((key_head * heads + head) * HEAD_DIM, HEAD_DIM)
                rows = pl.ds(row, HEAD_DIM)
                columns = pl.ds(pl.multiple_of(head * slots, slots), slots)
                scores = dot(key_ref[:span, lanes], turned_t_ref[rows, :], ((1,), (0,)))
                scores = scores + bias_ref[...]
                prob_grad = dot(key_ref[:span, value_lanes], grad_t_ref[rows, :], ((1,), (0,)))
                peak = fold(scores, jnp.maximum, jnp.max)
                weights = jnp.exp2((scores - peak) * EXP2_SCALE)
                inverse = 1.0 / fold(weights, jnp.add, jnp.sum)
                delta = fold(weights * prob_grad, jnp.add, jnp.sum) * inverse
                prob = weights * jnp.where(live, inverse, 0.0)
                prob_ref[:, columns] = prob.astype(jnp.bfloat16)
                score_grad = (prob * (prob_grad - delta)).astype(jnp.bfloat16)
                score_grad_ref[key_head, :, columns] = score_grad
            return carry

        lax.fori_loop(0, heads // step_heads, step, 0)
        own_prob_ref[key_head] = prob_ref[pl.ds(own_rows(my_start, span, slots), slots), :]
        for chunk in range(0, span, CHUNK):

            @pl.when(chunk < my_start)
            def _():
                rows = slice(chunk, chunk + CHUNK)
                acc_ref[rows, :] = terms_of(
                    prob_ref[rows, :],
                    score_grad_ref[key_head, rows, :],
                    stacked(turned_ref, key_head * heads * HEAD_DIM, heads),
                    stacked(grad_ref, key_head * heads * HEAD_DIM, heads),
                )

        for hop, term_ref in zip(sent_hops, terms):
            start = pl.multiple_of(meta_ref[hop], ALIGN)
            term = acc_ref[pl.ds(start, slots), :].astype(term_ref.dtype)
            term_ref[:, 2 * key_head * HEAD_DIM : 2 * (key_head + 1) * HEAD_DIM] = term


def relayed(ctx_size):
    return ctx_size == 4


def scores(meta, turned, out_grad, turned_t, grad_t, blocks, routed, ctx_size):
    slots, width = blocks[0].shape
    key_heads = width // HEAD_DIM // 2
    heads = turned.shape[1] // HEAD_DIM // key_heads
    span = -(-(routed + ctx_size * ALIGN) // CHUNK) * CHUNK
    terms = [jax.ShapeDtypeStruct((slots, width), jnp.bfloat16)] * (ctx_size - 1)
    if relayed(ctx_size):
        terms[2] = jax.ShapeDtypeStruct((slots, width), jnp.float32)
    outs = pl.pallas_call(
        functools.partial(scores_kernel, ctx_size, key_heads, 4 if routed <= 512 else 1),
        out_shape=(
            *terms,
            jax.ShapeDtypeStruct((key_heads, span, heads * slots), jnp.bfloat16),
            jax.ShapeDtypeStruct((key_heads, slots, heads * slots), jnp.bfloat16),
            jax.ShapeDtypeStruct((key_heads * HEAD_DIM, span), jnp.bfloat16),
        ),
        in_specs=[SMEM] + [VMEM] * (4 + len(blocks)),
        out_specs=(VMEM,) * (ctx_size + 2),
        scratch_shapes=[
            pltpu.VMEM((span + slots, width), jnp.bfloat16),
            pltpu.VMEM((span, slots), jnp.float32),
            pltpu.VMEM((span, heads * slots), jnp.bfloat16),
            pltpu.VMEM((span + slots, 2 * HEAD_DIM), jnp.float32),
        ],
        compiler_params=vmem(routed, 28, 60),
        cost_estimate=pl.CostEstimate(
            flops=12 * 10**9, bytes_accessed=12 * 1024 * 1024, transcendentals=0
        ),
        name="scores",
    )(meta, turned, out_grad, turned_t, grad_t, *blocks)
    return outs[: ctx_size - 1], outs[ctx_size - 1 :]


def local_kernel(
    key_heads,
    meta_ref,
    cos_ref,
    sin_ref,
    turned_ref,
    grad_ref,
    score_grad_ref,
    own_prob_ref,
    key_t_ref,
    *refs,
):
    later = (len(refs) - 3) // 2
    dq_ref, own_ref = refs[later : later + 2]
    shift_ref = refs[-1]
    for index in range(later):
        refs[later + 2 + index][...] = refs[index][...]
    slots = turned_ref.shape[0]
    heads = turned_ref.shape[1] // HEAD_DIM // key_heads
    first_row = own_rows(meta_ref[0], score_grad_ref.shape[1], slots)
    shift = pl.multiple_of(meta_ref[0] - first_row, ALIGN)
    shift_ref[slots:, :] = jnp.zeros_like(own_ref)
    for key_head in range(key_heads):
        key_t = key_t_ref[key_head * HEAD_DIM : (key_head + 1) * HEAD_DIM, :]
        for head in range(heads):
            score_grad = score_grad_ref[key_head, :, head * slots : (head + 1) * slots]
            grad = (dot(key_t, score_grad, ((1,), (0,))) * SCORE_SCALE).T
            lane = (key_head * heads + head) * HEAD_DIM
            grad = turn_back(grad, cos_ref[...], sin_ref[...])
            dq_ref[:, lane : lane + HEAD_DIM] = grad.astype(jnp.bfloat16)
        lane = key_head * heads * HEAD_DIM
        shift_ref[:slots, 2 * key_head * HEAD_DIM : 2 * (key_head + 1) * HEAD_DIM] = terms_of(
            own_prob_ref[key_head],
            score_grad_ref[key_head, pl.ds(first_row, slots), :],
            stacked(turned_ref, lane, heads),
            stacked(grad_ref, lane, heads),
        )
    own_ref[...] = shift_ref[pl.ds(shift, slots), :]


def local_terms(meta, cos_full, sin_full, turned, out_grad, score_grad, own_prob, key_t, later):
    slots = turned.shape[0]
    key_heads = score_grad.shape[0]
    return pl.pallas_call(
        functools.partial(local_kernel, key_heads),
        out_shape=(
            jax.ShapeDtypeStruct(turned.shape, jnp.bfloat16),
            jax.ShapeDtypeStruct((slots, 2 * key_heads * HEAD_DIM), jnp.float32),
            *[jax.ShapeDtypeStruct(term.shape, term.dtype) for term in later],
        ),
        in_specs=[SMEM] + [VMEM] * (7 + len(later)),
        out_specs=(VMEM,) * (2 + len(later)),
        scratch_shapes=[pltpu.VMEM((2 * slots, 2 * key_heads * HEAD_DIM), jnp.float32)],
        compiler_params=vmem(key_t.shape[1] // 2, 24, 48),
        cost_estimate=pl.CostEstimate(
            flops=5 * 10**9, bytes_accessed=10 * 1024 * 1024, transcendentals=0
        ),
        name="local_terms",
    )(meta, cos_full, sin_full, turned, out_grad, score_grad, own_prob, key_t, *later)


def finish_kernel(ctx_size, meta_ref, cos_ref, sin_ref, own_ref, *refs):
    terms, (key_grad_ref, value_grad_ref) = refs[: ctx_size - 1], refs[ctx_size - 1 :]
    slots = own_ref.shape[0]
    live = lax.broadcasted_iota(jnp.int32, (slots, HEAD_DIM), 0) < meta_ref[ctx_size]
    total = own_ref[...]
    for index, term in enumerate(terms):
        term = term[...].astype(jnp.float32)
        if index == 0 and relayed(ctx_size):
            term = jnp.where(lax.axis_index("ctx") == 2, 0.0, term)
        total += term
    for lane in range(0, key_grad_ref.shape[1], HEAD_DIM):
        lanes = slice(lane, lane + HEAD_DIM)
        key_term = turn_back(total[:, 2 * lane : 2 * lane + HEAD_DIM], cos_ref[...], sin_ref[...])
        value_term = total[:, 2 * lane + HEAD_DIM : 2 * (lane + HEAD_DIM)]
        key_grad_ref[:, lanes] = jnp.where(live, key_term, 0.0).astype(jnp.bfloat16)
        value_grad_ref[:, lanes] = jnp.where(live, value_term, 0.0).astype(jnp.bfloat16)


def finish(meta, cos_full, sin_full, own, terms):
    slots, width = own.shape
    grad = jax.ShapeDtypeStruct((slots, width // 2), jnp.bfloat16)
    return pl.pallas_call(
        functools.partial(finish_kernel, len(terms) + 1),
        out_shape=(grad, grad),
        in_specs=[SMEM] + [VMEM] * (3 + len(terms)),
        out_specs=(VMEM, VMEM),
        compiler_params=vmem(0, 16, 16),
        name="finish",
    )(meta, cos_full, sin_full, own, *terms)


def part_of(part, size):
    return slice(part * size, (part + 1) * size)


def spread(sent, sent_again, ctx_size):
    if relayed(ctx_size):
        alpha = lax.ppermute(sent, "ctx", [(0, 2), (2, 3)])
        beta = lax.ppermute(sent, "ctx", [(1, 3)])
        gamma = lax.ppermute(sent_again, "ctx", [(0, 1), (1, 2)])
        return [sent, alpha, beta, gamma, lax.ppermute(alpha, "ctx", [(2, 3)])]
    blocks = [sent]
    for hop in range(1, ctx_size):
        pairs = [(shard, shard + 1) for shard in range(hop - 1, ctx_size - 1)]
        blocks.append(lax.ppermute(blocks[-1], "ctx", pairs))
    return blocks


def relay_first(first, third):
    first = lax.ppermute(first, "ctx", [(3, 2), (2, 1), (1, 0)])
    third = (third + first.astype(jnp.float32)).astype(jnp.bfloat16)
    return [first, lax.ppermute(third, "ctx", [(3, 2), (2, 0)])]


def descend(terms, ctx_size):
    arrived = []
    for hop, term in enumerate(terms, 1):
        pairs = [(shard + hop, shard) for shard in range(ctx_size - hop)]
        arrived.append(lax.ppermute(term, "ctx", pairs))
    return arrived


def body(positions, queries, keys, values, out_grad):
    ctx_size = lax.axis_size("ctx")
    routed = positions.shape[1]
    meta, cos_full, sin_full, sent = prepare(positions, keys[0], values[0], ctx_size)
    turned, turned_t, grad_t, sent_again = rotate_queries(
        cos_full, sin_full, queries[0], out_grad[0], sent
    )
    blocks = spread(sent, sent_again, ctx_size)
    parts = 1 if routed <= 512 else keys.shape[2] // HEAD_DIM
    wide, narrow = queries.shape[2] // parts, sent.shape[1] // parts
    terms, local = [], []
    for part in range(parts):
        columns = part_of(part, wide)
        outs = scores(
            meta,
            turned[:, columns],
            out_grad[0][:, columns],
            turned_t[columns],
            grad_t[columns],
            [block[:, part_of(part, narrow)] for block in blocks],
            routed,
            ctx_size,
        )
        terms.append(outs[0])
        local.append(outs[1])
    terms = [jnp.concatenate(term, axis=1) for term in zip(*terms)]
    if relayed(ctx_size):
        arrived, later = relay_first(terms[0], terms[2]), [terms[1]]
    else:
        arrived, later = descend(terms, ctx_size), []
    finals = []
    for part in range(parts):
        columns = part_of(part, wide)
        finals.append(
            local_terms(
                meta,
                cos_full,
                sin_full,
                turned[:, columns],
                out_grad[0][:, columns],
                *local[part],
                later,
            )
        )
    dq, own = [jnp.concatenate(final, axis=1) for final in zip(*[final[:2] for final in finals])]
    for term in finals[0][2:]:
        arrived.append(lax.ppermute(term, "ctx", [(3, 1)]))
    key_grad, value_grad = finish(meta, cos_full, sin_full, own, arrived)
    return (dq[None], key_grad[None], value_grad[None])


def solution(mesh):
    split = P(("groups", "dp"), "ctx", "mp")
    return jax.shard_map(
        body,
        mesh=mesh,
        in_specs=(P(("groups", "dp"), None), split, split, split, split),
        out_specs=(split, split, split),
        check_vma=False,
    )
```

```python
import functools
import math

import jax
import jax.numpy as jnp
import numpy as np
from jax import lax
from jax.experimental import pallas as pl
from jax.experimental.pallas import tpu as pltpu
from jax.sharding import PartitionSpec as P

HEAD_DIM = 128
HALF_DIM = HEAD_DIM // 2
TOK_SHARD = 1024
ROPE_BASE = 500000.0
SCORE_SCALE = 1.0 / math.sqrt(HEAD_DIM)
EXP2_SCALE = SCORE_SCALE * math.log2(math.e)
HIDDEN = -1e30
ALIGN = 16
CHUNK = 288
MIB = 1024 * 1024

VMEM = pl.BlockSpec(memory_space=pltpu.VMEM)
SMEM = pl.BlockSpec(memory_space=pltpu.SMEM)
HBM = pl.BlockSpec(memory_space=pltpu.HBM)


def vmem(routed, small, large):
    return pltpu.CompilerParams(vmem_limit_bytes=(small if routed <= 512 else large) * MIB)


def dot(left, right, contract):
    return lax.dot_general(left, right, (contract, ((), ())), preferred_element_type=jnp.float32)


def turn(field, cos_full, sin_full):
    return field * cos_full + pltpu.roll(field, HALF_DIM, 1) * sin_full


def turn_back(field, cos_full, sin_full):
    return field * cos_full - pltpu.roll(field, HALF_DIM, 1) * sin_full


def rope_rows():
    ladder = np.arange(HALF_DIM, dtype=np.float32)
    exponent = ladder * np.float32(-2.0 * math.log(ROPE_BASE) / HEAD_DIM)
    freq = np.exp(exponent.astype(np.float64)).astype(np.float32)
    sign = np.repeat(np.array([-1.0, 1.0], np.float32), HALF_DIM)
    return np.stack([np.concatenate([freq, freq]), sign])


def shard_layout(ctx_size, me, pos, meta_ref):
    shard_of = pos // TOK_SHARD
    for hop in range(2 * ctx_size):
        meta_ref[hop] = 0
    start = jnp.int32(0)
    first = jnp.int32(0)
    my_first = jnp.int32(0)
    for shard in range(ctx_size):
        count = jnp.sum(jnp.where(shard_of == shard, 1.0, 0.0)).astype(jnp.int32)
        my_first = jnp.where(me == shard, first, my_first)

        @pl.when(me >= shard)
        def _():
            meta_ref[me - shard] = start
            meta_ref[ctx_size + me - shard] = count

        first = first + count
        start = start + (count + ALIGN - 1) // ALIGN * ALIGN
    return my_first


def prepare_kernel(
    ctx_size, rows_hbm, pos_hbm, keys_hbm, values_hbm, meta_ref, cos_ref, sin_ref, sent_ref, *refs
):
    rows_ref, pos_ref, keys_ref, values_ref, sems = refs
    sources = (pos_hbm, rows_hbm, keys_hbm, values_hbm)
    targets = (pos_ref, rows_ref, keys_ref, values_ref)
    copies = [
        pltpu.make_async_copy(source, target, sems.at[index])
        for index, (source, target) in enumerate(zip(sources, targets))
    ]
    for copy in copies:
        copy.start()
    copies[0].wait()
    slots = keys_ref.shape[0]
    pos = pos_ref[...]
    my_first = shard_layout(ctx_size, lax.axis_index("ctx"), pos, meta_ref)
    shape = (slots, pos.shape[1])
    gap = lax.broadcasted_iota(jnp.int32, shape, 1) - lax.broadcasted_iota(jnp.int32, shape, 0)
    named = jnp.where(gap == my_first, pos.astype(jnp.float32), 0.0)
    copies[1].wait()
    angles = jnp.sum(named, axis=1, keepdims=True) * rows_ref[0:1, :]
    cos_full = jnp.cos(angles)
    sin_full = jnp.sin(angles) * rows_ref[1:2, :]
    cos_ref[...] = cos_full
    sin_ref[...] = sin_full
    copies[2].wait()
    copies[3].wait()
    for lane in range(0, keys_ref.shape[1], HEAD_DIM):
        lanes = slice(lane, lane + HEAD_DIM)
        key = turn(keys_ref[:, lanes].astype(jnp.float32), cos_full, sin_full)
        middle = 2 * lane + HEAD_DIM
        sent_ref[:, 2 * lane : middle] = key.astype(jnp.bfloat16)
        sent_ref[:, middle : middle + HEAD_DIM] = values_ref[:, lanes]


def prepare(positions, keys, values, ctx_size):
    slots, width = keys.shape
    rows = jnp.asarray(rope_rows())
    table = jax.ShapeDtypeStruct((slots, HEAD_DIM), jnp.float32)
    sent = jax.ShapeDtypeStruct((slots, 2 * width), jnp.bfloat16)
    operands = (rows, positions, keys, values)
    return pl.pallas_call(
        functools.partial(prepare_kernel, ctx_size),
        out_shape=(
            jax.ShapeDtypeStruct((2 * ctx_size,), jnp.int32),
            table,
            table,
            sent,
        ),
        in_specs=[HBM] * 4,
        out_specs=(SMEM, VMEM, VMEM, VMEM),
        scratch_shapes=[pltpu.VMEM(operand.shape, operand.dtype) for operand in operands]
        + [pltpu.SemaphoreType.DMA((4,))],
        compiler_params=vmem(positions.shape[1], 60, 60),
        name="prepare",
    )(*operands)


def queries_kernel(
    cos_ref,
    sin_ref,
    query_ref,
    grad_ref,
    sent_ref,
    turned_ref,
    turned_t_ref,
    grad_t_ref,
    sent_again_ref,
):
    sent_again_ref[...] = sent_ref[...]
    for lane in range(0, query_ref.shape[1], HEAD_DIM):
        lanes = slice(lane, lane + HEAD_DIM)
        query = turn(query_ref[:, lanes].astype(jnp.float32), cos_ref[...], sin_ref[...])
        turned_ref[:, lanes] = query.astype(jnp.bfloat16)
        turned_t_ref[lanes, :] = query.T.astype(jnp.bfloat16)
        grad_t_ref[lanes, :] = grad_ref[:, lanes].astype(jnp.float32).T.astype(jnp.bfloat16)


def rotate_queries(cos_full, sin_full, queries, out_grad, sent):
    slots, width = queries.shape
    straight = jax.ShapeDtypeStruct((slots, width), jnp.bfloat16)
    across = jax.ShapeDtypeStruct((width, slots), jnp.bfloat16)
    return pl.pallas_call(
        queries_kernel,
        out_shape=(straight, across, across, jax.ShapeDtypeStruct(sent.shape, sent.dtype)),
        in_specs=[VMEM] * 5,
        out_specs=(VMEM,) * 4,
        compiler_params=vmem(0, 16, 16),
        cost_estimate=pl.CostEstimate(
            flops=3 * 10**9, bytes_accessed=4 * 1024 * 1024, transcendentals=0
        ),
        name="rotate_queries",
    )(cos_full, sin_full, queries, out_grad, sent)


def stacked(ref, lane, heads):
    parts = [ref[:, lane + h * HEAD_DIM : lane + (h + 1) * HEAD_DIM] for h in range(heads)]
    return jnp.concatenate(parts, axis=0)


def terms_of(probs, score_grads, queries, grads):
    key_term = dot(score_grads, queries, ((1,), (0,))) * SCORE_SCALE
    return jnp.concatenate([key_term, dot(probs, grads, ((1,), (0,)))], axis=1)


def fold(field, join, reduce):
    while field.shape[0] % 16 == 0:
        half = field.shape[0] // 2
        field = join(field[:half], field[half:])
    return reduce(field, axis=0, keepdims=True)


def key_lanes(key_head):
    return slice(2 * key_head * HEAD_DIM, (2 * key_head + 1) * HEAD_DIM)


def value_lanes(key_head):
    return slice((2 * key_head + 1) * HEAD_DIM, 2 * (key_head + 1) * HEAD_DIM)


def own_kernel(step_heads, sent_ref, turned_t_ref, grad_t_ref, weight_ref, product_ref, sums_ref, bias_ref):
    slots = sent_ref.shape[0]
    key_heads = sent_ref.shape[1] // HEAD_DIM // 2
    heads = turned_t_ref.shape[0] // HEAD_DIM // key_heads
    key_id = lax.broadcasted_iota(jnp.int32, (slots, slots), 0)
    slot_id = lax.broadcasted_iota(jnp.int32, (slots, slots), 1)
    bias_ref[...] = jnp.where(key_id <= slot_id, 0.0, HIDDEN)
    for key_head in range(key_heads):

        def step(index, carry):
            for part in range(step_heads):
                head = key_head * heads + index * step_heads + part
                rows = pl.ds(pl.multiple_of(head * HEAD_DIM, HEAD_DIM), HEAD_DIM)
                scores = dot(sent_ref[:, key_lanes(key_head)], turned_t_ref[rows, :], ((1,), (0,)))
                scores = scores + bias_ref[...]
                prob_grad = dot(sent_ref[:, value_lanes(key_head)], grad_t_ref[rows, :], ((1,), (0,)))
                peak = fold(scores, jnp.maximum, jnp.max)
                weights = jnp.exp2((scores - peak) * EXP2_SCALE)
                weight_ref[head] = weights
                product_ref[head] = prob_grad
                sums_ref[head, 0:1, :] = peak
                sums_ref[head, 1:2, :] = fold(weights, jnp.add, jnp.sum)
                sums_ref[head, 2:3, :] = fold(weights * prob_grad, jnp.add, jnp.sum)
            return carry

        lax.fori_loop(0, heads // step_heads, step, 0)


def own_scores(sent, turned_t, grad_t):
    slots = sent.shape[0]
    heads = turned_t.shape[0] // HEAD_DIM
    square = jax.ShapeDtypeStruct((heads, slots, slots), jnp.float32)
    return pl.pallas_call(
        functools.partial(own_kernel, 4),
        out_shape=(square, square, jax.ShapeDtypeStruct((heads, 8, slots), jnp.float32)),
        in_specs=[VMEM] * 3,
        out_specs=(VMEM,) * 3,
        scratch_shapes=[pltpu.VMEM((slots, slots), jnp.float32)],
        compiler_params=vmem(0, 16, 16),
        cost_estimate=pl.CostEstimate(
            flops=5 * 10**9, bytes_accessed=10 * 1024 * 1024, transcendentals=0
        ),
        name="own_scores",
    )(sent, turned_t, grad_t)


def scores_kernel(
    ctx_size,
    sizes,
    step_heads,
    meta_ref,
    turned_ref,
    grad_ref,
    turned_t_ref,
    grad_t_ref,
    sums_ref,
    *refs,
):
    inputs = refs[: -6 - ctx_size]
    refs = refs[len(inputs) :]
    terms, refs = refs[: ctx_size - 1], refs[ctx_size - 1 :]
    score_grad_ref, joined_ref, key_t_ref, key_ref, bias_ref, prob_ref, acc_ref = refs
    blocks = [block[...] for block in inputs]
    slots = turned_ref.shape[0]
    span = bias_ref.shape[0]
    key_heads = key_ref.shape[1] // HEAD_DIM // 2
    heads = turned_ref.shape[1] // HEAD_DIM // key_heads
    starts = [pl.multiple_of(meta_ref[hop], ALIGN) for hop in range(ctx_size)]
    my_start, my_count = starts[0], meta_ref[ctx_size]
    sent_hops = list(range(1, ctx_size))
    if relayed(ctx_size):
        last = lax.axis_index("ctx") == ctx_size - 1
        alpha, beta, gamma, delta = blocks
        blocks = [jnp.where(last, alpha, gamma), jnp.where(last, beta, alpha), delta]
        sent_hops = [jnp.where(last, 3, 1), 2, jnp.where(last, 1, 2)]

    key_ref[...] = jnp.zeros_like(key_ref)
    for hop in range(ctx_size - 1, 0, -1):
        key_ref[pl.ds(starts[hop], slots), :] = blocks[hop - 1]
    place = lax.broadcasted_iota(jnp.int32, bias_ref.shape, 0)
    seen = place < 0
    for hop in range(1, ctx_size):
        end = starts[hop] + meta_ref[ctx_size + hop]
        seen = seen | ((place >= starts[hop]) & (place < end))
    bias_ref[...] = jnp.where(seen, 0.0, HIDDEN)
    live = lax.broadcasted_iota(jnp.int32, (1, slots), 1) < my_count
    acc_ref[...] = jnp.zeros_like(acc_ref)
    for key_head in range(key_heads):
        key_t = key_ref[:span, key_lanes(key_head)].astype(jnp.float32).T.astype(jnp.bfloat16)
        key_t_ref[key_head * HEAD_DIM : (key_head + 1) * HEAD_DIM, :] = key_t

    def one_head(key_head, head, rows, width):
        place = key_head * heads + head
        lanes = pl.ds(pl.multiple_of(place * HEAD_DIM, HEAD_DIM), HEAD_DIM)
        columns = pl.ds(pl.multiple_of(head * slots, slots), width)
        bias = jnp.concatenate([bias_ref[:rows, :]] * (width // HEAD_DIM), axis=1)
        scores = dot(
            key_ref[:rows, key_lanes(key_head)], turned_t_ref[lanes, :width], ((1,), (0,))
        )
        scores = scores + bias
        prob_grad = dot(
            key_ref[:rows, value_lanes(key_head)], grad_t_ref[lanes, :width], ((1,), (0,))
        )
        own_peak = sums_ref[place, 0:1, :width]
        peak = jnp.maximum(own_peak, fold(scores, jnp.maximum, jnp.max))
        share = jnp.exp2((own_peak - peak) * EXP2_SCALE)
        weights = jnp.exp2((scores - peak) * EXP2_SCALE)
        total = sums_ref[place, 1:2, :width] * share + fold(weights, jnp.add, jnp.sum)
        inverse = 1.0 / total
        product = sums_ref[place, 2:3, :width] * share
        delta = (product + fold(weights * prob_grad, jnp.add, jnp.sum)) * inverse
        inverse = jnp.where(live[:, :width], inverse, 0.0)
        joined_ref[place, 0:1, :width] = share * inverse
        joined_ref[place, 1:2, :width] = delta
        prob = weights * inverse
        prob_ref[:rows, columns] = prob.astype(jnp.bfloat16)
        score_grad = (prob * (prob_grad - delta)).astype(jnp.bfloat16)
        score_grad_ref[key_head, :rows, columns] = score_grad
        if width < slots:
            rest = pl.ds(pl.multiple_of(head * slots + width, HEAD_DIM), slots - width)
            none = jnp.zeros((rows, slots - width), jnp.bfloat16)
            prob_ref[:rows, rest] = none
            score_grad_ref[key_head, :rows, rest] = none
            joined_ref[place, 0:2, width:] = jnp.zeros((2, slots - width), jnp.float32)

    for key_head in range(key_heads):
        above = 0
        for rows, width in sizes:
            fits = (my_start > above) & (my_start <= rows)
            if width < slots:
                fits = (my_start > 0) & (my_count <= width)
            elif any(size[1] < slots for size in sizes):
                fits = fits & (my_count > sizes[-1][1])

            @pl.when(fits)
            def _():
                def step(index, carry):
                    for part in range(step_heads):
                        one_head(key_head, index * step_heads + part, rows, width)
                    return carry

                lax.fori_loop(0, heads // step_heads, step, 0)
                if rows % CHUNK:
                    beyond = slice(rows, rows + CHUNK - rows % CHUNK)
                    none = jnp.zeros((CHUNK - rows % CHUNK, heads * slots), jnp.bfloat16)
                    prob_ref[beyond, :] = none
                    score_grad_ref[key_head, beyond, :] = none

            above = rows if width == slots else above

        @pl.when(my_start == 0)
        def _():
            for place in range(key_head * heads, (key_head + 1) * heads):
                inverse = 1.0 / sums_ref[place, 1:2, :]
                joined_ref[place, 0:1, :] = jnp.where(live, inverse, 0.0)
                joined_ref[place, 1:2, :] = sums_ref[place, 2:3, :] * inverse

        for chunk in range(0, span, CHUNK):

            @pl.when(chunk < my_start)
            def _():
                rows = slice(chunk, chunk + CHUNK)
                acc_ref[rows, :] = terms_of(
                    prob_ref[rows, :],
                    score_grad_ref[key_head, rows, :],
                    stacked(turned_ref, key_head * heads * HEAD_DIM, heads),
                    stacked(grad_ref, key_head * heads * HEAD_DIM, heads),
                )

        for hop, term_ref in zip(sent_hops, terms):
            start = pl.multiple_of(meta_ref[hop], ALIGN)
            term = acc_ref[pl.ds(start, slots), :].astype(term_ref.dtype)
            term_ref[:, 2 * key_head * HEAD_DIM : 2 * (key_head + 1) * HEAD_DIM] = term


def relayed(ctx_size):
    return ctx_size == 4


def scores(meta, turned, out_grad, turned_t, grad_t, sums, blocks, routed, ctx_size):
    slots, width = blocks[0].shape
    key_heads = width // HEAD_DIM // 2
    heads = turned.shape[1] // HEAD_DIM // key_heads
    span = -(-(routed + ctx_size * ALIGN) // CHUNK) * CHUNK
    sizes, step_heads = [(span, slots)], 1
    if span == 2 * CHUNK and routed - slots // 2 + ctx_size * ALIGN <= 3 * CHUNK // 2 + ALIGN:
        sizes, step_heads = [(CHUNK, slots), (3 * CHUNK // 2, slots), (span, slots // 2)], 4
    terms = [jax.ShapeDtypeStruct((slots, width), jnp.bfloat16)] * (ctx_size - 1)
    if relayed(ctx_size):
        terms[2] = jax.ShapeDtypeStruct((slots, width), jnp.float32)
    outs = pl.pallas_call(
        functools.partial(scores_kernel, ctx_size, sizes, step_heads),
        out_shape=(
            *terms,
            jax.ShapeDtypeStruct((key_heads, span, heads * slots), jnp.bfloat16),
            jax.ShapeDtypeStruct((key_heads * heads, 8, slots), jnp.float32),
            jax.ShapeDtypeStruct((key_heads * HEAD_DIM, span), jnp.bfloat16),
        ),
        in_specs=[SMEM] + [VMEM] * (5 + len(blocks)),
        out_specs=(VMEM,) * (ctx_size + 2),
        scratch_shapes=[
            pltpu.VMEM((span + slots, width), jnp.bfloat16),
            pltpu.VMEM((span, HEAD_DIM), jnp.float32),
            pltpu.VMEM((span, heads * slots), jnp.bfloat16),
            pltpu.VMEM((span + slots, 2 * HEAD_DIM), jnp.float32),
        ],
        compiler_params=vmem(routed, 28, 60),
        cost_estimate=pl.CostEstimate(
            flops=8 * 10**9, bytes_accessed=12 * 1024 * 1024, transcendentals=0
        ),
        name="scores",
    )(meta, turned, out_grad, turned_t, grad_t, sums, *blocks)
    return outs[: ctx_size - 1], outs[ctx_size - 1 :]


def local_kernel(
    part,
    key_head,
    meta_ref,
    cos_ref,
    sin_ref,
    turned_ref,
    grad_ref,
    sent_ref,
    weight_ref,
    product_ref,
    score_grad_ref,
    joined_ref,
    key_t_ref,
    *refs,
):
    later = (len(refs) - 5) // 2
    dq_ref, own_ref = refs[later : later + 2]
    prob_ref, own_grad_ref, sum_ref = refs[-3:]
    for index in range(later):
        refs[later + 2 + index][...] = refs[index][...]
    slots = turned_ref.shape[0]
    heads = prob_ref.shape[1] // slots
    span = key_t_ref.shape[1]
    my_start = meta_ref[0]
    own_key_t = sent_ref[:, key_lanes(key_head)].astype(jnp.float32).T.astype(jnp.bfloat16)
    for head in range(heads):
        columns = slice(head * slots, (head + 1) * slots)
        place = part * heads + head
        prob = weight_ref[key_head * heads + head] * joined_ref[place, 0:1, :]
        prob_ref[:, columns] = prob.astype(jnp.bfloat16)
        product = product_ref[key_head * heads + head] - joined_ref[place, 1:2, :]
        score_grad = (prob * product).astype(jnp.bfloat16)
        own_grad_ref[:, columns] = score_grad
        sum_ref[head] = dot(own_key_t, score_grad, ((1,), (0,)))
    for chunk in range(0, span, CHUNK):

        @pl.when(chunk < my_start)
        def _():
            rows = slice(chunk, chunk + CHUNK)
            key_t = key_t_ref[part * HEAD_DIM : (part + 1) * HEAD_DIM, rows]
            for head in range(heads):
                columns = slice(head * slots, (head + 1) * slots)
                sum_ref[head] += dot(key_t, score_grad_ref[part, rows, columns], ((1,), (0,)))

    lane = key_head * heads * HEAD_DIM
    for head in range(heads):
        grad = turn_back((sum_ref[head] * SCORE_SCALE).T, cos_ref[...], sin_ref[...])
        dq_ref[:, head * HEAD_DIM : (head + 1) * HEAD_DIM] = grad.astype(jnp.bfloat16)
    own_ref[...] = terms_of(
        prob_ref[...],
        own_grad_ref[...],
        stacked(turned_ref, lane, heads),
        stacked(grad_ref, lane, heads),
    )


def local_terms(
    part, key_head, meta, cos_full, sin_full, turned, out_grad, sent, own, joined, later
):
    slots = turned.shape[0]
    heads = turned.shape[1] // (sent.shape[1] // 2)
    weight, product, _ = own
    operands = (meta, cos_full, sin_full, turned, out_grad, sent, weight, product, *joined, *later)
    return pl.pallas_call(
        functools.partial(local_kernel, part, key_head),
        out_shape=(
            jax.ShapeDtypeStruct((slots, heads * HEAD_DIM), jnp.bfloat16),
            jax.ShapeDtypeStruct((slots, 2 * HEAD_DIM), jnp.float32),
            *[jax.ShapeDtypeStruct(term.shape, term.dtype) for term in later],
        ),
        in_specs=[SMEM] + [VMEM] * (len(operands) - 1),
        out_specs=(VMEM,) * (2 + len(later)),
        scratch_shapes=[
            pltpu.VMEM((slots, heads * slots), jnp.bfloat16),
            pltpu.VMEM((slots, heads * slots), jnp.bfloat16),
            pltpu.VMEM((heads, HEAD_DIM, slots), jnp.float32),
        ],
        compiler_params=vmem(joined[2].shape[1] // 2, 16, 48),
        cost_estimate=pl.CostEstimate(
            flops=4 * 10**9, bytes_accessed=10 * 1024 * 1024, transcendentals=0
        ),
        name="local_terms",
    )(*operands)


def finish_kernel(ctx_size, meta_ref, cos_ref, sin_ref, *refs):
    key_grad_ref, value_grad_ref = refs[-2:]
    terms, owns = refs[: ctx_size - 1], refs[ctx_size - 1 : -2]
    slots = cos_ref.shape[0]
    live = lax.broadcasted_iota(jnp.int32, (slots, HEAD_DIM), 0) < meta_ref[ctx_size]
    total = jnp.concatenate([own[...] for own in owns], axis=1)
    for index, term in enumerate(terms):
        term = term[...].astype(jnp.float32)
        if index == 0 and relayed(ctx_size):
            term = jnp.where(lax.axis_index("ctx") == 2, 0.0, term)
        total += term
    for lane in range(0, key_grad_ref.shape[1], HEAD_DIM):
        lanes = slice(lane, lane + HEAD_DIM)
        key_term = turn_back(total[:, 2 * lane : 2 * lane + HEAD_DIM], cos_ref[...], sin_ref[...])
        value_term = total[:, 2 * lane + HEAD_DIM : 2 * (lane + HEAD_DIM)]
        key_grad_ref[:, lanes] = jnp.where(live, key_term, 0.0).astype(jnp.bfloat16)
        value_grad_ref[:, lanes] = jnp.where(live, value_term, 0.0).astype(jnp.bfloat16)


def finish(meta, cos_full, sin_full, owns, terms):
    slots, width = terms[0].shape
    grad = jax.ShapeDtypeStruct((slots, width // 2), jnp.bfloat16)
    return pl.pallas_call(
        functools.partial(finish_kernel, len(terms) + 1),
        out_shape=(grad, grad),
        in_specs=[SMEM] + [VMEM] * (2 + len(owns) + len(terms)),
        out_specs=(VMEM, VMEM),
        compiler_params=vmem(0, 16, 16),
        name="finish",
    )(meta, cos_full, sin_full, *terms, *owns)


def part_of(part, size):
    return slice(part * size, (part + 1) * size)


def spread(sent, sent_again, ctx_size):
    if relayed(ctx_size):
        alpha = lax.ppermute(sent, "ctx", [(0, 2), (2, 3)])
        beta = lax.ppermute(sent, "ctx", [(1, 3)])
        gamma = lax.ppermute(sent_again, "ctx", [(0, 1), (1, 2)])
        return [alpha, beta, gamma, lax.ppermute(alpha, "ctx", [(2, 3)])]
    blocks = [sent]
    for hop in range(1, ctx_size):
        pairs = [(shard, shard + 1) for shard in range(hop - 1, ctx_size - 1)]
        blocks.append(lax.ppermute(blocks[-1], "ctx", pairs))
    return blocks[1:]


def relay_first(first, third):
    first = lax.ppermute(first, "ctx", [(3, 2), (2, 1), (1, 0)])
    third = (third + first.astype(jnp.float32)).astype(jnp.bfloat16)
    return [first, lax.ppermute(third, "ctx", [(3, 2), (2, 0)])]


def descend(terms, ctx_size):
    arrived = []
    for hop, term in enumerate(terms, 1):
        pairs = [(shard + hop, shard) for shard in range(ctx_size - hop)]
        arrived.append(lax.ppermute(term, "ctx", pairs))
    return arrived


def body(positions, queries, keys, values, out_grad):
    ctx_size = lax.axis_size("ctx")
    routed = positions.shape[1]
    meta, cos_full, sin_full, sent = prepare(positions, keys[0], values[0], ctx_size)
    turned, turned_t, grad_t, sent_again = rotate_queries(
        cos_full, sin_full, queries[0], out_grad[0], sent
    )
    blocks = spread(sent, sent_again, ctx_size)
    own = own_scores(sent, turned_t, grad_t)
    key_heads = keys.shape[2] // HEAD_DIM
    parts = 1 if routed <= 512 else key_heads
    wide, narrow = queries.shape[2] // parts, sent.shape[1] // parts
    terms, joined = [], []
    for part in range(parts):
        columns = part_of(part, wide)
        outs = scores(
            meta,
            turned[:, columns],
            out_grad[0][:, columns],
            turned_t[columns],
            grad_t[columns],
            own[2][part_of(part, wide // HEAD_DIM)],
            [block[:, part_of(part, narrow)] for block in blocks],
            routed,
            ctx_size,
        )
        terms.append(outs[0])
        joined.append(outs[1])
    terms = [jnp.concatenate(term, axis=1) for term in zip(*terms)]
    if relayed(ctx_size):
        arrived, later = relay_first(terms[0], terms[2]), [terms[1]]
    else:
        arrived, later = descend(terms, ctx_size), []
    dqs, owns = [], []
    for key_head in range(key_heads):
        call, part = (0, key_head) if parts == 1 else (key_head, 0)
        dq, own_terms, *later = local_terms(
            part,
            key_head,
            meta,
            cos_full,
            sin_full,
            turned,
            out_grad[0],
            sent,
            own,
            joined[call],
            later,
        )
        dqs.append(dq)
        owns.append(own_terms)
        for term in later:
            arrived.append(lax.ppermute(term, "ctx", [(3, 1)]))
        later = []
    dq = jnp.concatenate(dqs, axis=1)
    key_grad, value_grad = finish(meta, cos_full, sin_full, owns, arrived)
    return (dq[None], key_grad[None], value_grad[None])


def solution(mesh):
    split = P(("groups", "dp"), "ctx", "mp")
    return jax.shard_map(
        body,
        mesh=mesh,
        in_specs=(P(("groups", "dp"), None), split, split, split, split),
        out_specs=(split, split, split),
        check_vma=False,
    )
```

```python
import functools
import math

import jax
import jax.numpy as jnp
import numpy as np
from jax import lax
from jax.experimental import pallas as pl
from jax.experimental.pallas import tpu as pltpu
from jax.sharding import PartitionSpec as P

HEAD_DIM = 128
HALF_DIM = HEAD_DIM // 2
TOK_SHARD = 1024
ROPE_BASE = 500000.0
SCORE_SCALE = 1.0 / math.sqrt(HEAD_DIM)
EXP2_SCALE = SCORE_SCALE * math.log2(math.e)
HIDDEN = -1e30
ALIGN = 16
CHUNK = 288
MIB = 1024 * 1024

VMEM = pl.BlockSpec(memory_space=pltpu.VMEM)
SMEM = pl.BlockSpec(memory_space=pltpu.SMEM)
HBM = pl.BlockSpec(memory_space=pltpu.HBM)


def vmem(routed, small, large):
    return pltpu.CompilerParams(vmem_limit_bytes=(small if routed <= 512 else large) * MIB)


def dot(left, right, contract):
    return lax.dot_general(left, right, (contract, ((), ())), preferred_element_type=jnp.float32)


def turn(field, cos_full, sin_full):
    return field * cos_full + pltpu.roll(field, HALF_DIM, 1) * sin_full


def turn_back(field, cos_full, sin_full):
    return field * cos_full - pltpu.roll(field, HALF_DIM, 1) * sin_full


def rope_rows():
    ladder = np.arange(HALF_DIM, dtype=np.float32)
    exponent = ladder * np.float32(-2.0 * math.log(ROPE_BASE) / HEAD_DIM)
    freq = np.exp(exponent.astype(np.float64)).astype(np.float32)
    sign = np.repeat(np.array([-1.0, 1.0], np.float32), HALF_DIM)
    return np.stack([np.concatenate([freq, freq]), sign])


def shard_layout(ctx_size, me, pos, meta_ref):
    shard_of = pos // TOK_SHARD
    for hop in range(2 * ctx_size):
        meta_ref[hop] = 0
    start = jnp.int32(0)
    first = jnp.int32(0)
    my_first = jnp.int32(0)
    for shard in range(ctx_size):
        count = jnp.sum(jnp.where(shard_of == shard, 1.0, 0.0)).astype(jnp.int32)
        my_first = jnp.where(me == shard, first, my_first)

        @pl.when(me >= shard)
        def _():
            meta_ref[me - shard] = start
            meta_ref[ctx_size + me - shard] = count

        first = first + count
        start = start + (count + ALIGN - 1) // ALIGN * ALIGN
    return my_first


def prepare_kernel(
    ctx_size, rows_hbm, pos_hbm, keys_hbm, values_hbm, meta_ref, cos_ref, sin_ref, sent_ref, turned_ref, *refs
):
    rows_ref, pos_ref, keys_ref, values_ref, sems = refs
    sources = (pos_hbm, rows_hbm, keys_hbm, values_hbm)
    targets = (pos_ref, rows_ref, keys_ref, values_ref)
    copies = [
        pltpu.make_async_copy(source, target, sems.at[index])
        for index, (source, target) in enumerate(zip(sources, targets))
    ]
    for copy in copies:
        copy.start()
    copies[0].wait()
    slots = keys_ref.shape[0]
    pos = pos_ref[...]
    my_first = shard_layout(ctx_size, lax.axis_index("ctx"), pos, meta_ref)
    shape = (slots, pos.shape[1])
    gap = lax.broadcasted_iota(jnp.int32, shape, 1) - lax.broadcasted_iota(jnp.int32, shape, 0)
    named = jnp.where(gap == my_first, pos.astype(jnp.float32), 0.0)
    copies[1].wait()
    angles = jnp.sum(named, axis=1, keepdims=True) * rows_ref[0:1, :]
    cos_full = jnp.cos(angles)
    sin_full = jnp.sin(angles) * rows_ref[1:2, :]
    cos_ref[...] = cos_full
    sin_ref[...] = sin_full
    copies[2].wait()
    copies[3].wait()
    for lane in range(0, keys_ref.shape[1], HEAD_DIM):
        lanes = slice(lane, lane + HEAD_DIM)
        key = turn(keys_ref[:, lanes].astype(jnp.float32), cos_full, sin_full)
        middle = 2 * lane + HEAD_DIM
        turned_ref[:, lanes] = key.astype(jnp.bfloat16)
        sent_ref[:, 2 * lane : middle] = key.astype(jnp.bfloat16)
        sent_ref[:, middle : middle + HEAD_DIM] = values_ref[:, lanes]


def prepare(positions, keys, values, ctx_size):
    slots, width = keys.shape
    rows = jnp.asarray(rope_rows())
    table = jax.ShapeDtypeStruct((slots, HEAD_DIM), jnp.float32)
    sent = jax.ShapeDtypeStruct((slots, 2 * width), jnp.bfloat16)
    operands = (rows, positions, keys, values)
    return pl.pallas_call(
        functools.partial(prepare_kernel, ctx_size),
        out_shape=(
            jax.ShapeDtypeStruct((2 * ctx_size,), jnp.int32),
            table,
            table,
            sent,
            jax.ShapeDtypeStruct((slots, width), jnp.bfloat16),
        ),
        in_specs=[HBM] * 4,
        out_specs=(SMEM, VMEM, VMEM, VMEM, VMEM),
        scratch_shapes=[pltpu.VMEM(operand.shape, operand.dtype) for operand in operands]
        + [pltpu.SemaphoreType.DMA((4,))],
        compiler_params=vmem(positions.shape[1], 60, 60),
        name="prepare",
    )(*operands)


def queries_kernel(
    cos_ref,
    sin_ref,
    query_ref,
    grad_ref,
    sent_ref,
    turned_ref,
    turned_t_ref,
    grad_t_ref,
    sent_again_ref,
):
    sent_again_ref[...] = sent_ref[...]
    for lane in range(0, query_ref.shape[1], HEAD_DIM):
        lanes = slice(lane, lane + HEAD_DIM)
        query = turn(query_ref[:, lanes].astype(jnp.float32), cos_ref[...], sin_ref[...])
        turned_ref[:, lanes] = query.astype(jnp.bfloat16)
        turned_t_ref[lanes, :] = query.T.astype(jnp.bfloat16)
        grad_t_ref[lanes, :] = grad_ref[:, lanes].astype(jnp.float32).T.astype(jnp.bfloat16)


def rotate_queries(cos_full, sin_full, queries, out_grad, sent):
    slots, width = queries.shape
    straight = jax.ShapeDtypeStruct((slots, width), jnp.bfloat16)
    across = jax.ShapeDtypeStruct((width, slots), jnp.bfloat16)
    return pl.pallas_call(
        queries_kernel,
        out_shape=(straight, across, across, jax.ShapeDtypeStruct(sent.shape, sent.dtype)),
        in_specs=[VMEM] * 5,
        out_specs=(VMEM,) * 4,
        compiler_params=vmem(0, 16, 16),
        cost_estimate=pl.CostEstimate(
            flops=3 * 10**9, bytes_accessed=4 * 1024 * 1024, transcendentals=0
        ),
        name="rotate_queries",
    )(cos_full, sin_full, queries, out_grad, sent)


def stacked(ref, lane, heads, width):
    parts = [ref[:width, lane + h * HEAD_DIM : lane + (h + 1) * HEAD_DIM] for h in range(heads)]
    return jnp.concatenate(parts, axis=0)


def beside(ref, rows, slots, width):
    if width == slots:
        return ref[:rows, :]
    parts = [ref[:rows, lane : lane + width] for lane in range(0, ref.shape[1], slots)]
    return jnp.concatenate(parts, axis=1)


def woven(keys, values):
    parts = []
    for lane in range(0, keys.shape[1], HEAD_DIM):
        parts += [keys[:, lane : lane + HEAD_DIM], values[:, lane : lane + HEAD_DIM]]
    return jnp.concatenate(parts, axis=1)


def terms_of(probs, score_grads, queries, grads):
    key_term = dot(score_grads, queries, ((1,), (0,))) * SCORE_SCALE
    return jnp.concatenate([key_term, dot(probs, grads, ((1,), (0,)))], axis=1)


def fold(field, join, reduce):
    while field.shape[0] % 16 == 0:
        half = field.shape[0] // 2
        field = join(field[:half], field[half:])
    return reduce(field, axis=0, keepdims=True)


def head_lanes(head):
    return slice(head * HEAD_DIM, (head + 1) * HEAD_DIM)


def key_lanes(key_head):
    return slice(2 * key_head * HEAD_DIM, (2 * key_head + 1) * HEAD_DIM)


def value_lanes(key_head):
    return slice((2 * key_head + 1) * HEAD_DIM, 2 * (key_head + 1) * HEAD_DIM)


def own_kernel(step_heads, sent_ref, turned_t_ref, grad_t_ref, weight_ref, product_ref, sums_ref, bias_ref):
    slots = sent_ref.shape[0]
    key_heads = sent_ref.shape[1] // HEAD_DIM // 2
    heads = turned_t_ref.shape[0] // HEAD_DIM // key_heads
    key_id = lax.broadcasted_iota(jnp.int32, (slots, slots), 0)
    slot_id = lax.broadcasted_iota(jnp.int32, (slots, slots), 1)
    bias_ref[...] = jnp.where(key_id <= slot_id, 0.0, HIDDEN)
    for key_head in range(key_heads):

        def step(index, carry):
            for part in range(step_heads):
                head = key_head * heads + index * step_heads + part
                rows = pl.ds(pl.multiple_of(head * HEAD_DIM, HEAD_DIM), HEAD_DIM)
                scores = dot(sent_ref[:, key_lanes(key_head)], turned_t_ref[rows, :], ((1,), (0,)))
                scores = scores + bias_ref[...]
                prob_grad = dot(sent_ref[:, value_lanes(key_head)], grad_t_ref[rows, :], ((1,), (0,)))
                peak = fold(scores, jnp.maximum, jnp.max)
                weights = jnp.exp2((scores - peak) * EXP2_SCALE)
                weight_ref[head] = weights
                product_ref[head] = prob_grad
                sums_ref[head, 0:1, :] = peak
                sums_ref[head, 1:2, :] = fold(weights, jnp.add, jnp.sum)
                sums_ref[head, 2:3, :] = fold(weights * prob_grad, jnp.add, jnp.sum)
            return carry

        lax.fori_loop(0, heads // step_heads, step, 0)


def own_scores(sent, turned_t, grad_t):
    slots = sent.shape[0]
    heads = turned_t.shape[0] // HEAD_DIM
    square = jax.ShapeDtypeStruct((heads, slots, slots), jnp.float32)
    return pl.pallas_call(
        functools.partial(own_kernel, 4),
        out_shape=(square, square, jax.ShapeDtypeStruct((heads, 8, slots), jnp.float32)),
        in_specs=[VMEM] * 3,
        out_specs=(VMEM,) * 3,
        scratch_shapes=[pltpu.VMEM((slots, slots), jnp.float32)],
        compiler_params=vmem(0, 16, 16),
        cost_estimate=pl.CostEstimate(
            flops=5 * 10**9, bytes_accessed=10 * 1024 * 1024, transcendentals=0
        ),
        name="own_scores",
    )(sent, turned_t, grad_t)


def scores_kernel(
    ctx_size,
    sizes,
    step_heads,
    meta_ref,
    turned_ref,
    grad_ref,
    turned_t_ref,
    grad_t_ref,
    sums_ref,
    *refs,
):
    inputs = refs[: -6 - ctx_size]
    refs = refs[len(inputs) :]
    terms, refs = refs[: ctx_size - 1], refs[ctx_size - 1 :]
    score_grad_ref, joined_ref, key_ref, value_ref, bias_ref, prob_ref, acc_ref = refs
    blocks = [block[...] for block in inputs]
    slots = turned_ref.shape[0]
    span = bias_ref.shape[0]
    key_heads = key_ref.shape[1] // HEAD_DIM
    heads = turned_ref.shape[1] // HEAD_DIM // key_heads
    starts = [pl.multiple_of(meta_ref[hop], ALIGN) for hop in range(ctx_size)]
    my_start, my_count = starts[0], meta_ref[ctx_size]
    sent_hops = list(range(1, ctx_size))
    if relayed(ctx_size):
        last = lax.axis_index("ctx") == ctx_size - 1
        alpha, beta, gamma, delta = woven(*blocks[:2]), blocks[2], blocks[3], woven(*blocks[4:])
        blocks = [jnp.where(last, alpha, gamma), jnp.where(last, beta, alpha), delta]
        sent_hops = [jnp.where(last, 3, 1), 2, jnp.where(last, 1, 2)]

    key_ref[slots:span, :] = jnp.zeros_like(key_ref[slots:span, :])
    value_ref[slots:span, :] = jnp.zeros_like(key_ref[slots:span, :])
    for hop in range(ctx_size - 1, 0, -1):
        for key_head in range(key_heads):
            lanes = head_lanes(key_head)
            key_ref[pl.ds(starts[hop], slots), lanes] = blocks[hop - 1][:, key_lanes(key_head)]
            value_ref[pl.ds(starts[hop], slots), lanes] = blocks[hop - 1][:, value_lanes(key_head)]
    place = lax.broadcasted_iota(jnp.int32, bias_ref.shape, 0)
    seen = place < 0
    for hop in range(1, ctx_size):
        end = starts[hop] + meta_ref[ctx_size + hop]
        seen = seen | ((place >= starts[hop]) & (place < end))
    bias_ref[...] = jnp.where(seen, 0.0, HIDDEN)
    live = lax.broadcasted_iota(jnp.int32, (1, slots), 1) < my_count

    def one_head(key_head, head, rows, width):
        place = key_head * heads + head
        lanes = pl.ds(pl.multiple_of(place * HEAD_DIM, HEAD_DIM), HEAD_DIM)
        columns = pl.ds(pl.multiple_of(head * slots, slots), width)
        bias = jnp.concatenate([bias_ref[:rows, :]] * (width // HEAD_DIM), axis=1)
        scores = dot(
            key_ref[:rows, head_lanes(key_head)], turned_t_ref[lanes, :width], ((1,), (0,))
        )
        scores = scores + bias
        prob_grad = dot(
            value_ref[:rows, head_lanes(key_head)], grad_t_ref[lanes, :width], ((1,), (0,))
        )
        own_peak = sums_ref[place, 0:1, :width]
        peak = jnp.maximum(own_peak, fold(scores, jnp.maximum, jnp.max))
        share = jnp.exp2((own_peak - peak) * EXP2_SCALE)
        weights = jnp.exp2((scores - peak) * EXP2_SCALE)
        total = sums_ref[place, 1:2, :width] * share + fold(weights, jnp.add, jnp.sum)
        inverse = 1.0 / total
        product = sums_ref[place, 2:3, :width] * share
        delta = (product + fold(weights * prob_grad, jnp.add, jnp.sum)) * inverse
        inverse = jnp.where(live[:, :width], inverse, 0.0)
        joined_ref[place, 0:1, :width] = share * inverse
        joined_ref[place, 1:2, :width] = delta
        prob = weights * inverse
        prob_ref[:rows, columns] = prob.astype(jnp.bfloat16)
        score_grad = (prob * (prob_grad - delta)).astype(jnp.bfloat16)
        score_grad_ref[key_head, :rows, columns] = score_grad
        if width < slots:
            rest = pl.ds(pl.multiple_of(head * slots + width, HEAD_DIM), slots - width)
            none = jnp.zeros((rows, slots - width), jnp.bfloat16)
            score_grad_ref[key_head, :rows, rest] = none
            joined_ref[place, 0:2, width:] = jnp.zeros((2, slots - width), jnp.float32)

    for key_head in range(key_heads):
        above = 0
        for rows, width in sizes:
            fits = (my_start > above) & (my_start <= rows)
            if width < slots:
                fits = (my_start > 0) & (my_count <= width)
            elif any(size[1] < slots for size in sizes):
                fits = fits & (my_count > sizes[-1][1])

            @pl.when(fits)
            def _():
                def step(index, carry):
                    for part in range(step_heads):
                        one_head(key_head, index * step_heads + part, rows, width)
                    return carry

                lax.fori_loop(0, heads // step_heads, step, 0)
                if rows % CHUNK:
                    beyond = slice(rows, rows + CHUNK - rows % CHUNK)
                    none = jnp.zeros((CHUNK - rows % CHUNK, heads * slots), jnp.bfloat16)
                    score_grad_ref[key_head, beyond, :] = none
                lane = key_head * heads * HEAD_DIM
                acc_ref[:rows, :] = terms_of(
                    beside(prob_ref, rows, slots, width),
                    beside(score_grad_ref.at[key_head], rows, slots, width),
                    stacked(turned_ref, lane, heads, width),
                    stacked(grad_ref, lane, heads, width),
                )

            above = rows if width == slots else above

        @pl.when(my_start == 0)
        def _():
            for place in range(key_head * heads, (key_head + 1) * heads):
                inverse = 1.0 / sums_ref[place, 1:2, :]
                joined_ref[place, 0:1, :] = jnp.where(live, inverse, 0.0)
                joined_ref[place, 1:2, :] = sums_ref[place, 2:3, :] * inverse

        for hop, term_ref in zip(sent_hops, terms):
            start = pl.multiple_of(meta_ref[hop], ALIGN)
            term = acc_ref[pl.ds(start, slots), :].astype(term_ref.dtype)
            term_ref[:, 2 * key_head * HEAD_DIM : 2 * (key_head + 1) * HEAD_DIM] = term


def relayed(ctx_size):
    return ctx_size == 4


def scores(meta, turned, out_grad, turned_t, grad_t, sums, blocks, routed, ctx_size):
    slots, width = blocks[0].shape
    if relayed(ctx_size):
        width = blocks[2].shape[1]
    key_heads = width // HEAD_DIM // 2
    heads = turned.shape[1] // HEAD_DIM // key_heads
    span = -(-(routed + ctx_size * ALIGN) // CHUNK) * CHUNK
    sizes, step_heads = [(span, slots)], 1
    if span == 2 * CHUNK and routed - slots // 2 + ctx_size * ALIGN <= 3 * CHUNK // 2 + ALIGN:
        sizes, step_heads = [(CHUNK, slots), (3 * CHUNK // 2, slots), (span, slots // 2)], 4
    terms = [jax.ShapeDtypeStruct((slots, width), jnp.bfloat16)] * (ctx_size - 1)
    if relayed(ctx_size):
        terms[2] = jax.ShapeDtypeStruct((slots, width), jnp.float32)
    outs = pl.pallas_call(
        functools.partial(scores_kernel, ctx_size, sizes, step_heads),
        out_shape=(
            *terms,
            jax.ShapeDtypeStruct((key_heads, span, heads * slots), jnp.bfloat16),
            jax.ShapeDtypeStruct((key_heads * heads, 8, slots), jnp.float32),
            jax.ShapeDtypeStruct((span + slots, key_heads * HEAD_DIM), jnp.bfloat16),
        ),
        in_specs=[SMEM] + [VMEM] * (5 + len(blocks)),
        out_specs=(VMEM,) * (ctx_size + 2),
        scratch_shapes=[
            pltpu.VMEM((span + slots, width // 2), jnp.bfloat16),
            pltpu.VMEM((span, HEAD_DIM), jnp.float32),
            pltpu.VMEM((span, heads * slots), jnp.bfloat16),
            pltpu.VMEM((span + slots, 2 * HEAD_DIM), jnp.float32),
        ],
        compiler_params=vmem(routed, 28, 60),
        cost_estimate=pl.CostEstimate(
            flops=8 * 10**9, bytes_accessed=12 * 1024 * 1024, transcendentals=0
        ),
        name="scores",
    )(meta, turned, out_grad, turned_t, grad_t, sums, *blocks)
    return outs[: ctx_size - 1], outs[ctx_size - 1 :]


def local_kernel(
    part,
    key_head,
    meta_ref,
    cos_ref,
    sin_ref,
    turned_ref,
    grad_ref,
    sent_ref,
    weight_ref,
    product_ref,
    score_grad_ref,
    joined_ref,
    key_ref,
    *refs,
):
    later = (len(refs) - 5) // 2
    dq_ref, own_ref = refs[later : later + 2]
    prob_ref, own_grad_ref, sum_ref = refs[-3:]
    for index in range(later):
        refs[later + 2 + index][...] = refs[index][...]
    slots = turned_ref.shape[0]
    heads = prob_ref.shape[1] // slots
    span = score_grad_ref.shape[1]
    my_start = meta_ref[0]
    own_key_t = sent_ref[:, key_lanes(key_head)].astype(jnp.float32).T.astype(jnp.bfloat16)
    for head in range(heads):
        columns = slice(head * slots, (head + 1) * slots)
        place = part * heads + head
        prob = weight_ref[key_head * heads + head] * joined_ref[place, 0:1, :]
        prob_ref[:, columns] = prob.astype(jnp.bfloat16)
        product = product_ref[key_head * heads + head] - joined_ref[place, 1:2, :]
        score_grad = (prob * product).astype(jnp.bfloat16)
        own_grad_ref[:, columns] = score_grad
        sum_ref[head] = dot(own_key_t, score_grad, ((1,), (0,)))
    for chunk in range(0, span, CHUNK):

        @pl.when(chunk < my_start)
        def _():
            rows = slice(chunk, chunk + CHUNK)
            key_t = key_ref[rows, head_lanes(part)].astype(jnp.float32).T.astype(jnp.bfloat16)
            for head in range(heads):
                columns = slice(head * slots, (head + 1) * slots)
                sum_ref[head] += dot(key_t, score_grad_ref[part, rows, columns], ((1,), (0,)))

    lane = key_head * heads * HEAD_DIM
    for head in range(heads):
        grad = turn_back((sum_ref[head] * SCORE_SCALE).T, cos_ref[...], sin_ref[...])
        dq_ref[:, head * HEAD_DIM : (head + 1) * HEAD_DIM] = grad.astype(jnp.bfloat16)
    own_ref[...] = terms_of(
        prob_ref[...],
        own_grad_ref[...],
        stacked(turned_ref, lane, heads, slots),
        stacked(grad_ref, lane, heads, slots),
    )


def local_terms(
    part, key_head, meta, cos_full, sin_full, turned, out_grad, sent, own, joined, later
):
    slots = turned.shape[0]
    heads = turned.shape[1] // (sent.shape[1] // 2)
    weight, product, _ = own
    operands = (meta, cos_full, sin_full, turned, out_grad, sent, weight, product, *joined, *later)
    return pl.pallas_call(
        functools.partial(local_kernel, part, key_head),
        out_shape=(
            jax.ShapeDtypeStruct((slots, heads * HEAD_DIM), jnp.bfloat16),
            jax.ShapeDtypeStruct((slots, 2 * HEAD_DIM), jnp.float32),
            *[jax.ShapeDtypeStruct(term.shape, term.dtype) for term in later],
        ),
        in_specs=[SMEM] + [VMEM] * (len(operands) - 1),
        out_specs=(VMEM,) * (2 + len(later)),
        scratch_shapes=[
            pltpu.VMEM((slots, heads * slots), jnp.bfloat16),
            pltpu.VMEM((slots, heads * slots), jnp.bfloat16),
            pltpu.VMEM((heads, HEAD_DIM, slots), jnp.float32),
        ],
        compiler_params=vmem(joined[0].shape[1] // 2, 16, 48),
        cost_estimate=pl.CostEstimate(
            flops=4 * 10**9, bytes_accessed=10 * 1024 * 1024, transcendentals=0
        ),
        name="local_terms",
    )(*operands)


def finish_kernel(ctx_size, meta_ref, cos_ref, sin_ref, *refs):
    key_grad_ref, value_grad_ref = refs[-2:]
    terms, owns = refs[: ctx_size - 1], refs[ctx_size - 1 : -2]
    slots = cos_ref.shape[0]
    live = lax.broadcasted_iota(jnp.int32, (slots, HEAD_DIM), 0) < meta_ref[ctx_size]
    total = jnp.concatenate([own[...] for own in owns], axis=1)
    for index, term in enumerate(terms):
        term = term[...].astype(jnp.float32)
        if index == 0 and relayed(ctx_size):
            term = jnp.where(lax.axis_index("ctx") == 2, 0.0, term)
        total += term
    for lane in range(0, key_grad_ref.shape[1], HEAD_DIM):
        lanes = slice(lane, lane + HEAD_DIM)
        key_term = turn_back(total[:, 2 * lane : 2 * lane + HEAD_DIM], cos_ref[...], sin_ref[...])
        value_term = total[:, 2 * lane + HEAD_DIM : 2 * (lane + HEAD_DIM)]
        key_grad_ref[:, lanes] = jnp.where(live, key_term, 0.0).astype(jnp.bfloat16)
        value_grad_ref[:, lanes] = jnp.where(live, value_term, 0.0).astype(jnp.bfloat16)


def finish(meta, cos_full, sin_full, owns, terms):
    slots, width = terms[0].shape
    grad = jax.ShapeDtypeStruct((slots, width // 2), jnp.bfloat16)
    return pl.pallas_call(
        functools.partial(finish_kernel, len(terms) + 1),
        out_shape=(grad, grad),
        in_specs=[SMEM] + [VMEM] * (2 + len(owns) + len(terms)),
        out_specs=(VMEM, VMEM),
        compiler_params=vmem(0, 16, 16),
        name="finish",
    )(meta, cos_full, sin_full, *terms, *owns)


def part_of(part, size):
    return slice(part * size, (part + 1) * size)


def spread(sent, sent_again, turned_keys, values, ctx_size):
    if relayed(ctx_size):
        alpha = [lax.ppermute(part, "ctx", [(0, 2), (2, 3)]) for part in (turned_keys, values)]
        beta = lax.ppermute(sent, "ctx", [(1, 3)])
        gamma = lax.ppermute(sent_again, "ctx", [(0, 1), (1, 2)])
        delta = [lax.ppermute(part, "ctx", [(2, 3)]) for part in alpha]
        return [*alpha, beta, gamma, *delta]
    blocks = [sent]
    for hop in range(1, ctx_size):
        pairs = [(shard, shard + 1) for shard in range(hop - 1, ctx_size - 1)]
        blocks.append(lax.ppermute(blocks[-1], "ctx", pairs))
    return blocks[1:]


def relay_first(first, third):
    first = lax.ppermute(first, "ctx", [(3, 2), (2, 1), (1, 0)])
    third = (third + first.astype(jnp.float32)).astype(jnp.bfloat16)
    return [first, lax.ppermute(third, "ctx", [(3, 2), (2, 0)])]


def descend(terms, ctx_size):
    arrived = []
    for hop, term in enumerate(terms, 1):
        pairs = [(shard + hop, shard) for shard in range(ctx_size - hop)]
        arrived.append(lax.ppermute(term, "ctx", pairs))
    return arrived


def body(positions, queries, keys, values, out_grad):
    ctx_size = lax.axis_size("ctx")
    routed = positions.shape[1]
    meta, cos_full, sin_full, sent, turned_keys = prepare(positions, keys[0], values[0], ctx_size)
    turned, turned_t, grad_t, sent_again = rotate_queries(
        cos_full, sin_full, queries[0], out_grad[0], sent
    )
    blocks = spread(sent, sent_again, turned_keys, values[0], ctx_size)
    own = own_scores(sent, turned_t, grad_t)
    key_heads = keys.shape[2] // HEAD_DIM
    parts = 1 if routed <= 512 else key_heads
    wide, narrow = queries.shape[2] // parts, sent.shape[1] // parts
    terms, joined = [], []
    for part in range(parts):
        columns = part_of(part, wide)
        outs = scores(
            meta,
            turned[:, columns],
            out_grad[0][:, columns],
            turned_t[columns],
            grad_t[columns],
            own[2][part_of(part, wide // HEAD_DIM)],
            [block[:, part_of(part, narrow)] for block in blocks],
            routed,
            ctx_size,
        )
        terms.append(outs[0])
        joined.append(outs[1])
    terms = [jnp.concatenate(term, axis=1) for term in zip(*terms)]
    if relayed(ctx_size):
        arrived, later = relay_first(terms[0], terms[2]), [terms[1]]
    else:
        arrived, later = descend(terms, ctx_size), []
    dqs, owns = [], []
    for key_head in range(key_heads):
        call, part = (0, key_head) if parts == 1 else (key_head, 0)
        dq, own_terms, *later = local_terms(
            part,
            key_head,
            meta,
            cos_full,
            sin_full,
            turned,
            out_grad[0],
            sent,
            own,
            joined[call],
            later,
        )
        dqs.append(dq)
        owns.append(own_terms)
        for term in later:
            arrived.append(lax.ppermute(term, "ctx", [(3, 1)]))
        later = []
    dq = jnp.concatenate(dqs, axis=1)
    key_grad, value_grad = finish(meta, cos_full, sin_full, owns, arrived)
    return (dq[None], key_grad[None], value_grad[None])


def solution(mesh):
    split = P(("groups", "dp"), "ctx", "mp")
    return jax.shard_map(
        body,
        mesh=mesh,
        in_specs=(P(("groups", "dp"), None), split, split, split, split),
        out_specs=(split, split, split),
        check_vma=False,
    )
```

```python
import functools
import math

import jax
import jax.numpy as jnp
import numpy as np
from jax import lax
from jax.experimental import pallas as pl
from jax.experimental.pallas import tpu as pltpu
from jax.sharding import PartitionSpec as P

HEAD_DIM = 128
HALF_DIM = HEAD_DIM // 2
TOK_SHARD = 1024
ROPE_BASE = 500000.0
SCORE_SCALE = 1.0 / math.sqrt(HEAD_DIM)
EXP2_SCALE = SCORE_SCALE * math.log2(math.e)
HIDDEN = -1e30
ALIGN = 16
CHUNK = 288
MIB = 1024 * 1024

VMEM = pl.BlockSpec(memory_space=pltpu.VMEM)
SMEM = pl.BlockSpec(memory_space=pltpu.SMEM)


def vmem(routed, small, large):
    return pltpu.CompilerParams(vmem_limit_bytes=(small if routed <= 512 else large) * MIB)


def dot(left, right, contract):
    return lax.dot_general(left, right, (contract, ((), ())), preferred_element_type=jnp.float32)


def turn(field, cos_full, sin_full):
    return field * cos_full + pltpu.roll(field, HALF_DIM, 1) * sin_full


def turn_back(field, cos_full, sin_full):
    return field * cos_full - pltpu.roll(field, HALF_DIM, 1) * sin_full


def frequencies():
    ladder = np.arange(HALF_DIM, dtype=np.float32)
    exponent = ladder * np.float32(-2.0 * math.log(ROPE_BASE) / HEAD_DIM)
    freq = np.exp(exponent.astype(np.float64)).astype(np.float32)
    entry = lax.broadcasted_iota(jnp.int32, (1, HEAD_DIM), 1) % HALF_DIM
    row = jnp.zeros((1, HEAD_DIM), jnp.float32)
    for index in range(HALF_DIM):
        row = jnp.where(entry == index, float(freq[index]), row)
    return row


def shard_layout(ctx_size, me, pos, meta_ref):
    shard_of = pos // TOK_SHARD
    for hop in range(2 * ctx_size):
        meta_ref[hop] = 0
    start = jnp.int32(0)
    first = jnp.int32(0)
    my_first = jnp.int32(0)
    for shard in range(ctx_size):
        count = jnp.sum(jnp.where(shard_of == shard, 1.0, 0.0)).astype(jnp.int32)
        my_first = jnp.where(me == shard, first, my_first)

        @pl.when(me >= shard)
        def _():
            meta_ref[me - shard] = start
            meta_ref[ctx_size + me - shard] = count

        first = first + count
        start = start + (count + ALIGN - 1) // ALIGN * ALIGN
    return my_first


def prepare_kernel(
    ctx_size, pos_ref, keys_ref, values_ref, meta_ref, cos_ref, sin_ref, sent_ref, turned_ref
):
    slots = keys_ref.shape[0]
    pos = pos_ref[...]
    my_first = shard_layout(ctx_size, lax.axis_index("ctx"), pos, meta_ref)
    shape = (slots, pos.shape[1])
    gap = lax.broadcasted_iota(jnp.int32, shape, 1) - lax.broadcasted_iota(jnp.int32, shape, 0)
    named = jnp.where(gap == my_first, pos.astype(jnp.float32), 0.0)
    angles = jnp.sum(named, axis=1, keepdims=True) * frequencies()
    cos_full = jnp.cos(angles)
    front = lax.broadcasted_iota(jnp.int32, angles.shape, 1) < HALF_DIM
    sin_full = jnp.where(front, -jnp.sin(angles), jnp.sin(angles))
    cos_ref[...] = cos_full
    sin_ref[...] = sin_full
    for lane in range(0, keys_ref.shape[1], HEAD_DIM):
        lanes = slice(lane, lane + HEAD_DIM)
        key = turn(keys_ref[:, lanes].astype(jnp.float32), cos_full, sin_full)
        middle = 2 * lane + HEAD_DIM
        turned_ref[:, lanes] = key.astype(jnp.bfloat16)
        sent_ref[:, 2 * lane : middle] = key.astype(jnp.bfloat16)
        sent_ref[:, middle : middle + HEAD_DIM] = values_ref[:, lanes]


def prepare(positions, keys, values, ctx_size):
    slots, width = keys.shape
    table = jax.ShapeDtypeStruct((slots, HEAD_DIM), jnp.float32)
    sent = jax.ShapeDtypeStruct((slots, 2 * width), jnp.bfloat16)
    return pl.pallas_call(
        functools.partial(prepare_kernel, ctx_size),
        out_shape=(
            jax.ShapeDtypeStruct((2 * ctx_size,), jnp.int32),
            table,
            table,
            sent,
            jax.ShapeDtypeStruct((slots, width), jnp.bfloat16),
        ),
        in_specs=[VMEM] * 3,
        out_specs=(SMEM, VMEM, VMEM, VMEM, VMEM),
        compiler_params=vmem(positions.shape[1], 16, 32),
        name="prepare",
    )(positions, keys, values)


def queries_kernel(cos_ref, sin_ref, query_ref, grad_ref, *refs):
    turned_ref, turned_t_ref, grad_t_ref = refs[-3:]
    for lane in range(0, query_ref.shape[1], HEAD_DIM):
        lanes = slice(lane, lane + HEAD_DIM)
        query = turn(query_ref[:, lanes].astype(jnp.float32), cos_ref[...], sin_ref[...])
        turned_ref[:, lanes] = query.astype(jnp.bfloat16)
        turned_t_ref[lanes, :] = query.T.astype(jnp.bfloat16)
        grad_t_ref[lanes, :] = grad_ref[:, lanes].astype(jnp.float32).T.astype(jnp.bfloat16)


def rotate_queries(cos_full, sin_full, queries, out_grad, after):
    slots, width = queries.shape
    straight = jax.ShapeDtypeStruct((slots, width), jnp.bfloat16)
    across = jax.ShapeDtypeStruct((width, slots), jnp.bfloat16)
    return pl.pallas_call(
        queries_kernel,
        out_shape=(straight, across, across),
        in_specs=[VMEM] * 5,
        out_specs=(VMEM,) * 3,
        compiler_params=vmem(0, 16, 16),
        cost_estimate=pl.CostEstimate(
            flops=3 * 10**9, bytes_accessed=4 * 1024 * 1024, transcendentals=0
        ),
        name="rotate_queries",
    )(cos_full, sin_full, queries, out_grad, after)


def stacked(ref, lane, heads, width):
    parts = [ref[:width, lane + h * HEAD_DIM : lane + (h + 1) * HEAD_DIM] for h in range(heads)]
    return jnp.concatenate(parts, axis=0)


def beside(ref, rows, column, heads, slots, width):
    if width == slots:
        return ref[:rows, column : column + heads * slots]
    columns = [column + head * slots for head in range(heads)]
    return jnp.concatenate([ref[:rows, start : start + width] for start in columns], axis=1)


def woven(keys, values):
    parts = []
    for lane in range(0, keys.shape[1], HEAD_DIM):
        parts += [keys[:, lane : lane + HEAD_DIM], values[:, lane : lane + HEAD_DIM]]
    return jnp.concatenate(parts, axis=1)


def terms_of(probs, score_grads, queries, grads):
    key_term = dot(score_grads, queries, ((1,), (0,))) * SCORE_SCALE
    return jnp.concatenate([key_term, dot(probs, grads, ((1,), (0,)))], axis=1)


def fold(field, join, reduce):
    while field.shape[0] % 16 == 0:
        half = field.shape[0] // 2
        field = join(field[:half], field[half:])
    return reduce(field, axis=0, keepdims=True)


def head_lanes(head):
    return slice(head * HEAD_DIM, (head + 1) * HEAD_DIM)


def key_lanes(key_head):
    return slice(2 * key_head * HEAD_DIM, (2 * key_head + 1) * HEAD_DIM)


def value_lanes(key_head):
    return slice((2 * key_head + 1) * HEAD_DIM, 2 * (key_head + 1) * HEAD_DIM)


def own_kernel(step_heads, sent_ref, turned_t_ref, grad_t_ref, weight_ref, product_ref, sums_ref, bias_ref):
    slots = sent_ref.shape[0]
    key_heads = sent_ref.shape[1] // HEAD_DIM // 2
    heads = turned_t_ref.shape[0] // HEAD_DIM // key_heads
    key_id = lax.broadcasted_iota(jnp.int32, (slots, slots), 0)
    slot_id = lax.broadcasted_iota(jnp.int32, (slots, slots), 1)
    bias_ref[...] = jnp.where(key_id <= slot_id, 0.0, HIDDEN)
    for key_head in range(key_heads):

        def step(index, carry):
            for part in range(step_heads):
                head = key_head * heads + index * step_heads + part
                rows = pl.ds(pl.multiple_of(head * HEAD_DIM, HEAD_DIM), HEAD_DIM)
                scores = dot(sent_ref[:, key_lanes(key_head)], turned_t_ref[rows, :], ((1,), (0,)))
                scores = scores + bias_ref[...]
                prob_grad = dot(sent_ref[:, value_lanes(key_head)], grad_t_ref[rows, :], ((1,), (0,)))
                peak = fold(scores, jnp.maximum, jnp.max)
                weights = jnp.exp2((scores - peak) * EXP2_SCALE)
                weight_ref[head] = weights
                product_ref[head] = prob_grad
                sums_ref[head, 0:1, :] = peak
                sums_ref[head, 1:2, :] = fold(weights, jnp.add, jnp.sum)
                sums_ref[head, 2:3, :] = fold(weights * prob_grad, jnp.add, jnp.sum)
            return carry

        lax.fori_loop(0, heads // step_heads, step, 0)


def own_scores(sent, turned_t, grad_t):
    slots = sent.shape[0]
    heads = turned_t.shape[0] // HEAD_DIM
    square = jax.ShapeDtypeStruct((heads, slots, slots), jnp.float32)
    return pl.pallas_call(
        functools.partial(own_kernel, 4),
        out_shape=(square, square, jax.ShapeDtypeStruct((heads, 8, slots), jnp.float32)),
        in_specs=[VMEM] * 3,
        out_specs=(VMEM,) * 3,
        scratch_shapes=[pltpu.VMEM((slots, slots), jnp.float32)],
        compiler_params=vmem(0, 16, 16),
        cost_estimate=pl.CostEstimate(
            flops=5 * 10**9, bytes_accessed=10 * 1024 * 1024, transcendentals=0
        ),
        name="own_scores",
    )(sent, turned_t, grad_t)


def scores_kernel(
    ctx_size,
    sizes,
    step_units,
    meta_ref,
    turned_ref,
    grad_ref,
    turned_t_ref,
    grad_t_ref,
    sums_ref,
    *refs,
):
    inputs = refs[: -6 - ctx_size]
    refs = refs[len(inputs) :]
    terms, refs = refs[: ctx_size - 1], refs[ctx_size - 1 :]
    score_grad_ref, joined_ref, key_ref, value_ref, bias_ref, prob_ref, acc_ref = refs
    blocks = [block[...] for block in inputs]
    slots = turned_ref.shape[0]
    span = bias_ref.shape[0]
    key_heads = key_ref.shape[1] // HEAD_DIM
    heads = turned_ref.shape[1] // HEAD_DIM // key_heads
    starts = [pl.multiple_of(meta_ref[hop], ALIGN) for hop in range(ctx_size)]
    my_start, my_count = starts[0], meta_ref[ctx_size]
    sent_hops = list(range(1, ctx_size))
    if relayed(ctx_size):
        last = lax.axis_index("ctx") == ctx_size - 1
        alpha, beta, gamma, delta = woven(*blocks[:2]), blocks[2], blocks[3], woven(*blocks[4:])
        blocks = [jnp.where(last, alpha, gamma), jnp.where(last, beta, alpha), delta]
        sent_hops = [jnp.where(last, 3, 1), 2, jnp.where(last, 1, 2)]

    key_ref[slots:span, :] = jnp.zeros_like(key_ref[slots:span, :])
    value_ref[slots:span, :] = jnp.zeros_like(key_ref[slots:span, :])
    for hop in range(ctx_size - 1, 0, -1):
        for key_head in range(key_heads):
            lanes = head_lanes(key_head)
            key_ref[pl.ds(starts[hop], slots), lanes] = blocks[hop - 1][:, key_lanes(key_head)]
            value_ref[pl.ds(starts[hop], slots), lanes] = blocks[hop - 1][:, value_lanes(key_head)]
    place = lax.broadcasted_iota(jnp.int32, bias_ref.shape, 0)
    seen = place < 0
    for hop in range(1, ctx_size):
        end = starts[hop] + meta_ref[ctx_size + hop]
        seen = seen | ((place >= starts[hop]) & (place < end))
    bias_ref[...] = jnp.where(seen, 0.0, HIDDEN)
    live = lax.broadcasted_iota(jnp.int32, (1, slots), 1) < my_count

    def unit(places, rows, width):
        def joint(ref, index):
            return jnp.concatenate([ref[index(place)] for place in places], axis=1)

        def head_rows(place):
            row = pl.multiple_of(place * HEAD_DIM, HEAD_DIM)
            return (pl.ds(row, HEAD_DIM), slice(0, width))

        def sum_row(row):
            return joint(sums_ref, lambda place: (place, slice(row, row + 1), slice(0, width)))

        lane = pl.multiple_of(places[0] // heads * HEAD_DIM, HEAD_DIM)
        lanes = pl.ds(lane, HEAD_DIM)
        bias = jnp.concatenate([bias_ref[:rows, :]] * (len(places) * width // HEAD_DIM), axis=1)
        scores = dot(key_ref[:rows, lanes], joint(turned_t_ref, head_rows), ((1,), (0,))) + bias
        prob_grad = dot(value_ref[:rows, lanes], joint(grad_t_ref, head_rows), ((1,), (0,)))
        own_peak = sum_row(0)
        peak = jnp.maximum(own_peak, fold(scores, jnp.maximum, jnp.max))
        share = jnp.exp2((own_peak - peak) * EXP2_SCALE)
        weights = jnp.exp2((scores - peak) * EXP2_SCALE)
        inverse = 1.0 / (sum_row(1) * share + fold(weights, jnp.add, jnp.sum))
        delta = (sum_row(2) * share + fold(weights * prob_grad, jnp.add, jnp.sum)) * inverse
        inverse = jnp.where(jnp.concatenate([live[:, :width]] * len(places), axis=1), inverse, 0.0)
        factor = share * inverse
        prob = weights * inverse
        score_grad = (prob * (prob_grad - delta)).astype(jnp.bfloat16)
        prob = prob.astype(jnp.bfloat16)
        for index, place in enumerate(places):
            part = slice(index * width, (index + 1) * width)
            columns = pl.ds(pl.multiple_of(place * slots, slots), width)
            prob_ref[:rows, columns] = prob[:, part]
            score_grad_ref[:rows, columns] = score_grad[:, part]
            joined_ref[place, 0:1, :width] = factor[:, part]
            joined_ref[place, 1:2, :width] = delta[:, part]
            if width < slots:
                rest = pl.ds(pl.multiple_of(place * slots + width, HEAD_DIM), slots - width)
                score_grad_ref[:rows, rest] = jnp.zeros((rows, slots - width), jnp.bfloat16)
                joined_ref[place, 0:2, width:] = jnp.zeros((2, slots - width), jnp.float32)

    all_heads = key_heads * heads
    above = {}
    for rows, width in sizes:
        fits = (my_start > above.get(width, 0)) & (my_start <= rows)
        above[width] = rows
        if len(sizes) > 1:
            fits = fits & ((my_count > slots // 2) if width == slots else (my_count <= width))

        @pl.when(fits)
        def _():
            side = slots // width

            def step(index, carry):
                for part in range(step_units):
                    place = (index * step_units + part) * side
                    unit([place + item for item in range(side)], rows, width)
                return carry

            lax.fori_loop(0, all_heads // side // step_units, step, 0)
            if rows % CHUNK:
                beyond = slice(rows, rows + CHUNK - rows % CHUNK)
                none = jnp.zeros((CHUNK - rows % CHUNK, all_heads * slots), jnp.bfloat16)
                score_grad_ref[beyond, :] = none
            for key_head in range(key_heads):
                lane, column = key_head * heads * HEAD_DIM, key_head * heads * slots
                acc_ref[:rows, 2 * key_head * HEAD_DIM : 2 * (key_head + 1) * HEAD_DIM] = terms_of(
                    beside(prob_ref, rows, column, heads, slots, width),
                    beside(score_grad_ref, rows, column, heads, slots, width),
                    stacked(turned_ref, lane, heads, width),
                    stacked(grad_ref, lane, heads, width),
                )

    @pl.when(my_start == 0)
    def _():
        for place in range(all_heads):
            inverse = 1.0 / sums_ref[place, 1:2, :]
            joined_ref[place, 0:1, :] = jnp.where(live, inverse, 0.0)
            joined_ref[place, 1:2, :] = sums_ref[place, 2:3, :] * inverse

    for hop, term_ref in zip(sent_hops, terms):
        start = pl.multiple_of(meta_ref[hop], ALIGN)
        term_ref[...] = acc_ref[pl.ds(start, slots), :].astype(term_ref.dtype)


def relayed(ctx_size):
    return ctx_size == 4


def scores(meta, turned, out_grad, turned_t, grad_t, sums, blocks, routed, ctx_size):
    slots, width = blocks[0].shape
    if relayed(ctx_size):
        width = blocks[2].shape[1]
    key_heads = width // HEAD_DIM // 2
    heads = turned.shape[1] // HEAD_DIM // key_heads
    span = -(-(routed + ctx_size * ALIGN) // CHUNK) * CHUNK
    sizes, step_units = [(span, slots)], 1
    if span == 2 * CHUNK and routed - slots // 2 + ctx_size * ALIGN <= 3 * CHUNK // 2 + ALIGN:
        sizes = [(CHUNK, slots), (3 * CHUNK // 2, slots), (CHUNK, slots // 2), (span, slots // 2)]
        step_units = 2
    terms = [jax.ShapeDtypeStruct((slots, width), jnp.bfloat16)] * (ctx_size - 1)
    if relayed(ctx_size):
        terms[2] = jax.ShapeDtypeStruct((slots, width), jnp.float32)
    outs = pl.pallas_call(
        functools.partial(scores_kernel, ctx_size, sizes, step_units),
        out_shape=(
            *terms,
            jax.ShapeDtypeStruct((span, key_heads * heads * slots), jnp.bfloat16),
            jax.ShapeDtypeStruct((key_heads * heads, 8, slots), jnp.float32),
            jax.ShapeDtypeStruct((span + slots, key_heads * HEAD_DIM), jnp.bfloat16),
        ),
        in_specs=[SMEM] + [VMEM] * (5 + len(blocks)),
        out_specs=(VMEM,) * (ctx_size + 2),
        scratch_shapes=[
            pltpu.VMEM((span + slots, width // 2), jnp.bfloat16),
            pltpu.VMEM((span, HEAD_DIM), jnp.float32),
            pltpu.VMEM((span, key_heads * heads * slots), jnp.bfloat16),
            pltpu.VMEM((span + slots, width), jnp.float32),
        ],
        compiler_params=vmem(routed, 18, 60),
        cost_estimate=pl.CostEstimate(
            flops=8 * 10**9, bytes_accessed=12 * 1024 * 1024, transcendentals=0
        ),
        name="scores",
    )(meta, turned, out_grad, turned_t, grad_t, sums, *blocks)
    return outs[: ctx_size - 1], outs[ctx_size - 1 :]


def local_kernel(
    part,
    key_head,
    meta_ref,
    cos_ref,
    sin_ref,
    turned_ref,
    grad_ref,
    sent_ref,
    weight_ref,
    product_ref,
    score_grad_ref,
    joined_ref,
    key_ref,
    *refs,
):
    later = (len(refs) - 5) // 2
    dq_ref, own_ref = refs[later : later + 2]
    prob_ref, own_grad_ref, sum_ref = refs[-3:]
    for index in range(later):
        refs[later + 2 + index][...] = refs[index][...]
    slots = turned_ref.shape[0]
    heads = prob_ref.shape[1] // slots
    span = score_grad_ref.shape[0]
    my_start = meta_ref[0]
    own_key_t = sent_ref[:, key_lanes(key_head)].astype(jnp.float32).T.astype(jnp.bfloat16)
    for head in range(heads):
        columns = slice(head * slots, (head + 1) * slots)
        place = part * heads + head
        prob = weight_ref[key_head * heads + head] * joined_ref[place, 0:1, :]
        prob_ref[:, columns] = prob.astype(jnp.bfloat16)
        product = product_ref[key_head * heads + head] - joined_ref[place, 1:2, :]
        score_grad = (prob * product).astype(jnp.bfloat16)
        own_grad_ref[:, columns] = score_grad
        sum_ref[head] = dot(own_key_t, score_grad, ((1,), (0,)))
    for chunk in range(0, span, CHUNK):

        @pl.when(chunk < my_start)
        def _():
            rows = slice(chunk, chunk + CHUNK)
            key_t = key_ref[rows, head_lanes(part)].astype(jnp.float32).T.astype(jnp.bfloat16)
            for head in range(heads):
                place = part * heads + head
                score_grad = score_grad_ref[rows, place * slots : (place + 1) * slots]
                sum_ref[head] += dot(key_t, score_grad, ((1,), (0,)))

    lane = key_head * heads * HEAD_DIM
    for head in range(heads):
        grad = turn_back((sum_ref[head] * SCORE_SCALE).T, cos_ref[...], sin_ref[...])
        dq_ref[:, head * HEAD_DIM : (head + 1) * HEAD_DIM] = grad.astype(jnp.bfloat16)
    own_ref[...] = terms_of(
        prob_ref[...],
        own_grad_ref[...],
        stacked(turned_ref, lane, heads, slots),
        stacked(grad_ref, lane, heads, slots),
    )


def local_terms(
    part, key_head, meta, cos_full, sin_full, turned, out_grad, sent, own, joined, later
):
    slots = turned.shape[0]
    heads = turned.shape[1] // (sent.shape[1] // 2)
    weight, product, _ = own
    operands = (meta, cos_full, sin_full, turned, out_grad, sent, weight, product, *joined, *later)
    return pl.pallas_call(
        functools.partial(local_kernel, part, key_head),
        out_shape=(
            jax.ShapeDtypeStruct((slots, heads * HEAD_DIM), jnp.bfloat16),
            jax.ShapeDtypeStruct((slots, 2 * HEAD_DIM), jnp.float32),
            *[jax.ShapeDtypeStruct(term.shape, term.dtype) for term in later],
        ),
        in_specs=[SMEM] + [VMEM] * (len(operands) - 1),
        out_specs=(VMEM,) * (2 + len(later)),
        scratch_shapes=[
            pltpu.VMEM((slots, heads * slots), jnp.bfloat16),
            pltpu.VMEM((slots, heads * slots), jnp.bfloat16),
            pltpu.VMEM((heads, HEAD_DIM, slots), jnp.float32),
        ],
        compiler_params=vmem(joined[0].shape[0] // 2, 16, 48),
        cost_estimate=pl.CostEstimate(
            flops=4 * 10**9, bytes_accessed=10 * 1024 * 1024, transcendentals=0
        ),
        name="local_terms",
    )(*operands)


def finish_kernel(ctx_size, meta_ref, cos_ref, sin_ref, *refs):
    key_grad_ref, value_grad_ref = refs[-2:]
    terms, owns = refs[: ctx_size - 1], refs[ctx_size - 1 : -2]
    slots = cos_ref.shape[0]
    live = lax.broadcasted_iota(jnp.int32, (slots, HEAD_DIM), 0) < meta_ref[ctx_size]
    total = jnp.concatenate([own[...] for own in owns], axis=1)
    for index, term in enumerate(terms):
        term = term[...].astype(jnp.float32)
        if index == 0 and relayed(ctx_size):
            term = jnp.where(lax.axis_index("ctx") == 2, 0.0, term)
        total += term
    for lane in range(0, key_grad_ref.shape[1], HEAD_DIM):
        lanes = slice(lane, lane + HEAD_DIM)
        key_term = turn_back(total[:, 2 * lane : 2 * lane + HEAD_DIM], cos_ref[...], sin_ref[...])
        value_term = total[:, 2 * lane + HEAD_DIM : 2 * (lane + HEAD_DIM)]
        key_grad_ref[:, lanes] = jnp.where(live, key_term, 0.0).astype(jnp.bfloat16)
        value_grad_ref[:, lanes] = jnp.where(live, value_term, 0.0).astype(jnp.bfloat16)


def finish(meta, cos_full, sin_full, owns, terms):
    slots, width = terms[0].shape
    grad = jax.ShapeDtypeStruct((slots, width // 2), jnp.bfloat16)
    return pl.pallas_call(
        functools.partial(finish_kernel, len(terms) + 1),
        out_shape=(grad, grad),
        in_specs=[SMEM] + [VMEM] * (2 + len(owns) + len(terms)),
        out_specs=(VMEM, VMEM),
        compiler_params=vmem(0, 16, 16),
        name="finish",
    )(meta, cos_full, sin_full, *terms, *owns)


def part_of(part, size):
    return slice(part * size, (part + 1) * size)


def spread(sent, turned_keys, values, ctx_size):
    if relayed(ctx_size):
        alpha = [lax.ppermute(part, "ctx", [(0, 2), (2, 3)]) for part in (turned_keys, values)]
        beta = lax.ppermute(sent, "ctx", [(1, 3)])
        gamma = lax.ppermute(sent + 0 * alpha[1][:1, :1], "ctx", [(0, 1), (1, 2)])
        delta = [lax.ppermute(part, "ctx", [(2, 3)]) for part in alpha]
        return [*alpha, beta, gamma, *delta]
    blocks = [sent]
    for hop in range(1, ctx_size):
        pairs = [(shard, shard + 1) for shard in range(hop - 1, ctx_size - 1)]
        blocks.append(lax.ppermute(blocks[-1], "ctx", pairs))
    return blocks[1:]


def relay_first(first, third):
    first = lax.ppermute(first, "ctx", [(3, 2), (2, 1), (1, 0)])
    third = (third + first.astype(jnp.float32)).astype(jnp.bfloat16)
    return [first, lax.ppermute(third, "ctx", [(3, 2), (2, 0)])]


def descend(terms, ctx_size):
    arrived = []
    for hop, term in enumerate(terms, 1):
        pairs = [(shard + hop, shard) for shard in range(ctx_size - hop)]
        arrived.append(lax.ppermute(term, "ctx", pairs))
    return arrived


def body(positions, queries, keys, values, out_grad):
    ctx_size = lax.axis_size("ctx")
    routed = positions.shape[1]
    meta, cos_full, sin_full, sent, turned_keys = prepare(positions, keys[0], values[0], ctx_size)
    blocks = spread(sent, turned_keys, values[0], ctx_size)
    turned, turned_t, grad_t = rotate_queries(
        cos_full, sin_full, queries[0], out_grad[0], blocks[0]
    )
    own = own_scores(sent, turned_t, grad_t)
    key_heads = keys.shape[2] // HEAD_DIM
    parts = 1 if routed <= 512 else key_heads
    wide, narrow = queries.shape[2] // parts, sent.shape[1] // parts
    terms, joined = [], []
    for part in range(parts):
        columns = part_of(part, wide)
        outs = scores(
            meta,
            turned[:, columns],
            out_grad[0][:, columns],
            turned_t[columns],
            grad_t[columns],
            own[2][part_of(part, wide // HEAD_DIM)],
            [block[:, part_of(part, narrow)] for block in blocks],
            routed,
            ctx_size,
        )
        terms.append(outs[0])
        joined.append(outs[1])
    terms = [jnp.concatenate(term, axis=1) for term in zip(*terms)]
    if relayed(ctx_size):
        arrived, later = relay_first(terms[0], terms[2]), [terms[1]]
    else:
        arrived, later = descend(terms, ctx_size), []
    dqs, owns = [], []
    for key_head in range(key_heads):
        call, part = (0, key_head) if parts == 1 else (key_head, 0)
        dq, own_terms, *later = local_terms(
            part,
            key_head,
            meta,
            cos_full,
            sin_full,
            turned,
            out_grad[0],
            sent,
            own,
            joined[call],
            later,
        )
        dqs.append(dq)
        owns.append(own_terms)
        for term in later:
            arrived.append(lax.ppermute(term, "ctx", [(3, 1)]))
        later = []
    dq = jnp.concatenate(dqs, axis=1)
    key_grad, value_grad = finish(meta, cos_full, sin_full, owns, arrived)
    return (dq[None], key_grad[None], value_grad[None])


def solution(mesh):
    split = P(("groups", "dp"), "ctx", "mp")
    return jax.shard_map(
        body,
        mesh=mesh,
        in_specs=(P(("groups", "dp"), None), split, split, split, split),
        out_specs=(split, split, split),
        check_vma=False,
    )
```

```python
import functools
import math

import jax
import jax.numpy as jnp
import numpy as np
from jax import lax
from jax.experimental import pallas as pl
from jax.experimental.pallas import tpu as pltpu
from jax.sharding import PartitionSpec as P

HEAD_DIM = 128
HALF_DIM = HEAD_DIM // 2
TOK_SHARD = 1024
ROPE_BASE = 500000.0
SCORE_SCALE = 1.0 / math.sqrt(HEAD_DIM)
EXP2_SCALE = SCORE_SCALE * math.log2(math.e)
HIDDEN = -1e30
ALIGN = 16
CHUNK = 288
MIB = 1024 * 1024

VMEM = pl.BlockSpec(memory_space=pltpu.VMEM)
SMEM = pl.BlockSpec(memory_space=pltpu.SMEM)
HBM = pl.BlockSpec(memory_space=pltpu.HBM)


def vmem(routed, small, large):
    return pltpu.CompilerParams(vmem_limit_bytes=(small if routed <= 512 else large) * MIB)


def dot(left, right, contract):
    return lax.dot_general(left, right, (contract, ((), ())), preferred_element_type=jnp.float32)


def turn(field, cos_full, sin_full):
    return field * cos_full + pltpu.roll(field, HALF_DIM, 1) * sin_full


def turn_back(field, cos_full, sin_full):
    return field * cos_full - pltpu.roll(field, HALF_DIM, 1) * sin_full


def frequencies():
    ladder = np.arange(HALF_DIM, dtype=np.float32)
    exponent = ladder * np.float32(-2.0 * math.log(ROPE_BASE) / HEAD_DIM)
    freq = np.exp(exponent.astype(np.float64)).astype(np.float32)
    entry = lax.broadcasted_iota(jnp.int32, (1, HEAD_DIM), 1) % HALF_DIM
    row = jnp.zeros((1, HEAD_DIM), jnp.float32)
    for index in range(HALF_DIM):
        row = jnp.where(entry == index, float(freq[index]), row)
    return row


def shard_layout(ctx_size, me, pos, meta_ref):
    shard_of = pos // TOK_SHARD
    for hop in range(2 * ctx_size):
        meta_ref[hop] = 0
    start = jnp.int32(0)
    first = jnp.int32(0)
    my_first = jnp.int32(0)
    for shard in range(ctx_size):
        count = jnp.sum(jnp.where(shard_of == shard, 1.0, 0.0)).astype(jnp.int32)
        my_first = jnp.where(me == shard, first, my_first)

        @pl.when(me >= shard)
        def _():
            meta_ref[me - shard] = start
            meta_ref[ctx_size + me - shard] = count

        first = first + count
        start = start + (count + ALIGN - 1) // ALIGN * ALIGN
    return my_first


def prepare_kernel(
    ctx_size, pos_hbm, keys_hbm, values_hbm, meta_ref, cos_ref, sin_ref, sent_ref, *refs
):
    pos_ref, keys_ref, values_ref, sems = refs
    sources = (pos_hbm, keys_hbm, values_hbm)
    targets = (pos_ref, keys_ref, values_ref)
    copies = [
        pltpu.make_async_copy(source, target, sems.at[index])
        for index, (source, target) in enumerate(zip(sources, targets))
    ]
    for copy in copies:
        copy.start()
    copies[0].wait()
    slots = keys_ref.shape[0]
    pos = pos_ref[...]
    my_first = shard_layout(ctx_size, lax.axis_index("ctx"), pos, meta_ref)
    shape = (slots, pos.shape[1])
    gap = lax.broadcasted_iota(jnp.int32, shape, 1) - lax.broadcasted_iota(jnp.int32, shape, 0)
    named = jnp.where(gap == my_first, pos.astype(jnp.float32), 0.0)
    angles = jnp.sum(named, axis=1, keepdims=True) * frequencies()
    cos_full = jnp.cos(angles)
    front = lax.broadcasted_iota(jnp.int32, angles.shape, 1) < HALF_DIM
    sin_full = jnp.where(front, -jnp.sin(angles), jnp.sin(angles))
    cos_ref[...] = cos_full
    sin_ref[...] = sin_full
    copies[1].wait()
    copies[2].wait()
    for lane in range(0, keys_ref.shape[1], HEAD_DIM):
        lanes = slice(lane, lane + HEAD_DIM)
        key = turn(keys_ref[:, lanes].astype(jnp.float32), cos_full, sin_full)
        middle = 2 * lane + HEAD_DIM
        sent_ref[:, 2 * lane : middle] = key.astype(jnp.bfloat16)
        sent_ref[:, middle : middle + HEAD_DIM] = values_ref[:, lanes]


def prepare(positions, keys, values, ctx_size):
    slots, width = keys.shape
    table = jax.ShapeDtypeStruct((slots, HEAD_DIM), jnp.float32)
    sent = jax.ShapeDtypeStruct((slots, 2 * width), jnp.bfloat16)
    operands = (positions, keys, values)
    return pl.pallas_call(
        functools.partial(prepare_kernel, ctx_size),
        out_shape=(
            jax.ShapeDtypeStruct((2 * ctx_size,), jnp.int32),
            table,
            table,
            sent,
        ),
        in_specs=[HBM] * 3,
        out_specs=(SMEM, VMEM, VMEM, VMEM),
        scratch_shapes=[pltpu.VMEM(operand.shape, operand.dtype) for operand in operands]
        + [pltpu.SemaphoreType.DMA((3,))],
        compiler_params=vmem(positions.shape[1], 60, 60),
        name="prepare",
    )(*operands)


def queries_kernel(
    cos_ref,
    sin_ref,
    query_ref,
    grad_ref,
    sent_ref,
    turned_ref,
    turned_t_ref,
    grad_t_ref,
    sent_again_ref,
):
    sent_again_ref[...] = sent_ref[...]
    for lane in range(0, query_ref.shape[1], HEAD_DIM):
        lanes = slice(lane, lane + HEAD_DIM)
        query = turn(query_ref[:, lanes].astype(jnp.float32), cos_ref[...], sin_ref[...])
        turned_ref[:, lanes] = query.astype(jnp.bfloat16)
        turned_t_ref[lanes, :] = query.T.astype(jnp.bfloat16)
        grad_t_ref[lanes, :] = grad_ref[:, lanes].astype(jnp.float32).T.astype(jnp.bfloat16)


def rotate_queries(cos_full, sin_full, queries, out_grad, sent):
    slots, width = queries.shape
    straight = jax.ShapeDtypeStruct((slots, width), jnp.bfloat16)
    across = jax.ShapeDtypeStruct((width, slots), jnp.bfloat16)
    return pl.pallas_call(
        queries_kernel,
        out_shape=(straight, across, across, jax.ShapeDtypeStruct(sent.shape, sent.dtype)),
        in_specs=[VMEM] * 5,
        out_specs=(VMEM,) * 4,
        compiler_params=vmem(0, 16, 16),
        cost_estimate=pl.CostEstimate(
            flops=3 * 10**9, bytes_accessed=4 * 1024 * 1024, transcendentals=0
        ),
        name="rotate_queries",
    )(cos_full, sin_full, queries, out_grad, sent)


def stacked(ref, lane, heads, width):
    parts = [ref[:width, lane + h * HEAD_DIM : lane + (h + 1) * HEAD_DIM] for h in range(heads)]
    return jnp.concatenate(parts, axis=0)


def beside(ref, rows, heads, slots, width):
    if width == slots:
        return ref[:rows, :]
    columns = [head * slots for head in range(heads)]
    return jnp.concatenate([ref[:rows, start : start + width] for start in columns], axis=1)


def terms_of(probs, score_grads, queries, grads):
    key_term = dot(score_grads, queries, ((1,), (0,))) * SCORE_SCALE
    return jnp.concatenate([key_term, dot(probs, grads, ((1,), (0,)))], axis=1)


def fold(field, join, reduce):
    while field.shape[0] % 16 == 0:
        half = field.shape[0] // 2
        field = join(field[:half], field[half:])
    return reduce(field, axis=0, keepdims=True)


def head_lanes(head):
    return slice(head * HEAD_DIM, (head + 1) * HEAD_DIM)


def key_lanes(key_head):
    return slice(2 * key_head * HEAD_DIM, (2 * key_head + 1) * HEAD_DIM)


def value_lanes(key_head):
    return slice((2 * key_head + 1) * HEAD_DIM, 2 * (key_head + 1) * HEAD_DIM)


def own_kernel(step_heads, sent_ref, turned_t_ref, grad_t_ref, weight_ref, product_ref, sums_ref, bias_ref):
    slots = sent_ref.shape[0]
    key_heads = sent_ref.shape[1] // HEAD_DIM // 2
    heads = turned_t_ref.shape[0] // HEAD_DIM // key_heads
    key_id = lax.broadcasted_iota(jnp.int32, (slots, slots), 0)
    slot_id = lax.broadcasted_iota(jnp.int32, (slots, slots), 1)
    bias_ref[...] = jnp.where(key_id <= slot_id, 0.0, HIDDEN)
    for key_head in range(key_heads):

        def step(index, carry):
            for part in range(step_heads):
                head = key_head * heads + index * step_heads + part
                rows = pl.ds(pl.multiple_of(head * HEAD_DIM, HEAD_DIM), HEAD_DIM)
                scores = dot(sent_ref[:, key_lanes(key_head)], turned_t_ref[rows, :], ((1,), (0,)))
                scores = scores + bias_ref[...]
                prob_grad = dot(sent_ref[:, value_lanes(key_head)], grad_t_ref[rows, :], ((1,), (0,)))
                peak = fold(scores, jnp.maximum, jnp.max)
                weights = jnp.exp2((scores - peak) * EXP2_SCALE)
                weight_ref[head] = weights
                product_ref[head] = prob_grad
                sums_ref[head, 0:1, :] = peak
                sums_ref[head, 1:2, :] = fold(weights, jnp.add, jnp.sum)
                sums_ref[head, 2:3, :] = fold(weights * prob_grad, jnp.add, jnp.sum)
            return carry

        lax.fori_loop(0, heads // step_heads, step, 0)


def own_scores(sent, turned_t, grad_t):
    slots = sent.shape[0]
    heads = turned_t.shape[0] // HEAD_DIM
    square = jax.ShapeDtypeStruct((heads, slots, slots), jnp.float32)
    return pl.pallas_call(
        functools.partial(own_kernel, 4),
        out_shape=(square, square, jax.ShapeDtypeStruct((heads, 8, slots), jnp.float32)),
        in_specs=[VMEM] * 3,
        out_specs=(VMEM,) * 3,
        scratch_shapes=[pltpu.VMEM((slots, slots), jnp.float32)],
        compiler_params=vmem(0, 16, 16),
        cost_estimate=pl.CostEstimate(
            flops=5 * 10**9, bytes_accessed=10 * 1024 * 1024, transcendentals=0
        ),
        name="own_scores",
    )(sent, turned_t, grad_t)


def scores_kernel(
    ctx_size,
    sizes,
    step_units,
    key_head,
    meta_ref,
    turned_ref,
    grad_ref,
    turned_t_ref,
    grad_t_ref,
    sums_ref,
    *refs,
):
    inputs = refs[: -6 - ctx_size]
    refs = refs[len(inputs) :]
    terms, refs = refs[: ctx_size - 1], refs[ctx_size - 1 :]
    score_grad_ref, joined_ref, key_ref, value_ref, bias_ref, prob_ref, acc_ref = refs
    slots = turned_ref.shape[0]
    span = bias_ref.shape[0]
    heads = joined_ref.shape[0]
    starts = [pl.multiple_of(meta_ref[hop], ALIGN) for hop in range(ctx_size)]
    my_start, my_count = starts[0], meta_ref[ctx_size]
    sent_hops = list(range(1, ctx_size))
    if relayed(ctx_size):
        last = lax.axis_index("ctx") == ctx_size - 1
        sent_hops = [jnp.where(last, 3, 1), 2, jnp.where(last, 1, 2)]

    def blocks_of(lanes):
        blocks = [block[:, lanes] for block in inputs]
        if relayed(ctx_size):
            alpha, beta, gamma, delta = blocks
            blocks = [jnp.where(last, alpha, gamma), jnp.where(last, beta, alpha), delta]
        return blocks

    for ref, lanes in ((key_ref, key_lanes(key_head)), (value_ref, value_lanes(key_head))):
        ref[slots:span, :] = jnp.zeros((span - slots, HEAD_DIM), jnp.bfloat16)
        blocks = blocks_of(lanes)
        for hop in range(ctx_size - 1, 0, -1):
            ref[pl.ds(starts[hop], slots), :] = blocks[hop - 1]
    place = lax.broadcasted_iota(jnp.int32, bias_ref.shape, 0)
    seen = place < 0
    for hop in range(1, ctx_size):
        end = starts[hop] + meta_ref[ctx_size + hop]
        seen = seen | ((place >= starts[hop]) & (place < end))
    bias_ref[...] = jnp.where(seen, 0.0, HIDDEN)
    live = lax.broadcasted_iota(jnp.int32, (1, slots), 1) < my_count

    def joint(ref, places, rows, width):
        return jnp.concatenate([ref[rows(place) + (slice(0, width),)] for place in places], axis=1)

    def head_rows(place):
        return (pl.ds(pl.multiple_of((key_head * heads + place) * HEAD_DIM, HEAD_DIM), HEAD_DIM),)

    def units(groups, rows, width):
        side = slots // width
        bias = jnp.concatenate([bias_ref[:rows, :]] * (slots // HEAD_DIM), axis=1)
        alive = jnp.concatenate([live[:, :width]] * side, axis=1)
        queries = [joint(turned_t_ref, group, head_rows, width) for group in groups]
        grads = [joint(grad_t_ref, group, head_rows, width) for group in groups]

        def sums(row):
            index = lambda place: (key_head * heads + place, slice(row, row + 1))
            return [joint(sums_ref, group, index, width) for group in groups]

        own_peaks, own_totals, own_products = sums(0), sums(1), sums(2)
        scores = [dot(key_ref[:rows, :], query, ((1,), (0,))) + bias for query in queries]
        prob_grads = [dot(value_ref[:rows, :], grad, ((1,), (0,))) for grad in grads]
        peaks = [
            jnp.maximum(own, fold(score, jnp.maximum, jnp.max))
            for own, score in zip(own_peaks, scores)
        ]
        weights = [jnp.exp2((score - peak) * EXP2_SCALE) for score, peak in zip(scores, peaks)]
        shares = [jnp.exp2((own - peak) * EXP2_SCALE) for own, peak in zip(own_peaks, peaks)]
        totals = [
            own * share + fold(weight, jnp.add, jnp.sum)
            for own, share, weight in zip(own_totals, shares, weights)
        ]
        products = [
            own * share + fold(weight * prob_grad, jnp.add, jnp.sum)
            for own, share, weight, prob_grad in zip(own_products, shares, weights, prob_grads)
        ]
        inverses = [1.0 / total for total in totals]
        deltas = [product * inverse for product, inverse in zip(products, inverses)]
        inverses = [jnp.where(alive, inverse, 0.0) for inverse in inverses]
        factors = [share * inverse for share, inverse in zip(shares, inverses)]
        probs = [weight * inverse for weight, inverse in zip(weights, inverses)]
        score_grads = [
            (prob * (prob_grad - delta)).astype(jnp.bfloat16)
            for prob, prob_grad, delta in zip(probs, prob_grads, deltas)
        ]
        probs = [prob.astype(jnp.bfloat16) for prob in probs]
        for group, prob, score_grad, factor, delta in zip(
            groups, probs, score_grads, factors, deltas
        ):
            for index, place in enumerate(group):
                part = slice(index * width, (index + 1) * width)
                columns = pl.ds(pl.multiple_of(place * slots, slots), width)
                prob_ref[:rows, columns] = prob[:, part]
                score_grad_ref[:rows, columns] = score_grad[:, part]
                joined_ref[place, 0:1, :width] = factor[:, part]
                joined_ref[place, 1:2, :width] = delta[:, part]
                if width < slots:
                    rest = pl.ds(pl.multiple_of(place * slots + width, HEAD_DIM), slots - width)
                    score_grad_ref[:rows, rest] = jnp.zeros((rows, slots - width), jnp.bfloat16)
                    joined_ref[place, 0:2, width:] = jnp.zeros((2, slots - width), jnp.float32)

    above = {}
    for rows, width in sizes:
        fits = (my_start > above.get(width, 0)) & (my_start <= rows)
        above[width] = rows
        if len(sizes) > 1:
            fits = fits & ((my_count > slots // 2) if width == slots else (my_count <= width))

        @pl.when(fits)
        def _():
            side = slots // width

            def step(index, carry):
                base = index * step_units * side
                units(
                    [[base + part * side + item for item in range(side)] for part in range(step_units)],
                    rows,
                    width,
                )
                return carry

            lax.fori_loop(0, heads // side // step_units, step, 0)
            if rows % CHUNK:
                beyond = slice(rows, rows + CHUNK - rows % CHUNK)
                none = jnp.zeros((CHUNK - rows % CHUNK, heads * slots), jnp.bfloat16)
                score_grad_ref[beyond, :] = none
            lane = key_head * heads * HEAD_DIM
            acc_ref[:rows, :] = terms_of(
                beside(prob_ref, rows, heads, slots, width),
                beside(score_grad_ref, rows, heads, slots, width),
                stacked(turned_ref, lane, heads, width),
                stacked(grad_ref, lane, heads, width),
            )

    @pl.when(my_start == 0)
    def _():
        for place in range(heads):
            inverse = 1.0 / sums_ref[key_head * heads + place, 1:2, :]
            joined_ref[place, 0:1, :] = jnp.where(live, inverse, 0.0)
            joined_ref[place, 1:2, :] = sums_ref[key_head * heads + place, 2:3, :] * inverse

    for hop, term_ref in zip(sent_hops, terms):
        start = pl.multiple_of(meta_ref[hop], ALIGN)
        term_ref[...] = acc_ref[pl.ds(start, slots), :].astype(term_ref.dtype)


def relayed(ctx_size):
    return ctx_size == 4


def scores(key_head, meta, turned, out_grad, turned_t, grad_t, sums, blocks, routed, ctx_size):
    slots, width = blocks[0].shape
    heads = turned.shape[1] // (width // 2)
    span = -(-(routed + ctx_size * ALIGN) // CHUNK) * CHUNK
    sizes, step_units = [(span, slots)], 1
    if span == 2 * CHUNK and routed - slots // 2 + ctx_size * ALIGN <= 3 * CHUNK // 2 + ALIGN:
        sizes = [(CHUNK, slots), (3 * CHUNK // 2, slots), (CHUNK, slots // 2), (span, slots // 2)]
        step_units = 4
    terms = [jax.ShapeDtypeStruct((slots, 2 * HEAD_DIM), jnp.bfloat16)] * (ctx_size - 1)
    if relayed(ctx_size):
        terms[2] = jax.ShapeDtypeStruct((slots, 2 * HEAD_DIM), jnp.float32)
    outs = pl.pallas_call(
        functools.partial(scores_kernel, ctx_size, sizes, step_units, key_head),
        out_shape=(
            *terms,
            jax.ShapeDtypeStruct((span, heads * slots), jnp.bfloat16),
            jax.ShapeDtypeStruct((heads, 8, slots), jnp.float32),
            jax.ShapeDtypeStruct((span + slots, HEAD_DIM), jnp.bfloat16),
        ),
        in_specs=[SMEM] + [VMEM] * (5 + len(blocks)),
        out_specs=(VMEM,) * (ctx_size + 2),
        scratch_shapes=[
            pltpu.VMEM((span + slots, HEAD_DIM), jnp.bfloat16),
            pltpu.VMEM((span, HEAD_DIM), jnp.float32),
            pltpu.VMEM((span, heads * slots), jnp.bfloat16),
            pltpu.VMEM((span + slots, 2 * HEAD_DIM), jnp.float32),
        ],
        compiler_params=vmem(routed, 20, 60),
        cost_estimate=pl.CostEstimate(
            flops=4 * 10**9, bytes_accessed=6 * 1024 * 1024, transcendentals=0
        ),
        name="scores",
    )(meta, turned, out_grad, turned_t, grad_t, sums, *blocks)
    return outs[: ctx_size - 1], outs[ctx_size - 1 :]


def local_kernel(
    key_head,
    later,
    meta_ref,
    cos_ref,
    sin_ref,
    turned_ref,
    grad_ref,
    sent_ref,
    weight_ref,
    product_ref,
    score_grad_ref,
    joined_ref,
    key_ref,
    *refs,
):
    handed = refs[:later]
    dq_ref, own_ref, handed_ref = (refs[-6:-3] if later else (*refs[-5:-3], None))
    prob_ref, own_grad_ref, sum_ref = refs[-3:]
    for index in range(later):
        handed_ref[:, 2 * index * HEAD_DIM : 2 * (index + 1) * HEAD_DIM] = handed[index][...]
    slots = turned_ref.shape[0]
    heads = joined_ref.shape[0]
    span = score_grad_ref.shape[0]
    my_start = meta_ref[0]
    own_key_t = sent_ref[:, key_lanes(key_head)].astype(jnp.float32).T.astype(jnp.bfloat16)
    for head in range(heads):
        columns = slice(head * slots, (head + 1) * slots)
        prob = weight_ref[key_head * heads + head] * joined_ref[head, 0:1, :]
        prob_ref[:, columns] = prob.astype(jnp.bfloat16)
        product = product_ref[key_head * heads + head] - joined_ref[head, 1:2, :]
        score_grad = (prob * product).astype(jnp.bfloat16)
        own_grad_ref[:, columns] = score_grad
        sum_ref[head] = dot(own_key_t, score_grad, ((1,), (0,)))
    for chunk in range(0, span, CHUNK):

        @pl.when(chunk < my_start)
        def _():
            rows = slice(chunk, chunk + CHUNK)
            key_t = key_ref[rows, :].astype(jnp.float32).T.astype(jnp.bfloat16)
            for head in range(heads):
                score_grad = score_grad_ref[rows, head * slots : (head + 1) * slots]
                sum_ref[head] += dot(key_t, score_grad, ((1,), (0,)))

    lane = key_head * heads * HEAD_DIM
    for head in range(heads):
        grad = turn_back((sum_ref[head] * SCORE_SCALE).T, cos_ref[...], sin_ref[...])
        dq_ref[:, head * HEAD_DIM : (head + 1) * HEAD_DIM] = grad.astype(jnp.bfloat16)
    own_ref[...] = terms_of(
        prob_ref[...],
        own_grad_ref[...],
        stacked(turned_ref, lane, heads, slots),
        stacked(grad_ref, lane, heads, slots),
    )


def local_terms(
    key_head, meta, cos_full, sin_full, turned, out_grad, sent, own, joined, later, after
):
    slots = turned.shape[0]
    heads = joined[1].shape[0]
    weight, product, _ = own
    operands = (meta, cos_full, sin_full, turned, out_grad, sent, weight, product, *joined, *later)
    operands += tuple(after)
    handed = [jax.ShapeDtypeStruct((slots, 2 * HEAD_DIM * len(later)), jnp.bfloat16)] if later else []
    return pl.pallas_call(
        functools.partial(local_kernel, key_head, len(later)),
        out_shape=(
            jax.ShapeDtypeStruct((slots, heads * HEAD_DIM), jnp.bfloat16),
            jax.ShapeDtypeStruct((slots, 2 * HEAD_DIM), jnp.float32),
            *handed,
        ),
        in_specs=[SMEM] + [VMEM] * (len(operands) - 1),
        out_specs=(VMEM,) * (2 + len(handed)),
        scratch_shapes=[
            pltpu.VMEM((slots, heads * slots), jnp.bfloat16),
            pltpu.VMEM((slots, heads * slots), jnp.bfloat16),
            pltpu.VMEM((heads, HEAD_DIM, slots), jnp.float32),
        ],
        compiler_params=vmem(joined[0].shape[0] // 2, 16, 48),
        cost_estimate=pl.CostEstimate(
            flops=4 * 10**9, bytes_accessed=10 * 1024 * 1024, transcendentals=0
        ),
        name="local_terms",
    )(*operands)


def finish_kernel(ctx_size, key_heads, meta_ref, cos_ref, sin_ref, *refs):
    key_grad_ref, value_grad_ref = refs[-2:]
    owns, terms = refs[:key_heads], list(refs[key_heads:-2])
    slots = cos_ref.shape[0]
    live = lax.broadcasted_iota(jnp.int32, (slots, HEAD_DIM), 0) < meta_ref[ctx_size]
    totals = [own[...] for own in owns]
    for index in range(ctx_size - 1):
        parts = [terms.pop(0)]
        if parts[0].shape[1] == 2 * HEAD_DIM:
            parts += [terms.pop(0) for _ in range(key_heads - 1)]
        term = jnp.concatenate([part[...] for part in parts], axis=1).astype(jnp.float32)
        if index == 0 and relayed(ctx_size):
            term = jnp.where(lax.axis_index("ctx") == 2, 0.0, term)
        for head in range(key_heads):
            totals[head] += term[:, 2 * head * HEAD_DIM : 2 * (head + 1) * HEAD_DIM]
    for head, total in enumerate(totals):
        lanes = head_lanes(head)
        key_term = turn_back(total[:, :HEAD_DIM], cos_ref[...], sin_ref[...])
        key_grad_ref[:, lanes] = jnp.where(live, key_term, 0.0).astype(jnp.bfloat16)
        value_grad_ref[:, lanes] = jnp.where(live, total[:, HEAD_DIM:], 0.0).astype(jnp.bfloat16)


def finish(meta, cos_full, sin_full, owns, terms, ctx_size):
    slots = cos_full.shape[0]
    key_heads = len(owns)
    grad = jax.ShapeDtypeStruct((slots, key_heads * HEAD_DIM), jnp.bfloat16)
    return pl.pallas_call(
        functools.partial(finish_kernel, ctx_size, key_heads),
        out_shape=(grad, grad),
        in_specs=[SMEM] + [VMEM] * (2 + len(owns) + len(terms)),
        out_specs=(VMEM, VMEM),
        compiler_params=vmem(0, 16, 16),
        name="finish",
    )(meta, cos_full, sin_full, *owns, *terms)


def spread(sent, sent_again, ctx_size):
    if relayed(ctx_size):
        alpha = lax.ppermute(sent, "ctx", [(0, 2), (2, 3)])
        beta = lax.ppermute(sent, "ctx", [(1, 3)])
        gamma = lax.ppermute(sent_again, "ctx", [(0, 1), (1, 2)])
        return [alpha, beta, gamma, lax.ppermute(alpha, "ctx", [(2, 3)])]
    blocks = [sent]
    for hop in range(1, ctx_size):
        pairs = [(shard, shard + 1) for shard in range(hop - 1, ctx_size - 1)]
        blocks.append(lax.ppermute(blocks[-1], "ctx", pairs))
    return blocks[1:]


def relay(first, third):
    first = lax.ppermute(first, "ctx", [(3, 2), (2, 1), (1, 0)])
    third = (third + first.astype(jnp.float32)).astype(jnp.bfloat16)
    return first, lax.ppermute(third, "ctx", [(3, 2), (2, 0)])


def descend(terms, ctx_size):
    arrived = []
    for hop, term in enumerate(terms, 1):
        pairs = [(shard + hop, shard) for shard in range(ctx_size - hop)]
        arrived.append(lax.ppermute(term, "ctx", pairs))
    return arrived


def body(positions, queries, keys, values, out_grad):
    ctx_size = lax.axis_size("ctx")
    routed = positions.shape[1]
    key_heads = keys.shape[2] // HEAD_DIM
    meta, cos_full, sin_full, sent = prepare(positions, keys[0], values[0], ctx_size)
    turned, turned_t, grad_t, sent_again = rotate_queries(
        cos_full, sin_full, queries[0], out_grad[0], sent
    )
    blocks = spread(sent, sent_again, ctx_size)
    own = own_scores(sent, turned_t, grad_t)
    terms, joined, dqs, owns, arrived = [], [], [], [], []
    for head in range(key_heads):
        outs = scores(
            head, meta, turned, out_grad[0], turned_t, grad_t, own[2], blocks, routed, ctx_size
        )
        terms.append(outs[0])
        joined.append(outs[1])
    later, after = [], [[]] * key_heads
    if relayed(ctx_size):
        pairs = [relay(first, third) for first, _, third in terms]
        arrived = [first for first, _ in pairs] + [third for _, third in pairs]
        later = [second for _, second, _ in terms]
        after = [[first] for first, _ in pairs]
    else:
        arrived = [part for hop in zip(*[descend(term, ctx_size) for term in terms]) for part in hop]
    for head in range(key_heads):
        dq, own_terms, *handed = local_terms(
            head,
            meta,
            cos_full,
            sin_full,
            turned,
            out_grad[0],
            sent,
            own,
            joined[head],
            later,
            after[head],
        )
        dqs.append(dq)
        owns.append(own_terms)
        for term in handed:
            arrived.append(lax.ppermute(term, "ctx", [(3, 1)]))
        later = []
    dq = jnp.concatenate(dqs, axis=1)
    key_grad, value_grad = finish(meta, cos_full, sin_full, owns, arrived, ctx_size)
    return (dq[None], key_grad[None], value_grad[None])


def solution(mesh):
    split = P(("groups", "dp"), "ctx", "mp")
    return jax.shard_map(
        body,
        mesh=mesh,
        in_specs=(P(("groups", "dp"), None), split, split, split, split),
        out_specs=(split, split, split),
        check_vma=False,
    )
```

```python
import functools
import math

import jax
import jax.numpy as jnp
import numpy as np
from jax import lax
from jax.experimental import pallas as pl
from jax.experimental.pallas import tpu as pltpu
from jax.sharding import PartitionSpec as P

HEAD_DIM = 128
HALF_DIM = HEAD_DIM // 2
TOK_SHARD = 1024
ROPE_BASE = 500000.0
SCORE_SCALE = 1.0 / math.sqrt(HEAD_DIM)
EXP2_SCALE = SCORE_SCALE * math.log2(math.e)
HIDDEN = -1e30
ALIGN = 16
CHUNK = 288
MIB = 1024 * 1024

VMEM = pl.BlockSpec(memory_space=pltpu.VMEM)
SMEM = pl.BlockSpec(memory_space=pltpu.SMEM)
HBM = pl.BlockSpec(memory_space=pltpu.HBM)


def vmem(routed, small, large):
    return pltpu.CompilerParams(vmem_limit_bytes=(small if routed <= 512 else large) * MIB)


def dot(left, right, contract):
    return lax.dot_general(left, right, (contract, ((), ())), preferred_element_type=jnp.float32)


def turn(field, cos_full, sin_full):
    return field * cos_full + pltpu.roll(field, HALF_DIM, 1) * sin_full


def turn_back(field, cos_full, sin_full):
    return field * cos_full - pltpu.roll(field, HALF_DIM, 1) * sin_full


def frequencies():
    ladder = np.arange(HALF_DIM, dtype=np.float32)
    exponent = ladder * np.float32(-2.0 * math.log(ROPE_BASE) / HEAD_DIM)
    freq = np.exp(exponent.astype(np.float64)).astype(np.float32)
    entry = lax.broadcasted_iota(jnp.int32, (1, HEAD_DIM), 1) % HALF_DIM
    row = jnp.zeros((1, HEAD_DIM), jnp.float32)
    for index in range(HALF_DIM):
        row = jnp.where(entry == index, float(freq[index]), row)
    return row


def shard_layout(ctx_size, me, pos, meta_ref):
    shard_of = pos // TOK_SHARD
    for hop in range(2 * ctx_size):
        meta_ref[hop] = 0
    start = jnp.int32(0)
    first = jnp.int32(0)
    my_first = jnp.int32(0)
    for shard in range(ctx_size):
        count = jnp.sum(jnp.where(shard_of == shard, 1.0, 0.0)).astype(jnp.int32)
        my_first = jnp.where(me == shard, first, my_first)

        @pl.when(me >= shard)
        def _():
            meta_ref[me - shard] = start
            meta_ref[ctx_size + me - shard] = count

        first = first + count
        start = start + (count + ALIGN - 1) // ALIGN * ALIGN
    return my_first


def prepare_kernel(
    ctx_size, pos_hbm, keys_hbm, values_hbm, meta_ref, cos_ref, sin_ref, sent_ref, *refs
):
    pos_ref, keys_ref, values_ref, sems = refs
    sources = (pos_hbm, keys_hbm, values_hbm)
    targets = (pos_ref, keys_ref, values_ref)
    copies = [
        pltpu.make_async_copy(source, target, sems.at[index])
        for index, (source, target) in enumerate(zip(sources, targets))
    ]
    for copy in copies:
        copy.start()
    copies[0].wait()
    slots = keys_ref.shape[0]
    pos = pos_ref[...]
    my_first = shard_layout(ctx_size, lax.axis_index("ctx"), pos, meta_ref)
    shape = (slots, pos.shape[1])
    gap = lax.broadcasted_iota(jnp.int32, shape, 1) - lax.broadcasted_iota(jnp.int32, shape, 0)
    named = jnp.where(gap == my_first, pos.astype(jnp.float32), 0.0)
    angles = jnp.sum(named, axis=1, keepdims=True) * frequencies()
    cos_full = jnp.cos(angles)
    front = lax.broadcasted_iota(jnp.int32, angles.shape, 1) < HALF_DIM
    sin_full = jnp.where(front, -jnp.sin(angles), jnp.sin(angles))
    cos_ref[...] = cos_full
    sin_ref[...] = sin_full
    copies[1].wait()
    copies[2].wait()
    for lane in range(0, keys_ref.shape[1], HEAD_DIM):
        lanes = slice(lane, lane + HEAD_DIM)
        key = turn(keys_ref[:, lanes].astype(jnp.float32), cos_full, sin_full)
        middle = 2 * lane + HEAD_DIM
        sent_ref[:, 2 * lane : middle] = key.astype(jnp.bfloat16)
        sent_ref[:, middle : middle + HEAD_DIM] = values_ref[:, lanes]


def prepare(positions, keys, values, ctx_size):
    slots, width = keys.shape
    table = jax.ShapeDtypeStruct((slots, HEAD_DIM), jnp.float32)
    sent = jax.ShapeDtypeStruct((slots, 2 * width), jnp.bfloat16)
    operands = (positions, keys, values)
    return pl.pallas_call(
        functools.partial(prepare_kernel, ctx_size),
        out_shape=(
            jax.ShapeDtypeStruct((2 * ctx_size,), jnp.int32),
            table,
            table,
            sent,
        ),
        in_specs=[HBM] * 3,
        out_specs=(SMEM, VMEM, VMEM, VMEM),
        scratch_shapes=[pltpu.VMEM(operand.shape, operand.dtype) for operand in operands]
        + [pltpu.SemaphoreType.DMA((3,))],
        compiler_params=vmem(positions.shape[1], 60, 60),
        name="prepare",
    )(*operands)


def queries_kernel(
    cos_ref,
    sin_ref,
    query_ref,
    grad_ref,
    sent_ref,
    turned_ref,
    turned_t_ref,
    grad_t_ref,
    sent_again_ref,
):
    sent_again_ref[...] = sent_ref[...]
    for lane in range(0, query_ref.shape[1], HEAD_DIM):
        lanes = slice(lane, lane + HEAD_DIM)
        query = turn(query_ref[:, lanes].astype(jnp.float32), cos_ref[...], sin_ref[...])
        turned_ref[:, lanes] = query.astype(jnp.bfloat16)
        turned_t_ref[lanes, :] = query.T.astype(jnp.bfloat16)
        grad_t_ref[lanes, :] = grad_ref[:, lanes].astype(jnp.float32).T.astype(jnp.bfloat16)


def rotate_queries(cos_full, sin_full, queries, out_grad, sent):
    slots, width = queries.shape
    straight = jax.ShapeDtypeStruct((slots, width), jnp.bfloat16)
    across = jax.ShapeDtypeStruct((width, slots), jnp.bfloat16)
    return pl.pallas_call(
        queries_kernel,
        out_shape=(straight, across, across, jax.ShapeDtypeStruct(sent.shape, sent.dtype)),
        in_specs=[VMEM] * 5,
        out_specs=(VMEM,) * 4,
        compiler_params=vmem(0, 16, 16),
        cost_estimate=pl.CostEstimate(
            flops=3 * 10**9, bytes_accessed=4 * 1024 * 1024, transcendentals=0
        ),
        name="rotate_queries",
    )(cos_full, sin_full, queries, out_grad, sent)


def stacked(ref, lane, heads, width):
    parts = [ref[:width, lane + h * HEAD_DIM : lane + (h + 1) * HEAD_DIM] for h in range(heads)]
    return jnp.concatenate(parts, axis=0)


def beside(ref, rows, heads, slots, width):
    if width == slots:
        return ref[:rows, :]
    columns = [head * slots for head in range(heads)]
    return jnp.concatenate([ref[:rows, start : start + width] for start in columns], axis=1)


def terms_of(probs, score_grads, queries, grads):
    key_term = dot(score_grads, queries, ((1,), (0,))) * SCORE_SCALE
    return jnp.concatenate([key_term, dot(probs, grads, ((1,), (0,)))], axis=1)


def fold(field, join, reduce):
    while field.shape[0] % 16 == 0:
        half = field.shape[0] // 2
        field = join(field[:half], field[half:])
    return reduce(field, axis=0, keepdims=True)


def head_lanes(head):
    return slice(head * HEAD_DIM, (head + 1) * HEAD_DIM)


def key_lanes(key_head):
    return slice(2 * key_head * HEAD_DIM, (2 * key_head + 1) * HEAD_DIM)


def value_lanes(key_head):
    return slice((2 * key_head + 1) * HEAD_DIM, 2 * (key_head + 1) * HEAD_DIM)


def own_kernel(step_heads, sent_ref, turned_t_ref, grad_t_ref, weight_ref, product_ref, sums_ref, bias_ref):
    slots = sent_ref.shape[0]
    key_heads = sent_ref.shape[1] // HEAD_DIM // 2
    heads = turned_t_ref.shape[0] // HEAD_DIM // key_heads
    key_id = lax.broadcasted_iota(jnp.int32, (slots, slots), 0)
    slot_id = lax.broadcasted_iota(jnp.int32, (slots, slots), 1)
    bias_ref[...] = jnp.where(key_id <= slot_id, 0.0, HIDDEN)
    for key_head in range(key_heads):

        def step(index, carry):
            for part in range(step_heads):
                head = key_head * heads + index * step_heads + part
                rows = pl.ds(pl.multiple_of(head * HEAD_DIM, HEAD_DIM), HEAD_DIM)
                scores = dot(sent_ref[:, key_lanes(key_head)], turned_t_ref[rows, :], ((1,), (0,)))
                scores = scores + bias_ref[...]
                prob_grad = dot(sent_ref[:, value_lanes(key_head)], grad_t_ref[rows, :], ((1,), (0,)))
                peak = fold(scores, jnp.maximum, jnp.max)
                weights = jnp.exp2((scores - peak) * EXP2_SCALE)
                weight_ref[head] = weights
                product_ref[head] = prob_grad
                sums_ref[head, 0:1, :] = peak
                sums_ref[head, 1:2, :] = fold(weights, jnp.add, jnp.sum)
                sums_ref[head, 2:3, :] = fold(weights * prob_grad, jnp.add, jnp.sum)
            return carry

        lax.fori_loop(0, heads // step_heads, step, 0)


def own_scores(sent, turned_t, grad_t):
    slots = sent.shape[0]
    heads = turned_t.shape[0] // HEAD_DIM
    square = jax.ShapeDtypeStruct((heads, slots, slots), jnp.float32)
    return pl.pallas_call(
        functools.partial(own_kernel, 4),
        out_shape=(square, square, jax.ShapeDtypeStruct((heads, 8, slots), jnp.float32)),
        in_specs=[VMEM] * 3,
        out_specs=(VMEM,) * 3,
        scratch_shapes=[pltpu.VMEM((slots, slots), jnp.float32)],
        compiler_params=vmem(0, 16, 16),
        cost_estimate=pl.CostEstimate(
            flops=5 * 10**9, bytes_accessed=10 * 1024 * 1024, transcendentals=0
        ),
        name="own_scores",
    )(sent, turned_t, grad_t)


def scores_kernel(
    ctx_size,
    sizes,
    step_units,
    key_head,
    meta_ref,
    turned_ref,
    grad_ref,
    turned_t_ref,
    grad_t_ref,
    sums_ref,
    *refs,
):
    inputs = refs[: 4 if relayed(ctx_size) else ctx_size - 1]
    refs = refs[-6 - ctx_size :]
    terms, refs = refs[: ctx_size - 1], refs[ctx_size - 1 :]
    score_grad_ref, joined_ref, key_ref, value_ref, bias_ref, prob_ref, acc_ref = refs
    slots = turned_ref.shape[0]
    span = bias_ref.shape[0]
    heads = joined_ref.shape[0]
    starts = [pl.multiple_of(meta_ref[hop], ALIGN) for hop in range(ctx_size)]
    my_start, my_count = starts[0], meta_ref[ctx_size]
    sent_hops = list(range(1, ctx_size))
    if relayed(ctx_size):
        last = lax.axis_index("ctx") == ctx_size - 1
        sent_hops = [jnp.where(last, 3, 1), 2, jnp.where(last, 1, 2)]

    def blocks_of(lanes):
        blocks = [block[:, lanes] for block in inputs]
        if relayed(ctx_size):
            alpha, beta, gamma, delta = blocks
            blocks = [jnp.where(last, alpha, gamma), jnp.where(last, beta, alpha), delta]
        return blocks

    for ref, lanes in ((key_ref, key_lanes(key_head)), (value_ref, value_lanes(key_head))):
        ref[slots:span, :] = jnp.zeros((span - slots, HEAD_DIM), jnp.bfloat16)
        blocks = blocks_of(lanes)
        for hop in range(ctx_size - 1, 0, -1):
            ref[pl.ds(starts[hop], slots), :] = blocks[hop - 1]
    place = lax.broadcasted_iota(jnp.int32, bias_ref.shape, 0)
    seen = place < 0
    for hop in range(1, ctx_size):
        end = starts[hop] + meta_ref[ctx_size + hop]
        seen = seen | ((place >= starts[hop]) & (place < end))
    bias_ref[...] = jnp.where(seen, 0.0, HIDDEN)
    live = lax.broadcasted_iota(jnp.int32, (1, slots), 1) < my_count
    acc_ref[...] = jnp.zeros_like(acc_ref)

    def joint(ref, places, rows, width):
        return jnp.concatenate([ref[rows(place) + (slice(0, width),)] for place in places], axis=1)

    def head_rows(place):
        return (pl.ds(pl.multiple_of((key_head * heads + place) * HEAD_DIM, HEAD_DIM), HEAD_DIM),)

    def units(groups, rows, width):
        side = slots // width
        bias = jnp.concatenate([bias_ref[:rows, :]] * (slots // HEAD_DIM), axis=1)
        alive = jnp.concatenate([live[:, :width]] * side, axis=1)
        queries = [joint(turned_t_ref, group, head_rows, width) for group in groups]
        grads = [joint(grad_t_ref, group, head_rows, width) for group in groups]

        def sums(row):
            index = lambda place: (key_head * heads + place, slice(row, row + 1))
            return [joint(sums_ref, group, index, width) for group in groups]

        own_peaks, own_totals, own_products = sums(0), sums(1), sums(2)
        scores = [dot(key_ref[:rows, :], query, ((1,), (0,))) + bias for query in queries]
        prob_grads = [dot(value_ref[:rows, :], grad, ((1,), (0,))) for grad in grads]
        peaks = [
            jnp.maximum(own, fold(score, jnp.maximum, jnp.max))
            for own, score in zip(own_peaks, scores)
        ]
        weights = [jnp.exp2((score - peak) * EXP2_SCALE) for score, peak in zip(scores, peaks)]
        shares = [jnp.exp2((own - peak) * EXP2_SCALE) for own, peak in zip(own_peaks, peaks)]
        totals = [
            own * share + fold(weight, jnp.add, jnp.sum)
            for own, share, weight in zip(own_totals, shares, weights)
        ]
        products = [
            own * share + fold(weight * prob_grad, jnp.add, jnp.sum)
            for own, share, weight, prob_grad in zip(own_products, shares, weights, prob_grads)
        ]
        inverses = [1.0 / total for total in totals]
        deltas = [product * inverse for product, inverse in zip(products, inverses)]
        inverses = [jnp.where(alive, inverse, 0.0) for inverse in inverses]
        factors = [share * inverse for share, inverse in zip(shares, inverses)]
        probs = [weight * inverse for weight, inverse in zip(weights, inverses)]
        score_grads = [
            (prob * (prob_grad - delta)).astype(jnp.bfloat16)
            for prob, prob_grad, delta in zip(probs, prob_grads, deltas)
        ]
        probs = [prob.astype(jnp.bfloat16) for prob in probs]
        for group, prob, score_grad, factor, delta in zip(
            groups, probs, score_grads, factors, deltas
        ):
            for index, place in enumerate(group):
                part = slice(index * width, (index + 1) * width)
                columns = pl.ds(pl.multiple_of(place * slots, slots), width)
                prob_ref[:rows, columns] = prob[:, part]
                score_grad_ref[:rows, columns] = score_grad[:, part]
                joined_ref[place, 0:1, :width] = factor[:, part]
                joined_ref[place, 1:2, :width] = delta[:, part]
                if width < slots:
                    rest = pl.ds(pl.multiple_of(place * slots + width, HEAD_DIM), slots - width)
                    score_grad_ref[:rows, rest] = jnp.zeros((rows, slots - width), jnp.bfloat16)
                    joined_ref[place, 0:2, width:] = jnp.zeros((2, slots - width), jnp.float32)

    above = {}
    for rows, width in sizes:
        fits = (my_start > above.get(width, 0)) & (my_start <= rows)
        above[width] = rows
        if len(sizes) > 1:
            fits = fits & ((my_count > slots // 2) if width == slots else (my_count <= width))

        @pl.when(fits)
        def _():
            side = slots // width

            def step(index, carry):
                base = index * step_units * side
                units(
                    [[base + part * side + item for item in range(side)] for part in range(step_units)],
                    rows,
                    width,
                )
                return carry

            lax.fori_loop(0, heads // side // step_units, step, 0)
            if rows % CHUNK:
                beyond = slice(rows, rows + CHUNK - rows % CHUNK)
                none = jnp.zeros((CHUNK - rows % CHUNK, heads * slots), jnp.bfloat16)
                score_grad_ref[beyond, :] = none
            lane = key_head * heads * HEAD_DIM
            acc_ref[:rows, :] = terms_of(
                beside(prob_ref, rows, heads, slots, width),
                beside(score_grad_ref, rows, heads, slots, width),
                stacked(turned_ref, lane, heads, width),
                stacked(grad_ref, lane, heads, width),
            )

    @pl.when(my_start == 0)
    def _():
        for place in range(heads):
            inverse = 1.0 / sums_ref[key_head * heads + place, 1:2, :]
            joined_ref[place, 0:1, :] = jnp.where(live, inverse, 0.0)
            joined_ref[place, 1:2, :] = sums_ref[key_head * heads + place, 2:3, :] * inverse

    for hop, term_ref in zip(sent_hops, terms):
        start = pl.multiple_of(meta_ref[hop], ALIGN)
        term_ref[...] = acc_ref[pl.ds(start, slots), :].astype(term_ref.dtype)


def relayed(ctx_size):
    return ctx_size == 4


def scores(key_head, meta, turned, out_grad, turned_t, grad_t, sums, blocks, after, routed, ctx_size):
    slots, width = blocks[0].shape
    heads = turned.shape[1] // (width // 2)
    span = -(-(routed + ctx_size * ALIGN) // CHUNK) * CHUNK
    sizes, step_units = [(span, slots)], 1
    if span == 2 * CHUNK and routed - slots // 2 + ctx_size * ALIGN <= 3 * CHUNK // 2 + ALIGN:
        sizes = [(CHUNK, slots), (3 * CHUNK // 2, slots), (CHUNK, slots // 2), (span, slots // 2)]
        step_units = 4
    terms = [jax.ShapeDtypeStruct((slots, 2 * HEAD_DIM), jnp.bfloat16)] * (ctx_size - 1)
    if relayed(ctx_size):
        terms[2] = jax.ShapeDtypeStruct((slots, 2 * HEAD_DIM), jnp.float32)
    outs = pl.pallas_call(
        functools.partial(scores_kernel, ctx_size, sizes, step_units, key_head),
        out_shape=(
            *terms,
            jax.ShapeDtypeStruct((span, heads * slots), jnp.bfloat16),
            jax.ShapeDtypeStruct((heads, 8, slots), jnp.float32),
            jax.ShapeDtypeStruct((span + slots, HEAD_DIM), jnp.bfloat16),
        ),
        in_specs=[SMEM] + [VMEM] * (5 + len(blocks) + len(after)),
        out_specs=(VMEM,) * (ctx_size + 2),
        scratch_shapes=[
            pltpu.VMEM((span + slots, HEAD_DIM), jnp.bfloat16),
            pltpu.VMEM((span, HEAD_DIM), jnp.float32),
            pltpu.VMEM((span, heads * slots), jnp.bfloat16),
            pltpu.VMEM((span + slots, 2 * HEAD_DIM), jnp.float32),
        ],
        compiler_params=vmem(routed, 20, 60),
        cost_estimate=pl.CostEstimate(
            flops=4 * 10**9, bytes_accessed=6 * 1024 * 1024, transcendentals=0
        ),
        name="scores",
    )(meta, turned, out_grad, turned_t, grad_t, sums, *blocks, *after)
    return outs[: ctx_size - 1], outs[ctx_size - 1 :]


def local_kernel(
    key_head,
    meta_ref,
    cos_ref,
    sin_ref,
    turned_ref,
    grad_ref,
    sent_ref,
    weight_ref,
    product_ref,
    score_grad_ref,
    joined_ref,
    key_ref,
    *refs,
):
    dq_ref, own_ref, prob_ref, own_grad_ref, sum_ref = refs[-5:]
    slots = turned_ref.shape[0]
    heads = joined_ref.shape[0]
    span = score_grad_ref.shape[0]
    my_start = meta_ref[0]
    own_key_t = sent_ref[:, key_lanes(key_head)].astype(jnp.float32).T.astype(jnp.bfloat16)
    for head in range(heads):
        columns = slice(head * slots, (head + 1) * slots)
        prob = weight_ref[key_head * heads + head] * joined_ref[head, 0:1, :]
        prob_ref[:, columns] = prob.astype(jnp.bfloat16)
        product = product_ref[key_head * heads + head] - joined_ref[head, 1:2, :]
        score_grad = (prob * product).astype(jnp.bfloat16)
        own_grad_ref[:, columns] = score_grad
        sum_ref[head] = dot(own_key_t, score_grad, ((1,), (0,)))
    for chunk in range(0, span, CHUNK):

        @pl.when(chunk < my_start)
        def _():
            rows = slice(chunk, chunk + CHUNK)
            key_t = key_ref[rows, :].astype(jnp.float32).T.astype(jnp.bfloat16)
            for head in range(heads):
                score_grad = score_grad_ref[rows, head * slots : (head + 1) * slots]
                sum_ref[head] += dot(key_t, score_grad, ((1,), (0,)))

    lane = key_head * heads * HEAD_DIM
    for head in range(heads):
        grad = turn_back((sum_ref[head] * SCORE_SCALE).T, cos_ref[...], sin_ref[...])
        dq_ref[:, head * HEAD_DIM : (head + 1) * HEAD_DIM] = grad.astype(jnp.bfloat16)
    own_ref[...] = terms_of(
        prob_ref[...],
        own_grad_ref[...],
        stacked(turned_ref, lane, heads, slots),
        stacked(grad_ref, lane, heads, slots),
    )


def local_terms(key_head, meta, cos_full, sin_full, turned, out_grad, sent, own, joined, after):
    slots = turned.shape[0]
    heads = joined[1].shape[0]
    weight, product, _ = own
    operands = (meta, cos_full, sin_full, turned, out_grad, sent, weight, product, *joined, *after)
    return pl.pallas_call(
        functools.partial(local_kernel, key_head),
        out_shape=(
            jax.ShapeDtypeStruct((slots, heads * HEAD_DIM), jnp.bfloat16),
            jax.ShapeDtypeStruct((slots, 2 * HEAD_DIM), jnp.float32),
        ),
        in_specs=[SMEM] + [VMEM] * (len(operands) - 1),
        out_specs=(VMEM, VMEM),
        scratch_shapes=[
            pltpu.VMEM((slots, heads * slots), jnp.bfloat16),
            pltpu.VMEM((slots, heads * slots), jnp.bfloat16),
            pltpu.VMEM((heads, HEAD_DIM, slots), jnp.float32),
        ],
        compiler_params=vmem(joined[0].shape[0] // 2, 16, 48),
        cost_estimate=pl.CostEstimate(
            flops=4 * 10**9, bytes_accessed=10 * 1024 * 1024, transcendentals=0
        ),
        name="local_terms",
    )(*operands)


def add_kernel(own_ref, arrived_ref, handed_ref, *refs):
    sum_ref, handed_again_ref = refs[-2:]
    sum_ref[...] = (own_ref[...] + arrived_ref[...].astype(jnp.float32)).astype(jnp.bfloat16)
    handed_again_ref[...] = handed_ref[...]


def add_terms(own, arrived, handed, after):
    result = jax.ShapeDtypeStruct(arrived.shape, jnp.bfloat16)
    return pl.pallas_call(
        add_kernel,
        out_shape=(result, result),
        in_specs=[VMEM] * (3 + len(after)),
        out_specs=(VMEM, VMEM),
        compiler_params=vmem(0, 16, 16),
        cost_estimate=pl.CostEstimate(flops=10**6, bytes_accessed=10**6, transcendentals=0),
        name="add_terms",
    )(own, arrived, handed, *after)


def finish_kernel(ctx_size, key_heads, meta_ref, cos_ref, sin_ref, *refs):
    key_grad_ref, value_grad_ref = refs[-2:]
    owns, terms = refs[:key_heads], list(refs[key_heads:-2])
    slots = cos_ref.shape[0]
    live = lax.broadcasted_iota(jnp.int32, (slots, HEAD_DIM), 0) < meta_ref[ctx_size]
    totals = [own[...] for own in owns]
    for index in range(ctx_size - 1):
        parts = [terms.pop(0)]
        if parts[0].shape[1] == 2 * HEAD_DIM:
            parts += [terms.pop(0) for _ in range(key_heads - 1)]
        term = jnp.concatenate([part[...] for part in parts], axis=1).astype(jnp.float32)
        if index == 0 and relayed(ctx_size):
            term = jnp.where(lax.axis_index("ctx") == 2, 0.0, term)
        for head in range(key_heads):
            totals[head] += term[:, 2 * head * HEAD_DIM : 2 * (head + 1) * HEAD_DIM]
    for head, total in enumerate(totals):
        lanes = head_lanes(head)
        key_term = turn_back(total[:, :HEAD_DIM], cos_ref[...], sin_ref[...])
        key_grad_ref[:, lanes] = jnp.where(live, key_term, 0.0).astype(jnp.bfloat16)
        value_grad_ref[:, lanes] = jnp.where(live, total[:, HEAD_DIM:], 0.0).astype(jnp.bfloat16)


def finish(meta, cos_full, sin_full, owns, terms, ctx_size):
    slots = cos_full.shape[0]
    key_heads = len(owns)
    grad = jax.ShapeDtypeStruct((slots, key_heads * HEAD_DIM), jnp.bfloat16)
    return pl.pallas_call(
        functools.partial(finish_kernel, ctx_size, key_heads),
        out_shape=(grad, grad),
        in_specs=[SMEM] + [VMEM] * (2 + len(owns) + len(terms)),
        out_specs=(VMEM, VMEM),
        compiler_params=vmem(0, 16, 16),
        name="finish",
    )(meta, cos_full, sin_full, *owns, *terms)


def spread(sent, sent_again, ctx_size):
    if relayed(ctx_size):
        alpha = lax.ppermute(sent, "ctx", [(0, 2), (2, 3)])
        beta = lax.ppermute(sent, "ctx", [(1, 3)])
        gamma = lax.ppermute(sent_again, "ctx", [(0, 1), (1, 2)])
        return [alpha, beta, gamma, lax.ppermute(alpha, "ctx", [(2, 3)])]
    blocks = [sent]
    for hop in range(1, ctx_size):
        pairs = [(shard, shard + 1) for shard in range(hop - 1, ctx_size - 1)]
        blocks.append(lax.ppermute(blocks[-1], "ctx", pairs))
    return blocks[1:]


def relay(terms):
    firsts, seconds, thirds, after = [], [], [], []
    for first, second, third in terms:
        firsts.append(lax.ppermute(first, "ctx", [(3, 2), (2, 1), (1, 0)]))
        third, handed = add_terms(third, firsts[-1], second, after)
        thirds.append(lax.ppermute(third, "ctx", [(3, 2), (2, 0)]))
        seconds.append(lax.ppermute(handed if after else second, "ctx", [(3, 1)]))
        after = [third]
    return firsts + thirds + seconds


def descend(terms, ctx_size):
    arrived = []
    for hop, term in enumerate(terms, 1):
        pairs = [(shard + hop, shard) for shard in range(ctx_size - hop)]
        arrived.append(lax.ppermute(term, "ctx", pairs))
    return arrived


def body(positions, queries, keys, values, out_grad):
    ctx_size = lax.axis_size("ctx")
    routed = positions.shape[1]
    key_heads = keys.shape[2] // HEAD_DIM
    meta, cos_full, sin_full, sent = prepare(positions, keys[0], values[0], ctx_size)
    turned, turned_t, grad_t, sent_again = rotate_queries(
        cos_full, sin_full, queries[0], out_grad[0], sent
    )
    blocks = spread(sent, sent_again, ctx_size)
    own = own_scores(sent, turned_t, grad_t)
    terms, joined, dqs, owns = [], [], [], []
    for head in range(key_heads):
        after = [terms[-1][0]] if terms else []
        outs = scores(
            head,
            meta,
            turned,
            out_grad[0],
            turned_t,
            grad_t,
            own[2],
            blocks,
            after,
            routed,
            ctx_size,
        )
        terms.append(outs[0])
        joined.append(outs[1])
    if relayed(ctx_size):
        arrived = relay(terms)
    else:
        arrived = [part for hop in zip(*[descend(term, ctx_size) for term in terms]) for part in hop]
    for head in range(key_heads):
        after = [arrived[0]] if relayed(ctx_size) and head > 0 else []
        dq, own_terms = local_terms(
            head, meta, cos_full, sin_full, turned, out_grad[0], sent, own, joined[head], after
        )
        dqs.append(dq)
        owns.append(own_terms)
    dq = jnp.concatenate(dqs, axis=1)
    key_grad, value_grad = finish(meta, cos_full, sin_full, owns, arrived, ctx_size)
    return (dq[None], key_grad[None], value_grad[None])


def solution(mesh):
    split = P(("groups", "dp"), "ctx", "mp")
    return jax.shard_map(
        body,
        mesh=mesh,
        in_specs=(P(("groups", "dp"), None), split, split, split, split),
        out_specs=(split, split, split),
        check_vma=False,
    )
```

```python
import functools
import math

import jax
import jax.numpy as jnp
import numpy as np
from jax import lax
from jax.experimental import pallas as pl
from jax.experimental.pallas import tpu as pltpu
from jax.sharding import PartitionSpec as P

HEAD_DIM = 128
HALF_DIM = HEAD_DIM // 2
TOK_SHARD = 1024
ROPE_BASE = 500000.0
SCORE_SCALE = 1.0 / math.sqrt(HEAD_DIM)
EXP2_SCALE = SCORE_SCALE * math.log2(math.e)
HIDDEN = -1e30
ALIGN = 16
CHUNK = 288
MIB = 1024 * 1024

VMEM = pl.BlockSpec(memory_space=pltpu.VMEM)
SMEM = pl.BlockSpec(memory_space=pltpu.SMEM)
HBM = pl.BlockSpec(memory_space=pltpu.HBM)


def vmem(routed, small, large):
    return pltpu.CompilerParams(vmem_limit_bytes=(small if routed <= 512 else large) * MIB)


def dot(left, right, contract):
    return lax.dot_general(left, right, (contract, ((), ())), preferred_element_type=jnp.float32)


def turn(field, cos_full, sin_full):
    return field * cos_full + pltpu.roll(field, HALF_DIM, 1) * sin_full


def turn_back(field, cos_full, sin_full):
    return field * cos_full - pltpu.roll(field, HALF_DIM, 1) * sin_full


def frequencies():
    ladder = np.arange(HALF_DIM, dtype=np.float32)
    exponent = ladder * np.float32(-2.0 * math.log(ROPE_BASE) / HEAD_DIM)
    freq = np.exp(exponent.astype(np.float64)).astype(np.float32)
    entry = lax.broadcasted_iota(jnp.int32, (1, HEAD_DIM), 1) % HALF_DIM
    row = jnp.zeros((1, HEAD_DIM), jnp.float32)
    for index in range(HALF_DIM):
        row = jnp.where(entry == index, float(freq[index]), row)
    return row


def shard_layout(ctx_size, me, pos, meta_ref):
    shard_of = pos // TOK_SHARD
    for hop in range(2 * ctx_size):
        meta_ref[hop] = 0
    start = jnp.int32(0)
    first = jnp.int32(0)
    my_first = jnp.int32(0)
    for shard in range(ctx_size):
        count = jnp.sum(jnp.where(shard_of == shard, 1.0, 0.0)).astype(jnp.int32)
        my_first = jnp.where(me == shard, first, my_first)

        @pl.when(me >= shard)
        def _():
            meta_ref[me - shard] = start
            meta_ref[ctx_size + me - shard] = count

        first = first + count
        start = start + (count + ALIGN - 1) // ALIGN * ALIGN
    return my_first


def prepare_kernel(
    ctx_size, pos_hbm, keys_hbm, values_hbm, meta_ref, cos_ref, sin_ref, sent_ref, *refs
):
    pos_ref, keys_ref, values_ref, sems = refs
    sources = (pos_hbm, keys_hbm, values_hbm)
    targets = (pos_ref, keys_ref, values_ref)
    copies = [
        pltpu.make_async_copy(source, target, sems.at[index])
        for index, (source, target) in enumerate(zip(sources, targets))
    ]
    for copy in copies:
        copy.start()
    copies[0].wait()
    slots = keys_ref.shape[0]
    pos = pos_ref[...]
    my_first = shard_layout(ctx_size, lax.axis_index("ctx"), pos, meta_ref)
    shape = (slots, pos.shape[1])
    gap = lax.broadcasted_iota(jnp.int32, shape, 1) - lax.broadcasted_iota(jnp.int32, shape, 0)
    named = jnp.where(gap == my_first, pos.astype(jnp.float32), 0.0)
    angles = jnp.sum(named, axis=1, keepdims=True) * frequencies()
    cos_full = jnp.cos(angles)
    front = lax.broadcasted_iota(jnp.int32, angles.shape, 1) < HALF_DIM
    sin_full = jnp.where(front, -jnp.sin(angles), jnp.sin(angles))
    cos_ref[...] = cos_full
    sin_ref[...] = sin_full
    copies[1].wait()
    copies[2].wait()
    for lane in range(0, keys_ref.shape[1], HEAD_DIM):
        lanes = slice(lane, lane + HEAD_DIM)
        key = turn(keys_ref[:, lanes].astype(jnp.float32), cos_full, sin_full)
        middle = 2 * lane + HEAD_DIM
        sent_ref[:, 2 * lane : middle] = key.astype(jnp.bfloat16)
        sent_ref[:, middle : middle + HEAD_DIM] = values_ref[:, lanes]


def prepare(positions, keys, values, ctx_size):
    slots, width = keys.shape
    table = jax.ShapeDtypeStruct((slots, HEAD_DIM), jnp.float32)
    sent = jax.ShapeDtypeStruct((slots, 2 * width), jnp.bfloat16)
    operands = (positions, keys, values)
    return pl.pallas_call(
        functools.partial(prepare_kernel, ctx_size),
        out_shape=(
            jax.ShapeDtypeStruct((2 * ctx_size,), jnp.int32),
            table,
            table,
            sent,
        ),
        in_specs=[HBM] * 3,
        out_specs=(SMEM, VMEM, VMEM, VMEM),
        scratch_shapes=[pltpu.VMEM(operand.shape, operand.dtype) for operand in operands]
        + [pltpu.SemaphoreType.DMA((3,))],
        compiler_params=vmem(positions.shape[1], 60, 60),
        name="prepare",
    )(*operands)


def queries_kernel(
    cos_ref,
    sin_ref,
    query_ref,
    grad_ref,
    sent_ref,
    turned_ref,
    turned_t_ref,
    grad_t_ref,
    sent_again_ref,
):
    sent_again_ref[...] = sent_ref[...]
    for lane in range(0, query_ref.shape[1], HEAD_DIM):
        lanes = slice(lane, lane + HEAD_DIM)
        query = turn(query_ref[:, lanes].astype(jnp.float32), cos_ref[...], sin_ref[...])
        turned_ref[:, lanes] = query.astype(jnp.bfloat16)
        turned_t_ref[lanes, :] = query.T.astype(jnp.bfloat16)
        grad_t_ref[lanes, :] = grad_ref[:, lanes].astype(jnp.float32).T.astype(jnp.bfloat16)


def rotate_queries(cos_full, sin_full, queries, out_grad, sent):
    slots, width = queries.shape
    straight = jax.ShapeDtypeStruct((slots, width), jnp.bfloat16)
    across = jax.ShapeDtypeStruct((width, slots), jnp.bfloat16)
    return pl.pallas_call(
        queries_kernel,
        out_shape=(straight, across, across, jax.ShapeDtypeStruct(sent.shape, sent.dtype)),
        in_specs=[VMEM] * 5,
        out_specs=(VMEM,) * 4,
        compiler_params=vmem(0, 16, 16),
        cost_estimate=pl.CostEstimate(
            flops=3 * 10**9, bytes_accessed=4 * 1024 * 1024, transcendentals=0
        ),
        name="rotate_queries",
    )(cos_full, sin_full, queries, out_grad, sent)


def stacked(ref, lane, heads, width):
    parts = [ref[:width, lane + h * HEAD_DIM : lane + (h + 1) * HEAD_DIM] for h in range(heads)]
    return jnp.concatenate(parts, axis=0)


def beside(ref, rows, heads, slots, width):
    if width == slots:
        return ref[:rows, :]
    columns = [head * slots for head in range(heads)]
    return jnp.concatenate([ref[:rows, start : start + width] for start in columns], axis=1)


def terms_of(probs, score_grads, queries, grads):
    key_term = dot(score_grads, queries, ((1,), (0,))) * SCORE_SCALE
    return jnp.concatenate([key_term, dot(probs, grads, ((1,), (0,)))], axis=1)


def fold(field, join, reduce):
    while field.shape[0] % 16 == 0:
        half = field.shape[0] // 2
        field = join(field[:half], field[half:])
    return reduce(field, axis=0, keepdims=True)


def head_lanes(head):
    return slice(head * HEAD_DIM, (head + 1) * HEAD_DIM)


def key_lanes(key_head):
    return slice(2 * key_head * HEAD_DIM, (2 * key_head + 1) * HEAD_DIM)


def value_lanes(key_head):
    return slice((2 * key_head + 1) * HEAD_DIM, 2 * (key_head + 1) * HEAD_DIM)


def own_kernel(step_heads, sent_ref, turned_t_ref, grad_t_ref, weight_ref, product_ref, sums_ref, bias_ref):
    slots = sent_ref.shape[0]
    key_heads = sent_ref.shape[1] // HEAD_DIM // 2
    heads = turned_t_ref.shape[0] // HEAD_DIM // key_heads
    key_id = lax.broadcasted_iota(jnp.int32, (slots, slots), 0)
    slot_id = lax.broadcasted_iota(jnp.int32, (slots, slots), 1)
    bias_ref[...] = jnp.where(key_id <= slot_id, 0.0, HIDDEN)
    for key_head in range(key_heads):

        def step(index, carry):
            for part in range(step_heads):
                head = key_head * heads + index * step_heads + part
                rows = pl.ds(pl.multiple_of(head * HEAD_DIM, HEAD_DIM), HEAD_DIM)
                scores = dot(sent_ref[:, key_lanes(key_head)], turned_t_ref[rows, :], ((1,), (0,)))
                scores = scores + bias_ref[...]
                prob_grad = dot(sent_ref[:, value_lanes(key_head)], grad_t_ref[rows, :], ((1,), (0,)))
                peak = fold(scores, jnp.maximum, jnp.max)
                weights = jnp.exp2((scores - peak) * EXP2_SCALE)
                weight_ref[head] = weights
                product_ref[head] = prob_grad
                sums_ref[head, 0:1, :] = peak
                sums_ref[head, 1:2, :] = fold(weights, jnp.add, jnp.sum)
                sums_ref[head, 2:3, :] = fold(weights * prob_grad, jnp.add, jnp.sum)
            return carry

        lax.fori_loop(0, heads // step_heads, step, 0)


def own_scores(sent, turned_t, grad_t):
    slots = sent.shape[0]
    heads = turned_t.shape[0] // HEAD_DIM
    square = jax.ShapeDtypeStruct((heads, slots, slots), jnp.float32)
    return pl.pallas_call(
        functools.partial(own_kernel, 4),
        out_shape=(square, square, jax.ShapeDtypeStruct((heads, 8, slots), jnp.float32)),
        in_specs=[VMEM] * 3,
        out_specs=(VMEM,) * 3,
        scratch_shapes=[pltpu.VMEM((slots, slots), jnp.float32)],
        compiler_params=vmem(0, 16, 16),
        cost_estimate=pl.CostEstimate(
            flops=5 * 10**9, bytes_accessed=10 * 1024 * 1024, transcendentals=0
        ),
        name="own_scores",
    )(sent, turned_t, grad_t)


def scores_kernel(
    ctx_size,
    sizes,
    step_units,
    key_head,
    meta_ref,
    turned_ref,
    grad_ref,
    turned_t_ref,
    grad_t_ref,
    sums_ref,
    *refs,
):
    count = 4 if relayed(ctx_size) else ctx_size - 1
    inputs, before = refs[:count], refs[count : -6 - ctx_size]
    refs = refs[-6 - ctx_size :]
    terms, refs = refs[: ctx_size - 1], refs[ctx_size - 1 :]
    score_grad_ref, joined_ref, key_ref, value_ref, bias_ref, prob_ref, acc_ref = refs
    slots = turned_ref.shape[0]
    span = bias_ref.shape[0]
    heads = joined_ref.shape[0]
    starts = [pl.multiple_of(meta_ref[hop], ALIGN) for hop in range(ctx_size)]
    my_start, my_count = starts[0], meta_ref[ctx_size]
    sent_hops = list(range(1, ctx_size))
    if relayed(ctx_size):
        last = lax.axis_index("ctx") == ctx_size - 1
        sent_hops = [jnp.where(last, 3, 1), 2, jnp.where(last, 1, 2)]

    def blocks_of(lanes):
        blocks = [block[:, lanes] for block in inputs]
        if relayed(ctx_size):
            alpha, beta, gamma, delta = blocks
            blocks = [jnp.where(last, alpha, gamma), jnp.where(last, beta, alpha), delta]
        return blocks

    for ref, lanes in ((key_ref, key_lanes(key_head)), (value_ref, value_lanes(key_head))):
        ref[slots:span, :] = jnp.zeros((span - slots, HEAD_DIM), jnp.bfloat16)
        blocks = blocks_of(lanes)
        for hop in range(ctx_size - 1, 0, -1):
            ref[pl.ds(starts[hop], slots), :] = blocks[hop - 1]
    place = lax.broadcasted_iota(jnp.int32, bias_ref.shape, 0)
    seen = place < 0
    for hop in range(1, ctx_size):
        end = starts[hop] + meta_ref[ctx_size + hop]
        seen = seen | ((place >= starts[hop]) & (place < end))
    bias_ref[...] = jnp.where(seen, 0.0, HIDDEN)
    live = lax.broadcasted_iota(jnp.int32, (1, slots), 1) < my_count
    acc_ref[...] = jnp.zeros_like(acc_ref)

    def joint(ref, places, rows, width):
        return jnp.concatenate([ref[rows(place) + (slice(0, width),)] for place in places], axis=1)

    def head_rows(place):
        return (pl.ds(pl.multiple_of((key_head * heads + place) * HEAD_DIM, HEAD_DIM), HEAD_DIM),)

    def units(groups, rows, width):
        side = slots // width
        bias = jnp.concatenate([bias_ref[:rows, :]] * (slots // HEAD_DIM), axis=1)
        alive = jnp.concatenate([live[:, :width]] * side, axis=1)
        queries = [joint(turned_t_ref, group, head_rows, width) for group in groups]
        grads = [joint(grad_t_ref, group, head_rows, width) for group in groups]

        def sums(row):
            index = lambda place: (key_head * heads + place, slice(row, row + 1))
            return [joint(sums_ref, group, index, width) for group in groups]

        own_peaks, own_totals, own_products = sums(0), sums(1), sums(2)
        scores = [dot(key_ref[:rows, :], query, ((1,), (0,))) + bias for query in queries]
        prob_grads = [dot(value_ref[:rows, :], grad, ((1,), (0,))) for grad in grads]
        peaks = [
            jnp.maximum(own, fold(score, jnp.maximum, jnp.max))
            for own, score in zip(own_peaks, scores)
        ]
        weights = [jnp.exp2((score - peak) * EXP2_SCALE) for score, peak in zip(scores, peaks)]
        shares = [jnp.exp2((own - peak) * EXP2_SCALE) for own, peak in zip(own_peaks, peaks)]
        totals = [
            own * share + fold(weight, jnp.add, jnp.sum)
            for own, share, weight in zip(own_totals, shares, weights)
        ]
        products = [
            own * share + fold(weight * prob_grad, jnp.add, jnp.sum)
            for own, share, weight, prob_grad in zip(own_products, shares, weights, prob_grads)
        ]
        inverses = [1.0 / total for total in totals]
        deltas = [product * inverse for product, inverse in zip(products, inverses)]
        inverses = [jnp.where(alive, inverse, 0.0) for inverse in inverses]
        factors = [share * inverse for share, inverse in zip(shares, inverses)]
        probs = [weight * inverse for weight, inverse in zip(weights, inverses)]
        score_grads = [
            (prob * (prob_grad - delta)).astype(jnp.bfloat16)
            for prob, prob_grad, delta in zip(probs, prob_grads, deltas)
        ]
        probs = [prob.astype(jnp.bfloat16) for prob in probs]
        for group, prob, score_grad, factor, delta in zip(
            groups, probs, score_grads, factors, deltas
        ):
            for index, place in enumerate(group):
                part = slice(index * width, (index + 1) * width)
                columns = pl.ds(pl.multiple_of(place * slots, slots), width)
                prob_ref[:rows, columns] = prob[:, part]
                score_grad_ref[:rows, columns] = score_grad[:, part]
                joined_ref[place, 0:1, :width] = factor[:, part]
                joined_ref[place, 1:2, :width] = delta[:, part]
                if width < slots:
                    rest = pl.ds(pl.multiple_of(place * slots + width, HEAD_DIM), slots - width)
                    score_grad_ref[:rows, rest] = jnp.zeros((rows, slots - width), jnp.bfloat16)
                    joined_ref[place, 0:2, width:] = jnp.zeros((2, slots - width), jnp.float32)

    above = {}
    for rows, width in sizes:
        fits = (my_start > above.get(width, 0)) & (my_start <= rows)
        above[width] = rows
        if len(sizes) > 1:
            fits = fits & ((my_count > slots // 2) if width == slots else (my_count <= width))

        @pl.when(fits)
        def _():
            side = slots // width

            def step(index, carry):
                base = index * step_units * side
                units(
                    [[base + part * side + item for item in range(side)] for part in range(step_units)],
                    rows,
                    width,
                )
                return carry

            lax.fori_loop(0, heads // side // step_units, step, 0)
            if rows % CHUNK:
                beyond = slice(rows, rows + CHUNK - rows % CHUNK)
                none = jnp.zeros((CHUNK - rows % CHUNK, heads * slots), jnp.bfloat16)
                score_grad_ref[beyond, :] = none
            lane = key_head * heads * HEAD_DIM
            acc_ref[:rows, :] = terms_of(
                beside(prob_ref, rows, heads, slots, width),
                beside(score_grad_ref, rows, heads, slots, width),
                stacked(turned_ref, lane, heads, width),
                stacked(grad_ref, lane, heads, width),
            )

    @pl.when(my_start == 0)
    def _():
        for place in range(heads):
            inverse = 1.0 / sums_ref[key_head * heads + place, 1:2, :]
            joined_ref[place, 0:1, :] = jnp.where(live, inverse, 0.0)
            joined_ref[place, 1:2, :] = sums_ref[key_head * heads + place, 2:3, :] * inverse

    for hop, term_ref in zip(sent_hops, terms):
        start = pl.multiple_of(meta_ref[hop], ALIGN)
        term = acc_ref[pl.ds(start, slots), :].astype(term_ref.dtype)
        if term_ref.shape == term.shape:
            term_ref[...] = term
        else:
            term_ref[:, : -2 * HEAD_DIM] = before[0][...]
            term_ref[:, -2 * HEAD_DIM :] = term


def relayed(ctx_size):
    return ctx_size == 4


def scores(key_head, meta, turned, out_grad, turned_t, grad_t, sums, blocks, after, routed, ctx_size):
    slots, width = blocks[0].shape
    heads = turned.shape[1] // (width // 2)
    span = -(-(routed + ctx_size * ALIGN) // CHUNK) * CHUNK
    sizes, step_units = [(span, slots)], 1
    if span == 2 * CHUNK and routed - slots // 2 + ctx_size * ALIGN <= 3 * CHUNK // 2 + ALIGN:
        sizes = [(CHUNK, slots), (3 * CHUNK // 2, slots), (CHUNK, slots // 2), (span, slots // 2)]
        step_units = 4
    terms = [jax.ShapeDtypeStruct((slots, 2 * HEAD_DIM), jnp.bfloat16)] * (ctx_size - 1)
    if relayed(ctx_size):
        terms[1] = jax.ShapeDtypeStruct((slots, 2 * (key_head + 1) * HEAD_DIM), jnp.bfloat16)
        terms[2] = jax.ShapeDtypeStruct((slots, 2 * HEAD_DIM), jnp.float32)
    outs = pl.pallas_call(
        functools.partial(scores_kernel, ctx_size, sizes, step_units, key_head),
        out_shape=(
            *terms,
            jax.ShapeDtypeStruct((span, heads * slots), jnp.bfloat16),
            jax.ShapeDtypeStruct((heads, 8, slots), jnp.float32),
            jax.ShapeDtypeStruct((span + slots, HEAD_DIM), jnp.bfloat16),
        ),
        in_specs=[SMEM] + [VMEM] * (5 + len(blocks) + len(after)),
        out_specs=(VMEM,) * (ctx_size + 2),
        scratch_shapes=[
            pltpu.VMEM((span + slots, HEAD_DIM), jnp.bfloat16),
            pltpu.VMEM((span, HEAD_DIM), jnp.float32),
            pltpu.VMEM((span, heads * slots), jnp.bfloat16),
            pltpu.VMEM((span + slots, 2 * HEAD_DIM), jnp.float32),
        ],
        compiler_params=vmem(routed, 20, 60),
        cost_estimate=pl.CostEstimate(
            flops=4 * 10**9, bytes_accessed=6 * 1024 * 1024, transcendentals=0
        ),
        name="scores",
    )(meta, turned, out_grad, turned_t, grad_t, sums, *blocks, *after)
    return outs[: ctx_size - 1], outs[ctx_size - 1 :]


def local_kernel(
    key_head,
    meta_ref,
    cos_ref,
    sin_ref,
    turned_ref,
    grad_ref,
    sent_ref,
    weight_ref,
    product_ref,
    score_grad_ref,
    joined_ref,
    key_ref,
    *refs,
):
    dq_ref, own_ref, prob_ref, own_grad_ref, sum_ref = refs[-5:]
    slots = turned_ref.shape[0]
    heads = joined_ref.shape[0]
    span = score_grad_ref.shape[0]
    my_start = meta_ref[0]
    own_key_t = sent_ref[:, key_lanes(key_head)].astype(jnp.float32).T.astype(jnp.bfloat16)
    for head in range(heads):
        columns = slice(head * slots, (head + 1) * slots)
        prob = weight_ref[key_head * heads + head] * joined_ref[head, 0:1, :]
        prob_ref[:, columns] = prob.astype(jnp.bfloat16)
        product = product_ref[key_head * heads + head] - joined_ref[head, 1:2, :]
        score_grad = (prob * product).astype(jnp.bfloat16)
        own_grad_ref[:, columns] = score_grad
        sum_ref[head] = dot(own_key_t, score_grad, ((1,), (0,)))
    for chunk in range(0, span, CHUNK):

        @pl.when(chunk < my_start)
        def _():
            rows = slice(chunk, chunk + CHUNK)
            key_t = key_ref[rows, :].astype(jnp.float32).T.astype(jnp.bfloat16)
            for head in range(heads):
                score_grad = score_grad_ref[rows, head * slots : (head + 1) * slots]
                sum_ref[head] += dot(key_t, score_grad, ((1,), (0,)))

    lane = key_head * heads * HEAD_DIM
    for head in range(heads):
        grad = turn_back((sum_ref[head] * SCORE_SCALE).T, cos_ref[...], sin_ref[...])
        dq_ref[:, head * HEAD_DIM : (head + 1) * HEAD_DIM] = grad.astype(jnp.bfloat16)
    own_ref[...] = terms_of(
        prob_ref[...],
        own_grad_ref[...],
        stacked(turned_ref, lane, heads, slots),
        stacked(grad_ref, lane, heads, slots),
    )


def local_terms(key_head, meta, cos_full, sin_full, turned, out_grad, sent, own, joined, dq, after):
    slots = turned.shape[0]
    heads = joined[1].shape[0]
    weight, product, _ = own
    operands = [meta, cos_full, sin_full, turned, out_grad, sent, weight, product, *joined, *after]
    in_specs = [SMEM] + [VMEM] * (len(operands) - 1)
    aliases = {}
    if dq is not None:
        aliases = {len(operands): 0}
        operands.append(dq)
        in_specs.append(pl.BlockSpec(memory_space=pl.ANY))
    return pl.pallas_call(
        functools.partial(local_kernel, key_head),
        grid=(1,),
        out_shape=(
            jax.ShapeDtypeStruct(turned.shape, jnp.bfloat16),
            jax.ShapeDtypeStruct((slots, 2 * HEAD_DIM), jnp.float32),
        ),
        in_specs=in_specs,
        out_specs=(pl.BlockSpec((slots, heads * HEAD_DIM), lambda step: (0, key_head)), VMEM),
        scratch_shapes=[
            pltpu.VMEM((slots, heads * slots), jnp.bfloat16),
            pltpu.VMEM((slots, heads * slots), jnp.bfloat16),
            pltpu.VMEM((heads, HEAD_DIM, slots), jnp.float32),
        ],
        input_output_aliases=aliases,
        compiler_params=vmem(joined[0].shape[0] // 2, 16, 48),
        cost_estimate=pl.CostEstimate(
            flops=4 * 10**9, bytes_accessed=10 * 1024 * 1024, transcendentals=0
        ),
        name="local_terms",
    )(*operands)


def add_kernel(own_ref, arrived_ref, *refs):
    refs[-1][...] = (own_ref[...] + arrived_ref[...].astype(jnp.float32)).astype(jnp.bfloat16)


def add_terms(own, arrived, after):
    return pl.pallas_call(
        add_kernel,
        out_shape=jax.ShapeDtypeStruct(arrived.shape, jnp.bfloat16),
        in_specs=[VMEM] * (2 + len(after)),
        out_specs=VMEM,
        compiler_params=vmem(0, 16, 16),
        cost_estimate=pl.CostEstimate(flops=10**6, bytes_accessed=10**6, transcendentals=0),
        name="add_terms",
    )(own, arrived, *after)


def finish_kernel(ctx_size, key_heads, meta_ref, cos_ref, sin_ref, *refs):
    key_grad_ref, value_grad_ref = refs[-2:]
    owns, terms = refs[:key_heads], list(refs[key_heads:-2])
    slots = cos_ref.shape[0]
    live = lax.broadcasted_iota(jnp.int32, (slots, HEAD_DIM), 0) < meta_ref[ctx_size]
    totals = [own[...] for own in owns]
    for index in range(ctx_size - 1):
        parts = [terms.pop(0)]
        if parts[0].shape[1] == 2 * HEAD_DIM:
            parts += [terms.pop(0) for _ in range(key_heads - 1)]
        term = jnp.concatenate([part[...] for part in parts], axis=1).astype(jnp.float32)
        if index == 0 and relayed(ctx_size):
            term = jnp.where(lax.axis_index("ctx") == 2, 0.0, term)
        for head in range(key_heads):
            totals[head] += term[:, 2 * head * HEAD_DIM : 2 * (head + 1) * HEAD_DIM]
    for head, total in enumerate(totals):
        lanes = head_lanes(head)
        key_term = turn_back(total[:, :HEAD_DIM], cos_ref[...], sin_ref[...])
        key_grad_ref[:, lanes] = jnp.where(live, key_term, 0.0).astype(jnp.bfloat16)
        value_grad_ref[:, lanes] = jnp.where(live, total[:, HEAD_DIM:], 0.0).astype(jnp.bfloat16)


def finish(meta, cos_full, sin_full, owns, terms, ctx_size):
    slots = cos_full.shape[0]
    key_heads = len(owns)
    grad = jax.ShapeDtypeStruct((slots, key_heads * HEAD_DIM), jnp.bfloat16)
    return pl.pallas_call(
        functools.partial(finish_kernel, ctx_size, key_heads),
        out_shape=(grad, grad),
        in_specs=[SMEM] + [VMEM] * (2 + len(owns) + len(terms)),
        out_specs=(VMEM, VMEM),
        compiler_params=vmem(0, 16, 16),
        name="finish",
    )(meta, cos_full, sin_full, *owns, *terms)


def spread(sent, sent_again, ctx_size):
    if relayed(ctx_size):
        alpha = lax.ppermute(sent, "ctx", [(0, 2), (2, 3)])
        beta = lax.ppermute(sent, "ctx", [(1, 3)])
        gamma = lax.ppermute(sent_again, "ctx", [(0, 1), (1, 2)])
        return [alpha, beta, gamma, lax.ppermute(alpha, "ctx", [(2, 3)])]
    blocks = [sent]
    for hop in range(1, ctx_size):
        pairs = [(shard, shard + 1) for shard in range(hop - 1, ctx_size - 1)]
        blocks.append(lax.ppermute(blocks[-1], "ctx", pairs))
    return blocks[1:]


def relay(terms):
    firsts, thirds, after = [], [], []
    for first, _, third in terms:
        firsts.append(lax.ppermute(first, "ctx", [(3, 2), (2, 1), (1, 0)]))
        third = add_terms(third, firsts[-1], after)
        thirds.append(lax.ppermute(third, "ctx", [(3, 2), (2, 0)]))
        after = [third]
    return firsts + thirds + [lax.ppermute(terms[-1][1], "ctx", [(3, 1)])]


def descend(terms, ctx_size):
    arrived = []
    for hop, term in enumerate(terms, 1):
        pairs = [(shard + hop, shard) for shard in range(ctx_size - hop)]
        arrived.append(lax.ppermute(term, "ctx", pairs))
    return arrived


def body(positions, queries, keys, values, out_grad):
    ctx_size = lax.axis_size("ctx")
    routed = positions.shape[1]
    key_heads = keys.shape[2] // HEAD_DIM
    meta, cos_full, sin_full, sent = prepare(positions, keys[0], values[0], ctx_size)
    turned, turned_t, grad_t, sent_again = rotate_queries(
        cos_full, sin_full, queries[0], out_grad[0], sent
    )
    blocks = spread(sent, sent_again, ctx_size)
    own = own_scores(sent, turned_t, grad_t)
    terms, joined, owns = [], [], []
    for head in range(key_heads):
        after = [terms[-1][1]] if terms else []
        outs = scores(
            head,
            meta,
            turned,
            out_grad[0],
            turned_t,
            grad_t,
            own[2],
            blocks,
            after,
            routed,
            ctx_size,
        )
        terms.append(outs[0])
        joined.append(outs[1])
    if relayed(ctx_size):
        arrived = relay(terms)
    else:
        arrived = [part for hop in zip(*[descend(term, ctx_size) for term in terms]) for part in hop]
    dq = None
    for head in range(key_heads):
        after = [arrived[0]] if relayed(ctx_size) and head > 0 else []
        dq, own_terms = local_terms(
            head, meta, cos_full, sin_full, turned, out_grad[0], sent, own, joined[head], dq, after
        )
        owns.append(own_terms)
    key_grad, value_grad = finish(meta, cos_full, sin_full, owns, arrived, ctx_size)
    return (dq[None], key_grad[None], value_grad[None])


def solution(mesh):
    split = P(("groups", "dp"), "ctx", "mp")
    return jax.shard_map(
        body,
        mesh=mesh,
        in_specs=(P(("groups", "dp"), None), split, split, split, split),
        out_specs=(split, split, split),
        check_vma=False,
    )
```

```python
import functools
import math

import jax
import jax.numpy as jnp
import numpy as np
from jax import lax
from jax.experimental import pallas as pl
from jax.experimental.pallas import tpu as pltpu
from jax.sharding import PartitionSpec as P

HEAD_DIM = 128
HALF_DIM = HEAD_DIM // 2
TOK_SHARD = 1024
ROPE_BASE = 500000.0
SCORE_SCALE = 1.0 / math.sqrt(HEAD_DIM)
EXP2_SCALE = SCORE_SCALE * math.log2(math.e)
HIDDEN = -1e30
ALIGN = 16
CHUNK = 288
MIB = 1024 * 1024

VMEM = pl.BlockSpec(memory_space=pltpu.VMEM)
SMEM = pl.BlockSpec(memory_space=pltpu.SMEM)
HBM = pl.BlockSpec(memory_space=pltpu.HBM)


def vmem(routed, small, large):
    return pltpu.CompilerParams(vmem_limit_bytes=(small if routed <= 512 else large) * MIB)


def dot(left, right, contract):
    return lax.dot_general(left, right, (contract, ((), ())), preferred_element_type=jnp.float32)


def turn(field, cos_full, sin_full):
    return field * cos_full + pltpu.roll(field, HALF_DIM, 1) * sin_full


def turn_back(field, cos_full, sin_full):
    return field * cos_full - pltpu.roll(field, HALF_DIM, 1) * sin_full


def frequencies():
    ladder = np.arange(HALF_DIM, dtype=np.float32)
    exponent = ladder * np.float32(-2.0 * math.log(ROPE_BASE) / HEAD_DIM)
    freq = np.exp(exponent.astype(np.float64)).astype(np.float32)
    entry = lax.broadcasted_iota(jnp.int32, (1, HEAD_DIM), 1) % HALF_DIM
    row = jnp.zeros((1, HEAD_DIM), jnp.float32)
    for index in range(HALF_DIM):
        row = jnp.where(entry == index, float(freq[index]), row)
    return row


def shard_layout(ctx_size, me, pos, meta_ref):
    shard_of = pos // TOK_SHARD
    for hop in range(2 * ctx_size):
        meta_ref[hop] = 0
    start = jnp.int32(0)
    first = jnp.int32(0)
    my_first = jnp.int32(0)
    for shard in range(ctx_size):
        count = jnp.sum(jnp.where(shard_of == shard, 1.0, 0.0)).astype(jnp.int32)
        my_first = jnp.where(me == shard, first, my_first)

        @pl.when(me >= shard)
        def _():
            meta_ref[me - shard] = start
            meta_ref[ctx_size + me - shard] = count

        first = first + count
        start = start + (count + ALIGN - 1) // ALIGN * ALIGN
    return my_first


def prepare_kernel(
    ctx_size, pos_hbm, keys_hbm, values_hbm, meta_ref, cos_ref, sin_ref, sent_ref, *refs
):
    pos_ref, keys_ref, values_ref, sems = refs
    sources = (pos_hbm, keys_hbm, values_hbm)
    targets = (pos_ref, keys_ref, values_ref)
    copies = [
        pltpu.make_async_copy(source, target, sems.at[index])
        for index, (source, target) in enumerate(zip(sources, targets))
    ]
    for copy in copies:
        copy.start()
    copies[0].wait()
    slots = keys_ref.shape[0]
    pos = pos_ref[...]
    my_first = shard_layout(ctx_size, lax.axis_index("ctx"), pos, meta_ref)
    shape = (slots, pos.shape[1])
    gap = lax.broadcasted_iota(jnp.int32, shape, 1) - lax.broadcasted_iota(jnp.int32, shape, 0)
    named = jnp.where(gap == my_first, pos.astype(jnp.float32), 0.0)
    angles = jnp.sum(named, axis=1, keepdims=True) * frequencies()
    cos_full = jnp.cos(angles)
    front = lax.broadcasted_iota(jnp.int32, angles.shape, 1) < HALF_DIM
    sin_full = jnp.where(front, -jnp.sin(angles), jnp.sin(angles))
    cos_ref[...] = cos_full
    sin_ref[...] = sin_full
    copies[1].wait()
    copies[2].wait()
    for lane in range(0, keys_ref.shape[1], HEAD_DIM):
        lanes = slice(lane, lane + HEAD_DIM)
        key = turn(keys_ref[:, lanes].astype(jnp.float32), cos_full, sin_full)
        middle = 2 * lane + HEAD_DIM
        sent_ref[:, 2 * lane : middle] = key.astype(jnp.bfloat16)
        sent_ref[:, middle : middle + HEAD_DIM] = values_ref[:, lanes]


def prepare(positions, keys, values, ctx_size):
    slots, width = keys.shape
    table = jax.ShapeDtypeStruct((slots, HEAD_DIM), jnp.float32)
    sent = jax.ShapeDtypeStruct((slots, 2 * width), jnp.bfloat16)
    operands = (positions, keys, values)
    return pl.pallas_call(
        functools.partial(prepare_kernel, ctx_size),
        out_shape=(
            jax.ShapeDtypeStruct((2 * ctx_size,), jnp.int32),
            table,
            table,
            sent,
        ),
        in_specs=[HBM] * 3,
        out_specs=(SMEM, VMEM, VMEM, VMEM),
        scratch_shapes=[pltpu.VMEM(operand.shape, operand.dtype) for operand in operands]
        + [pltpu.SemaphoreType.DMA((3,))],
        compiler_params=vmem(positions.shape[1], 60, 60),
        name="prepare",
    )(*operands)


def queries_kernel(
    cos_ref,
    sin_ref,
    query_ref,
    grad_ref,
    sent_ref,
    turned_ref,
    turned_t_ref,
    grad_t_ref,
    sent_again_ref,
):
    sent_again_ref[...] = sent_ref[...]
    for lane in range(0, query_ref.shape[1], HEAD_DIM):
        lanes = slice(lane, lane + HEAD_DIM)
        query = turn(query_ref[:, lanes].astype(jnp.float32), cos_ref[...], sin_ref[...])
        turned_ref[:, lanes] = query.astype(jnp.bfloat16)
        turned_t_ref[lanes, :] = query.T.astype(jnp.bfloat16)
        grad_t_ref[lanes, :] = grad_ref[:, lanes].astype(jnp.float32).T.astype(jnp.bfloat16)


def rotate_queries(cos_full, sin_full, queries, out_grad, sent):
    slots, width = queries.shape
    straight = jax.ShapeDtypeStruct((slots, width), jnp.bfloat16)
    across = jax.ShapeDtypeStruct((width, slots), jnp.bfloat16)
    return pl.pallas_call(
        queries_kernel,
        out_shape=(straight, across, across, jax.ShapeDtypeStruct(sent.shape, sent.dtype)),
        in_specs=[VMEM] * 5,
        out_specs=(VMEM,) * 4,
        compiler_params=vmem(0, 16, 16),
        cost_estimate=pl.CostEstimate(
            flops=3 * 10**9, bytes_accessed=4 * 1024 * 1024, transcendentals=0
        ),
        name="rotate_queries",
    )(cos_full, sin_full, queries, out_grad, sent)


def stacked(ref, lane, heads, width):
    parts = [ref[:width, lane + h * HEAD_DIM : lane + (h + 1) * HEAD_DIM] for h in range(heads)]
    return jnp.concatenate(parts, axis=0)


def beside(ref, rows, heads, slots, width):
    if width == slots:
        return ref[:rows, :]
    columns = [head * slots for head in range(heads)]
    return jnp.concatenate([ref[:rows, start : start + width] for start in columns], axis=1)


def terms_of(probs, score_grads, queries, grads):
    key_term = dot(score_grads, queries, ((1,), (0,))) * SCORE_SCALE
    return jnp.concatenate([key_term, dot(probs, grads, ((1,), (0,)))], axis=1)


def fold(field, join, reduce):
    while field.shape[0] % 16 == 0:
        half = field.shape[0] // 2
        field = join(field[:half], field[half:])
    return reduce(field, axis=0, keepdims=True)


def head_lanes(head):
    return slice(head * HEAD_DIM, (head + 1) * HEAD_DIM)


def key_lanes(key_head):
    return slice(2 * key_head * HEAD_DIM, (2 * key_head + 1) * HEAD_DIM)


def value_lanes(key_head):
    return slice((2 * key_head + 1) * HEAD_DIM, 2 * (key_head + 1) * HEAD_DIM)


def own_kernel(step_heads, sent_ref, turned_t_ref, grad_t_ref, weight_ref, product_ref, sums_ref, bias_ref):
    slots = sent_ref.shape[0]
    key_heads = sent_ref.shape[1] // HEAD_DIM // 2
    heads = turned_t_ref.shape[0] // HEAD_DIM // key_heads
    key_id = lax.broadcasted_iota(jnp.int32, (slots, slots), 0)
    slot_id = lax.broadcasted_iota(jnp.int32, (slots, slots), 1)
    bias_ref[...] = jnp.where(key_id <= slot_id, 0.0, HIDDEN)
    for key_head in range(key_heads):

        def step(index, carry):
            for part in range(step_heads):
                head = key_head * heads + index * step_heads + part
                rows = pl.ds(pl.multiple_of(head * HEAD_DIM, HEAD_DIM), HEAD_DIM)
                scores = dot(sent_ref[:, key_lanes(key_head)], turned_t_ref[rows, :], ((1,), (0,)))
                scores = scores + bias_ref[...]
                prob_grad = dot(sent_ref[:, value_lanes(key_head)], grad_t_ref[rows, :], ((1,), (0,)))
                peak = fold(scores, jnp.maximum, jnp.max)
                weights = jnp.exp2((scores - peak) * EXP2_SCALE)
                weight_ref[head] = weights
                product_ref[head] = prob_grad
                sums_ref[head, 0:1, :] = peak
                sums_ref[head, 1:2, :] = fold(weights, jnp.add, jnp.sum)
                sums_ref[head, 2:3, :] = fold(weights * prob_grad, jnp.add, jnp.sum)
            return carry

        lax.fori_loop(0, heads // step_heads, step, 0)


def own_scores(sent, turned_t, grad_t):
    slots = sent.shape[0]
    heads = turned_t.shape[0] // HEAD_DIM
    square = jax.ShapeDtypeStruct((heads, slots, slots), jnp.float32)
    return pl.pallas_call(
        functools.partial(own_kernel, 4),
        out_shape=(square, square, jax.ShapeDtypeStruct((heads, 8, slots), jnp.float32)),
        in_specs=[VMEM] * 3,
        out_specs=(VMEM,) * 3,
        scratch_shapes=[pltpu.VMEM((slots, slots), jnp.float32)],
        compiler_params=vmem(0, 16, 16),
        cost_estimate=pl.CostEstimate(
            flops=5 * 10**9, bytes_accessed=10 * 1024 * 1024, transcendentals=0
        ),
        name="own_scores",
    )(sent, turned_t, grad_t)


def scores_kernel(
    ctx_size,
    sizes,
    step_units,
    key_head,
    meta_ref,
    turned_ref,
    grad_ref,
    turned_t_ref,
    grad_t_ref,
    sums_ref,
    *refs,
):
    count = 4 if relayed(ctx_size) else ctx_size - 1
    inputs, before = refs[:count], refs[count : -6 - ctx_size]
    refs = refs[-6 - ctx_size :]
    terms, refs = refs[: ctx_size - 1], refs[ctx_size - 1 :]
    score_grad_ref, joined_ref, key_ref, value_ref, bias_ref, prob_ref, acc_ref = refs
    slots = turned_ref.shape[0]
    span = bias_ref.shape[0]
    heads = joined_ref.shape[0]
    starts = [pl.multiple_of(meta_ref[hop], ALIGN) for hop in range(ctx_size)]
    my_start, my_count = starts[0], meta_ref[ctx_size]
    sent_hops = list(range(1, ctx_size))
    if relayed(ctx_size):
        last = lax.axis_index("ctx") == ctx_size - 1
        sent_hops = [jnp.where(last, 3, 1), 2, jnp.where(last, 1, 2)]

    def blocks_of(lanes):
        blocks = [block[:, lanes] for block in inputs]
        if relayed(ctx_size):
            alpha, beta, gamma, delta = blocks
            blocks = [jnp.where(last, alpha, gamma), jnp.where(last, beta, alpha), delta]
        return blocks

    for ref, lanes in ((key_ref, key_lanes(key_head)), (value_ref, value_lanes(key_head))):
        ref[slots:span, :] = jnp.zeros((span - slots, HEAD_DIM), jnp.bfloat16)
        blocks = blocks_of(lanes)
        for hop in range(ctx_size - 1, 0, -1):
            ref[pl.ds(starts[hop], slots), :] = blocks[hop - 1]
    place = lax.broadcasted_iota(jnp.int32, bias_ref.shape, 0)
    seen = place < 0
    for hop in range(1, ctx_size):
        end = starts[hop] + meta_ref[ctx_size + hop]
        seen = seen | ((place >= starts[hop]) & (place < end))
    bias_ref[...] = jnp.where(seen, 0.0, HIDDEN)
    live = lax.broadcasted_iota(jnp.int32, (1, slots), 1) < my_count
    acc_ref[...] = jnp.zeros_like(acc_ref)

    def joint(ref, places, rows, width):
        return jnp.concatenate([ref[rows(place) + (slice(0, width),)] for place in places], axis=1)

    def head_rows(place):
        return (pl.ds(pl.multiple_of((key_head * heads + place) * HEAD_DIM, HEAD_DIM), HEAD_DIM),)

    def units(groups, rows, width):
        side = slots // width
        bias = jnp.concatenate([bias_ref[:rows, :]] * (slots // HEAD_DIM), axis=1)
        alive = jnp.concatenate([live[:, :width]] * side, axis=1)
        queries = [joint(turned_t_ref, group, head_rows, width) for group in groups]
        grads = [joint(grad_t_ref, group, head_rows, width) for group in groups]

        def sums(row):
            index = lambda place: (key_head * heads + place, slice(row, row + 1))
            return [joint(sums_ref, group, index, width) for group in groups]

        own_peaks, own_totals, own_products = sums(0), sums(1), sums(2)
        scores = [dot(key_ref[:rows, :], query, ((1,), (0,))) + bias for query in queries]
        prob_grads = [dot(value_ref[:rows, :], grad, ((1,), (0,))) for grad in grads]
        peaks = [
            jnp.maximum(own, fold(score, jnp.maximum, jnp.max))
            for own, score in zip(own_peaks, scores)
        ]
        weights = [jnp.exp2((score - peak) * EXP2_SCALE) for score, peak in zip(scores, peaks)]
        shares = [jnp.exp2((own - peak) * EXP2_SCALE) for own, peak in zip(own_peaks, peaks)]
        totals = [
            own * share + fold(weight, jnp.add, jnp.sum)
            for own, share, weight in zip(own_totals, shares, weights)
        ]
        products = [
            own * share + fold(weight * prob_grad, jnp.add, jnp.sum)
            for own, share, weight, prob_grad in zip(own_products, shares, weights, prob_grads)
        ]
        inverses = [1.0 / total for total in totals]
        deltas = [product * inverse for product, inverse in zip(products, inverses)]
        inverses = [jnp.where(alive, inverse, 0.0) for inverse in inverses]
        factors = [share * inverse for share, inverse in zip(shares, inverses)]
        probs = [weight * inverse for weight, inverse in zip(weights, inverses)]
        score_grads = [
            (prob * (prob_grad - delta)).astype(jnp.bfloat16)
            for prob, prob_grad, delta in zip(probs, prob_grads, deltas)
        ]
        probs = [prob.astype(jnp.bfloat16) for prob in probs]
        for group, prob, score_grad, factor, delta in zip(
            groups, probs, score_grads, factors, deltas
        ):
            for index, place in enumerate(group):
                part = slice(index * width, (index + 1) * width)
                columns = pl.ds(pl.multiple_of(place * slots, slots), width)
                prob_ref[:rows, columns] = prob[:, part]
                score_grad_ref[:rows, columns] = score_grad[:, part]
                joined_ref[place, 0:1, :width] = factor[:, part]
                joined_ref[place, 1:2, :width] = delta[:, part]
                if width < slots:
                    rest = pl.ds(pl.multiple_of(place * slots + width, HEAD_DIM), slots - width)
                    score_grad_ref[:rows, rest] = jnp.zeros((rows, slots - width), jnp.bfloat16)
                    joined_ref[place, 0:2, width:] = jnp.zeros((2, slots - width), jnp.float32)

    above = {}
    for rows, width in sizes:
        fits = (my_start > above.get(width, 0)) & (my_start <= rows)
        above[width] = rows
        if len(sizes) > 1:
            fits = fits & ((my_count > slots // 2) if width == slots else (my_count <= width))

        @pl.when(fits)
        def _():
            side = slots // width

            def step(index, carry):
                base = index * step_units * side
                units(
                    [[base + part * side + item for item in range(side)] for part in range(step_units)],
                    rows,
                    width,
                )
                return carry

            lax.fori_loop(0, heads // side // step_units, step, 0)
            if rows % CHUNK:
                beyond = slice(rows, rows + CHUNK - rows % CHUNK)
                none = jnp.zeros((CHUNK - rows % CHUNK, heads * slots), jnp.bfloat16)
                score_grad_ref[beyond, :] = none
            lane = key_head * heads * HEAD_DIM
            acc_ref[:rows, :] = terms_of(
                beside(prob_ref, rows, heads, slots, width),
                beside(score_grad_ref, rows, heads, slots, width),
                stacked(turned_ref, lane, heads, width),
                stacked(grad_ref, lane, heads, width),
            )

    @pl.when(my_start == 0)
    def _():
        for place in range(heads):
            inverse = 1.0 / sums_ref[key_head * heads + place, 1:2, :]
            joined_ref[place, 0:1, :] = jnp.where(live, inverse, 0.0)
            joined_ref[place, 1:2, :] = sums_ref[key_head * heads + place, 2:3, :] * inverse

    for hop, term_ref in zip(sent_hops, terms):
        start = pl.multiple_of(meta_ref[hop], ALIGN)
        term = acc_ref[pl.ds(start, slots), :].astype(term_ref.dtype)
        if term_ref.shape == term.shape:
            term_ref[...] = term
        elif term_ref is terms[0]:
            term_ref[:, : 2 * HEAD_DIM] = term
            nearest = acc_ref[pl.ds(starts[1], slots), :].astype(term_ref.dtype)
            term_ref[:, 2 * HEAD_DIM :] = nearest
        else:
            term_ref[:, : -2 * HEAD_DIM] = before[0][...]
            term_ref[:, -2 * HEAD_DIM :] = term


def relayed(ctx_size):
    return ctx_size == 4


def scores(key_head, meta, turned, out_grad, turned_t, grad_t, sums, blocks, after, routed, ctx_size):
    slots, width = blocks[0].shape
    heads = turned.shape[1] // (width // 2)
    span = -(-(routed + ctx_size * ALIGN) // CHUNK) * CHUNK
    sizes, step_units = [(span, slots)], 1
    if span == 2 * CHUNK and routed - slots // 2 + ctx_size * ALIGN <= 3 * CHUNK // 2 + ALIGN:
        sizes = [(CHUNK, slots), (3 * CHUNK // 2, slots), (CHUNK, slots // 2), (span, slots // 2)]
        step_units = 4
    terms = [jax.ShapeDtypeStruct((slots, 2 * HEAD_DIM), jnp.bfloat16)] * (ctx_size - 1)
    if relayed(ctx_size):
        if key_head == 0:
            terms[0] = jax.ShapeDtypeStruct((slots, 4 * HEAD_DIM), jnp.bfloat16)
        terms[1] = jax.ShapeDtypeStruct((slots, 2 * (key_head + 1) * HEAD_DIM), jnp.bfloat16)
        terms[2] = jax.ShapeDtypeStruct((slots, 2 * HEAD_DIM), jnp.float32)
    outs = pl.pallas_call(
        functools.partial(scores_kernel, ctx_size, sizes, step_units, key_head),
        out_shape=(
            *terms,
            jax.ShapeDtypeStruct((span, heads * slots), jnp.bfloat16),
            jax.ShapeDtypeStruct((heads, 8, slots), jnp.float32),
            jax.ShapeDtypeStruct((span + slots, HEAD_DIM), jnp.bfloat16),
        ),
        in_specs=[SMEM] + [VMEM] * (5 + len(blocks) + len(after)),
        out_specs=(VMEM,) * (ctx_size + 2),
        scratch_shapes=[
            pltpu.VMEM((span + slots, HEAD_DIM), jnp.bfloat16),
            pltpu.VMEM((span, HEAD_DIM), jnp.float32),
            pltpu.VMEM((span, heads * slots), jnp.bfloat16),
            pltpu.VMEM((span + slots, 2 * HEAD_DIM), jnp.float32),
        ],
        compiler_params=vmem(routed, 20, 60),
        cost_estimate=pl.CostEstimate(
            flops=4 * 10**9, bytes_accessed=6 * 1024 * 1024, transcendentals=0
        ),
        name="scores",
    )(meta, turned, out_grad, turned_t, grad_t, sums, *blocks, *after)
    return outs[: ctx_size - 1], outs[ctx_size - 1 :]


def local_kernel(
    key_head,
    meta_ref,
    cos_ref,
    sin_ref,
    turned_ref,
    grad_ref,
    sent_ref,
    weight_ref,
    product_ref,
    score_grad_ref,
    joined_ref,
    key_ref,
    *refs,
):
    dq_ref, own_ref, prob_ref, own_grad_ref, sum_ref = refs[-5:]
    slots = turned_ref.shape[0]
    heads = joined_ref.shape[0]
    span = score_grad_ref.shape[0]
    my_start = meta_ref[0]
    own_key_t = sent_ref[:, key_lanes(key_head)].astype(jnp.float32).T.astype(jnp.bfloat16)
    for head in range(heads):
        columns = slice(head * slots, (head + 1) * slots)
        prob = weight_ref[key_head * heads + head] * joined_ref[head, 0:1, :]
        prob_ref[:, columns] = prob.astype(jnp.bfloat16)
        product = product_ref[key_head * heads + head] - joined_ref[head, 1:2, :]
        score_grad = (prob * product).astype(jnp.bfloat16)
        own_grad_ref[:, columns] = score_grad
        sum_ref[head] = dot(own_key_t, score_grad, ((1,), (0,)))
    for chunk in range(0, span, CHUNK):

        @pl.when(chunk < my_start)
        def _():
            rows = slice(chunk, chunk + CHUNK)
            key_t = key_ref[rows, :].astype(jnp.float32).T.astype(jnp.bfloat16)
            for head in range(heads):
                score_grad = score_grad_ref[rows, head * slots : (head + 1) * slots]
                sum_ref[head] += dot(key_t, score_grad, ((1,), (0,)))

    lane = key_head * heads * HEAD_DIM
    for head in range(heads):
        grad = turn_back((sum_ref[head] * SCORE_SCALE).T, cos_ref[...], sin_ref[...])
        dq_ref[:, head * HEAD_DIM : (head + 1) * HEAD_DIM] = grad.astype(jnp.bfloat16)
    own_ref[...] = terms_of(
        prob_ref[...],
        own_grad_ref[...],
        stacked(turned_ref, lane, heads, slots),
        stacked(grad_ref, lane, heads, slots),
    )


def local_terms(meta, cos_full, sin_full, turned, out_grad, sent, own, key_head, joined, dq, after):
    slots = turned.shape[0]
    heads = joined[1].shape[0]
    weight, product, _ = own
    operands = [meta, cos_full, sin_full, turned, out_grad, sent, weight, product, *joined, *after]
    in_specs = [SMEM] + [VMEM] * (len(operands) - 1)
    aliases = {}
    if dq is not None:
        aliases = {len(operands): 0}
        operands.append(dq)
        in_specs.append(pl.BlockSpec(memory_space=pl.ANY))
    return pl.pallas_call(
        functools.partial(local_kernel, key_head),
        grid=(1,),
        out_shape=(
            jax.ShapeDtypeStruct(turned.shape, jnp.bfloat16),
            jax.ShapeDtypeStruct((slots, 2 * HEAD_DIM), jnp.float32),
        ),
        in_specs=in_specs,
        out_specs=(pl.BlockSpec((slots, heads * HEAD_DIM), lambda step: (0, key_head)), VMEM),
        scratch_shapes=[
            pltpu.VMEM((slots, heads * slots), jnp.bfloat16),
            pltpu.VMEM((slots, heads * slots), jnp.bfloat16),
            pltpu.VMEM((heads, HEAD_DIM, slots), jnp.float32),
        ],
        input_output_aliases=aliases,
        compiler_params=vmem(joined[0].shape[0] // 2, 16, 48),
        cost_estimate=pl.CostEstimate(
            flops=4 * 10**9, bytes_accessed=10 * 1024 * 1024, transcendentals=0
        ),
        name="local_terms",
    )(*operands)


def add_kernel(own_ref, arrived_ref, *refs):
    arrived = arrived_ref[:, : own_ref.shape[1]].astype(jnp.float32)
    refs[-1][...] = (own_ref[...] + arrived).astype(jnp.bfloat16)


def add_terms(own, arrived, after):
    return pl.pallas_call(
        add_kernel,
        out_shape=jax.ShapeDtypeStruct(own.shape, jnp.bfloat16),
        in_specs=[VMEM] * (2 + len(after)),
        out_specs=VMEM,
        compiler_params=vmem(0, 16, 16),
        cost_estimate=pl.CostEstimate(flops=10**6, bytes_accessed=10**6, transcendentals=0),
        name="add_terms",
    )(own, arrived, *after)


def finish_kernel(ctx_size, key_heads, meta_ref, cos_ref, sin_ref, *refs):
    key_grad_ref, value_grad_ref = refs[-2:]
    owns, terms = refs[:key_heads], list(refs[key_heads:-2])
    slots = cos_ref.shape[0]
    live = lax.broadcasted_iota(jnp.int32, (slots, HEAD_DIM), 0) < meta_ref[ctx_size]
    totals = [own[...] for own in owns]
    if relayed(ctx_size):
        second = lax.axis_index("ctx") == 2
        for head in range(key_heads):
            first = terms.pop(0)[...].astype(jnp.float32)
            beside = first[:, 2 * HEAD_DIM :] if first.shape[1] > 2 * HEAD_DIM else 0.0
            totals[head] += jnp.where(second, beside, first[:, : 2 * HEAD_DIM])
    while terms:
        parts = [terms.pop(0)]
        if parts[0].shape[1] == 2 * HEAD_DIM:
            parts += [terms.pop(0) for _ in range(key_heads - 1)]
        term = jnp.concatenate([part[...] for part in parts], axis=1).astype(jnp.float32)
        for head in range(key_heads):
            totals[head] += term[:, 2 * head * HEAD_DIM : 2 * (head + 1) * HEAD_DIM]
    for head, total in enumerate(totals):
        lanes = head_lanes(head)
        key_term = turn_back(total[:, :HEAD_DIM], cos_ref[...], sin_ref[...])
        key_grad_ref[:, lanes] = jnp.where(live, key_term, 0.0).astype(jnp.bfloat16)
        value_grad_ref[:, lanes] = jnp.where(live, total[:, HEAD_DIM:], 0.0).astype(jnp.bfloat16)


def finish(meta, cos_full, sin_full, owns, terms, ctx_size):
    slots = cos_full.shape[0]
    key_heads = len(owns)
    grad = jax.ShapeDtypeStruct((slots, key_heads * HEAD_DIM), jnp.bfloat16)
    return pl.pallas_call(
        functools.partial(finish_kernel, ctx_size, key_heads),
        out_shape=(grad, grad),
        in_specs=[SMEM] + [VMEM] * (2 + len(owns) + len(terms)),
        out_specs=(VMEM, VMEM),
        compiler_params=vmem(0, 16, 16),
        name="finish",
    )(meta, cos_full, sin_full, *owns, *terms)


def spread(sent, sent_again, ctx_size):
    if relayed(ctx_size):
        alpha = lax.ppermute(sent, "ctx", [(0, 2), (2, 3)])
        beta = lax.ppermute(sent, "ctx", [(1, 3)])
        gamma = lax.ppermute(sent_again, "ctx", [(0, 1), (1, 2)])
        return [alpha, beta, gamma, lax.ppermute(alpha, "ctx", [(2, 3)])]
    blocks = [sent]
    for hop in range(1, ctx_size):
        pairs = [(shard, shard + 1) for shard in range(hop - 1, ctx_size - 1)]
        blocks.append(lax.ppermute(blocks[-1], "ctx", pairs))
    return blocks[1:]


def descend(terms, ctx_size):
    arrived = []
    for hop, term in enumerate(terms, 1):
        pairs = [(shard + hop, shard) for shard in range(ctx_size - hop)]
        arrived.append(lax.ppermute(term, "ctx", pairs))
    return arrived


def body(positions, queries, keys, values, out_grad):
    ctx_size = lax.axis_size("ctx")
    routed = positions.shape[1]
    key_heads = keys.shape[2] // HEAD_DIM
    meta, cos_full, sin_full, sent = prepare(positions, keys[0], values[0], ctx_size)
    turned, turned_t, grad_t, sent_again = rotate_queries(
        cos_full, sin_full, queries[0], out_grad[0], sent
    )
    blocks = spread(sent, sent_again, ctx_size)
    own = own_scores(sent, turned_t, grad_t)
    terms, joined, owns = [], [], []
    for head in range(key_heads):
        after = [terms[-1][1]] if terms else []
        outs = scores(
            head,
            meta,
            turned,
            out_grad[0],
            turned_t,
            grad_t,
            own[2],
            blocks,
            after,
            routed,
            ctx_size,
        )
        terms.append(outs[0])
        joined.append(outs[1])
    local = functools.partial(
        local_terms, meta, cos_full, sin_full, turned, out_grad[0], sent, own
    )
    dq = None
    if relayed(ctx_size):
        down = [(3, 2), (2, 1), (1, 0)]
        firsts = [lax.ppermute(first, "ctx", down) for first, _, _ in terms]
        relays = []
        for head in range(key_heads):
            total = add_terms(terms[head][2], firsts[head], owns[-1:])
            relays.append(lax.ppermute(total, "ctx", [(3, 2), (2, 0)] if relays else [(2, 0)]))
            dq, own_terms = local(head, joined[head], dq, [total])
            owns.append(own_terms)
        arrived = firsts + relays + [lax.ppermute(terms[-1][1], "ctx", [(3, 1)])]
    else:
        arrived = [part for hop in zip(*[descend(term, ctx_size) for term in terms]) for part in hop]
        for head in range(key_heads):
            dq, own_terms = local(head, joined[head], dq, [])
            owns.append(own_terms)
    key_grad, value_grad = finish(meta, cos_full, sin_full, owns, arrived, ctx_size)
    return (dq[None], key_grad[None], value_grad[None])


def solution(mesh):
    split = P(("groups", "dp"), "ctx", "mp")
    return jax.shard_map(
        body,
        mesh=mesh,
        in_specs=(P(("groups", "dp"), None), split, split, split, split),
        out_specs=(split, split, split),
        check_vma=False,
    )
```

```python
import functools
import math

import jax
import jax.numpy as jnp
import numpy as np
from jax import lax
from jax.experimental import pallas as pl
from jax.experimental.pallas import tpu as pltpu
from jax.sharding import PartitionSpec as P

HEAD_DIM = 128
HALF_DIM = HEAD_DIM // 2
TOK_SHARD = 1024
ROPE_BASE = 500000.0
SCORE_SCALE = 1.0 / math.sqrt(HEAD_DIM)
EXP2_SCALE = SCORE_SCALE * math.log2(math.e)
HIDDEN = -1e30
ALIGN = 16
CHUNK = 288
MIB = 1024 * 1024

VMEM = pl.BlockSpec(memory_space=pltpu.VMEM)
SMEM = pl.BlockSpec(memory_space=pltpu.SMEM)
HBM = pl.BlockSpec(memory_space=pltpu.HBM)


def vmem(routed, small, large):
    return pltpu.CompilerParams(vmem_limit_bytes=(small if routed <= 512 else large) * MIB)


def dot(left, right, contract):
    return lax.dot_general(left, right, (contract, ((), ())), preferred_element_type=jnp.float32)


def turn(field, cos_full, sin_full):
    return field * cos_full + pltpu.roll(field, HALF_DIM, 1) * sin_full


def turn_back(field, cos_full, sin_full):
    return field * cos_full - pltpu.roll(field, HALF_DIM, 1) * sin_full


def frequencies():
    ladder = np.arange(HALF_DIM, dtype=np.float32)
    exponent = ladder * np.float32(-2.0 * math.log(ROPE_BASE) / HEAD_DIM)
    freq = np.exp(exponent.astype(np.float64)).astype(np.float32)
    entry = lax.broadcasted_iota(jnp.int32, (1, HEAD_DIM), 1) % HALF_DIM
    row = jnp.zeros((1, HEAD_DIM), jnp.float32)
    for index in range(HALF_DIM):
        row = jnp.where(entry == index, float(freq[index]), row)
    return row


def shard_layout(ctx_size, me, pos, meta_ref):
    shard_of = pos // TOK_SHARD
    for hop in range(2 * ctx_size):
        meta_ref[hop] = 0
    start = jnp.int32(0)
    first = jnp.int32(0)
    my_first = jnp.int32(0)
    for shard in range(ctx_size):
        count = jnp.sum(jnp.where(shard_of == shard, 1.0, 0.0)).astype(jnp.int32)
        my_first = jnp.where(me == shard, first, my_first)

        @pl.when(me >= shard)
        def _():
            meta_ref[me - shard] = start
            meta_ref[ctx_size + me - shard] = count

        first = first + count
        start = start + (count + ALIGN - 1) // ALIGN * ALIGN
    return my_first


def prepare_kernel(
    ctx_size, pos_hbm, keys_hbm, values_hbm, meta_ref, cos_ref, sin_ref, sent_ref, *refs
):
    sent_heads, (pos_ref, keys_ref, values_ref, sems) = refs[:-4], refs[-4:]
    sources = (pos_hbm, keys_hbm, values_hbm)
    targets = (pos_ref, keys_ref, values_ref)
    copies = [
        pltpu.make_async_copy(source, target, sems.at[index])
        for index, (source, target) in enumerate(zip(sources, targets))
    ]
    for copy in copies:
        copy.start()
    copies[0].wait()
    slots = keys_ref.shape[0]
    pos = pos_ref[...]
    my_first = shard_layout(ctx_size, lax.axis_index("ctx"), pos, meta_ref)
    shape = (slots, pos.shape[1])
    gap = lax.broadcasted_iota(jnp.int32, shape, 1) - lax.broadcasted_iota(jnp.int32, shape, 0)
    named = jnp.where(gap == my_first, pos.astype(jnp.float32), 0.0)
    angles = jnp.sum(named, axis=1, keepdims=True) * frequencies()
    cos_full = jnp.cos(angles)
    front = lax.broadcasted_iota(jnp.int32, angles.shape, 1) < HALF_DIM
    sin_full = jnp.where(front, -jnp.sin(angles), jnp.sin(angles))
    cos_ref[...] = cos_full
    sin_ref[...] = sin_full
    copies[1].wait()
    copies[2].wait()
    for lane in range(0, keys_ref.shape[1], HEAD_DIM):
        lanes = slice(lane, lane + HEAD_DIM)
        key = turn(keys_ref[:, lanes].astype(jnp.float32), cos_full, sin_full)
        both = jnp.concatenate([key.astype(jnp.bfloat16), values_ref[:, lanes]], axis=1)
        sent_ref[:, 2 * lane : 2 * (lane + HEAD_DIM)] = both
        sent_heads[lane // HEAD_DIM][...] = both


def prepare(positions, keys, values, ctx_size):
    slots, width = keys.shape
    table = jax.ShapeDtypeStruct((slots, HEAD_DIM), jnp.float32)
    sent = jax.ShapeDtypeStruct((slots, 2 * width), jnp.bfloat16)
    operands = (positions, keys, values)
    return pl.pallas_call(
        functools.partial(prepare_kernel, ctx_size),
        out_shape=(
            jax.ShapeDtypeStruct((2 * ctx_size,), jnp.int32),
            table,
            table,
            sent,
            *[jax.ShapeDtypeStruct((slots, 2 * HEAD_DIM), jnp.bfloat16)] * (width // HEAD_DIM),
        ),
        in_specs=[HBM] * 3,
        out_specs=(SMEM,) + (VMEM,) * (3 + width // HEAD_DIM),
        scratch_shapes=[pltpu.VMEM(operand.shape, operand.dtype) for operand in operands]
        + [pltpu.SemaphoreType.DMA((3,))],
        compiler_params=vmem(positions.shape[1], 60, 60),
        name="prepare",
    )(*operands)


def queries_kernel(
    cos_ref,
    sin_ref,
    query_ref,
    grad_ref,
    sent_ref,
    turned_ref,
    turned_t_ref,
    grad_t_ref,
    sent_again_ref,
):
    sent_again_ref[...] = sent_ref[...]
    for lane in range(0, query_ref.shape[1], HEAD_DIM):
        lanes = slice(lane, lane + HEAD_DIM)
        query = turn(query_ref[:, lanes].astype(jnp.float32), cos_ref[...], sin_ref[...])
        turned_ref[:, lanes] = query.astype(jnp.bfloat16)
        turned_t_ref[lanes, :] = query.T.astype(jnp.bfloat16)
        grad_t_ref[lanes, :] = grad_ref[:, lanes].astype(jnp.float32).T.astype(jnp.bfloat16)


def rotate_queries(cos_full, sin_full, queries, out_grad, sent):
    slots, width = queries.shape
    straight = jax.ShapeDtypeStruct((slots, width), jnp.bfloat16)
    across = jax.ShapeDtypeStruct((width, slots), jnp.bfloat16)
    return pl.pallas_call(
        queries_kernel,
        out_shape=(straight, across, across, jax.ShapeDtypeStruct(sent.shape, sent.dtype)),
        in_specs=[VMEM] * 5,
        out_specs=(VMEM,) * 4,
        compiler_params=vmem(0, 16, 16),
        cost_estimate=pl.CostEstimate(
            flops=3 * 10**9, bytes_accessed=4 * 1024 * 1024, transcendentals=0
        ),
        name="rotate_queries",
    )(cos_full, sin_full, queries, out_grad, sent)


def stacked(ref, lane, heads, width):
    parts = [ref[:width, lane + h * HEAD_DIM : lane + (h + 1) * HEAD_DIM] for h in range(heads)]
    return jnp.concatenate(parts, axis=0)


def beside(ref, rows, heads, slots, width):
    if width == slots:
        return ref[:rows, :]
    columns = [head * slots for head in range(heads)]
    return jnp.concatenate([ref[:rows, start : start + width] for start in columns], axis=1)


def terms_of(probs, score_grads, queries, grads):
    key_term = dot(score_grads, queries, ((1,), (0,))) * SCORE_SCALE
    return jnp.concatenate([key_term, dot(probs, grads, ((1,), (0,)))], axis=1)


def fold(field, join, reduce):
    while field.shape[0] % 16 == 0:
        half = field.shape[0] // 2
        field = join(field[:half], field[half:])
    return reduce(field, axis=0, keepdims=True)


def head_lanes(head):
    return slice(head * HEAD_DIM, (head + 1) * HEAD_DIM)


def key_lanes(key_head):
    return slice(2 * key_head * HEAD_DIM, (2 * key_head + 1) * HEAD_DIM)


def value_lanes(key_head):
    return slice((2 * key_head + 1) * HEAD_DIM, 2 * (key_head + 1) * HEAD_DIM)


def own_kernel(step_heads, count, sent_ref, turned_t_ref, grad_t_ref, *refs):
    weight_ref, product_ref, sums_ref = refs[count : count + 3]
    bias_ref = refs[-1]
    for source, target in zip(refs[:count], refs[count + 3 : -1]):
        target[...] = source[...]
    slots = sent_ref.shape[0]
    key_heads = sent_ref.shape[1] // HEAD_DIM // 2
    heads = turned_t_ref.shape[0] // HEAD_DIM // key_heads
    key_id = lax.broadcasted_iota(jnp.int32, (slots, slots), 0)
    slot_id = lax.broadcasted_iota(jnp.int32, (slots, slots), 1)
    bias_ref[...] = jnp.where(key_id <= slot_id, 0.0, HIDDEN)
    for key_head in range(key_heads):

        def step(index, carry):
            for part in range(step_heads):
                head = key_head * heads + index * step_heads + part
                rows = pl.ds(pl.multiple_of(head * HEAD_DIM, HEAD_DIM), HEAD_DIM)
                scores = dot(sent_ref[:, key_lanes(key_head)], turned_t_ref[rows, :], ((1,), (0,)))
                scores = scores + bias_ref[...]
                prob_grad = dot(sent_ref[:, value_lanes(key_head)], grad_t_ref[rows, :], ((1,), (0,)))
                peak = fold(scores, jnp.maximum, jnp.max)
                weights = jnp.exp2((scores - peak) * EXP2_SCALE)
                weight_ref[head] = weights
                product_ref[head] = prob_grad
                sums_ref[head, 0:1, :] = peak
                sums_ref[head, 1:2, :] = fold(weights, jnp.add, jnp.sum)
                sums_ref[head, 2:3, :] = fold(weights * prob_grad, jnp.add, jnp.sum)
            return carry

        lax.fori_loop(0, heads // step_heads, step, 0)


def own_scores(sent, turned_t, grad_t, handed):
    slots = sent.shape[0]
    heads = turned_t.shape[0] // HEAD_DIM
    square = jax.ShapeDtypeStruct((heads, slots, slots), jnp.float32)
    outs = pl.pallas_call(
        functools.partial(own_kernel, 4, len(handed)),
        out_shape=(
            square,
            square,
            jax.ShapeDtypeStruct((heads, 8, slots), jnp.float32),
            *[jax.ShapeDtypeStruct(array.shape, array.dtype) for array in handed],
        ),
        in_specs=[VMEM] * (3 + len(handed)),
        out_specs=(VMEM,) * (3 + len(handed)),
        scratch_shapes=[pltpu.VMEM((slots, slots), jnp.float32)],
        compiler_params=vmem(0, 16, 16),
        cost_estimate=pl.CostEstimate(
            flops=5 * 10**9, bytes_accessed=10 * 1024 * 1024, transcendentals=0
        ),
        name="own_scores",
    )(sent, turned_t, grad_t, *handed)
    return outs[:3], outs[3:]


def scores_kernel(
    ctx_size,
    sizes,
    step_units,
    key_head,
    meta_ref,
    turned_ref,
    grad_ref,
    turned_t_ref,
    grad_t_ref,
    sums_ref,
    *refs,
):
    count = 4 if relayed(ctx_size) else ctx_size - 1
    inputs, before = refs[:count], refs[count : -6 - ctx_size]
    refs = refs[-6 - ctx_size :]
    terms, refs = refs[: ctx_size - 1], refs[ctx_size - 1 :]
    score_grad_ref, joined_ref, key_ref, value_ref, bias_ref, prob_ref, acc_ref = refs
    slots = turned_ref.shape[0]
    span = bias_ref.shape[0]
    heads = joined_ref.shape[0]
    starts = [pl.multiple_of(meta_ref[hop], ALIGN) for hop in range(ctx_size)]
    my_start, my_count = starts[0], meta_ref[ctx_size]
    sent_hops = list(range(1, ctx_size))
    if relayed(ctx_size):
        last = lax.axis_index("ctx") == ctx_size - 1
        sent_hops = [jnp.where(last, 3, 1), 2, jnp.where(last, 1, 2)]

    def blocks_of(lanes, lanes_alone):
        alone = [block.shape[1] == 2 * HEAD_DIM for block in inputs]
        blocks = [block[:, lanes_alone if one else lanes] for block, one in zip(inputs, alone)]
        if relayed(ctx_size):
            alpha, beta, gamma, delta = blocks
            blocks = [jnp.where(last, alpha, gamma), jnp.where(last, beta, alpha), delta]
        return blocks

    for ref, lanes in ((key_ref, key_lanes), (value_ref, value_lanes)):
        ref[slots:span, :] = jnp.zeros((span - slots, HEAD_DIM), jnp.bfloat16)
        blocks = blocks_of(lanes(key_head), lanes(0))
        for hop in range(ctx_size - 1, 0, -1):
            ref[pl.ds(starts[hop], slots), :] = blocks[hop - 1]
    place = lax.broadcasted_iota(jnp.int32, bias_ref.shape, 0)
    seen = place < 0
    for hop in range(1, ctx_size):
        end = starts[hop] + meta_ref[ctx_size + hop]
        seen = seen | ((place >= starts[hop]) & (place < end))
    bias_ref[...] = jnp.where(seen, 0.0, HIDDEN)
    live = lax.broadcasted_iota(jnp.int32, (1, slots), 1) < my_count
    acc_ref[...] = jnp.zeros_like(acc_ref)

    def joint(ref, places, rows, width):
        return jnp.concatenate([ref[rows(place) + (slice(0, width),)] for place in places], axis=1)

    def head_rows(place):
        return (pl.ds(pl.multiple_of((key_head * heads + place) * HEAD_DIM, HEAD_DIM), HEAD_DIM),)

    def units(groups, rows, width):
        side = slots // width
        bias = jnp.concatenate([bias_ref[:rows, :]] * (slots // HEAD_DIM), axis=1)
        alive = jnp.concatenate([live[:, :width]] * side, axis=1)
        queries = [joint(turned_t_ref, group, head_rows, width) for group in groups]
        grads = [joint(grad_t_ref, group, head_rows, width) for group in groups]

        def sums(row):
            index = lambda place: (key_head * heads + place, slice(row, row + 1))
            return [joint(sums_ref, group, index, width) for group in groups]

        own_peaks, own_totals, own_products = sums(0), sums(1), sums(2)
        scores = [dot(key_ref[:rows, :], query, ((1,), (0,))) + bias for query in queries]
        prob_grads = [dot(value_ref[:rows, :], grad, ((1,), (0,))) for grad in grads]
        peaks = [
            jnp.maximum(own, fold(score, jnp.maximum, jnp.max))
            for own, score in zip(own_peaks, scores)
        ]
        weights = [jnp.exp2((score - peak) * EXP2_SCALE) for score, peak in zip(scores, peaks)]
        shares = [jnp.exp2((own - peak) * EXP2_SCALE) for own, peak in zip(own_peaks, peaks)]
        totals = [
            own * share + fold(weight, jnp.add, jnp.sum)
            for own, share, weight in zip(own_totals, shares, weights)
        ]
        products = [
            own * share + fold(weight * prob_grad, jnp.add, jnp.sum)
            for own, share, weight, prob_grad in zip(own_products, shares, weights, prob_grads)
        ]
        inverses = [1.0 / total for total in totals]
        deltas = [product * inverse for product, inverse in zip(products, inverses)]
        inverses = [jnp.where(alive, inverse, 0.0) for inverse in inverses]
        factors = [share * inverse for share, inverse in zip(shares, inverses)]
        probs = [weight * inverse for weight, inverse in zip(weights, inverses)]
        score_grads = [
            (prob * (prob_grad - delta)).astype(jnp.bfloat16)
            for prob, prob_grad, delta in zip(probs, prob_grads, deltas)
        ]
        probs = [prob.astype(jnp.bfloat16) for prob in probs]
        for group, prob, score_grad, factor, delta in zip(
            groups, probs, score_grads, factors, deltas
        ):
            for index, place in enumerate(group):
                part = slice(index * width, (index + 1) * width)
                columns = pl.ds(pl.multiple_of(place * slots, slots), width)
                prob_ref[:rows, columns] = prob[:, part]
                score_grad_ref[:rows, columns] = score_grad[:, part]
                joined_ref[place, 0:1, :width] = factor[:, part]
                joined_ref[place, 1:2, :width] = delta[:, part]
                if width < slots:
                    rest = pl.ds(pl.multiple_of(place * slots + width, HEAD_DIM), slots - width)
                    score_grad_ref[:rows, rest] = jnp.zeros((rows, slots - width), jnp.bfloat16)
                    joined_ref[place, 0:2, width:] = jnp.zeros((2, slots - width), jnp.float32)

    above = {}
    for rows, width in sizes:
        fits = (my_start > above.get(width, 0)) & (my_start <= rows)
        above[width] = rows
        if len(sizes) > 1:
            fits = fits & ((my_count > slots // 2) if width == slots else (my_count <= width))

        @pl.when(fits)
        def _():
            side = slots // width

            def step(index, carry):
                base = index * step_units * side
                units(
                    [[base + part * side + item for item in range(side)] for part in range(step_units)],
                    rows,
                    width,
                )
                return carry

            lax.fori_loop(0, heads // side // step_units, step, 0)
            if rows % CHUNK:
                beyond = slice(rows, rows + CHUNK - rows % CHUNK)
                none = jnp.zeros((CHUNK - rows % CHUNK, heads * slots), jnp.bfloat16)
                score_grad_ref[beyond, :] = none
            lane = key_head * heads * HEAD_DIM
            acc_ref[:rows, :] = terms_of(
                beside(prob_ref, rows, heads, slots, width),
                beside(score_grad_ref, rows, heads, slots, width),
                stacked(turned_ref, lane, heads, width),
                stacked(grad_ref, lane, heads, width),
            )

    @pl.when(my_start == 0)
    def _():
        for place in range(heads):
            inverse = 1.0 / sums_ref[key_head * heads + place, 1:2, :]
            joined_ref[place, 0:1, :] = jnp.where(live, inverse, 0.0)
            joined_ref[place, 1:2, :] = sums_ref[key_head * heads + place, 2:3, :] * inverse

    for hop, term_ref in zip(sent_hops, terms):
        start = pl.multiple_of(meta_ref[hop], ALIGN)
        term = acc_ref[pl.ds(start, slots), :].astype(term_ref.dtype)
        if term_ref.shape == term.shape:
            term_ref[...] = term
        elif term_ref is terms[0]:
            term_ref[:, : 2 * HEAD_DIM] = term
            nearest = acc_ref[pl.ds(starts[1], slots), :].astype(term_ref.dtype)
            term_ref[:, 2 * HEAD_DIM :] = nearest
        else:
            term_ref[:, : -2 * HEAD_DIM] = before[0][...]
            term_ref[:, -2 * HEAD_DIM :] = term


def relayed(ctx_size):
    return ctx_size == 4


def scores(key_head, heads, meta, turned, out_grad, turned_t, grad_t, sums, blocks, after, routed, ctx_size):
    slots = turned.shape[0]
    span = -(-(routed + ctx_size * ALIGN) // CHUNK) * CHUNK
    sizes, step_units = [(span, slots)], 1
    if span == 2 * CHUNK and routed - slots // 2 + ctx_size * ALIGN <= 3 * CHUNK // 2 + ALIGN:
        sizes = [(CHUNK, slots), (3 * CHUNK // 2, slots), (CHUNK, slots // 2), (span, slots // 2)]
        step_units = 4
    terms = [jax.ShapeDtypeStruct((slots, 2 * HEAD_DIM), jnp.bfloat16)] * (ctx_size - 1)
    if relayed(ctx_size):
        if key_head == 0:
            terms[0] = jax.ShapeDtypeStruct((slots, 4 * HEAD_DIM), jnp.bfloat16)
        terms[1] = jax.ShapeDtypeStruct((slots, 2 * (key_head + 1) * HEAD_DIM), jnp.bfloat16)
        terms[2] = jax.ShapeDtypeStruct((slots, 2 * HEAD_DIM), jnp.float32)
    outs = pl.pallas_call(
        functools.partial(scores_kernel, ctx_size, sizes, step_units, key_head),
        out_shape=(
            *terms,
            jax.ShapeDtypeStruct((span, heads * slots), jnp.bfloat16),
            jax.ShapeDtypeStruct((heads, 8, slots), jnp.float32),
            jax.ShapeDtypeStruct((span + slots, HEAD_DIM), jnp.bfloat16),
        ),
        in_specs=[SMEM] + [VMEM] * (5 + len(blocks) + len(after)),
        out_specs=(VMEM,) * (ctx_size + 2),
        scratch_shapes=[
            pltpu.VMEM((span + slots, HEAD_DIM), jnp.bfloat16),
            pltpu.VMEM((span, HEAD_DIM), jnp.float32),
            pltpu.VMEM((span, heads * slots), jnp.bfloat16),
            pltpu.VMEM((span + slots, 2 * HEAD_DIM), jnp.float32),
        ],
        compiler_params=vmem(routed, 20, 60),
        cost_estimate=pl.CostEstimate(
            flops=4 * 10**9, bytes_accessed=6 * 1024 * 1024, transcendentals=0
        ),
        name="scores",
    )(meta, turned, out_grad, turned_t, grad_t, sums, *blocks, *after)
    return outs[: ctx_size - 1], outs[ctx_size - 1 :]


def local_kernel(
    key_head,
    meta_ref,
    cos_ref,
    sin_ref,
    turned_ref,
    grad_ref,
    sent_ref,
    weight_ref,
    product_ref,
    score_grad_ref,
    joined_ref,
    key_ref,
    *refs,
):
    dq_ref, own_ref, prob_ref, own_grad_ref, sum_ref = refs[-5:]
    slots = turned_ref.shape[0]
    heads = joined_ref.shape[0]
    span = score_grad_ref.shape[0]
    my_start = meta_ref[0]
    own_key_t = sent_ref[:, key_lanes(key_head)].astype(jnp.float32).T.astype(jnp.bfloat16)
    for head in range(heads):
        columns = slice(head * slots, (head + 1) * slots)
        prob = weight_ref[key_head * heads + head] * joined_ref[head, 0:1, :]
        prob_ref[:, columns] = prob.astype(jnp.bfloat16)
        product = product_ref[key_head * heads + head] - joined_ref[head, 1:2, :]
        score_grad = (prob * product).astype(jnp.bfloat16)
        own_grad_ref[:, columns] = score_grad
        sum_ref[head] = dot(own_key_t, score_grad, ((1,), (0,)))
    for chunk in range(0, span, CHUNK):

        @pl.when(chunk < my_start)
        def _():
            rows = slice(chunk, chunk + CHUNK)
            key_t = key_ref[rows, :].astype(jnp.float32).T.astype(jnp.bfloat16)
            for head in range(heads):
                score_grad = score_grad_ref[rows, head * slots : (head + 1) * slots]
                sum_ref[head] += dot(key_t, score_grad, ((1,), (0,)))

    lane = key_head * heads * HEAD_DIM
    for head in range(heads):
        grad = turn_back((sum_ref[head] * SCORE_SCALE).T, cos_ref[...], sin_ref[...])
        dq_ref[:, head * HEAD_DIM : (head + 1) * HEAD_DIM] = grad.astype(jnp.bfloat16)
    own_ref[...] = terms_of(
        prob_ref[...],
        own_grad_ref[...],
        stacked(turned_ref, lane, heads, slots),
        stacked(grad_ref, lane, heads, slots),
    )


def local_terms(meta, cos_full, sin_full, turned, out_grad, sent, own, key_head, joined, dq, after):
    slots = turned.shape[0]
    heads = joined[1].shape[0]
    weight, product, _ = own
    operands = [meta, cos_full, sin_full, turned, out_grad, sent, weight, product, *joined, *after]
    in_specs = [SMEM] + [VMEM] * (len(operands) - 1)
    aliases = {}
    if dq is not None:
        aliases = {len(operands): 0}
        operands.append(dq)
        in_specs.append(pl.BlockSpec(memory_space=pl.ANY))
    return pl.pallas_call(
        functools.partial(local_kernel, key_head),
        grid=(1,),
        out_shape=(
            jax.ShapeDtypeStruct(turned.shape, jnp.bfloat16),
            jax.ShapeDtypeStruct((slots, 2 * HEAD_DIM), jnp.float32),
        ),
        in_specs=in_specs,
        out_specs=(pl.BlockSpec((slots, heads * HEAD_DIM), lambda step: (0, key_head)), VMEM),
        scratch_shapes=[
            pltpu.VMEM((slots, heads * slots), jnp.bfloat16),
            pltpu.VMEM((slots, heads * slots), jnp.bfloat16),
            pltpu.VMEM((heads, HEAD_DIM, slots), jnp.float32),
        ],
        input_output_aliases=aliases,
        compiler_params=vmem(joined[0].shape[0] // 2, 16, 48),
        cost_estimate=pl.CostEstimate(
            flops=4 * 10**9, bytes_accessed=10 * 1024 * 1024, transcendentals=0
        ),
        name="local_terms",
    )(*operands)


def add_kernel(own_ref, arrived_ref, *refs):
    arrived = arrived_ref[:, : own_ref.shape[1]].astype(jnp.float32)
    refs[-1][...] = (own_ref[...] + arrived).astype(jnp.bfloat16)


def add_terms(own, arrived, after):
    return pl.pallas_call(
        add_kernel,
        out_shape=jax.ShapeDtypeStruct(own.shape, jnp.bfloat16),
        in_specs=[VMEM] * (2 + len(after)),
        out_specs=VMEM,
        compiler_params=vmem(0, 16, 16),
        cost_estimate=pl.CostEstimate(flops=10**6, bytes_accessed=10**6, transcendentals=0),
        name="add_terms",
    )(own, arrived, *after)


def finish_kernel(ctx_size, key_heads, meta_ref, cos_ref, sin_ref, *refs):
    key_grad_ref, value_grad_ref = refs[-2:]
    owns, terms = refs[:key_heads], list(refs[key_heads:-2])
    slots = cos_ref.shape[0]
    live = lax.broadcasted_iota(jnp.int32, (slots, HEAD_DIM), 0) < meta_ref[ctx_size]
    totals = [own[...] for own in owns]
    if relayed(ctx_size):
        second = lax.axis_index("ctx") == 2
        for head in range(key_heads):
            first = terms.pop(0)[...].astype(jnp.float32)
            beside = first[:, 2 * HEAD_DIM :] if first.shape[1] > 2 * HEAD_DIM else 0.0
            totals[head] += jnp.where(second, beside, first[:, : 2 * HEAD_DIM])
    while terms:
        parts = [terms.pop(0)]
        if parts[0].shape[1] == 2 * HEAD_DIM:
            parts += [terms.pop(0) for _ in range(key_heads - 1)]
        term = jnp.concatenate([part[...] for part in parts], axis=1).astype(jnp.float32)
        for head in range(key_heads):
            totals[head] += term[:, 2 * head * HEAD_DIM : 2 * (head + 1) * HEAD_DIM]
    for head, total in enumerate(totals):
        lanes = head_lanes(head)
        key_term = turn_back(total[:, :HEAD_DIM], cos_ref[...], sin_ref[...])
        key_grad_ref[:, lanes] = jnp.where(live, key_term, 0.0).astype(jnp.bfloat16)
        value_grad_ref[:, lanes] = jnp.where(live, total[:, HEAD_DIM:], 0.0).astype(jnp.bfloat16)


def finish(meta, cos_full, sin_full, owns, terms, ctx_size):
    slots = cos_full.shape[0]
    key_heads = len(owns)
    grad = jax.ShapeDtypeStruct((slots, key_heads * HEAD_DIM), jnp.bfloat16)
    return pl.pallas_call(
        functools.partial(finish_kernel, ctx_size, key_heads),
        out_shape=(grad, grad),
        in_specs=[SMEM] + [VMEM] * (2 + len(owns) + len(terms)),
        out_specs=(VMEM, VMEM),
        compiler_params=vmem(0, 16, 16),
        name="finish",
    )(meta, cos_full, sin_full, *owns, *terms)


def climb(sent, ctx_size):
    blocks = [sent]
    for hop in range(1, ctx_size):
        pairs = [(shard, shard + 1) for shard in range(hop - 1, ctx_size - 1)]
        blocks.append(lax.ppermute(blocks[-1], "ctx", pairs))
    return blocks[1:]


def descend(terms, ctx_size):
    arrived = []
    for hop, term in enumerate(terms, 1):
        pairs = [(shard + hop, shard) for shard in range(ctx_size - hop)]
        arrived.append(lax.ppermute(term, "ctx", pairs))
    return arrived


def body(positions, queries, keys, values, out_grad):
    ctx_size = lax.axis_size("ctx")
    routed = positions.shape[1]
    key_heads = keys.shape[2] // HEAD_DIM
    meta, cos_full, sin_full, sent, *sent_heads = prepare(positions, keys[0], values[0], ctx_size)
    turned, turned_t, grad_t, sent_again = rotate_queries(
        cos_full, sin_full, queries[0], out_grad[0], sent_heads[0]
    )
    if relayed(ctx_size):
        alphas = [lax.ppermute(part, "ctx", [(0, 2), (2, 3)]) for part in sent_heads]
        beta = lax.ppermute(sent, "ctx", [(1, 3)])
        own, handed = own_scores(sent, turned_t, grad_t, sent_heads[1:] + alphas[1:])
        blocks = []
        for head, alpha in enumerate(alphas):
            near, far = sent_again, alpha
            if head > 0:
                near, far = handed[head - 1], handed[head + key_heads - 2]
            gamma = lax.ppermute(near, "ctx", [(0, 1), (1, 2)])
            blocks.append([alpha, beta, gamma, lax.ppermute(far, "ctx", [(2, 3)])])
    else:
        blocks = [climb(sent, ctx_size)] * key_heads
        own, _ = own_scores(sent, turned_t, grad_t, [])
    terms, joined, owns = [], [], []
    for head in range(key_heads):
        after = [terms[-1][1]] if terms else []
        outs = scores(
            head,
            queries.shape[2] // HEAD_DIM // key_heads,
            meta,
            turned,
            out_grad[0],
            turned_t,
            grad_t,
            own[2],
            blocks[head],
            after,
            routed,
            ctx_size,
        )
        terms.append(outs[0])
        joined.append(outs[1])
    local = functools.partial(
        local_terms, meta, cos_full, sin_full, turned, out_grad[0], sent, own
    )
    dq = None
    if relayed(ctx_size):
        down = [(3, 2), (2, 1), (1, 0)]
        firsts = [lax.ppermute(first, "ctx", down) for first, _, _ in terms]
        relays = []
        for head in range(key_heads):
            total = add_terms(terms[head][2], firsts[head], owns[-1:])
            relays.append(lax.ppermute(total, "ctx", [(3, 2), (2, 0)] if relays else [(2, 0)]))
            dq, own_terms = local(head, joined[head], dq, [total])
            owns.append(own_terms)
        arrived = firsts + relays + [lax.ppermute(terms[-1][1], "ctx", [(3, 1)])]
    else:
        arrived = [part for hop in zip(*[descend(term, ctx_size) for term in terms]) for part in hop]
        for head in range(key_heads):
            dq, own_terms = local(head, joined[head], dq, [])
            owns.append(own_terms)
    key_grad, value_grad = finish(meta, cos_full, sin_full, owns, arrived, ctx_size)
    return (dq[None], key_grad[None], value_grad[None])


def solution(mesh):
    split = P(("groups", "dp"), "ctx", "mp")
    return jax.shard_map(
        body,
        mesh=mesh,
        in_specs=(P(("groups", "dp"), None), split, split, split, split),
        out_specs=(split, split, split),
        check_vma=False,
    )
```

```python
import functools
import math

import jax
import jax.numpy as jnp
import numpy as np
from jax import lax
from jax.experimental import pallas as pl
from jax.experimental.pallas import tpu as pltpu
from jax.sharding import PartitionSpec as P

HEAD_DIM = 128
HALF_DIM = HEAD_DIM // 2
TOK_SHARD = 1024
ROPE_BASE = 500000.0
SCORE_SCALE = 1.0 / math.sqrt(HEAD_DIM)
EXP2_SCALE = SCORE_SCALE * math.log2(math.e)
HIDDEN = -1e30
ALIGN = 16
CHUNK = 288
MIB = 1024 * 1024

VMEM = pl.BlockSpec(memory_space=pltpu.VMEM)
SMEM = pl.BlockSpec(memory_space=pltpu.SMEM)
HBM = pl.BlockSpec(memory_space=pltpu.HBM)


def vmem(routed, small, large):
    return pltpu.CompilerParams(vmem_limit_bytes=(small if routed <= 512 else large) * MIB)


def dot(left, right, contract):
    return lax.dot_general(left, right, (contract, ((), ())), preferred_element_type=jnp.float32)


def turn(field, cos_full, sin_full):
    return field * cos_full + pltpu.roll(field, HALF_DIM, 1) * sin_full


def turn_back(field, cos_full, sin_full):
    return field * cos_full - pltpu.roll(field, HALF_DIM, 1) * sin_full


def frequencies():
    ladder = np.arange(HALF_DIM, dtype=np.float32)
    exponent = ladder * np.float32(-2.0 * math.log(ROPE_BASE) / HEAD_DIM)
    freq = np.exp(exponent.astype(np.float64)).astype(np.float32)
    entry = lax.broadcasted_iota(jnp.int32, (1, HEAD_DIM), 1) % HALF_DIM
    row = jnp.zeros((1, HEAD_DIM), jnp.float32)
    for index in range(HALF_DIM):
        row = jnp.where(entry == index, float(freq[index]), row)
    return row


def shard_layout(ctx_size, me, pos, meta_ref):
    shard_of = pos // TOK_SHARD
    for hop in range(2 * ctx_size):
        meta_ref[hop] = 0
    start = jnp.int32(0)
    first = jnp.int32(0)
    my_first = jnp.int32(0)
    for shard in range(ctx_size):
        count = jnp.sum(jnp.where(shard_of == shard, 1.0, 0.0)).astype(jnp.int32)
        my_first = jnp.where(me == shard, first, my_first)

        @pl.when(me >= shard)
        def _():
            meta_ref[me - shard] = start
            meta_ref[ctx_size + me - shard] = count

        first = first + count
        start = start + (count + ALIGN - 1) // ALIGN * ALIGN
    return my_first


def prepare_kernel(
    ctx_size, pos_hbm, keys_hbm, values_hbm, meta_ref, cos_ref, sin_ref, sent_ref, *refs
):
    sent_heads, (pos_ref, keys_ref, values_ref, sems) = refs[:-4], refs[-4:]
    sources = (pos_hbm, keys_hbm, values_hbm)
    targets = (pos_ref, keys_ref, values_ref)
    copies = [
        pltpu.make_async_copy(source, target, sems.at[index])
        for index, (source, target) in enumerate(zip(sources, targets))
    ]
    for copy in copies:
        copy.start()
    copies[0].wait()
    slots = keys_ref.shape[0]
    pos = pos_ref[...]
    my_first = shard_layout(ctx_size, lax.axis_index("ctx"), pos, meta_ref)
    shape = (slots, pos.shape[1])
    gap = lax.broadcasted_iota(jnp.int32, shape, 1) - lax.broadcasted_iota(jnp.int32, shape, 0)
    named = jnp.where(gap == my_first, pos.astype(jnp.float32), 0.0)
    angles = jnp.sum(named, axis=1, keepdims=True) * frequencies()
    cos_full = jnp.cos(angles)
    front = lax.broadcasted_iota(jnp.int32, angles.shape, 1) < HALF_DIM
    sin_full = jnp.where(front, -jnp.sin(angles), jnp.sin(angles))
    cos_ref[...] = cos_full
    sin_ref[...] = sin_full
    copies[1].wait()
    copies[2].wait()
    for lane in range(0, keys_ref.shape[1], HEAD_DIM):
        lanes = slice(lane, lane + HEAD_DIM)
        key = turn(keys_ref[:, lanes].astype(jnp.float32), cos_full, sin_full)
        both = jnp.concatenate([key.astype(jnp.bfloat16), values_ref[:, lanes]], axis=1)
        sent_ref[:, 2 * lane : 2 * (lane + HEAD_DIM)] = both
        sent_heads[lane // HEAD_DIM][...] = both


def prepare(positions, keys, values, ctx_size):
    slots, width = keys.shape
    table = jax.ShapeDtypeStruct((slots, HEAD_DIM), jnp.float32)
    sent = jax.ShapeDtypeStruct((slots, 2 * width), jnp.bfloat16)
    operands = (positions, keys, values)
    return pl.pallas_call(
        functools.partial(prepare_kernel, ctx_size),
        out_shape=(
            jax.ShapeDtypeStruct((2 * ctx_size,), jnp.int32),
            table,
            table,
            sent,
            *[jax.ShapeDtypeStruct((slots, 2 * HEAD_DIM), jnp.bfloat16)] * (width // HEAD_DIM),
        ),
        in_specs=[HBM] * 3,
        out_specs=(SMEM,) + (VMEM,) * (3 + width // HEAD_DIM),
        scratch_shapes=[pltpu.VMEM(operand.shape, operand.dtype) for operand in operands]
        + [pltpu.SemaphoreType.DMA((3,))],
        compiler_params=vmem(positions.shape[1], 54, 60),
        name="prepare",
    )(*operands)


def queries_kernel(
    cos_ref,
    sin_ref,
    query_ref,
    grad_ref,
    sent_ref,
    turned_ref,
    turned_t_ref,
    grad_t_ref,
    sent_again_ref,
):
    sent_again_ref[...] = sent_ref[...]
    for lane in range(0, query_ref.shape[1], HEAD_DIM):
        lanes = slice(lane, lane + HEAD_DIM)
        query = turn(query_ref[:, lanes].astype(jnp.float32), cos_ref[...], sin_ref[...])
        turned_ref[:, lanes] = query.astype(jnp.bfloat16)
        turned_t_ref[lanes, :] = query.T.astype(jnp.bfloat16)
        grad_t_ref[lanes, :] = grad_ref[:, lanes].astype(jnp.float32).T.astype(jnp.bfloat16)


def rotate_queries(cos_full, sin_full, queries, out_grad, sent):
    slots, width = queries.shape
    straight = jax.ShapeDtypeStruct((slots, width), jnp.bfloat16)
    across = jax.ShapeDtypeStruct((width, slots), jnp.bfloat16)
    return pl.pallas_call(
        queries_kernel,
        out_shape=(straight, across, across, jax.ShapeDtypeStruct(sent.shape, sent.dtype)),
        in_specs=[VMEM] * 5,
        out_specs=(VMEM,) * 4,
        compiler_params=vmem(0, 16, 16),
        cost_estimate=pl.CostEstimate(
            flops=3 * 10**9, bytes_accessed=4 * 1024 * 1024, transcendentals=0
        ),
        name="rotate_queries",
    )(cos_full, sin_full, queries, out_grad, sent)


def stacked(ref, lane, heads, width):
    parts = [ref[:width, lane + h * HEAD_DIM : lane + (h + 1) * HEAD_DIM] for h in range(heads)]
    return jnp.concatenate(parts, axis=0)


def beside(ref, rows, heads, slots, width):
    if width == slots:
        return ref[:rows, :]
    columns = [head * slots for head in range(heads)]
    return jnp.concatenate([ref[:rows, start : start + width] for start in columns], axis=1)


def terms_of(probs, score_grads, queries, grads):
    key_term = dot(score_grads, queries, ((1,), (0,))) * SCORE_SCALE
    return jnp.concatenate([key_term, dot(probs, grads, ((1,), (0,)))], axis=1)


def fold(field, join, reduce):
    while field.shape[0] % 16 == 0:
        half = field.shape[0] // 2
        field = join(field[:half], field[half:])
    return reduce(field, axis=0, keepdims=True)


def head_lanes(head):
    return slice(head * HEAD_DIM, (head + 1) * HEAD_DIM)


def key_lanes(key_head):
    return slice(2 * key_head * HEAD_DIM, (2 * key_head + 1) * HEAD_DIM)


def value_lanes(key_head):
    return slice((2 * key_head + 1) * HEAD_DIM, 2 * (key_head + 1) * HEAD_DIM)


def own_kernel(step_heads, count, sent_ref, turned_t_ref, grad_t_ref, *refs):
    weight_ref, product_ref, sums_ref = refs[count : count + 3]
    bias_ref = refs[-1]
    for source, target in zip(refs[:count], refs[count + 3 : -1]):
        target[...] = source[...]
    slots = sent_ref.shape[0]
    key_heads = sent_ref.shape[1] // HEAD_DIM // 2
    heads = turned_t_ref.shape[0] // HEAD_DIM // key_heads
    key_id = lax.broadcasted_iota(jnp.int32, (slots, slots), 0)
    slot_id = lax.broadcasted_iota(jnp.int32, (slots, slots), 1)
    bias_ref[...] = jnp.where(key_id <= slot_id, 0.0, HIDDEN)
    for key_head in range(key_heads):

        def step(index, carry):
            for part in range(step_heads):
                head = key_head * heads + index * step_heads + part
                rows = pl.ds(pl.multiple_of(head * HEAD_DIM, HEAD_DIM), HEAD_DIM)
                scores = dot(sent_ref[:, key_lanes(key_head)], turned_t_ref[rows, :], ((1,), (0,)))
                scores = scores + bias_ref[...]
                prob_grad = dot(sent_ref[:, value_lanes(key_head)], grad_t_ref[rows, :], ((1,), (0,)))
                peak = fold(scores, jnp.maximum, jnp.max)
                weights = jnp.exp2((scores - peak) * EXP2_SCALE)
                weight_ref[head] = weights
                product_ref[head] = prob_grad
                sums_ref[head, 0:1, :] = peak
                sums_ref[head, 1:2, :] = fold(weights, jnp.add, jnp.sum)
                sums_ref[head, 2:3, :] = fold(weights * prob_grad, jnp.add, jnp.sum)
            return carry

        lax.fori_loop(0, heads // step_heads, step, 0)


def own_scores(sent, turned_t, grad_t, handed):
    slots = sent.shape[0]
    heads = turned_t.shape[0] // HEAD_DIM
    square = jax.ShapeDtypeStruct((heads, slots, slots), jnp.float32)
    outs = pl.pallas_call(
        functools.partial(own_kernel, 4, len(handed)),
        out_shape=(
            square,
            square,
            jax.ShapeDtypeStruct((heads, 8, slots), jnp.float32),
            *[jax.ShapeDtypeStruct(array.shape, array.dtype) for array in handed],
        ),
        in_specs=[VMEM] * (3 + len(handed)),
        out_specs=(VMEM,) * (3 + len(handed)),
        scratch_shapes=[pltpu.VMEM((slots, slots), jnp.float32)],
        compiler_params=vmem(0, 16, 16),
        cost_estimate=pl.CostEstimate(
            flops=5 * 10**9, bytes_accessed=10 * 1024 * 1024, transcendentals=0
        ),
        name="own_scores",
    )(sent, turned_t, grad_t, *handed)
    return outs[:3], outs[3:]


def scores_kernel(
    ctx_size,
    sizes,
    step_units,
    key_head,
    meta_ref,
    turned_ref,
    grad_ref,
    turned_t_ref,
    grad_t_ref,
    sums_ref,
    *refs,
):
    count = 4 if relayed(ctx_size) else ctx_size - 1
    inputs, before = refs[:count], refs[count : -6 - ctx_size]
    refs = refs[-6 - ctx_size :]
    terms, refs = refs[: ctx_size - 1], refs[ctx_size - 1 :]
    score_grad_ref, joined_ref, key_ref, value_ref, bias_ref, prob_ref, acc_ref = refs
    slots = turned_ref.shape[0]
    span = bias_ref.shape[0]
    heads = joined_ref.shape[0]
    starts = [pl.multiple_of(meta_ref[hop], ALIGN) for hop in range(ctx_size)]
    my_start, my_count = starts[0], meta_ref[ctx_size]
    sent_hops = list(range(1, ctx_size))
    if relayed(ctx_size):
        last = lax.axis_index("ctx") == ctx_size - 1
        sent_hops = [jnp.where(last, 3, 1), jnp.where(last, 2, 1), jnp.where(last, 1, 2)]

    def blocks_of(lanes, lanes_alone):
        alone = [block.shape[1] == 2 * HEAD_DIM for block in inputs]
        blocks = [block[:, lanes_alone if one else lanes] for block, one in zip(inputs, alone)]
        if relayed(ctx_size):
            alpha, beta, gamma, delta = blocks
            blocks = [jnp.where(last, alpha, gamma), jnp.where(last, beta, alpha), delta]
        return blocks

    for ref, lanes in ((key_ref, key_lanes), (value_ref, value_lanes)):
        ref[slots:span, :] = jnp.zeros((span - slots, HEAD_DIM), jnp.bfloat16)
        blocks = blocks_of(lanes(key_head), lanes(0))
        for hop in range(ctx_size - 1, 0, -1):
            ref[pl.ds(starts[hop], slots), :] = blocks[hop - 1]
    place = lax.broadcasted_iota(jnp.int32, bias_ref.shape, 0)
    seen = place < 0
    for hop in range(1, ctx_size):
        end = starts[hop] + meta_ref[ctx_size + hop]
        seen = seen | ((place >= starts[hop]) & (place < end))
    bias_ref[...] = jnp.where(seen, 0.0, HIDDEN)
    live = lax.broadcasted_iota(jnp.int32, (1, slots), 1) < my_count
    acc_ref[...] = jnp.zeros_like(acc_ref)

    def joint(ref, places, rows, width):
        return jnp.concatenate([ref[rows(place) + (slice(0, width),)] for place in places], axis=1)

    def head_rows(place):
        return (pl.ds(pl.multiple_of((key_head * heads + place) * HEAD_DIM, HEAD_DIM), HEAD_DIM),)

    def units(groups, rows, width):
        side = slots // width
        bias = jnp.concatenate([bias_ref[:rows, :]] * (slots // HEAD_DIM), axis=1)
        alive = jnp.concatenate([live[:, :width]] * side, axis=1)
        queries = [joint(turned_t_ref, group, head_rows, width) for group in groups]
        grads = [joint(grad_t_ref, group, head_rows, width) for group in groups]

        def sums(row):
            index = lambda place: (key_head * heads + place, slice(row, row + 1))
            return [joint(sums_ref, group, index, width) for group in groups]

        own_peaks, own_totals, own_products = sums(0), sums(1), sums(2)
        scores = [dot(key_ref[:rows, :], query, ((1,), (0,))) + bias for query in queries]
        prob_grads = [dot(value_ref[:rows, :], grad, ((1,), (0,))) for grad in grads]
        peaks = [
            jnp.maximum(own, fold(score, jnp.maximum, jnp.max))
            for own, score in zip(own_peaks, scores)
        ]
        weights = [jnp.exp2((score - peak) * EXP2_SCALE) for score, peak in zip(scores, peaks)]
        shares = [jnp.exp2((own - peak) * EXP2_SCALE) for own, peak in zip(own_peaks, peaks)]
        totals = [
            own * share + fold(weight, jnp.add, jnp.sum)
            for own, share, weight in zip(own_totals, shares, weights)
        ]
        products = [
            own * share + fold(weight * prob_grad, jnp.add, jnp.sum)
            for own, share, weight, prob_grad in zip(own_products, shares, weights, prob_grads)
        ]
        inverses = [1.0 / total for total in totals]
        deltas = [product * inverse for product, inverse in zip(products, inverses)]
        inverses = [jnp.where(alive, inverse, 0.0) for inverse in inverses]
        factors = [share * inverse for share, inverse in zip(shares, inverses)]
        probs = [weight * inverse for weight, inverse in zip(weights, inverses)]
        score_grads = [
            (prob * (prob_grad - delta)).astype(jnp.bfloat16)
            for prob, prob_grad, delta in zip(probs, prob_grads, deltas)
        ]
        probs = [prob.astype(jnp.bfloat16) for prob in probs]
        for group, prob, score_grad, factor, delta in zip(
            groups, probs, score_grads, factors, deltas
        ):
            for index, place in enumerate(group):
                part = slice(index * width, (index + 1) * width)
                columns = pl.ds(pl.multiple_of(place * slots, slots), width)
                prob_ref[:rows, columns] = prob[:, part]
                score_grad_ref[:rows, columns] = score_grad[:, part]
                joined_ref[place, 0:1, :width] = factor[:, part]
                joined_ref[place, 1:2, :width] = delta[:, part]
                if width < slots:
                    rest = pl.ds(pl.multiple_of(place * slots + width, HEAD_DIM), slots - width)
                    score_grad_ref[:rows, rest] = jnp.zeros((rows, slots - width), jnp.bfloat16)
                    joined_ref[place, 0:2, width:] = jnp.zeros((2, slots - width), jnp.float32)

    above = {}
    for rows, width in sizes:
        fits = (my_start > above.get(width, 0)) & (my_start <= rows)
        above[width] = rows
        if len(sizes) > 1:
            fits = fits & ((my_count > slots // 2) if width == slots else (my_count <= width))

        @pl.when(fits)
        def _():
            side = slots // width

            def step(index, carry):
                base = index * step_units * side
                units(
                    [[base + part * side + item for item in range(side)] for part in range(step_units)],
                    rows,
                    width,
                )
                return carry

            lax.fori_loop(0, heads // side // step_units, step, 0)
            if rows % CHUNK:
                beyond = slice(rows, rows + CHUNK - rows % CHUNK)
                none = jnp.zeros((CHUNK - rows % CHUNK, heads * slots), jnp.bfloat16)
                score_grad_ref[beyond, :] = none
            lane = key_head * heads * HEAD_DIM
            acc_ref[:rows, :] = terms_of(
                beside(prob_ref, rows, heads, slots, width),
                beside(score_grad_ref, rows, heads, slots, width),
                stacked(turned_ref, lane, heads, width),
                stacked(grad_ref, lane, heads, width),
            )

    @pl.when(my_start == 0)
    def _():
        for place in range(heads):
            inverse = 1.0 / sums_ref[key_head * heads + place, 1:2, :]
            joined_ref[place, 0:1, :] = jnp.where(live, inverse, 0.0)
            joined_ref[place, 1:2, :] = sums_ref[key_head * heads + place, 2:3, :] * inverse

    for hop, term_ref in zip(sent_hops, terms):
        start = pl.multiple_of(meta_ref[hop], ALIGN)
        term = acc_ref[pl.ds(start, slots), :].astype(term_ref.dtype)
        if term_ref.shape == term.shape:
            term_ref[...] = term
        elif term_ref is terms[0]:
            term_ref[:, : 2 * HEAD_DIM] = term
            nearest = acc_ref[pl.ds(starts[1], slots), :].astype(term_ref.dtype)
            term_ref[:, 2 * HEAD_DIM :] = nearest
        else:
            term_ref[:, : -2 * HEAD_DIM] = before[0][...]
            term_ref[:, -2 * HEAD_DIM :] = term


def relayed(ctx_size):
    return ctx_size == 4


def scores(key_head, heads, meta, turned, out_grad, turned_t, grad_t, sums, blocks, after, routed, ctx_size):
    slots = turned.shape[0]
    span = -(-(routed + ctx_size * ALIGN) // CHUNK) * CHUNK
    sizes, step_units = [(span, slots)], 1
    if span == 2 * CHUNK and routed - slots // 2 + ctx_size * ALIGN <= 3 * CHUNK // 2 + ALIGN:
        sizes = [(CHUNK, slots), (3 * CHUNK // 2, slots), (CHUNK, slots // 2), (span, slots // 2)]
        step_units = 4
    terms = [jax.ShapeDtypeStruct((slots, 2 * HEAD_DIM), jnp.bfloat16)] * (ctx_size - 1)
    if relayed(ctx_size):
        if key_head == 0:
            terms[0] = jax.ShapeDtypeStruct((slots, 4 * HEAD_DIM), jnp.bfloat16)
        terms[1] = jax.ShapeDtypeStruct((slots, 2 * (key_head + 1) * HEAD_DIM), jnp.bfloat16)
        terms[2] = jax.ShapeDtypeStruct((slots, 2 * HEAD_DIM), jnp.float32)
    outs = pl.pallas_call(
        functools.partial(scores_kernel, ctx_size, sizes, step_units, key_head),
        out_shape=(
            *terms,
            jax.ShapeDtypeStruct((span, heads * slots), jnp.bfloat16),
            jax.ShapeDtypeStruct((heads, 8, slots), jnp.float32),
            jax.ShapeDtypeStruct((span + slots, HEAD_DIM), jnp.bfloat16),
        ),
        in_specs=[SMEM] + [VMEM] * (5 + len(blocks) + len(after)),
        out_specs=(VMEM,) * (ctx_size + 2),
        scratch_shapes=[
            pltpu.VMEM((span + slots, HEAD_DIM), jnp.bfloat16),
            pltpu.VMEM((span, HEAD_DIM), jnp.float32),
            pltpu.VMEM((span, heads * slots), jnp.bfloat16),
            pltpu.VMEM((span + slots, 2 * HEAD_DIM), jnp.float32),
        ],
        compiler_params=vmem(routed, 20, 60),
        cost_estimate=pl.CostEstimate(
            flops=4 * 10**9, bytes_accessed=6 * 1024 * 1024, transcendentals=0
        ),
        name="scores",
    )(meta, turned, out_grad, turned_t, grad_t, sums, *blocks, *after)
    return outs[: ctx_size - 1], outs[ctx_size - 1 :]


def local_kernel(
    key_head,
    meta_ref,
    cos_ref,
    sin_ref,
    turned_ref,
    grad_ref,
    sent_ref,
    weight_ref,
    product_ref,
    score_grad_ref,
    joined_ref,
    key_ref,
    *refs,
):
    dq_ref, own_ref, prob_ref, own_grad_ref, sum_ref = refs[-5:]
    slots = turned_ref.shape[0]
    heads = joined_ref.shape[0]
    span = score_grad_ref.shape[0]
    my_start = meta_ref[0]
    own_key_t = sent_ref[:, key_lanes(key_head)].astype(jnp.float32).T.astype(jnp.bfloat16)
    for head in range(heads):
        columns = slice(head * slots, (head + 1) * slots)
        prob = weight_ref[key_head * heads + head] * joined_ref[head, 0:1, :]
        prob_ref[:, columns] = prob.astype(jnp.bfloat16)
        product = product_ref[key_head * heads + head] - joined_ref[head, 1:2, :]
        score_grad = (prob * product).astype(jnp.bfloat16)
        own_grad_ref[:, columns] = score_grad
        sum_ref[head] = dot(own_key_t, score_grad, ((1,), (0,)))
    for chunk in range(0, span, CHUNK):

        @pl.when(chunk < my_start)
        def _():
            rows = slice(chunk, chunk + CHUNK)
            key_t = key_ref[rows, :].astype(jnp.float32).T.astype(jnp.bfloat16)
            for head in range(heads):
                score_grad = score_grad_ref[rows, head * slots : (head + 1) * slots]
                sum_ref[head] += dot(key_t, score_grad, ((1,), (0,)))

    lane = key_head * heads * HEAD_DIM
    for head in range(heads):
        grad = turn_back((sum_ref[head] * SCORE_SCALE).T, cos_ref[...], sin_ref[...])
        dq_ref[:, head * HEAD_DIM : (head + 1) * HEAD_DIM] = grad.astype(jnp.bfloat16)
    own_ref[...] = terms_of(
        prob_ref[...],
        own_grad_ref[...],
        stacked(turned_ref, lane, heads, slots),
        stacked(grad_ref, lane, heads, slots),
    )


def local_terms(meta, cos_full, sin_full, turned, out_grad, sent, own, key_head, joined, dq, after):
    slots = turned.shape[0]
    heads = joined[1].shape[0]
    weight, product, _ = own
    operands = [meta, cos_full, sin_full, turned, out_grad, sent, weight, product, *joined, *after]
    in_specs = [SMEM] + [VMEM] * (len(operands) - 1)
    aliases = {}
    if dq is not None:
        aliases = {len(operands): 0}
        operands.append(dq)
        in_specs.append(pl.BlockSpec(memory_space=pl.ANY))
    return pl.pallas_call(
        functools.partial(local_kernel, key_head),
        grid=(1,),
        out_shape=(
            jax.ShapeDtypeStruct(turned.shape, jnp.bfloat16),
            jax.ShapeDtypeStruct((slots, 2 * HEAD_DIM), jnp.float32),
        ),
        in_specs=in_specs,
        out_specs=(pl.BlockSpec((slots, heads * HEAD_DIM), lambda step: (0, key_head)), VMEM),
        scratch_shapes=[
            pltpu.VMEM((slots, heads * slots), jnp.bfloat16),
            pltpu.VMEM((slots, heads * slots), jnp.bfloat16),
            pltpu.VMEM((heads, HEAD_DIM, slots), jnp.float32),
        ],
        input_output_aliases=aliases,
        compiler_params=vmem(joined[0].shape[0] // 2, 16, 48),
        cost_estimate=pl.CostEstimate(
            flops=4 * 10**9, bytes_accessed=10 * 1024 * 1024, transcendentals=0
        ),
        name="local_terms",
    )(*operands)


def add_kernel(own_ref, arrived_ref, *refs):
    arrived = arrived_ref[:, : own_ref.shape[1]].astype(jnp.float32)
    refs[-1][...] = (own_ref[...] + arrived).astype(jnp.bfloat16)


def add_terms(own, arrived, after):
    return pl.pallas_call(
        add_kernel,
        out_shape=jax.ShapeDtypeStruct(own.shape, jnp.bfloat16),
        in_specs=[VMEM] * (2 + len(after)),
        out_specs=VMEM,
        compiler_params=vmem(0, 16, 16),
        cost_estimate=pl.CostEstimate(flops=10**6, bytes_accessed=10**6, transcendentals=0),
        name="add_terms",
    )(own, arrived, *after)


def finish_kernel(ctx_size, key_heads, meta_ref, cos_ref, sin_ref, *refs):
    key_grad_ref, value_grad_ref = refs[-2:]
    owns, terms = refs[:key_heads], list(refs[key_heads:-2])
    slots = cos_ref.shape[0]
    live = lax.broadcasted_iota(jnp.int32, (slots, HEAD_DIM), 0) < meta_ref[ctx_size]
    totals = [own[...] for own in owns]
    if relayed(ctx_size):
        second = lax.axis_index("ctx") == 2
        for head in range(key_heads):
            first = terms.pop(0)[...].astype(jnp.float32)
            beside = first[:, 2 * HEAD_DIM :] if first.shape[1] > 2 * HEAD_DIM else 0.0
            totals[head] += jnp.where(second, beside, first[:, : 2 * HEAD_DIM])
    while terms:
        parts = [terms.pop(0)]
        if parts[0].shape[1] == 2 * HEAD_DIM:
            parts += [terms.pop(0) for _ in range(key_heads - 1)]
        term = jnp.concatenate([part[...] for part in parts], axis=1).astype(jnp.float32)
        for head in range(key_heads):
            totals[head] += term[:, 2 * head * HEAD_DIM : 2 * (head + 1) * HEAD_DIM]
    for head, total in enumerate(totals):
        lanes = head_lanes(head)
        key_term = turn_back(total[:, :HEAD_DIM], cos_ref[...], sin_ref[...])
        key_grad_ref[:, lanes] = jnp.where(live, key_term, 0.0).astype(jnp.bfloat16)
        value_grad_ref[:, lanes] = jnp.where(live, total[:, HEAD_DIM:], 0.0).astype(jnp.bfloat16)


def finish(meta, cos_full, sin_full, owns, terms, ctx_size):
    slots = cos_full.shape[0]
    key_heads = len(owns)
    grad = jax.ShapeDtypeStruct((slots, key_heads * HEAD_DIM), jnp.bfloat16)
    return pl.pallas_call(
        functools.partial(finish_kernel, ctx_size, key_heads),
        out_shape=(grad, grad),
        in_specs=[SMEM] + [VMEM] * (2 + len(owns) + len(terms)),
        out_specs=(VMEM, VMEM),
        compiler_params=vmem(0, 16, 16),
        name="finish",
    )(meta, cos_full, sin_full, *owns, *terms)


def climb(sent, ctx_size):
    blocks = [sent]
    for hop in range(1, ctx_size):
        pairs = [(shard, shard + 1) for shard in range(hop - 1, ctx_size - 1)]
        blocks.append(lax.ppermute(blocks[-1], "ctx", pairs))
    return blocks[1:]


def descend(terms, ctx_size):
    arrived = []
    for hop, term in enumerate(terms, 1):
        pairs = [(shard + hop, shard) for shard in range(ctx_size - hop)]
        arrived.append(lax.ppermute(term, "ctx", pairs))
    return arrived


def body(positions, queries, keys, values, out_grad):
    ctx_size = lax.axis_size("ctx")
    routed = positions.shape[1]
    key_heads = keys.shape[2] // HEAD_DIM
    meta, cos_full, sin_full, sent, *sent_heads = prepare(positions, keys[0], values[0], ctx_size)
    turned, turned_t, grad_t, sent_again = rotate_queries(
        cos_full, sin_full, queries[0], out_grad[0], sent_heads[0]
    )
    if relayed(ctx_size):
        alphas = [lax.ppermute(part, "ctx", [(0, 2), (2, 3)]) for part in sent_heads]
        beta = lax.ppermute(sent, "ctx", [(1, 3)])
        own, handed = own_scores(sent, turned_t, grad_t, sent_heads[1:] + alphas[1:])
        blocks = []
        for head, alpha in enumerate(alphas):
            near, far = sent_again, alpha
            if head > 0:
                near, far = handed[head - 1], handed[head + key_heads - 2]
            gamma = lax.ppermute(near, "ctx", [(0, 1), (1, 2)])
            blocks.append([alpha, beta, gamma, lax.ppermute(far, "ctx", [(2, 3)])])
    else:
        blocks = [climb(sent, ctx_size)] * key_heads
        own, _ = own_scores(sent, turned_t, grad_t, [])
    terms, joined, owns = [], [], []
    for head in range(key_heads):
        after = [terms[-1][1]] if terms else []
        outs = scores(
            head,
            queries.shape[2] // HEAD_DIM // key_heads,
            meta,
            turned,
            out_grad[0],
            turned_t,
            grad_t,
            own[2],
            blocks[head],
            after,
            routed,
            ctx_size,
        )
        terms.append(outs[0])
        joined.append(outs[1])
    local = functools.partial(
        local_terms, meta, cos_full, sin_full, turned, out_grad[0], sent, own
    )
    dq = None
    if relayed(ctx_size):
        firsts = [lax.ppermute(first, "ctx", [(3, 2), (2, 1)]) for first, _, _ in terms]
        relays = []
        for head in range(key_heads):
            total = add_terms(terms[head][2], firsts[head], owns[-1:])
            relays.append(lax.ppermute(total, "ctx", [(3, 2), (2, 0)] if relays else [(2, 0)]))
            dq, own_terms = local(head, joined[head], dq, [total])
            owns.append(own_terms)
        arrived = firsts + relays + [lax.ppermute(terms[-1][1], "ctx", [(3, 1), (1, 0)])]
    else:
        arrived = [part for hop in zip(*[descend(term, ctx_size) for term in terms]) for part in hop]
        for head in range(key_heads):
            dq, own_terms = local(head, joined[head], dq, [])
            owns.append(own_terms)
    key_grad, value_grad = finish(meta, cos_full, sin_full, owns, arrived, ctx_size)
    return (dq[None], key_grad[None], value_grad[None])


def solution(mesh):
    split = P(("groups", "dp"), "ctx", "mp")
    return jax.shard_map(
        body,
        mesh=mesh,
        in_specs=(P(("groups", "dp"), None), split, split, split, split),
        out_specs=(split, split, split),
        check_vma=False,
    )
```

```python
import functools
import math

import jax
import jax.numpy as jnp
import numpy as np
from jax import lax
from jax.experimental import pallas as pl
from jax.experimental.pallas import tpu as pltpu
from jax.sharding import PartitionSpec as P

HEAD_DIM = 128
HALF_DIM = HEAD_DIM // 2
TOK_SHARD = 1024
ROPE_BASE = 500000.0
SCORE_SCALE = 1.0 / math.sqrt(HEAD_DIM)
EXP2_SCALE = SCORE_SCALE * math.log2(math.e)
HIDDEN = -1e30
ALIGN = 16
CHUNK = 288
MIB = 1024 * 1024

VMEM = pl.BlockSpec(memory_space=pltpu.VMEM)
SMEM = pl.BlockSpec(memory_space=pltpu.SMEM)
HBM = pl.BlockSpec(memory_space=pltpu.HBM)


def vmem(routed, small, large):
    return pltpu.CompilerParams(vmem_limit_bytes=(small if routed <= 512 else large) * MIB)


def dot(left, right, contract):
    return lax.dot_general(left, right, (contract, ((), ())), preferred_element_type=jnp.float32)


def turn(field, cos_full, sin_full):
    return field * cos_full + pltpu.roll(field, HALF_DIM, 1) * sin_full


def turn_back(field, cos_full, sin_full):
    return field * cos_full - pltpu.roll(field, HALF_DIM, 1) * sin_full


def frequencies():
    ladder = np.arange(HALF_DIM, dtype=np.float32)
    exponent = ladder * np.float32(-2.0 * math.log(ROPE_BASE) / HEAD_DIM)
    freq = np.exp(exponent.astype(np.float64)).astype(np.float32)
    entry = lax.broadcasted_iota(jnp.int32, (1, HEAD_DIM), 1) % HALF_DIM
    row = jnp.zeros((1, HEAD_DIM), jnp.float32)
    for index in range(HALF_DIM):
        row = jnp.where(entry == index, float(freq[index]), row)
    return row


def shard_layout(ctx_size, me, pos, meta_ref):
    shard_of = pos // TOK_SHARD
    for hop in range(2 * ctx_size):
        meta_ref[hop] = 0
    start = jnp.int32(0)
    first = jnp.int32(0)
    my_first = jnp.int32(0)
    for shard in range(ctx_size):
        count = jnp.sum(jnp.where(shard_of == shard, 1.0, 0.0)).astype(jnp.int32)
        my_first = jnp.where(me == shard, first, my_first)

        @pl.when(me >= shard)
        def _():
            meta_ref[me - shard] = start
            meta_ref[ctx_size + me - shard] = count

        first = first + count
        start = start + (count + ALIGN - 1) // ALIGN * ALIGN
    return my_first


def prepare_kernel(
    ctx_size, pos_hbm, keys_hbm, values_hbm, meta_ref, table_ref, sent_ref, *refs
):
    sent_heads, (pos_ref, keys_ref, values_ref, sems) = refs[:-4], refs[-4:]
    sources = (pos_hbm, keys_hbm, values_hbm)
    targets = (pos_ref, keys_ref, values_ref)
    copies = [
        pltpu.make_async_copy(source, target, sems.at[index])
        for index, (source, target) in enumerate(zip(sources, targets))
    ]
    for copy in copies:
        copy.start()
    copies[0].wait()
    slots = keys_ref.shape[0]
    pos = pos_ref[...]
    my_first = shard_layout(ctx_size, lax.axis_index("ctx"), pos, meta_ref)
    shape = (slots, pos.shape[1])
    gap = lax.broadcasted_iota(jnp.int32, shape, 1) - lax.broadcasted_iota(jnp.int32, shape, 0)
    named = jnp.where(gap == my_first, pos.astype(jnp.float32), 0.0)
    angles = jnp.sum(named, axis=1, keepdims=True) * frequencies()
    cos_full = jnp.cos(angles)
    front = lax.broadcasted_iota(jnp.int32, angles.shape, 1) < HALF_DIM
    sin_full = jnp.where(front, -jnp.sin(angles), jnp.sin(angles))
    table_ref[:, :HEAD_DIM] = cos_full
    table_ref[:, HEAD_DIM:] = sin_full
    copies[1].wait()
    copies[2].wait()
    for lane in range(0, keys_ref.shape[1], HEAD_DIM):
        lanes = slice(lane, lane + HEAD_DIM)
        key = turn(keys_ref[:, lanes].astype(jnp.float32), cos_full, sin_full)
        both = jnp.concatenate([key.astype(jnp.bfloat16), values_ref[:, lanes]], axis=1)
        sent_ref[:, 2 * lane : 2 * (lane + HEAD_DIM)] = both
        sent_heads[lane // HEAD_DIM][...] = both


def prepare(positions, keys, values, ctx_size):
    slots, width = keys.shape
    table = jax.ShapeDtypeStruct((slots, 2 * HEAD_DIM), jnp.float32)
    sent = jax.ShapeDtypeStruct((slots, 2 * width), jnp.bfloat16)
    operands = (positions, keys, values)
    return pl.pallas_call(
        functools.partial(prepare_kernel, ctx_size),
        out_shape=(
            jax.ShapeDtypeStruct((2 * ctx_size,), jnp.int32),
            table,
            sent,
            *[jax.ShapeDtypeStruct((slots, 2 * HEAD_DIM), jnp.bfloat16)] * (width // HEAD_DIM),
        ),
        in_specs=[HBM] * 3,
        out_specs=(SMEM,) + (VMEM,) * (2 + width // HEAD_DIM),
        scratch_shapes=[pltpu.VMEM(operand.shape, operand.dtype) for operand in operands]
        + [pltpu.SemaphoreType.DMA((3,))],
        compiler_params=vmem(positions.shape[1], 54, 60),
        name="prepare",
    )(*operands)


def queries_kernel(table_ref, query_ref, grad_ref, turned_ref, turned_t_ref, grad_t_ref):
    for lane in range(0, query_ref.shape[1], HEAD_DIM):
        lanes = slice(lane, lane + HEAD_DIM)
        query = turn(query_ref[:, lanes].astype(jnp.float32), table_ref[:, :HEAD_DIM], table_ref[:, HEAD_DIM:])
        turned_ref[:, lanes] = query.astype(jnp.bfloat16)
        turned_t_ref[lanes, :] = query.T.astype(jnp.bfloat16)
        grad_t_ref[lanes, :] = grad_ref[:, lanes].astype(jnp.float32).T.astype(jnp.bfloat16)


def rotate_queries(table, queries, out_grad):
    slots, width = queries.shape
    straight = jax.ShapeDtypeStruct((slots, width), jnp.bfloat16)
    across = jax.ShapeDtypeStruct((width, slots), jnp.bfloat16)
    return pl.pallas_call(
        queries_kernel,
        out_shape=(straight, across, across),
        in_specs=[VMEM] * 3,
        out_specs=(VMEM,) * 3,
        compiler_params=vmem(0, 16, 16),
        cost_estimate=pl.CostEstimate(
            flops=3 * 10**9, bytes_accessed=4 * 1024 * 1024, transcendentals=0
        ),
        name="rotate_queries",
    )(table, queries, out_grad)


def stacked(ref, lane, heads, width):
    parts = [ref[:width, lane + h * HEAD_DIM : lane + (h + 1) * HEAD_DIM] for h in range(heads)]
    return jnp.concatenate(parts, axis=0)


def beside(ref, rows, heads, slots, width):
    if width == slots:
        return ref[:rows, :]
    columns = [head * slots for head in range(heads)]
    return jnp.concatenate([ref[:rows, start : start + width] for start in columns], axis=1)


def terms_of(probs, score_grads, queries, grads):
    key_term = dot(score_grads, queries, ((1,), (0,))) * SCORE_SCALE
    return jnp.concatenate([key_term, dot(probs, grads, ((1,), (0,)))], axis=1)


def fold(field, join, reduce):
    while field.shape[0] % 16 == 0:
        half = field.shape[0] // 2
        field = join(field[:half], field[half:])
    return reduce(field, axis=0, keepdims=True)


def head_lanes(head):
    return slice(head * HEAD_DIM, (head + 1) * HEAD_DIM)


def key_lanes(key_head):
    return slice(2 * key_head * HEAD_DIM, (2 * key_head + 1) * HEAD_DIM)


def value_lanes(key_head):
    return slice((2 * key_head + 1) * HEAD_DIM, 2 * (key_head + 1) * HEAD_DIM)


def own_kernel(step_heads, count, sent_ref, turned_t_ref, grad_t_ref, *refs):
    weight_ref, product_ref, sums_ref = refs[count : count + 3]
    bias_ref = refs[-1]
    for source, target in zip(refs[:count], refs[count + 3 : -1]):
        target[...] = source[...]
    slots = sent_ref.shape[0]
    key_heads = sent_ref.shape[1] // HEAD_DIM // 2
    heads = turned_t_ref.shape[0] // HEAD_DIM // key_heads
    key_id = lax.broadcasted_iota(jnp.int32, (slots, slots), 0)
    slot_id = lax.broadcasted_iota(jnp.int32, (slots, slots), 1)
    bias_ref[...] = jnp.where(key_id <= slot_id, 0.0, HIDDEN)
    for key_head in range(key_heads):

        def step(index, carry):
            for part in range(step_heads):
                head = key_head * heads + index * step_heads + part
                rows = pl.ds(pl.multiple_of(head * HEAD_DIM, HEAD_DIM), HEAD_DIM)
                scores = dot(sent_ref[:, key_lanes(key_head)], turned_t_ref[rows, :], ((1,), (0,)))
                scores = scores + bias_ref[...]
                prob_grad = dot(sent_ref[:, value_lanes(key_head)], grad_t_ref[rows, :], ((1,), (0,)))
                peak = fold(scores, jnp.maximum, jnp.max)
                weights = jnp.exp2((scores - peak) * EXP2_SCALE)
                weight_ref[head] = weights
                product_ref[head] = prob_grad
                sums_ref[head, 0:1, :] = peak
                sums_ref[head, 1:2, :] = fold(weights, jnp.add, jnp.sum)
                sums_ref[head, 2:3, :] = fold(weights * prob_grad, jnp.add, jnp.sum)
            return carry

        lax.fori_loop(0, heads // step_heads, step, 0)


def own_scores(sent, turned_t, grad_t, handed):
    slots = sent.shape[0]
    heads = turned_t.shape[0] // HEAD_DIM
    square = jax.ShapeDtypeStruct((heads, slots, slots), jnp.float32)
    outs = pl.pallas_call(
        functools.partial(own_kernel, 4, len(handed)),
        out_shape=(
            square,
            square,
            jax.ShapeDtypeStruct((heads, 8, slots), jnp.float32),
            *[jax.ShapeDtypeStruct(array.shape, array.dtype) for array in handed],
        ),
        in_specs=[VMEM] * (3 + len(handed)),
        out_specs=(VMEM,) * (3 + len(handed)),
        scratch_shapes=[pltpu.VMEM((slots, slots), jnp.float32)],
        compiler_params=vmem(0, 16, 16),
        cost_estimate=pl.CostEstimate(
            flops=5 * 10**9, bytes_accessed=10 * 1024 * 1024, transcendentals=0
        ),
        name="own_scores",
    )(sent, turned_t, grad_t, *handed)
    return outs[:3], outs[3:]


def scores_kernel(
    ctx_size,
    sizes,
    step_units,
    key_head,
    meta_ref,
    turned_ref,
    grad_ref,
    turned_t_ref,
    grad_t_ref,
    sums_ref,
    *refs,
):
    count = 4 if relayed(ctx_size) else ctx_size - 1
    inputs, before = refs[:count], refs[count : -6 - ctx_size]
    refs = refs[-6 - ctx_size :]
    terms, refs = refs[: ctx_size - 1], refs[ctx_size - 1 :]
    score_grad_ref, joined_ref, key_ref, value_ref, bias_ref, prob_ref, acc_ref = refs
    slots = turned_ref.shape[0]
    span = bias_ref.shape[0]
    heads = joined_ref.shape[0]
    starts = [pl.multiple_of(meta_ref[hop], ALIGN) for hop in range(ctx_size)]
    my_start, my_count = starts[0], meta_ref[ctx_size]
    sent_hops = list(range(1, ctx_size))
    if relayed(ctx_size):
        last = lax.axis_index("ctx") == ctx_size - 1
        sent_hops = [jnp.where(last, 3, 1), jnp.where(last, 2, 1), jnp.where(last, 1, 2)]

    def blocks_of(lanes, lanes_alone):
        alone = [block.shape[1] == 2 * HEAD_DIM for block in inputs]
        blocks = [block[:, lanes_alone if one else lanes] for block, one in zip(inputs, alone)]
        if relayed(ctx_size):
            alpha, beta, gamma, delta = blocks
            blocks = [jnp.where(last, alpha, gamma), jnp.where(last, beta, alpha), delta]
        return blocks

    for ref, lanes in ((key_ref, key_lanes), (value_ref, value_lanes)):
        ref[slots:span, :] = jnp.zeros((span - slots, HEAD_DIM), jnp.bfloat16)
        blocks = blocks_of(lanes(key_head), lanes(0))
        for hop in range(ctx_size - 1, 0, -1):
            ref[pl.ds(starts[hop], slots), :] = blocks[hop - 1]
    place = lax.broadcasted_iota(jnp.int32, bias_ref.shape, 0)
    seen = place < 0
    for hop in range(1, ctx_size):
        end = starts[hop] + meta_ref[ctx_size + hop]
        seen = seen | ((place >= starts[hop]) & (place < end))
    bias_ref[...] = jnp.where(seen, 0.0, HIDDEN)
    live = lax.broadcasted_iota(jnp.int32, (1, slots), 1) < my_count
    acc_ref[...] = jnp.zeros_like(acc_ref)

    def joint(ref, places, rows, width):
        return jnp.concatenate([ref[rows(place) + (slice(0, width),)] for place in places], axis=1)

    def head_rows(place):
        return (pl.ds(pl.multiple_of((key_head * heads + place) * HEAD_DIM, HEAD_DIM), HEAD_DIM),)

    def units(groups, rows, width):
        side = slots // width
        bias = jnp.concatenate([bias_ref[:rows, :]] * (slots // HEAD_DIM), axis=1)
        alive = jnp.concatenate([live[:, :width]] * side, axis=1)
        queries = [joint(turned_t_ref, group, head_rows, width) for group in groups]
        grads = [joint(grad_t_ref, group, head_rows, width) for group in groups]

        def sums(row):
            index = lambda place: (key_head * heads + place, slice(row, row + 1))
            return [joint(sums_ref, group, index, width) for group in groups]

        own_peaks, own_totals, own_products = sums(0), sums(1), sums(2)
        scores = [dot(key_ref[:rows, :], query, ((1,), (0,))) + bias for query in queries]
        prob_grads = [dot(value_ref[:rows, :], grad, ((1,), (0,))) for grad in grads]
        peaks = [
            jnp.maximum(own, fold(score, jnp.maximum, jnp.max))
            for own, score in zip(own_peaks, scores)
        ]
        weights = [jnp.exp2((score - peak) * EXP2_SCALE) for score, peak in zip(scores, peaks)]
        shares = [jnp.exp2((own - peak) * EXP2_SCALE) for own, peak in zip(own_peaks, peaks)]
        totals = [
            own * share + fold(weight, jnp.add, jnp.sum)
            for own, share, weight in zip(own_totals, shares, weights)
        ]
        products = [
            own * share + fold(weight * prob_grad, jnp.add, jnp.sum)
            for own, share, weight, prob_grad in zip(own_products, shares, weights, prob_grads)
        ]
        inverses = [1.0 / total for total in totals]
        deltas = [product * inverse for product, inverse in zip(products, inverses)]
        inverses = [jnp.where(alive, inverse, 0.0) for inverse in inverses]
        factors = [share * inverse for share, inverse in zip(shares, inverses)]
        probs = [weight * inverse for weight, inverse in zip(weights, inverses)]
        score_grads = [
            (prob * (prob_grad - delta)).astype(jnp.bfloat16)
            for prob, prob_grad, delta in zip(probs, prob_grads, deltas)
        ]
        probs = [prob.astype(jnp.bfloat16) for prob in probs]
        for group, prob, score_grad, factor, delta in zip(
            groups, probs, score_grads, factors, deltas
        ):
            for index, place in enumerate(group):
                part = slice(index * width, (index + 1) * width)
                columns = pl.ds(pl.multiple_of(place * slots, slots), width)
                prob_ref[:rows, columns] = prob[:, part]
                score_grad_ref[:rows, columns] = score_grad[:, part]
                joined_ref[place, 0:1, :width] = factor[:, part]
                joined_ref[place, 1:2, :width] = delta[:, part]
                if width < slots:
                    rest = pl.ds(pl.multiple_of(place * slots + width, HEAD_DIM), slots - width)
                    score_grad_ref[:rows, rest] = jnp.zeros((rows, slots - width), jnp.bfloat16)
                    joined_ref[place, 0:2, width:] = jnp.zeros((2, slots - width), jnp.float32)

    above = {}
    for rows, width in sizes:
        fits = (my_start > above.get(width, 0)) & (my_start <= rows)
        above[width] = rows
        if len(sizes) > 1:
            fits = fits & ((my_count > slots // 2) if width == slots else (my_count <= width))

        @pl.when(fits)
        def _():
            side = slots // width

            def step(index, carry):
                base = index * step_units * side
                units(
                    [[base + part * side + item for item in range(side)] for part in range(step_units)],
                    rows,
                    width,
                )
                return carry

            lax.fori_loop(0, heads // side // step_units, step, 0)
            if rows % CHUNK:
                beyond = slice(rows, rows + CHUNK - rows % CHUNK)
                none = jnp.zeros((CHUNK - rows % CHUNK, heads * slots), jnp.bfloat16)
                score_grad_ref[beyond, :] = none
            lane = key_head * heads * HEAD_DIM
            acc_ref[:rows, :] = terms_of(
                beside(prob_ref, rows, heads, slots, width),
                beside(score_grad_ref, rows, heads, slots, width),
                stacked(turned_ref, lane, heads, width),
                stacked(grad_ref, lane, heads, width),
            )

    @pl.when(my_start == 0)
    def _():
        for place in range(heads):
            inverse = 1.0 / sums_ref[key_head * heads + place, 1:2, :]
            joined_ref[place, 0:1, :] = jnp.where(live, inverse, 0.0)
            joined_ref[place, 1:2, :] = sums_ref[key_head * heads + place, 2:3, :] * inverse

    for hop, term_ref in zip(sent_hops, terms):
        start = pl.multiple_of(meta_ref[hop], ALIGN)
        term = acc_ref[pl.ds(start, slots), :].astype(term_ref.dtype)
        if term_ref.shape == term.shape:
            term_ref[...] = term
        elif term_ref is terms[0]:
            term_ref[:, : 2 * HEAD_DIM] = term
            nearest = acc_ref[pl.ds(starts[1], slots), :].astype(term_ref.dtype)
            term_ref[:, 2 * HEAD_DIM :] = nearest
        else:
            term_ref[:, : -2 * HEAD_DIM] = before[0][...]
            term_ref[:, -2 * HEAD_DIM :] = term


def relayed(ctx_size):
    return ctx_size == 4


def scores(key_head, heads, meta, turned, out_grad, turned_t, grad_t, sums, blocks, after, routed, ctx_size):
    slots = turned.shape[0]
    span = -(-(routed + ctx_size * ALIGN) // CHUNK) * CHUNK
    sizes, step_units = [(span, slots)], 1
    if span == 2 * CHUNK and routed - slots // 2 + ctx_size * ALIGN <= 3 * CHUNK // 2 + ALIGN:
        sizes = [(CHUNK, slots), (3 * CHUNK // 2, slots), (CHUNK, slots // 2), (span, slots // 2)]
        step_units = 4
    terms = [jax.ShapeDtypeStruct((slots, 2 * HEAD_DIM), jnp.bfloat16)] * (ctx_size - 1)
    if relayed(ctx_size):
        if key_head == 0:
            terms[0] = jax.ShapeDtypeStruct((slots, 4 * HEAD_DIM), jnp.bfloat16)
        terms[1] = jax.ShapeDtypeStruct((slots, 2 * (key_head + 1) * HEAD_DIM), jnp.bfloat16)
        terms[2] = jax.ShapeDtypeStruct((slots, 2 * HEAD_DIM), jnp.float32)
    outs = pl.pallas_call(
        functools.partial(scores_kernel, ctx_size, sizes, step_units, key_head),
        out_shape=(
            *terms,
            jax.ShapeDtypeStruct((span, heads * slots), jnp.bfloat16),
            jax.ShapeDtypeStruct((heads, 8, slots), jnp.float32),
            jax.ShapeDtypeStruct((span + slots, HEAD_DIM), jnp.bfloat16),
        ),
        in_specs=[SMEM] + [VMEM] * (5 + len(blocks) + len(after)),
        out_specs=(VMEM,) * (ctx_size + 2),
        scratch_shapes=[
            pltpu.VMEM((span + slots, HEAD_DIM), jnp.bfloat16),
            pltpu.VMEM((span, HEAD_DIM), jnp.float32),
            pltpu.VMEM((span, heads * slots), jnp.bfloat16),
            pltpu.VMEM((span + slots, 2 * HEAD_DIM), jnp.float32),
        ],
        compiler_params=vmem(routed, 20, 60),
        cost_estimate=pl.CostEstimate(
            flops=4 * 10**9, bytes_accessed=6 * 1024 * 1024, transcendentals=0
        ),
        name="scores",
    )(meta, turned, out_grad, turned_t, grad_t, sums, *blocks, *after)
    return outs[: ctx_size - 1], outs[ctx_size - 1 :]


def local_kernel(
    key_head,
    meta_ref,
    table_ref,
    turned_ref,
    grad_ref,
    sent_ref,
    weight_ref,
    product_ref,
    score_grad_ref,
    joined_ref,
    key_ref,
    *refs,
):
    dq_ref, own_ref, prob_ref, own_grad_ref, sum_ref = refs[-5:]
    slots = turned_ref.shape[0]
    heads = joined_ref.shape[0]
    span = score_grad_ref.shape[0]
    my_start = meta_ref[0]
    own_key_t = sent_ref[:, key_lanes(key_head)].astype(jnp.float32).T.astype(jnp.bfloat16)
    for head in range(heads):
        columns = slice(head * slots, (head + 1) * slots)
        prob = weight_ref[key_head * heads + head] * joined_ref[head, 0:1, :]
        prob_ref[:, columns] = prob.astype(jnp.bfloat16)
        product = product_ref[key_head * heads + head] - joined_ref[head, 1:2, :]
        score_grad = (prob * product).astype(jnp.bfloat16)
        own_grad_ref[:, columns] = score_grad
        sum_ref[head] = dot(own_key_t, score_grad, ((1,), (0,)))
    for chunk in range(0, span, CHUNK):

        @pl.when(chunk < my_start)
        def _():
            rows = slice(chunk, chunk + CHUNK)
            key_t = key_ref[rows, :].astype(jnp.float32).T.astype(jnp.bfloat16)
            for head in range(heads):
                score_grad = score_grad_ref[rows, head * slots : (head + 1) * slots]
                sum_ref[head] += dot(key_t, score_grad, ((1,), (0,)))

    lane = key_head * heads * HEAD_DIM
    for head in range(heads):
        grad = turn_back((sum_ref[head] * SCORE_SCALE).T, table_ref[:, :HEAD_DIM], table_ref[:, HEAD_DIM:])
        dq_ref[:, head * HEAD_DIM : (head + 1) * HEAD_DIM] = grad.astype(jnp.bfloat16)
    own_ref[...] = terms_of(
        prob_ref[...],
        own_grad_ref[...],
        stacked(turned_ref, lane, heads, slots),
        stacked(grad_ref, lane, heads, slots),
    )


def local_terms(meta, table, turned, out_grad, sent, own, key_head, joined, dq, after):
    slots = turned.shape[0]
    heads = joined[1].shape[0]
    weight, product, _ = own
    operands = [meta, table, turned, out_grad, sent, weight, product, *joined, *after]
    in_specs = [SMEM] + [VMEM] * (len(operands) - 1)
    aliases = {}
    if dq is not None:
        aliases = {len(operands): 0}
        operands.append(dq)
        in_specs.append(pl.BlockSpec(memory_space=pl.ANY))
    return pl.pallas_call(
        functools.partial(local_kernel, key_head),
        grid=(1,),
        out_shape=(
            jax.ShapeDtypeStruct(turned.shape, jnp.bfloat16),
            jax.ShapeDtypeStruct((slots, 2 * HEAD_DIM), jnp.float32),
        ),
        in_specs=in_specs,
        out_specs=(pl.BlockSpec((slots, heads * HEAD_DIM), lambda step: (0, key_head)), VMEM),
        scratch_shapes=[
            pltpu.VMEM((slots, heads * slots), jnp.bfloat16),
            pltpu.VMEM((slots, heads * slots), jnp.bfloat16),
            pltpu.VMEM((heads, HEAD_DIM, slots), jnp.float32),
        ],
        input_output_aliases=aliases,
        compiler_params=vmem(joined[0].shape[0] // 2, 16, 48),
        cost_estimate=pl.CostEstimate(
            flops=4 * 10**9, bytes_accessed=10 * 1024 * 1024, transcendentals=0
        ),
        name="local_terms",
    )(*operands)


def add_kernel(own_ref, arrived_ref, *refs):
    arrived = arrived_ref[:, : own_ref.shape[1]].astype(jnp.float32)
    refs[-1][...] = (own_ref[...] + arrived).astype(jnp.bfloat16)


def add_terms(own, arrived, after):
    return pl.pallas_call(
        add_kernel,
        out_shape=jax.ShapeDtypeStruct(own.shape, jnp.bfloat16),
        in_specs=[VMEM] * (2 + len(after)),
        out_specs=VMEM,
        compiler_params=vmem(0, 16, 16),
        cost_estimate=pl.CostEstimate(flops=10**6, bytes_accessed=10**6, transcendentals=0),
        name="add_terms",
    )(own, arrived, *after)


def finish_kernel(ctx_size, key_heads, meta_ref, table_ref, *refs):
    key_grad_ref, value_grad_ref = refs[-2:]
    owns, terms = refs[:key_heads], list(refs[key_heads:-2])
    slots = table_ref.shape[0]
    live = lax.broadcasted_iota(jnp.int32, (slots, HEAD_DIM), 0) < meta_ref[ctx_size]
    totals = [own[...] for own in owns]
    if relayed(ctx_size):
        second = lax.axis_index("ctx") == 2
        for head in range(key_heads):
            first = terms.pop(0)[...].astype(jnp.float32)
            beside = first[:, 2 * HEAD_DIM :] if first.shape[1] > 2 * HEAD_DIM else 0.0
            totals[head] += jnp.where(second, beside, first[:, : 2 * HEAD_DIM])
    while terms:
        parts = [terms.pop(0)]
        if parts[0].shape[1] == 2 * HEAD_DIM:
            parts += [terms.pop(0) for _ in range(key_heads - 1)]
        term = jnp.concatenate([part[...] for part in parts], axis=1).astype(jnp.float32)
        for head in range(key_heads):
            totals[head] += term[:, 2 * head * HEAD_DIM : 2 * (head + 1) * HEAD_DIM]
    for head, total in enumerate(totals):
        lanes = head_lanes(head)
        key_term = turn_back(total[:, :HEAD_DIM], table_ref[:, :HEAD_DIM], table_ref[:, HEAD_DIM:])
        key_grad_ref[:, lanes] = jnp.where(live, key_term, 0.0).astype(jnp.bfloat16)
        value_grad_ref[:, lanes] = jnp.where(live, total[:, HEAD_DIM:], 0.0).astype(jnp.bfloat16)


def finish(meta, table, owns, terms, ctx_size):
    slots = table.shape[0]
    key_heads = len(owns)
    grad = jax.ShapeDtypeStruct((slots, key_heads * HEAD_DIM), jnp.bfloat16)
    return pl.pallas_call(
        functools.partial(finish_kernel, ctx_size, key_heads),
        out_shape=(grad, grad),
        in_specs=[SMEM] + [VMEM] * (1 + len(owns) + len(terms)),
        out_specs=(VMEM, VMEM),
        compiler_params=vmem(0, 16, 16),
        name="finish",
    )(meta, table, *owns, *terms)


def climb(sent, ctx_size):
    blocks = [sent]
    for hop in range(1, ctx_size):
        pairs = [(shard, shard + 1) for shard in range(hop - 1, ctx_size - 1)]
        blocks.append(lax.ppermute(blocks[-1], "ctx", pairs))
    return blocks[1:]


def descend(terms, ctx_size):
    arrived = []
    for hop, term in enumerate(terms, 1):
        pairs = [(shard + hop, shard) for shard in range(ctx_size - hop)]
        arrived.append(lax.ppermute(term, "ctx", pairs))
    return arrived


def body(positions, queries, keys, values, out_grad):
    ctx_size = lax.axis_size("ctx")
    routed = positions.shape[1]
    key_heads = keys.shape[2] // HEAD_DIM
    meta, table, sent, *sent_heads = prepare(positions, keys[0], values[0], ctx_size)
    turned, turned_t, grad_t = rotate_queries(table, queries[0], out_grad[0])
    if relayed(ctx_size):
        alphas = [lax.ppermute(part, "ctx", [(0, 2), (2, 3)]) for part in sent_heads]
        beta = lax.ppermute(sent, "ctx", [(1, 3)])
        own, handed = own_scores(sent, turned_t, grad_t, sent_heads[1:] + alphas[1:])
        blocks = []
        for head, alpha in enumerate(alphas):
            near, far = sent_heads[0], alpha
            if head > 0:
                near, far = handed[head - 1], handed[head + key_heads - 2]
            gamma = lax.ppermute(near, "ctx", [(0, 1), (1, 2)])
            blocks.append([alpha, beta, gamma, lax.ppermute(far, "ctx", [(2, 3)])])
    else:
        blocks = [climb(sent, ctx_size)] * key_heads
        own, _ = own_scores(sent, turned_t, grad_t, [])
    terms, joined, owns = [], [], []
    for head in range(key_heads):
        after = [terms[-1][1]] if terms else []
        outs = scores(
            head,
            queries.shape[2] // HEAD_DIM // key_heads,
            meta,
            turned,
            out_grad[0],
            turned_t,
            grad_t,
            own[2],
            blocks[head],
            after,
            routed,
            ctx_size,
        )
        terms.append(outs[0])
        joined.append(outs[1])
    local = functools.partial(
        local_terms, meta, table, turned, out_grad[0], sent, own
    )
    dq = None
    if relayed(ctx_size):
        firsts = [lax.ppermute(first, "ctx", [(3, 2), (2, 1)]) for first, _, _ in terms]
        relays = []
        for head in range(key_heads):
            total = add_terms(terms[head][2], firsts[head], owns[-1:])
            relays.append(lax.ppermute(total, "ctx", [(3, 2), (2, 0)] if relays else [(2, 0)]))
            dq, own_terms = local(head, joined[head], dq, [total])
            owns.append(own_terms)
        arrived = firsts + relays + [lax.ppermute(terms[-1][1], "ctx", [(3, 1), (1, 0)])]
    else:
        arrived = [part for hop in zip(*[descend(term, ctx_size) for term in terms]) for part in hop]
        for head in range(key_heads):
            dq, own_terms = local(head, joined[head], dq, [])
            owns.append(own_terms)
    key_grad, value_grad = finish(meta, table, owns, arrived, ctx_size)
    return (dq[None], key_grad[None], value_grad[None])


def solution(mesh):
    split = P(("groups", "dp"), "ctx", "mp")
    return jax.shard_map(
        body,
        mesh=mesh,
        in_specs=(P(("groups", "dp"), None), split, split, split, split),
        out_specs=(split, split, split),
        check_vma=False,
    )
```

```python
import functools
import math

import jax
import jax.numpy as jnp
import numpy as np
from jax import lax
from jax.experimental import pallas as pl
from jax.experimental.pallas import tpu as pltpu
from jax.sharding import PartitionSpec as P

HEAD_DIM = 128
HALF_DIM = HEAD_DIM // 2
TOK_SHARD = 1024
ROPE_BASE = 500000.0
SCORE_SCALE = 1.0 / math.sqrt(HEAD_DIM)
EXP2_SCALE = SCORE_SCALE * math.log2(math.e)
HIDDEN = -1e30
ALIGN = 16
CHUNK = 288
MIB = 1024 * 1024

VMEM = pl.BlockSpec(memory_space=pltpu.VMEM)
SMEM = pl.BlockSpec(memory_space=pltpu.SMEM)
HBM = pl.BlockSpec(memory_space=pltpu.HBM)


def vmem(routed, small, large):
    return pltpu.CompilerParams(vmem_limit_bytes=(small if routed <= 512 else large) * MIB)


def dot(left, right, contract):
    return lax.dot_general(left, right, (contract, ((), ())), preferred_element_type=jnp.float32)


def turn(field, cos_full, sin_full):
    return field * cos_full + pltpu.roll(field, HALF_DIM, 1) * sin_full


def turn_back(field, cos_full, sin_full):
    return field * cos_full - pltpu.roll(field, HALF_DIM, 1) * sin_full


def frequencies():
    ladder = np.arange(HALF_DIM, dtype=np.float32)
    exponent = ladder * np.float32(-2.0 * math.log(ROPE_BASE) / HEAD_DIM)
    freq = np.exp(exponent.astype(np.float64)).astype(np.float32)
    entry = lax.broadcasted_iota(jnp.int32, (1, HEAD_DIM), 1) % HALF_DIM
    row = jnp.zeros((1, HEAD_DIM), jnp.float32)
    for index in range(HALF_DIM):
        row = jnp.where(entry == index, float(freq[index]), row)
    return row


def shard_layout(ctx_size, me, pos, meta_ref):
    shard_of = pos // TOK_SHARD
    for hop in range(2 * ctx_size):
        meta_ref[hop] = 0
    start = jnp.int32(0)
    first = jnp.int32(0)
    my_first = jnp.int32(0)
    for shard in range(ctx_size):
        count = jnp.sum(jnp.where(shard_of == shard, 1.0, 0.0)).astype(jnp.int32)
        my_first = jnp.where(me == shard, first, my_first)

        @pl.when(me >= shard)
        def _():
            meta_ref[me - shard] = start
            meta_ref[ctx_size + me - shard] = count

        first = first + count
        start = start + (count + ALIGN - 1) // ALIGN * ALIGN
    return my_first


def prepare_kernel(
    ctx_size, pos_hbm, keys_hbm, values_hbm, meta_ref, table_ref, sent_ref, *refs
):
    sent_heads, (pos_ref, keys_ref, values_ref, sems) = refs[:-4], refs[-4:]
    sources = (pos_hbm, keys_hbm, values_hbm)
    targets = (pos_ref, keys_ref, values_ref)
    copies = [
        pltpu.make_async_copy(source, target, sems.at[index])
        for index, (source, target) in enumerate(zip(sources, targets))
    ]
    for copy in copies:
        copy.start()
    copies[0].wait()
    slots = keys_ref.shape[0]
    pos = pos_ref[...]
    my_first = shard_layout(ctx_size, lax.axis_index("ctx"), pos, meta_ref)
    shape = (slots, pos.shape[1])
    gap = lax.broadcasted_iota(jnp.int32, shape, 1) - lax.broadcasted_iota(jnp.int32, shape, 0)
    named = jnp.where(gap == my_first, pos.astype(jnp.float32), 0.0)
    angles = jnp.sum(named, axis=1, keepdims=True) * frequencies()
    cos_full = jnp.cos(angles)
    front = lax.broadcasted_iota(jnp.int32, angles.shape, 1) < HALF_DIM
    sin_full = jnp.where(front, -jnp.sin(angles), jnp.sin(angles))
    table_ref[:, :HEAD_DIM] = cos_full
    table_ref[:, HEAD_DIM:] = sin_full
    copies[1].wait()
    copies[2].wait()
    for lane in range(0, keys_ref.shape[1], HEAD_DIM):
        lanes = slice(lane, lane + HEAD_DIM)
        key = turn(keys_ref[:, lanes].astype(jnp.float32), cos_full, sin_full)
        both = jnp.concatenate([key.astype(jnp.bfloat16), values_ref[:, lanes]], axis=1)
        sent_ref[:, 2 * lane : 2 * (lane + HEAD_DIM)] = both
        sent_heads[lane // HEAD_DIM][...] = both


def prepare(positions, keys, values, ctx_size):
    slots, width = keys.shape
    table = jax.ShapeDtypeStruct((slots, 2 * HEAD_DIM), jnp.float32)
    sent = jax.ShapeDtypeStruct((slots, 2 * width), jnp.bfloat16)
    operands = (positions, keys, values)
    return pl.pallas_call(
        functools.partial(prepare_kernel, ctx_size),
        out_shape=(
            jax.ShapeDtypeStruct((2 * ctx_size,), jnp.int32),
            table,
            sent,
            *[jax.ShapeDtypeStruct((slots, 2 * HEAD_DIM), jnp.bfloat16)] * (width // HEAD_DIM),
        ),
        in_specs=[HBM] * 3,
        out_specs=(SMEM,) + (VMEM,) * (2 + width // HEAD_DIM),
        scratch_shapes=[pltpu.VMEM(operand.shape, operand.dtype) for operand in operands]
        + [pltpu.SemaphoreType.DMA((3,))],
        compiler_params=vmem(positions.shape[1], 54, 60),
        name="prepare",
    )(*operands)


def queries_kernel(table_ref, query_ref, grad_ref, turned_ref, turned_t_ref, grad_t_ref):
    for lane in range(0, query_ref.shape[1], HEAD_DIM):
        lanes = slice(lane, lane + HEAD_DIM)
        query = turn(query_ref[:, lanes].astype(jnp.float32), table_ref[:, :HEAD_DIM], table_ref[:, HEAD_DIM:])
        turned_ref[:, lanes] = query.astype(jnp.bfloat16)
        turned_t_ref[lanes, :] = query.T.astype(jnp.bfloat16)
        grad_t_ref[lanes, :] = grad_ref[:, lanes].astype(jnp.float32).T.astype(jnp.bfloat16)


def rotate_queries(table, queries, out_grad):
    slots, width = queries.shape
    straight = jax.ShapeDtypeStruct((slots, width), jnp.bfloat16)
    across = jax.ShapeDtypeStruct((width, slots), jnp.bfloat16)
    return pl.pallas_call(
        queries_kernel,
        out_shape=(straight, across, across),
        in_specs=[VMEM] * 3,
        out_specs=(VMEM,) * 3,
        compiler_params=vmem(0, 16, 16),
        cost_estimate=pl.CostEstimate(
            flops=3 * 10**9, bytes_accessed=4 * 1024 * 1024, transcendentals=0
        ),
        name="rotate_queries",
    )(table, queries, out_grad)


def stacked(ref, lane, heads, width):
    parts = [ref[:width, lane + h * HEAD_DIM : lane + (h + 1) * HEAD_DIM] for h in range(heads)]
    return jnp.concatenate(parts, axis=0)


def beside(ref, rows, heads, slots, width):
    if width == slots:
        return ref[:rows, :]
    columns = [head * slots for head in range(heads)]
    return jnp.concatenate([ref[:rows, start : start + width] for start in columns], axis=1)


def terms_of(probs, score_grads, queries, grads):
    key_term = dot(score_grads, queries, ((1,), (0,))) * SCORE_SCALE
    return jnp.concatenate([key_term, dot(probs, grads, ((1,), (0,)))], axis=1)


def fold(field, join, reduce):
    while field.shape[0] % 16 == 0:
        half = field.shape[0] // 2
        field = join(field[:half], field[half:])
    return reduce(field, axis=0, keepdims=True)


def head_lanes(head):
    return slice(head * HEAD_DIM, (head + 1) * HEAD_DIM)


def key_lanes(key_head):
    return slice(2 * key_head * HEAD_DIM, (2 * key_head + 1) * HEAD_DIM)


def value_lanes(key_head):
    return slice((2 * key_head + 1) * HEAD_DIM, 2 * (key_head + 1) * HEAD_DIM)


def own_kernel(step_heads, count, sent_ref, turned_t_ref, grad_t_ref, *refs):
    weight_ref, product_ref, sums_ref = refs[count : count + 3]
    bias_ref = refs[-1]
    for source, target in zip(refs[:count], refs[count + 3 : -1]):
        target[...] = source[...]
    slots = sent_ref.shape[0]
    key_heads = sent_ref.shape[1] // HEAD_DIM // 2
    heads = turned_t_ref.shape[0] // HEAD_DIM // key_heads
    key_id = lax.broadcasted_iota(jnp.int32, (slots, slots), 0)
    slot_id = lax.broadcasted_iota(jnp.int32, (slots, slots), 1)
    bias_ref[...] = jnp.where(key_id <= slot_id, 0.0, HIDDEN)
    for key_head in range(key_heads):

        def step(index, carry):
            for part in range(step_heads):
                head = key_head * heads + index * step_heads + part
                rows = pl.ds(pl.multiple_of(head * HEAD_DIM, HEAD_DIM), HEAD_DIM)
                scores = dot(sent_ref[:, key_lanes(key_head)], turned_t_ref[rows, :], ((1,), (0,)))
                scores = scores + bias_ref[...]
                prob_grad = dot(sent_ref[:, value_lanes(key_head)], grad_t_ref[rows, :], ((1,), (0,)))
                peak = fold(scores, jnp.maximum, jnp.max)
                weights = jnp.exp2((scores - peak) * EXP2_SCALE)
                weight_ref[head] = weights
                product_ref[head] = prob_grad
                sums_ref[head, 0:1, :] = peak
                sums_ref[head, 1:2, :] = fold(weights, jnp.add, jnp.sum)
                sums_ref[head, 2:3, :] = fold(weights * prob_grad, jnp.add, jnp.sum)
            return carry

        lax.fori_loop(0, heads // step_heads, step, 0)


def own_scores(sent, turned_t, grad_t, handed):
    slots = sent.shape[0]
    heads = turned_t.shape[0] // HEAD_DIM
    square = jax.ShapeDtypeStruct((heads, slots, slots), jnp.float32)
    outs = pl.pallas_call(
        functools.partial(own_kernel, 4, len(handed)),
        out_shape=(
            square,
            square,
            jax.ShapeDtypeStruct((heads, 8, slots), jnp.float32),
            *[jax.ShapeDtypeStruct(array.shape, array.dtype) for array in handed],
        ),
        in_specs=[VMEM] * (3 + len(handed)),
        out_specs=(VMEM,) * (3 + len(handed)),
        scratch_shapes=[pltpu.VMEM((slots, slots), jnp.float32)],
        compiler_params=vmem(0, 16, 16),
        cost_estimate=pl.CostEstimate(
            flops=5 * 10**9, bytes_accessed=10 * 1024 * 1024, transcendentals=0
        ),
        name="own_scores",
    )(sent, turned_t, grad_t, *handed)
    return outs[:3], outs[3:]


def scores_kernel(
    ctx_size,
    sizes,
    step_units,
    key_head,
    meta_ref,
    turned_ref,
    grad_ref,
    turned_t_ref,
    grad_t_ref,
    sums_ref,
    *refs,
):
    count = 4 if relayed(ctx_size) else ctx_size - 1
    inputs, before = refs[:count], refs[count : -6 - ctx_size]
    refs = refs[-6 - ctx_size :]
    terms, refs = refs[: ctx_size - 1], refs[ctx_size - 1 :]
    score_grad_ref, joined_ref, key_ref, value_ref, bias_ref, prob_ref, acc_ref = refs
    slots = turned_ref.shape[0]
    span = bias_ref.shape[0]
    heads = joined_ref.shape[0]
    starts = [pl.multiple_of(meta_ref[hop], ALIGN) for hop in range(ctx_size)]
    my_start, my_count = starts[0], meta_ref[ctx_size]
    sent_hops = list(range(1, ctx_size))
    if relayed(ctx_size):
        last = lax.axis_index("ctx") == ctx_size - 1
        sent_hops = [jnp.where(last, 3, 1), jnp.where(last, 2, 1), jnp.where(last, 1, 2)]

    def blocks_of(lanes, lanes_alone):
        alone = [block.shape[1] == 2 * HEAD_DIM for block in inputs]
        blocks = [block[:, lanes_alone if one else lanes] for block, one in zip(inputs, alone)]
        if relayed(ctx_size):
            alpha, beta, gamma, delta = blocks
            blocks = [jnp.where(last, alpha, gamma), jnp.where(last, beta, alpha), delta]
        return blocks

    for ref, lanes in ((key_ref, key_lanes), (value_ref, value_lanes)):
        ref[slots:span, :] = jnp.zeros((span - slots, HEAD_DIM), jnp.bfloat16)
        blocks = blocks_of(lanes(key_head), lanes(0))
        for hop in range(ctx_size - 1, 0, -1):
            ref[pl.ds(starts[hop], slots), :] = blocks[hop - 1]
    place = lax.broadcasted_iota(jnp.int32, bias_ref.shape, 0)
    seen = place < 0
    for hop in range(1, ctx_size):
        end = starts[hop] + meta_ref[ctx_size + hop]
        seen = seen | ((place >= starts[hop]) & (place < end))
    bias_ref[...] = jnp.where(seen, 0.0, HIDDEN)
    live = lax.broadcasted_iota(jnp.int32, (1, slots), 1) < my_count
    acc_ref[...] = jnp.zeros_like(acc_ref)

    def joint(ref, places, rows, width):
        return jnp.concatenate([ref[rows(place) + (slice(0, width),)] for place in places], axis=1)

    def head_rows(place):
        return (pl.ds(pl.multiple_of((key_head * heads + place) * HEAD_DIM, HEAD_DIM), HEAD_DIM),)

    def units(groups, rows, width):
        side = slots // width
        bias = jnp.concatenate([bias_ref[:rows, :]] * (slots // HEAD_DIM), axis=1)
        alive = jnp.concatenate([live[:, :width]] * side, axis=1)
        queries = [joint(turned_t_ref, group, head_rows, width) for group in groups]
        grads = [joint(grad_t_ref, group, head_rows, width) for group in groups]

        def sums(row):
            index = lambda place: (key_head * heads + place, slice(row, row + 1))
            return [joint(sums_ref, group, index, width) for group in groups]

        own_peaks, own_totals, own_products = sums(0), sums(1), sums(2)
        scores = [dot(key_ref[:rows, :], query, ((1,), (0,))) + bias for query in queries]
        prob_grads = [dot(value_ref[:rows, :], grad, ((1,), (0,))) for grad in grads]
        peaks = [
            jnp.maximum(own, fold(score, jnp.maximum, jnp.max))
            for own, score in zip(own_peaks, scores)
        ]
        weights = [jnp.exp2((score - peak) * EXP2_SCALE) for score, peak in zip(scores, peaks)]
        shares = [jnp.exp2((own - peak) * EXP2_SCALE) for own, peak in zip(own_peaks, peaks)]
        totals = [
            own * share + fold(weight, jnp.add, jnp.sum)
            for own, share, weight in zip(own_totals, shares, weights)
        ]
        products = [
            own * share + fold(weight * prob_grad, jnp.add, jnp.sum)
            for own, share, weight, prob_grad in zip(own_products, shares, weights, prob_grads)
        ]
        inverses = [1.0 / total for total in totals]
        deltas = [product * inverse for product, inverse in zip(products, inverses)]
        inverses = [jnp.where(alive, inverse, 0.0) for inverse in inverses]
        factors = [share * inverse for share, inverse in zip(shares, inverses)]
        probs = [weight * inverse for weight, inverse in zip(weights, inverses)]
        score_grads = [
            (prob * (prob_grad - delta)).astype(jnp.bfloat16)
            for prob, prob_grad, delta in zip(probs, prob_grads, deltas)
        ]
        probs = [prob.astype(jnp.bfloat16) for prob in probs]
        for group, prob, score_grad, factor, delta in zip(
            groups, probs, score_grads, factors, deltas
        ):
            for index, place in enumerate(group):
                part = slice(index * width, (index + 1) * width)
                columns = pl.ds(pl.multiple_of(place * slots, slots), width)
                prob_ref[:rows, columns] = prob[:, part]
                score_grad_ref[:rows, columns] = score_grad[:, part]
                joined_ref[place, 0:1, :width] = factor[:, part]
                joined_ref[place, 1:2, :width] = delta[:, part]
                if width < slots:
                    rest = pl.ds(pl.multiple_of(place * slots + width, HEAD_DIM), slots - width)
                    score_grad_ref[:rows, rest] = jnp.zeros((rows, slots - width), jnp.bfloat16)
                    joined_ref[place, 0:2, width:] = jnp.zeros((2, slots - width), jnp.float32)

    above = {}
    for rows, width in sizes:
        fits = (my_start > above.get(width, 0)) & (my_start <= rows)
        above[width] = rows
        if len(sizes) > 1:
            fits = fits & ((my_count > slots // 2) if width == slots else (my_count <= width))

        @pl.when(fits)
        def _():
            side = slots // width

            def step(index, carry):
                base = index * step_units * side
                units(
                    [[base + part * side + item for item in range(side)] for part in range(step_units)],
                    rows,
                    width,
                )
                return carry

            lax.fori_loop(0, heads // side // step_units, step, 0)
            if rows % CHUNK:
                beyond = slice(rows, rows + CHUNK - rows % CHUNK)
                none = jnp.zeros((CHUNK - rows % CHUNK, heads * slots), jnp.bfloat16)
                score_grad_ref[beyond, :] = none
            lane = key_head * heads * HEAD_DIM
            acc_ref[:rows, :] = terms_of(
                beside(prob_ref, rows, heads, slots, width),
                beside(score_grad_ref, rows, heads, slots, width),
                stacked(turned_ref, lane, heads, width),
                stacked(grad_ref, lane, heads, width),
            )

    @pl.when(my_start == 0)
    def _():
        for place in range(heads):
            inverse = 1.0 / sums_ref[key_head * heads + place, 1:2, :]
            joined_ref[place, 0:1, :] = jnp.where(live, inverse, 0.0)
            joined_ref[place, 1:2, :] = sums_ref[key_head * heads + place, 2:3, :] * inverse

    for hop, term_ref in zip(sent_hops, terms):
        start = pl.multiple_of(meta_ref[hop], ALIGN)
        term = acc_ref[pl.ds(start, slots), :].astype(term_ref.dtype)
        if term_ref.shape == term.shape:
            term_ref[...] = term
        elif term_ref is terms[0]:
            term_ref[:, : 2 * HEAD_DIM] = term
            nearest = acc_ref[pl.ds(starts[1], slots), :].astype(term_ref.dtype)
            term_ref[:, 2 * HEAD_DIM :] = nearest
        else:
            term_ref[:, : -2 * HEAD_DIM] = before[0][...]
            term_ref[:, -2 * HEAD_DIM :] = term


def relayed(ctx_size):
    return ctx_size == 4


def scores(key_head, heads, meta, turned, out_grad, turned_t, grad_t, sums, blocks, after, routed, ctx_size):
    slots = turned.shape[0]
    span = -(-(routed + ctx_size * ALIGN) // CHUNK) * CHUNK
    sizes, step_units = [(span, slots)], 1
    if span == 2 * CHUNK and routed - slots // 2 + ctx_size * ALIGN <= 3 * CHUNK // 2 + ALIGN:
        sizes = [(CHUNK, slots), (3 * CHUNK // 2, slots), (CHUNK, slots // 2), (span, slots // 2)]
        step_units = 4
    terms = [jax.ShapeDtypeStruct((slots, 2 * HEAD_DIM), jnp.bfloat16)] * (ctx_size - 1)
    if relayed(ctx_size):
        if key_head == 0:
            terms[0] = jax.ShapeDtypeStruct((slots, 4 * HEAD_DIM), jnp.bfloat16)
        terms[1] = jax.ShapeDtypeStruct((slots, 2 * (key_head + 1) * HEAD_DIM), jnp.bfloat16)
        terms[2] = jax.ShapeDtypeStruct((slots, 2 * HEAD_DIM), jnp.float32)
    outs = pl.pallas_call(
        functools.partial(scores_kernel, ctx_size, sizes, step_units, key_head),
        out_shape=(
            *terms,
            jax.ShapeDtypeStruct((span, heads * slots), jnp.bfloat16),
            jax.ShapeDtypeStruct((heads, 8, slots), jnp.float32),
            jax.ShapeDtypeStruct((span + slots, HEAD_DIM), jnp.bfloat16),
        ),
        in_specs=[SMEM] + [VMEM] * (5 + len(blocks) + len(after)),
        out_specs=(VMEM,) * (ctx_size + 2),
        scratch_shapes=[
            pltpu.VMEM((span + slots, HEAD_DIM), jnp.bfloat16),
            pltpu.VMEM((span, HEAD_DIM), jnp.float32),
            pltpu.VMEM((span, heads * slots), jnp.bfloat16),
            pltpu.VMEM((span + slots, 2 * HEAD_DIM), jnp.float32),
        ],
        compiler_params=vmem(routed, 20, 60),
        cost_estimate=pl.CostEstimate(
            flops=4 * 10**9, bytes_accessed=6 * 1024 * 1024, transcendentals=0
        ),
        name="scores",
    )(meta, turned, out_grad, turned_t, grad_t, sums, *blocks, *after)
    return outs[: ctx_size - 1], outs[ctx_size - 1 :]


def local_kernel(
    key_head,
    meta_ref,
    table_ref,
    turned_ref,
    grad_ref,
    sent_ref,
    weight_ref,
    product_ref,
    score_grad_ref,
    joined_ref,
    key_ref,
    *refs,
):
    dq_ref, own_ref, prob_ref, own_grad_ref, sum_ref = refs[-5:]
    slots = turned_ref.shape[0]
    heads = joined_ref.shape[0]
    span = score_grad_ref.shape[0]
    my_start = meta_ref[0]
    own_key_t = sent_ref[:, key_lanes(key_head)].astype(jnp.float32).T.astype(jnp.bfloat16)
    for head in range(heads):
        columns = slice(head * slots, (head + 1) * slots)
        prob = weight_ref[key_head * heads + head] * joined_ref[head, 0:1, :]
        prob_ref[:, columns] = prob.astype(jnp.bfloat16)
        product = product_ref[key_head * heads + head] - joined_ref[head, 1:2, :]
        score_grad = (prob * product).astype(jnp.bfloat16)
        own_grad_ref[:, columns] = score_grad
        sum_ref[head] = dot(own_key_t, score_grad, ((1,), (0,)))
    for chunk in range(0, span, CHUNK):

        @pl.when(chunk < my_start)
        def _():
            rows = slice(chunk, chunk + CHUNK)
            key_t = key_ref[rows, :].astype(jnp.float32).T.astype(jnp.bfloat16)
            for head in range(heads):
                score_grad = score_grad_ref[rows, head * slots : (head + 1) * slots]
                sum_ref[head] += dot(key_t, score_grad, ((1,), (0,)))

    lane = key_head * heads * HEAD_DIM
    for head in range(heads):
        grad = turn_back((sum_ref[head] * SCORE_SCALE).T, table_ref[:, :HEAD_DIM], table_ref[:, HEAD_DIM:])
        dq_ref[:, head * HEAD_DIM : (head + 1) * HEAD_DIM] = grad.astype(jnp.bfloat16)
    own_ref[...] = terms_of(
        prob_ref[...],
        own_grad_ref[...],
        stacked(turned_ref, lane, heads, slots),
        stacked(grad_ref, lane, heads, slots),
    )


def local_terms(meta, table, turned, out_grad, sent, own, key_head, joined, dq, after):
    slots = turned.shape[0]
    heads = joined[1].shape[0]
    weight, product, _ = own
    operands = [meta, table, turned, out_grad, sent, weight, product, *joined, *after]
    in_specs = [SMEM] + [VMEM] * (len(operands) - 1)
    aliases = {}
    if dq is not None:
        aliases = {len(operands): 0}
        operands.append(dq)
        in_specs.append(pl.BlockSpec(memory_space=pl.ANY))
    return pl.pallas_call(
        functools.partial(local_kernel, key_head),
        grid=(1,),
        out_shape=(
            jax.ShapeDtypeStruct(turned.shape, jnp.bfloat16),
            jax.ShapeDtypeStruct((slots, 2 * HEAD_DIM), jnp.float32),
        ),
        in_specs=in_specs,
        out_specs=(pl.BlockSpec((slots, heads * HEAD_DIM), lambda step: (0, key_head)), VMEM),
        scratch_shapes=[
            pltpu.VMEM((slots, heads * slots), jnp.bfloat16),
            pltpu.VMEM((slots, heads * slots), jnp.bfloat16),
            pltpu.VMEM((heads, HEAD_DIM, slots), jnp.float32),
        ],
        input_output_aliases=aliases,
        compiler_params=vmem(joined[0].shape[0] // 2, 16, 48),
        cost_estimate=pl.CostEstimate(
            flops=4 * 10**9, bytes_accessed=10 * 1024 * 1024, transcendentals=0
        ),
        name="local_terms",
    )(*operands)


def add_kernel(own_ref, arrived_ref, *refs):
    arrived = arrived_ref[:, : own_ref.shape[1]].astype(jnp.float32)
    refs[-1][...] = (own_ref[...] + arrived).astype(jnp.bfloat16)


def add_terms(own, arrived, after):
    return pl.pallas_call(
        add_kernel,
        out_shape=jax.ShapeDtypeStruct(own.shape, jnp.bfloat16),
        in_specs=[VMEM] * (2 + len(after)),
        out_specs=VMEM,
        compiler_params=vmem(0, 16, 16),
        cost_estimate=pl.CostEstimate(flops=10**6, bytes_accessed=10**6, transcendentals=0),
        name="add_terms",
    )(own, arrived, *after)


def finish_kernel(ctx_size, key_heads, meta_ref, table_ref, *refs):
    key_grad_ref, value_grad_ref = refs[-2:]
    owns, terms = refs[:key_heads], list(refs[key_heads:-2])
    slots = table_ref.shape[0]
    live = lax.broadcasted_iota(jnp.int32, (slots, HEAD_DIM), 0) < meta_ref[ctx_size]
    totals = [own[...] for own in owns]
    if relayed(ctx_size):
        second = lax.axis_index("ctx") == 2
        for head in range(key_heads):
            first = terms.pop(0)[...].astype(jnp.float32)
            beside = first[:, 2 * HEAD_DIM :] if first.shape[1] > 2 * HEAD_DIM else 0.0
            totals[head] += jnp.where(second, beside, first[:, : 2 * HEAD_DIM])
    while terms:
        parts = [terms.pop(0)]
        if parts[0].shape[1] == 2 * HEAD_DIM:
            parts += [terms.pop(0) for _ in range(key_heads - 1)]
        term = jnp.concatenate([part[...] for part in parts], axis=1).astype(jnp.float32)
        for head in range(key_heads):
            totals[head] += term[:, 2 * head * HEAD_DIM : 2 * (head + 1) * HEAD_DIM]
    for head, total in enumerate(totals):
        lanes = head_lanes(head)
        key_term = turn_back(total[:, :HEAD_DIM], table_ref[:, :HEAD_DIM], table_ref[:, HEAD_DIM:])
        key_grad_ref[:, lanes] = jnp.where(live, key_term, 0.0).astype(jnp.bfloat16)
        value_grad_ref[:, lanes] = jnp.where(live, total[:, HEAD_DIM:], 0.0).astype(jnp.bfloat16)


def finish(meta, table, owns, terms, ctx_size):
    slots = table.shape[0]
    key_heads = len(owns)
    grad = jax.ShapeDtypeStruct((slots, key_heads * HEAD_DIM), jnp.bfloat16)
    return pl.pallas_call(
        functools.partial(finish_kernel, ctx_size, key_heads),
        out_shape=(grad, grad),
        in_specs=[SMEM] + [VMEM] * (1 + len(owns) + len(terms)),
        out_specs=(VMEM, VMEM),
        compiler_params=vmem(0, 16, 16),
        name="finish",
    )(meta, table, *owns, *terms)


def climb(sent, ctx_size):
    blocks = [sent]
    for hop in range(1, ctx_size):
        pairs = [(shard, shard + 1) for shard in range(hop - 1, ctx_size - 1)]
        blocks.append(lax.ppermute(blocks[-1], "ctx", pairs))
    return blocks[1:]


def descend(terms, ctx_size):
    arrived = []
    for hop, term in enumerate(terms, 1):
        pairs = [(shard + hop, shard) for shard in range(ctx_size - hop)]
        arrived.append(lax.ppermute(term, "ctx", pairs))
    return arrived


def body(positions, queries, keys, values, out_grad):
    ctx_size = lax.axis_size("ctx")
    routed = positions.shape[1]
    key_heads = keys.shape[2] // HEAD_DIM
    meta, table, sent, *sent_heads = prepare(positions, keys[0], values[0], ctx_size)
    turned, turned_t, grad_t = rotate_queries(table, queries[0], out_grad[0])
    if relayed(ctx_size):
        alphas = [lax.ppermute(part, "ctx", [(0, 2), (2, 3)]) for part in sent_heads]
        own, handed = own_scores(sent, turned_t, grad_t, sent_heads[1:] + alphas[1:])
        blocks = []
        for head, alpha in enumerate(alphas):
            near, far = sent_heads[0], alpha
            if head > 0:
                near, far = handed[head - 1], handed[head + key_heads - 2]
            beta = lax.ppermute(near, "ctx", [(1, 3)])
            gamma = lax.ppermute(near, "ctx", [(0, 1), (1, 2)])
            blocks.append([alpha, beta, gamma, lax.ppermute(far, "ctx", [(2, 3)])])
    else:
        blocks = [climb(sent, ctx_size)] * key_heads
        own, _ = own_scores(sent, turned_t, grad_t, [])
    terms, joined, owns = [], [], []
    for head in range(key_heads):
        after = [terms[-1][1]] if terms else []
        outs = scores(
            head,
            queries.shape[2] // HEAD_DIM // key_heads,
            meta,
            turned,
            out_grad[0],
            turned_t,
            grad_t,
            own[2],
            blocks[head],
            after,
            routed,
            ctx_size,
        )
        terms.append(outs[0])
        joined.append(outs[1])
    local = functools.partial(
        local_terms, meta, table, turned, out_grad[0], sent, own
    )
    dq = None
    if relayed(ctx_size):
        firsts = [lax.ppermute(first, "ctx", [(3, 2), (2, 1)]) for first, _, _ in terms]
        relays = []
        for head in range(key_heads):
            total = add_terms(terms[head][2], firsts[head], owns[-1:])
            relays.append(lax.ppermute(total, "ctx", [(3, 2), (2, 0)] if relays else [(2, 0)]))
            dq, own_terms = local(head, joined[head], dq, [total])
            owns.append(own_terms)
        arrived = firsts + relays + [lax.ppermute(terms[-1][1], "ctx", [(3, 1), (1, 0)])]
    else:
        arrived = [part for hop in zip(*[descend(term, ctx_size) for term in terms]) for part in hop]
        for head in range(key_heads):
            dq, own_terms = local(head, joined[head], dq, [])
            owns.append(own_terms)
    key_grad, value_grad = finish(meta, table, owns, arrived, ctx_size)
    return (dq[None], key_grad[None], value_grad[None])


def solution(mesh):
    split = P(("groups", "dp"), "ctx", "mp")
    return jax.shard_map(
        body,
        mesh=mesh,
        in_specs=(P(("groups", "dp"), None), split, split, split, split),
        out_specs=(split, split, split),
        check_vma=False,
    )
```
